32 devices in a mesh: dp: 16 (over z, y, x), pair: 2 (over core).
Axes of the slice: x: 2, y: 2, z: 4, core: 2. Of those that a mesh axis runs over, the one named last changes fastest.
Arguments:
- text_inputs: bfloat16 [8192, 768], P(('dp', 'pair')), may hold values from -6 to 6
- region_features: bfloat16 [8192, 2048], P(('dp', 'pair')), may hold values from -6 to 6
- text_masked: int32 [8192], P(('dp', 'pair')), may hold values 0 or 1
- region_masked: int32 [8192], P(('dp', 'pair')), may hold values 0 or 1
- text_anchors: int32 [2, 8192], P(None, ('dp', 'pair')), may hold values from 0 to 1023
- region_anchors: int32 [2, 8192], P(None, ('dp', 'pair')), may hold values from 0 to 1023
- backbone_weight: bfloat16 [2048, 768], P(('dp', 'pair')), may hold values from -0.125 to 0.125
- batch_gain: bfloat16 [768], P(('dp', 'pair')), may hold values from 0.5 to 1.5
- batch_shift: bfloat16 [768], P(('dp', 'pair')), may hold values from -4 to 4
- text_blank: bfloat16 [768], P(('dp', 'pair')), may hold values from -6 to 6
- region_blank: bfloat16 [768], P(('dp', 'pair')), may hold values from -6 to 6
- position_table: bfloat16 [1024, 1536], P(('dp', 'pair')), may hold values from -6 to 6
- stream_weights: bfloat16 [768, 7680], P(('dp', 'pair')), may hold values from -0.21875 to 0.21875
- linear_bias: bfloat16 [256, 12], P(('dp', 'pair')), may hold values from -6 to 6
- planar_bias: bfloat16 [256, 12], P(('dp', 'pair')), may hold values from -6 to 6
- merge_weight: bfloat16 [768, 768], P(('dp', 'pair')), may hold values from -1.75 to 1.75
- mixer_gain: bfloat16 [768], P(('dp', 'pair')), may hold values from 0.5 to 1.5
- mixer_shift: bfloat16 [768], P(('dp', 'pair')), may hold values from -4 to 4
- expand_weight: bfloat16 [768, 3072], P(('dp', 'pair')), may hold values from -0.21875 to 0.21875
- expand_bias: bfloat16 [3072], P(('dp', 'pair')), may hold values from -4 to 4
- reduce_weight: bfloat16 [3072, 768], P(('dp', 'pair')), may hold values from -0.109375 to 0.109375
- reduce_bias: bfloat16 [768], P(('dp', 'pair')), may hold values from -4 to 4
- output_gain: bfloat16 [768], P(('dp', 'pair')), may hold values from 0.5 to 1.5
- output_shift: bfloat16 [768], P(('dp', 'pair')), may hold values from -4 to 4
- cotangent: bfloat16 [8192, 768], P(('dp', 'pair')), may hold values from -6 to 6
Outputs:
- layer_output: bfloat16 [8192, 768], P(('dp', 'pair'))
- text_gradient: float32 [8192, 768], P(('dp', 'pair'))
- feature_gradient: float32 [8192, 2048], P(('dp', 'pair'))
- backbone_weight_gradient: float32 [2048, 768], P(('dp', 'pair'))
- batch_gain_gradient: float32 [768], P(('dp', 'pair'))
- batch_shift_gradient: float32 [768], P(('dp', 'pair'))
- text_blank_gradient: float32 [768], P(('dp', 'pair'))
- region_blank_gradient: float32 [768], P(('dp', 'pair'))
- position_table_gradient: float32 [1024, 1536], P(('dp', 'pair'))
- stream_weights_gradient: float32 [768, 7680], P(('dp', 'pair'))
- linear_bias_gradient: float32 [256, 12], P(('dp', 'pair'))
- planar_bias_gradient: float32 [256, 12], P(('dp', 'pair'))
- merge_weight_gradient: float32 [768, 768], P(('dp', 'pair'))
- mixer_gain_gradient: float32 [768], P(('dp', 'pair'))
- mixer_shift_gradient: float32 [768], P(('dp', 'pair'))
- expand_weight_gradient: float32 [768, 3072], P(('dp', 'pair'))
- expand_bias_gradient: float32 [3072], P(('dp', 'pair'))
- reduce_weight_gradient: float32 [3072, 768], P(('dp', 'pair'))
- reduce_bias_gradient: float32 [768], P(('dp', 'pair'))
- output_gain_gradient: float32 [768], P(('dp', 'pair'))
- output_shift_gradient: float32 [768], P(('dp', 'pair'))
The draws below stay inside these ranges and needn't reach their ends.
All inputs are finite; a program needn't handle non-finite values. No bound on the sum of `text_masked` or of `region_masked` on one device may be relied on, other than what follows from the above.
Results may differ from the reference program's by a relative error of at most 0.017.
Values may be sent and summed in bfloat16 or wider, within the bound.
A program may use at most 320 MiB of HBM per device.

```python
import jax
import jax.numpy as jnp
from jax import lax

HEADS = 12
HEAD_DIM = 64
FF = 3072
FEAT = 2048
COORDS = 1024
REL_B = 256
SP_SIDE = 16
PAGE_TOKENS = 256
MODEL_WIDTH = 768
SP_B = 256
COORD_STEP = 128
TOKENS = 8192


def with_ends(result, key, low, top_value):
    dims = result.shape
    place = [jax.random.randint(jax.random.fold_in(key, axis), (), 0, dims[axis]) for axis in range(len(dims))]
    result = result.at[tuple(place)].set(low)
    longest = dims.index(max(dims))
    place[longest] = (place[longest] + 1) % dims[longest]
    return result.at[tuple(place)].set(top_value)


def levels(key, extent, split, least, high):
    loudness = 1.0
    for axis_at, blocks in split:
        draws = jax.random.uniform(jax.random.fold_in(jax.random.fold_in(key, 6), axis_at), (blocks,), jnp.float32, least / len(split), high / len(split))
        loudness = loudness * jnp.repeat(jnp.exp(draws), extent[axis_at] // blocks).reshape((-1,) + (1,) * (len(extent) - 1 - axis_at))
    return loudness


def gaussian(stream_key, shape, width, reach, cuts=(), kind=jnp.bfloat16):
    result = jax.random.normal(stream_key, shape, jnp.float32) * width
    if len(cuts) > 0:
        result = levels(stream_key, shape, cuts, -0.22, 0.18) * result
    return jnp.clip(result, min=-reach, max=reach).astype(kind)


def setup_inputs(seed: int = 0) -> dict:
    key_of = jax.random.split(jax.random.key(seed), 26)
    return {
        "text_inputs": gaussian(key_of[0], (TOKENS, MODEL_WIDTH), 1.0, 6.0, ((0, 32),)),
        "region_features": gaussian(key_of[1], (TOKENS, FEAT), 1.0, 6.0, ((0, 32),)),
        "text_masked": with_ends((jax.random.randint(key_of[2], (TOKENS,), 0, 100) < 15).astype(jnp.int32), jax.random.fold_in(key_of[2], 1), 0, 1),
        "region_masked": with_ends((jax.random.randint(key_of[3], (TOKENS,), 0, 100) < 15).astype(jnp.int32), jax.random.fold_in(key_of[3], 1), 0, 1),
        "text_anchors": with_ends(jax.random.randint(key_of[4], (2, TOKENS), 0, COORDS), jax.random.fold_in(key_of[4], 1), 0, COORDS - 1).astype(jnp.int32),
        "region_anchors": with_ends(jax.random.randint(key_of[5], (2, TOKENS), 0, COORDS), jax.random.fold_in(key_of[5], 1), 0, COORDS - 1).astype(jnp.int32),
        "backbone_weight": gaussian(key_of[6], (FEAT, MODEL_WIDTH), FEAT ** -0.5, 0.125, ((0, 32),)),
        "batch_gain": jnp.clip(1.0 + 0.1 * jax.random.normal(key_of[7], (MODEL_WIDTH,), jnp.float32), 0.5, 1.5).astype(jnp.bfloat16),
        "batch_shift": gaussian(key_of[8], (MODEL_WIDTH,), 0.3, 4.0, ((0, 32),)),
        "text_blank": gaussian(key_of[9], (MODEL_WIDTH,), 1.0, 6.0, ((0, 32),)),
        "region_blank": gaussian(key_of[10], (MODEL_WIDTH,), 1.0, 6.0, ((0, 32),)),
        "position_table": gaussian(key_of[11], (COORDS, 2 * MODEL_WIDTH), 0.5, 6.0, ((0, 32),)),
        "stream_weights": gaussian(key_of[12], (MODEL_WIDTH, 10 * MODEL_WIDTH), MODEL_WIDTH ** -0.5, 0.21875, ((0, 32),)),
        "linear_bias": gaussian(key_of[13], (REL_B, HEADS), 0.5, 6.0, ((0, 32),)),
        "planar_bias": gaussian(key_of[14], (SP_B, HEADS), 0.5, 6.0, ((0, 32),)),
        "merge_weight": gaussian(key_of[15], (MODEL_WIDTH, MODEL_WIDTH), (MODEL_WIDTH // 64) ** -0.5, 1.75, ((0, 32),)),
        "mixer_gain": jnp.clip(1.0 + 0.1 * jax.random.normal(key_of[16], (MODEL_WIDTH,), jnp.float32), 0.5, 1.5).astype(jnp.bfloat16),
        "mixer_shift": gaussian(key_of[17], (MODEL_WIDTH,), 0.3, 4.0, ((0, 32),)),
        "expand_weight": gaussian(key_of[18], (MODEL_WIDTH, FF), MODEL_WIDTH ** -0.5, 0.21875, ((0, 32),)),
        "expand_bias": gaussian(key_of[19], (FF,), 0.3, 4.0, ((0, 32),)),
        "reduce_weight": gaussian(key_of[20], (FF, MODEL_WIDTH), FF ** -0.5, 0.109375, ((0, 32),)),
        "reduce_bias": gaussian(key_of[21], (MODEL_WIDTH,), 0.3, 4.0, ((0, 32),)),
        "output_gain": jnp.clip(1.0 + 0.1 * jax.random.normal(key_of[22], (MODEL_WIDTH,), jnp.float32), 0.5, 1.5).astype(jnp.bfloat16),
        "output_shift": gaussian(key_of[23], (MODEL_WIDTH,), 0.3, 4.0, ((0, 32),)),
        "cotangent": gaussian(key_of[24], (TOKENS, MODEL_WIDTH), 1.0, 6.0, ((0, 32),)),
    }


@jax.custom_vjp
def low(v):
    return lax.optimization_barrier(v.astype(jnp.bfloat16)).astype(jnp.float32)

@jax.custom_vjp
def low_back(v):
    return v

def low_keep(v):
    return (low(v), None)

def low_pass(kept, grad):
    return (grad,)

def back_keep(v):
    return (v, None)

def back_low(kept, grad):
    return (low(grad),)
low.defvjp(low_keep, low_pass)
low_back.defvjp(back_keep, back_low)
highest = lax.Precision.HIGHEST
norm_epsilon = 1e-05
batch_epsilon = 1e-05

def product(left, right):
    return jnp.dot(left, right, precision=highest, preferred_element_type=jnp.float32)

def layer_normalize(values, scale_vec, shift_vec):
    center = values - lax.optimization_barrier(jnp.mean(values, axis=-1, keepdims=True))
    spread = lax.optimization_barrier(jnp.mean(center * center, axis=-1, keepdims=True))
    return center * lax.rsqrt(spread + norm_epsilon) * scale_vec + shift_vec

def relative_index():
    places = jnp.arange(PAGE_TOKENS, dtype=jnp.int32)
    return jnp.clip(places[None, :] - places[:, None], -(REL_B // 2), REL_B // 2 - 1) + REL_B // 2

def spatial_index(anchor_rows):
    delta_x = (anchor_rows[0][None, :] - anchor_rows[0][:, None]) // COORD_STEP + SP_SIDE // 2
    delta_y = (anchor_rows[1][None, :] - anchor_rows[1][:, None]) // COORD_STEP + SP_SIDE // 2
    return (delta_x * SP_SIDE + delta_y).astype(jnp.int32)

def split_heads(matrix):
    return matrix.reshape(PAGE_TOKENS, HEADS, HEAD_DIM)

def stream(inputs, spatial, weights, linear_table, planar_table, rel_places, box_places):
    tokens_low = low(inputs)
    spatial_low = low(spatial)
    queries = low(low_back(product(tokens_low, weights[:, 0:MODEL_WIDTH])))
    keys_all = low(low_back(product(tokens_low, weights[:, MODEL_WIDTH:2 * MODEL_WIDTH])))
    values_all = low(low_back(product(tokens_low, weights[:, 2 * MODEL_WIDTH:3 * MODEL_WIDTH])))
    spatial_queries = low(low_back(product(spatial_low, weights[:, 3 * MODEL_WIDTH:4 * MODEL_WIDTH])))
    spatial_keys = low(low_back(product(spatial_low, weights[:, 4 * MODEL_WIDTH:5 * MODEL_WIDTH])))
    logits = jnp.einsum('ihe,jhe->hij', split_heads(queries), split_heads(keys_all), precision=highest)
    logits = logits + jnp.einsum('ihe,jhe->hij', split_heads(spatial_queries), split_heads(spatial_keys), precision=highest)
    logits = logits * HEAD_DIM ** (-0.5) + linear_table.T[:, rel_places] + planar_table.T[:, box_places]
    logits = low_back(logits)
    softmax_rows = low(jax.nn.softmax(logits, axis=-1))
    mixed = jnp.einsum('hij,jhe->ihe', softmax_rows, split_heads(values_all), precision=highest)
    return low_back(mixed.reshape(PAGE_TOKENS, MODEL_WIDTH))

def page_layer(pieces, params):
    text_in, region_in, text_space, region_space, text_box, region_box = pieces
    stream_weights, linear_bias, planar_bias, merge_weight, mixer_gain, mixer_shift, expand_weight, expand_bias, reduce_weight, reduce_bias, output_gain, output_shift = params
    rel_places = relative_index()
    text_out = stream(text_in, text_space, stream_weights[:, :5 * MODEL_WIDTH], linear_bias, planar_bias, rel_places, spatial_index(text_box))
    region_out = stream(region_in, region_space, stream_weights[:, 5 * MODEL_WIDTH:], linear_bias, planar_bias, rel_places, spatial_index(region_box))
    attended = low_back(product(low(text_out + region_out), merge_weight))
    hidden = layer_normalize(text_in + region_in + attended, mixer_gain, mixer_shift)
    inner = low_back(product(low(hidden), expand_weight) + expand_bias)
    dense = low_back(product(low(jax.nn.gelu(inner, approximate=False)), reduce_weight)) + reduce_bias
    return layer_normalize(hidden + dense, output_gain, output_shift)

def forward(text_masked, region_masked, text_anchors, region_anchors, text_inputs, region_features, backbone_weight, batch_gain, batch_shift, text_blank, region_blank, position_table, stream_weights, linear_bias, planar_bias, merge_weight, mixer_gain, mixer_shift, expand_weight, expand_bias, reduce_weight, reduce_bias, output_gain, output_shift):
    text_start = jnp.where(text_masked[:, None] == 1, text_blank[None, :], text_inputs)
    conv_out = low_back(product(region_features, backbone_weight))
    batch_center = conv_out - lax.optimization_barrier(jnp.mean(conv_out, axis=0))
    batch_spread = lax.optimization_barrier(jnp.mean(batch_center * batch_center, axis=0))
    normal_feat = batch_center * lax.rsqrt(batch_spread + batch_epsilon) * batch_gain + batch_shift
    region_start = jnp.where(region_masked[:, None] == 1, region_blank[None, :], normal_feat)
    text_space = position_table[text_anchors[0], :MODEL_WIDTH] + position_table[text_anchors[1], MODEL_WIDTH:]
    region_space = position_table[region_anchors[0], :MODEL_WIDTH] + position_table[region_anchors[1], MODEL_WIDTH:]
    page_count = TOKENS // PAGE_TOKENS

    def by_page(matrix):
        return matrix.reshape(page_count, PAGE_TOKENS, matrix.shape[-1])

    def anchors_by_page(anchor_rows):
        return anchor_rows.reshape(2, page_count, PAGE_TOKENS).transpose(1, 0, 2)
    params = (stream_weights, linear_bias, planar_bias, merge_weight, mixer_gain, mixer_shift, expand_weight, expand_bias, reduce_weight, reduce_bias, output_gain, output_shift)
    step_fn = jax.checkpoint(lambda pieces: page_layer(pieces, params))
    outputs = lax.map(step_fn, (by_page(text_start), by_page(region_start), by_page(text_space), by_page(region_space), anchors_by_page(text_anchors), anchors_by_page(region_anchors)))
    return outputs.reshape(TOKENS, MODEL_WIDTH)

def reference(text_inputs, region_features, text_masked, region_masked, text_anchors, region_anchors, backbone_weight, batch_gain, batch_shift, text_blank, region_blank, position_table, stream_weights, linear_bias, planar_bias, merge_weight, mixer_gain, mixer_shift, expand_weight, expand_bias, reduce_weight, reduce_bias, output_gain, output_shift, cotangent):
    floats = tuple((item.astype(jnp.float32) for item in (text_inputs, region_features, backbone_weight, batch_gain, batch_shift, text_blank, region_blank, position_table, stream_weights, linear_bias, planar_bias, merge_weight, mixer_gain, mixer_shift, expand_weight, expand_bias, reduce_weight, reduce_bias, output_gain, output_shift)))

    def run(*float_args):
        return forward(text_masked, region_masked, text_anchors, region_anchors, *float_args)
    layer_output, pullback = jax.vjp(run, *floats)
    text_gradient, feature_gradient, backbone_weight_gradient, batch_gain_gradient, batch_shift_gradient, text_blank_gradient, region_blank_gradient, position_table_gradient, stream_weights_gradient, linear_bias_gradient, planar_bias_gradient, merge_weight_gradient, mixer_gain_gradient, mixer_shift_gradient, expand_weight_gradient, expand_bias_gradient, reduce_weight_gradient, reduce_bias_gradient, output_gain_gradient, output_shift_gradient = pullback(cotangent.astype(jnp.float32))
    return (layer_output.astype(jnp.bfloat16), text_gradient, feature_gradient, backbone_weight_gradient, batch_gain_gradient, batch_shift_gradient, text_blank_gradient, region_blank_gradient, position_table_gradient, stream_weights_gradient, linear_bias_gradient, planar_bias_gradient, merge_weight_gradient, mixer_gain_gradient, mixer_shift_gradient, expand_weight_gradient, expand_bias_gradient, reduce_weight_gradient, reduce_bias_gradient, output_gain_gradient, output_shift_gradient)
```

```python
from functools import partial

import jax
import jax.numpy as jnp
from jax import lax
from jax.experimental import pallas as pl
from jax.experimental.pallas import tpu as pltpu
from jax.sharding import PartitionSpec as P

HEADS = 12
HEAD_DIM = 64
COORDS = 1024
REL_B = 256
SP_SIDE = 16
PAGE_TOKENS = 256
MODEL_WIDTH = 768
SP_B = 256
COORD_STEP = 128
PAIRS = HEADS // 2
LANES = 2 * HEAD_DIM


def dot_nt(left, right):
    return lax.dot_general(left, right, (((1,), (1,)), ((), ())), preferred_element_type=jnp.float32)


def dot_tn(left, right):
    return lax.dot_general(left, right, (((0,), (0,)), ((), ())), preferred_element_type=jnp.float32)


def dot_nn(left, right):
    return lax.dot_general(left, right, (((1,), (0,)), ((), ())), preferred_element_type=jnp.float32)


def head_columns(stream, kind, pair):
    return pl.ds(pl.multiple_of(((5 * stream + kind) * PAIRS + pair) * LANES, LANES), LANES)


def attend_kernel(proj_ref, linear_ref, planar_ref, rows_ref, cols_ref, merged_ref, probs_ref, box_ref):
    pair = pl.program_id(0)

    @pl.when(pair == 0)
    def _():
        for stream in range(2):
            part = []
            for axis in range(2):
                along = rows_ref[2 * stream + axis : 2 * stream + axis + 1, :]
                down = cols_ref[:, 2 * stream + axis : 2 * stream + axis + 1]
                part.append(((along - down) >> 7) + SP_SIDE // 2)
            box_ref[stream] = part[0] * SP_SIDE + part[1]

    lane_head = lax.broadcasted_iota(jnp.int32, (PAGE_TOKENS, LANES), 1) // HEAD_DIM
    mixed = [None, None]
    for inner in range(2):
        head = 2 * pair + inner
        mine = lane_head == inner
        spread = jnp.broadcast_to(linear_ref[head], (PAGE_TOKENS, 2 * PAGE_TOKENS))
        linear_term = pltpu.roll(spread, PAGE_TOKENS + 1, 1, stride=1, stride_axis=0)[:, :PAGE_TOKENS]
        low_table = jnp.broadcast_to(planar_ref[head, :, :128], (PAGE_TOKENS, 128))
        high_table = jnp.broadcast_to(planar_ref[head, :, 128:], (PAGE_TOKENS, 128))
        total = None
        for stream in range(2):
            pieces = [proj_ref[:, head_columns(stream, kind, pair)] for kind in range(5)]
            zero = jnp.zeros_like(pieces[0])
            left = jnp.concatenate([jnp.where(mine, pieces[0], zero), jnp.where(mine, pieces[3], zero)], axis=1)
            right = jnp.concatenate([pieces[1], pieces[4]], axis=1)
            logits = dot_nt(left, right) * HEAD_DIM ** (-0.5)
            planar = []
            for half in range(2):
                box = box_ref[stream, :, 128 * half : 128 * half + 128]
                place = box & 127
                planar.append(
                    jnp.where(
                        box < 128,
                        jnp.take_along_axis(low_table, place, axis=1),
                        jnp.take_along_axis(high_table, place, axis=1),
                    )
                )
            logits = logits + linear_term + jnp.concatenate(planar, axis=1)
            top = jnp.max(logits, axis=-1, keepdims=True)
            shifted = jnp.exp(logits - top)
            probs = shifted / jnp.sum(shifted, axis=-1, keepdims=True)
            probs_ref[stream, inner] = probs
            part = dot_nn(probs.astype(jnp.bfloat16), pieces[2])
            total = part if total is None else total + part
        mixed[inner] = total
    merged_ref[...] = jnp.where(lane_head == 0, mixed[0], mixed[1]).astype(jnp.bfloat16)


def attend(proj, linear_ext, planar_rows, anchor_rows, anchor_cols):
    return pl.pallas_call(
        attend_kernel,
        grid=(PAIRS,),
        in_specs=[
            pl.BlockSpec(proj.shape, lambda i: (0, 0)),
            pl.BlockSpec(linear_ext.shape, lambda i: (0, 0, 0)),
            pl.BlockSpec(planar_rows.shape, lambda i: (0, 0, 0)),
            pl.BlockSpec(anchor_rows.shape, lambda i: (0, 0)),
            pl.BlockSpec(anchor_cols.shape, lambda i: (0, 0)),
        ],
        out_specs=[
            pl.BlockSpec((PAGE_TOKENS, LANES), lambda i: (0, i)),
            pl.BlockSpec((2, 2, PAGE_TOKENS, PAGE_TOKENS), lambda i: (0, i, 0, 0)),
        ],
        out_shape=[
            jax.ShapeDtypeStruct((PAGE_TOKENS, MODEL_WIDTH), jnp.bfloat16),
            jax.ShapeDtypeStruct((2, HEADS, PAGE_TOKENS, PAGE_TOKENS), jnp.float32),
        ],
        scratch_shapes=[pltpu.VMEM((2, PAGE_TOKENS, PAGE_TOKENS), jnp.int32)],
        compiler_params=pltpu.CompilerParams(vmem_limit_bytes=48 << 20),
        name="attend",
    )(proj, linear_ext, planar_rows, anchor_rows, anchor_cols)


def attend_back_kernel(
    proj_ref, probs_ref, upstream_ref, rows_ref, cols_ref, grad_ref, linear_ref, planar_ref,
    place_ref, turned_ref, mask_ref, flip_ref,
):
    pair = pl.program_id(0)

    @pl.when(pair == 0)
    def _():
        lanes = lax.broadcasted_iota(jnp.int32, (PAGE_TOKENS, SP_B), 1)
        rows = lax.broadcasted_iota(jnp.int32, (PAGE_TOKENS, SP_B), 0)
        flip_ref[...] = (lanes + rows == PAGE_TOKENS - 1).astype(jnp.bfloat16)
        for stream in range(2):
            x_row = rows_ref[2 * stream : 2 * stream + 1, :]
            y_row = rows_ref[2 * stream + 1 : 2 * stream + 2, :]
            x_col = cols_ref[:, 2 * stream : 2 * stream + 1]
            y_col = cols_ref[:, 2 * stream + 1 : 2 * stream + 2]
            cell_row = (x_row >> 7) * SP_SIDE + (y_row >> 7)
            cell_col = (x_col >> 7) * SP_SIDE + (y_col >> 7)
            x_less = ((x_row & 127) < (x_col & 127)).astype(jnp.float32)
            y_less = ((y_row & 127) < (y_col & 127)).astype(jnp.float32)
            for x_side in range(2):
                for y_side in range(2):
                    side = 2 * x_side + y_side
                    place_ref[stream, side * PAGE_TOKENS : (side + 1) * PAGE_TOKENS, :] = (
                        lanes == cell_col + (SP_SIDE + 1 - SP_SIDE * x_side - y_side)
                    ).astype(jnp.bfloat16)
                    mask_ref[stream, side] = (
                        (x_less if x_side else 1.0 - x_less) * (y_less if y_side else 1.0 - y_less)
                    ).astype(jnp.bfloat16)
            turned_ref[stream] = (rows[:128] == 127 - cell_row).astype(jnp.bfloat16)

    lane_head = lax.broadcasted_iota(jnp.int32, (PAGE_TOKENS, LANES), 1) // HEAD_DIM
    wide_head = jnp.concatenate([lane_head, lane_head], axis=1)
    upstream = upstream_ref[...]
    scale = HEAD_DIM ** (-0.5)
    diagonal = [None, None]
    for stream in range(2):
        pieces = [proj_ref[:, head_columns(stream, kind, pair)] for kind in range(5)]
        queries = jnp.concatenate([pieces[0], pieces[3]], axis=1)
        keys = jnp.concatenate([pieces[1], pieces[4]], axis=1)
        grads = []
        for inner in range(2):
            head = 2 * pair + inner
            mine = lane_head == inner
            grad_probs = dot_nt(jnp.where(mine, upstream, jnp.zeros_like(upstream)), pieces[2])
            probs = probs_ref[stream, inner]
            weighted = probs * grad_probs
            grad_logits = (weighted - probs * jnp.sum(weighted, axis=-1, keepdims=True)).astype(jnp.bfloat16)
            grads.append(
                (
                    dot_nn(grad_logits, keys) * scale,
                    dot_tn(grad_logits, queries) * scale,
                    dot_tn(probs.astype(jnp.bfloat16), upstream),
                )
            )
            parts = jnp.concatenate([grad_logits * mask_ref[stream, side] for side in range(4)], axis=1)
            placed = dot_nn(parts, place_ref[stream])
            placed_high = placed.astype(jnp.bfloat16)
            placed_low = (placed - placed_high.astype(jnp.float32)).astype(jnp.bfloat16)
            turned = turned_ref[stream]
            cells = dot_nn(turned, placed_high) + dot_nn(turned, placed_low)
            sums = jnp.sum(
                pltpu.roll(cells, SP_B - SP_SIDE // 2, 1, stride=1, stride_axis=0), axis=0, keepdims=True
            )
            if stream == 0:
                planar_ref[head] = sums
            else:
                planar_ref[head] += sums
            turned_over = dot_nn(flip_ref[...], grad_logits)
            diagonal[inner] = turned_over if stream == 0 else diagonal[inner] + turned_over
        query_grad, key_grad = (jnp.where(wide_head == 0, grads[0][k], grads[1][k]) for k in range(2))
        value_grad = jnp.where(lane_head == 0, grads[0][2], grads[1][2])
        for kind, value in enumerate(
            (query_grad[:, :LANES], key_grad[:, :LANES], value_grad, query_grad[:, LANES:], key_grad[:, LANES:])
        ):
            grad_ref[:, head_columns(stream, kind, pair)] = value.astype(jnp.bfloat16)
    for inner in range(2):
        padded = jnp.concatenate([diagonal[inner], jnp.zeros_like(diagonal[inner])], axis=1)
        linear_ref[2 * pair + inner] = jnp.sum(
            pltpu.roll(padded, 0, 1, stride=1, stride_axis=0), axis=0, keepdims=True
        )


def attend_back(proj, probs, upstream, anchor_rows, anchor_cols):
    return pl.pallas_call(
        attend_back_kernel,
        grid=(PAIRS,),
        in_specs=[
            pl.BlockSpec(proj.shape, lambda i: (0, 0)),
            pl.BlockSpec((2, 2, PAGE_TOKENS, PAGE_TOKENS), lambda i: (0, i, 0, 0)),
            pl.BlockSpec((PAGE_TOKENS, LANES), lambda i: (0, i)),
            pl.BlockSpec(anchor_rows.shape, lambda i: (0, 0)),
            pl.BlockSpec(anchor_cols.shape, lambda i: (0, 0)),
        ],
        out_specs=[
            pl.BlockSpec(proj.shape, lambda i: (0, 0)),
            pl.BlockSpec((HEADS, 1, 2 * PAGE_TOKENS), lambda i: (0, 0, 0)),
            pl.BlockSpec((HEADS, 1, SP_B), lambda i: (0, 0, 0)),
        ],
        out_shape=[
            jax.ShapeDtypeStruct(proj.shape, jnp.bfloat16),
            jax.ShapeDtypeStruct((HEADS, 1, 2 * PAGE_TOKENS), jnp.float32),
            jax.ShapeDtypeStruct((HEADS, 1, SP_B), jnp.float32),
        ],
        scratch_shapes=[
            pltpu.VMEM((2, 4 * PAGE_TOKENS, SP_B), jnp.bfloat16),
            pltpu.VMEM((2, 128, PAGE_TOKENS), jnp.bfloat16),
            pltpu.VMEM((2, 4, PAGE_TOKENS, PAGE_TOKENS), jnp.bfloat16),
            pltpu.VMEM((PAGE_TOKENS, PAGE_TOKENS), jnp.bfloat16),
        ],
        compiler_params=pltpu.CompilerParams(vmem_limit_bytes=48 << 20),
        name="attend_back",
    )(proj, probs, upstream, anchor_rows, anchor_cols)


def linear_extended(linear_bias):
    rows = linear_bias.astype(jnp.float32).T
    low = jnp.broadcast_to(rows[:, :1], (HEADS, PAGE_TOKENS - 1 - REL_B // 2))
    high = jnp.broadcast_to(rows[:, -1:], (HEADS, PAGE_TOKENS - REL_B // 2 + 1))
    return jnp.concatenate([low, rows, high], axis=1)[:, None, :]


def linear_folded(sums):
    first = REL_B // 2
    last = PAGE_TOKENS - 1 + REL_B // 2 - 1
    return jnp.concatenate(
        [
            jnp.sum(sums[:, :first], axis=1, keepdims=True),
            sums[:, first:last],
            jnp.sum(sums[:, last : 2 * PAGE_TOKENS - 1], axis=1, keepdims=True),
        ],
        axis=1,
    )

AXES = ("dp", "pair")
norm_epsilon = 1e-05
batch_epsilon = 1e-05


def gathered(shard):
    return lax.all_gather(shard, AXES, axis=0, tiled=True)


def scattered(grad):
    return lax.psum_scatter(grad.astype(jnp.bfloat16), AXES, scatter_dimension=0, tiled=True).astype(
        jnp.float32
    )


def normal_parts(values):
    center = values - jnp.mean(values, axis=-1, keepdims=True)
    inverse = lax.rsqrt(jnp.mean(center * center, axis=-1, keepdims=True) + norm_epsilon)
    return center * inverse, inverse


def normal_back(normal, inverse, gain, grad):
    scaled = grad * gain
    return inverse * (
        scaled
        - jnp.mean(scaled, axis=-1, keepdims=True)
        - normal * jnp.mean(scaled * normal, axis=-1, keepdims=True)
    )


def place_onehot(anchor_rows):
    coords = jnp.arange(COORDS, dtype=jnp.int32)
    return (anchor_rows[:, None] == coords[None, :]).astype(jnp.bfloat16)


def per_device(
    text_inputs,
    region_features,
    text_masked,
    region_masked,
    text_anchors,
    region_anchors,
    backbone_weight,
    batch_gain,
    batch_shift,
    text_blank,
    region_blank,
    position_table,
    stream_weights,
    linear_bias,
    planar_bias,
    merge_weight,
    mixer_gain,
    mixer_shift,
    expand_weight,
    expand_bias,
    reduce_weight,
    reduce_bias,
    output_gain,
    output_shift,
    cotangent,
):
    devices = lax.axis_size(AXES)
    row_count = text_inputs.shape[0]
    token_total = row_count * devices
    share = MODEL_WIDTH // devices
    bias_share = REL_B // devices * HEADS
    vectors = (
        batch_gain, batch_shift, text_blank, region_blank, mixer_gain, mixer_shift, reduce_bias,
        output_gain, output_shift,
    )
    packed = gathered(
        jnp.concatenate(
            [*vectors, expand_bias, linear_bias.reshape(-1), planar_bias.reshape(-1)]
        )[None, :]
    ).astype(jnp.float32)
    whole_vectors = packed[:, : 9 * share].reshape(devices, 9, share).transpose(1, 0, 2).reshape(9, -1)
    (
        w_batch_gain, w_batch_shift, w_text_blank, w_region_blank, w_mixer_gain, w_mixer_shift,
        w_reduce_bias, w_output_gain, w_output_shift,
    ) = (whole_vectors[k] for k in range(9))
    start = 9 * share
    stop = start + expand_bias.shape[0]
    w_expand_bias = packed[:, start:stop].reshape(-1)
    w_linear = packed[:, stop : stop + bias_share].reshape(REL_B, HEADS)
    w_planar = packed[:, stop + bias_share :].reshape(SP_B, HEADS)

    w_backbone = gathered(backbone_weight)
    w_table = gathered(position_table)
    w_stream = gathered(stream_weights)
    w_merge = gathered(merge_weight)
    w_expand = gathered(expand_weight)
    w_reduce = gathered(reduce_weight)

    conv = jnp.dot(region_features, w_backbone, preferred_element_type=jnp.float32)
    local_mean = jnp.mean(conv, axis=0)
    local_center = conv - local_mean
    local_square = jnp.sum(local_center * local_center, axis=0)
    statistics = lax.all_gather(jnp.stack([local_mean, local_square]), AXES, axis=0)
    batch_mean = jnp.mean(statistics[:, 0], axis=0)
    mean_offset = statistics[:, 0] - batch_mean
    batch_var = (
        jnp.sum(statistics[:, 1], axis=0) + row_count * jnp.sum(mean_offset * mean_offset, axis=0)
    ) / token_total
    inverse_std = lax.rsqrt(batch_var + batch_epsilon)
    normal_feat = (conv - batch_mean) * inverse_std
    region_hit = region_masked[:, None] == 1
    text_hit = text_masked[:, None] == 1
    region_start = jnp.where(region_hit, w_region_blank[None, :], normal_feat * w_batch_gain + w_batch_shift)
    text_start = jnp.where(text_hit, w_text_blank[None, :], text_inputs.astype(jnp.float32))
    text_low = text_start.astype(jnp.bfloat16)
    region_low = region_start.astype(jnp.bfloat16)
    onehot_x = place_onehot(jnp.concatenate([text_anchors[0], region_anchors[0]]))
    onehot_y = place_onehot(jnp.concatenate([text_anchors[1], region_anchors[1]]))
    space = (
        jnp.dot(onehot_x, w_table[:, :MODEL_WIDTH], preferred_element_type=jnp.float32)
        + jnp.dot(onehot_y, w_table[:, MODEL_WIDTH:], preferred_element_type=jnp.float32)
    ).astype(jnp.bfloat16)
    text_space = space[:row_count]
    region_space = space[row_count:]

    def project(left, first, last):
        return jnp.dot(
            left,
            w_stream[:, first * MODEL_WIDTH : last * MODEL_WIDTH],
            preferred_element_type=jnp.float32,
        ).astype(jnp.bfloat16)

    proj = jnp.concatenate(
        [project(text_low, 0, 3), project(text_space, 3, 5), project(region_low, 5, 8), project(region_space, 8, 10)],
        axis=1,
    )
    anchor_rows = jnp.concatenate([text_anchors, region_anchors], axis=0)
    anchor_cols = anchor_rows.T
    merged_low, probs = attend(
        proj, linear_extended(w_linear), w_planar.T[:, None, :], anchor_rows, anchor_cols
    )
    attended = jnp.dot(merged_low, w_merge, preferred_element_type=jnp.float32)
    mixer_normal, mixer_inverse = normal_parts(text_start + region_start + attended)
    hidden = mixer_normal * w_mixer_gain + w_mixer_shift
    hidden_low = hidden.astype(jnp.bfloat16)
    inner = jnp.dot(hidden_low, w_expand, preferred_element_type=jnp.float32) + w_expand_bias
    activated_low = jax.nn.gelu(inner, approximate=False).astype(jnp.bfloat16)
    dense = jnp.dot(activated_low, w_reduce, preferred_element_type=jnp.float32) + w_reduce_bias
    output_normal, output_inverse = normal_parts(hidden + dense)
    layer_output = (output_normal * w_output_gain + w_output_shift).astype(jnp.bfloat16)

    upstream = cotangent.astype(jnp.float32)
    output_in_grad = normal_back(output_normal, output_inverse, w_output_gain, upstream)
    output_gain_grad = jnp.sum(upstream * output_normal, axis=0)
    output_shift_grad = jnp.sum(upstream, axis=0)
    dense_low = output_in_grad.astype(jnp.bfloat16)
    reduce_bias_grad = jnp.sum(output_in_grad, axis=0)
    reduce_weight_grad = scattered(jnp.dot(activated_low.T, dense_low, preferred_element_type=jnp.float32))
    activated_grad = jnp.dot(dense_low, w_reduce.T, preferred_element_type=jnp.float32)
    unused, gelu_pull = jax.vjp(partial(jax.nn.gelu, approximate=False), inner)
    inner_low = gelu_pull(activated_grad)[0].astype(jnp.bfloat16)
    expand_bias_grad = jnp.sum(inner_low.astype(jnp.float32), axis=0)
    expand_weight_grad = scattered(jnp.dot(hidden_low.T, inner_low, preferred_element_type=jnp.float32))
    hidden_grad = output_in_grad + jnp.dot(inner_low, w_expand.T, preferred_element_type=jnp.float32)
    mixer_in_grad = normal_back(mixer_normal, mixer_inverse, w_mixer_gain, hidden_grad)
    mixer_gain_grad = jnp.sum(hidden_grad * mixer_normal, axis=0)
    mixer_shift_grad = jnp.sum(hidden_grad, axis=0)
    attended_low = mixer_in_grad.astype(jnp.bfloat16)
    merge_weight_grad = scattered(jnp.dot(merged_low.T, attended_low, preferred_element_type=jnp.float32))
    merged_grad = jnp.dot(attended_low, w_merge.T, preferred_element_type=jnp.float32).astype(jnp.bfloat16)
    proj_grad, linear_sums, planar_sums = attend_back(proj, probs, merged_grad, anchor_rows, anchor_cols)

    def columns(first, last):
        return proj_grad[:, first * MODEL_WIDTH : last * MODEL_WIDTH]

    def weight_columns(left, first, last):
        return jnp.dot(left.T, columns(first, last), preferred_element_type=jnp.float32).astype(jnp.bfloat16)

    def input_columns(first, last):
        return jnp.dot(
            columns(first, last),
            w_stream[:, first * MODEL_WIDTH : last * MODEL_WIDTH].T,
            preferred_element_type=jnp.float32,
        )

    stream_weights_grad = scattered(
        jnp.concatenate(
            [
                weight_columns(text_low, 0, 3),
                weight_columns(text_space, 3, 5),
                weight_columns(region_low, 5, 8),
                weight_columns(region_space, 8, 10),
            ],
            axis=1,
        )
    )
    text_start_grad = mixer_in_grad + input_columns(0, 3)
    region_start_grad = mixer_in_grad + input_columns(5, 8)
    space_grads = jnp.concatenate([input_columns(3, 5), input_columns(8, 10)], axis=0).astype(jnp.bfloat16)
    position_table_grad = scattered(
        jnp.concatenate(
            [
                jnp.dot(onehot_x.T, space_grads, preferred_element_type=jnp.float32),
                jnp.dot(onehot_y.T, space_grads, preferred_element_type=jnp.float32),
            ],
            axis=1,
        )
    )
    text_gradient = jnp.where(text_hit, 0.0, text_start_grad)
    text_blank_grad = jnp.sum(jnp.where(text_hit, text_start_grad, 0.0), axis=0)
    region_blank_grad = jnp.sum(jnp.where(region_hit, region_start_grad, 0.0), axis=0)
    normal_grad = jnp.where(region_hit, 0.0, region_start_grad)
    batch_sums = jnp.stack([jnp.sum(normal_grad, axis=0), jnp.sum(normal_grad * normal_feat, axis=0)])
    shift_total, gain_total = lax.psum(batch_sums, AXES)
    conv_grad = (
        w_batch_gain
        * inverse_std
        * (normal_grad - shift_total / token_total - normal_feat * gain_total / token_total)
    ).astype(jnp.bfloat16)
    feature_gradient = jnp.dot(conv_grad, w_backbone.T, preferred_element_type=jnp.float32)
    backbone_weight_grad = scattered(
        jnp.dot(region_features.T, conv_grad, preferred_element_type=jnp.float32)
    )
    owner_start = lax.axis_index(AXES) * share
    batch_gain_gradient = lax.dynamic_slice_in_dim(gain_total, owner_start, share)
    batch_shift_gradient = lax.dynamic_slice_in_dim(shift_total, owner_start, share)
    vector_grads = jnp.stack(
        [
            text_blank_grad, region_blank_grad, mixer_gain_grad, mixer_shift_grad, reduce_bias_grad,
            output_gain_grad, output_shift_grad,
        ]
    )
    small = lax.psum_scatter(
        jnp.concatenate(
            [
                vector_grads.reshape(7, devices, share).transpose(1, 0, 2).reshape(devices, -1),
                expand_bias_grad.reshape(devices, -1),
                linear_folded(linear_sums[:, 0]).T.reshape(devices, -1),
                planar_sums[:, 0].T.reshape(devices, -1),
            ],
            axis=1,
        ),
        AXES,
        scatter_dimension=0,
        tiled=True,
    )[0]
    vector_shares = [small[k * share : (k + 1) * share] for k in range(7)]
    start = 7 * share
    stop = start + expand_bias.shape[0]
    return (
        layer_output,
        text_gradient,
        feature_gradient,
        backbone_weight_grad,
        batch_gain_gradient,
        batch_shift_gradient,
        vector_shares[0],
        vector_shares[1],
        position_table_grad,
        stream_weights_grad,
        small[stop : stop + bias_share].reshape(-1, HEADS),
        small[stop + bias_share :].reshape(-1, HEADS),
        merge_weight_grad,
        vector_shares[2],
        vector_shares[3],
        expand_weight_grad,
        small[start:stop],
        reduce_weight_grad,
        vector_shares[4],
        vector_shares[5],
        vector_shares[6],
    )


def solution(mesh):
    in_specs = (
        P(("dp", "pair"), None),
        P(("dp", "pair"), None),
        P(("dp", "pair")),
        P(("dp", "pair")),
        P(None, ("dp", "pair")),
        P(None, ("dp", "pair")),
        P(("dp", "pair"), None),
        P(("dp", "pair")),
        P(("dp", "pair")),
        P(("dp", "pair")),
        P(("dp", "pair")),
        P(("dp", "pair"), None),
        P(("dp", "pair"), None),
        P(("dp", "pair"), None),
        P(("dp", "pair"), None),
        P(("dp", "pair"), None),
        P(("dp", "pair")),
        P(("dp", "pair")),
        P(("dp", "pair"), None),
        P(("dp", "pair")),
        P(("dp", "pair"), None),
        P(("dp", "pair")),
        P(("dp", "pair")),
        P(("dp", "pair")),
        P(("dp", "pair"), None),
    )
    out_specs = (
        P(("dp", "pair"), None),
        P(("dp", "pair"), None),
        P(("dp", "pair"), None),
        P(("dp", "pair"), None),
        P(("dp", "pair")),
        P(("dp", "pair")),
        P(("dp", "pair")),
        P(("dp", "pair")),
        P(("dp", "pair"), None),
        P(("dp", "pair"), None),
        P(("dp", "pair"), None),
        P(("dp", "pair"), None),
        P(("dp", "pair"), None),
        P(("dp", "pair")),
        P(("dp", "pair")),
        P(("dp", "pair"), None),
        P(("dp", "pair")),
        P(("dp", "pair"), None),
        P(("dp", "pair")),
        P(("dp", "pair")),
        P(("dp", "pair")),
    )
    return jax.shard_map(
        per_device, mesh=mesh, in_specs=in_specs, out_specs=out_specs, check_vma=False
    )
```

```python
from functools import partial

import jax
import jax.numpy as jnp
from jax import lax
from jax.experimental import pallas as pl
from jax.experimental.pallas import tpu as pltpu
from jax.sharding import PartitionSpec as P

HEADS = 12
HEAD_DIM = 64
COORDS = 1024
REL_B = 256
SP_SIDE = 16
PAGE_TOKENS = 256
MODEL_WIDTH = 768
SP_B = 256
COORD_STEP = 128
PAIRS = HEADS // 2
LANES = 2 * HEAD_DIM


def dot_nt(left, right):
    return lax.dot_general(left, right, (((1,), (1,)), ((), ())), preferred_element_type=jnp.float32)


def dot_tn(left, right):
    return lax.dot_general(left, right, (((0,), (0,)), ((), ())), preferred_element_type=jnp.float32)


def dot_nn(left, right):
    return lax.dot_general(left, right, (((1,), (0,)), ((), ())), preferred_element_type=jnp.float32)


def head_columns(stream, kind, pair):
    return pl.ds(pl.multiple_of(((5 * stream + kind) * PAIRS + pair) * LANES, LANES), LANES)


def attend_kernel(proj_ref, linear_ref, planar_ref, rows_ref, cols_ref, merged_ref, probs_ref, box_ref):
    pair = pl.program_id(0)

    @pl.when(pair == 0)
    def _():
        for stream in range(2):
            part = []
            for axis in range(2):
                along = rows_ref[2 * stream + axis : 2 * stream + axis + 1, :]
                down = cols_ref[:, 2 * stream + axis : 2 * stream + axis + 1]
                part.append(((along - down) >> 7) + SP_SIDE // 2)
            box_ref[stream] = part[0] * SP_SIDE + part[1]

    lane_head = lax.broadcasted_iota(jnp.int32, (PAGE_TOKENS, LANES), 1) // HEAD_DIM
    mixed = [None, None]
    for inner in range(2):
        head = 2 * pair + inner
        mine = lane_head == inner
        spread = jnp.broadcast_to(linear_ref[head], (PAGE_TOKENS, 2 * PAGE_TOKENS))
        linear_term = pltpu.roll(spread, PAGE_TOKENS + 1, 1, stride=1, stride_axis=0)[:, :PAGE_TOKENS]
        low_table = jnp.broadcast_to(planar_ref[head, :, :128], (PAGE_TOKENS, 128))
        high_table = jnp.broadcast_to(planar_ref[head, :, 128:], (PAGE_TOKENS, 128))
        total = None
        for stream in range(2):
            pieces = [proj_ref[:, head_columns(stream, kind, pair)] for kind in range(5)]
            zero = jnp.zeros_like(pieces[0])
            left = jnp.concatenate([jnp.where(mine, pieces[0], zero), jnp.where(mine, pieces[3], zero)], axis=1)
            right = jnp.concatenate([pieces[1], pieces[4]], axis=1)
            logits = dot_nt(left, right) * HEAD_DIM ** (-0.5)
            planar = []
            for half in range(2):
                box = box_ref[stream, :, 128 * half : 128 * half + 128]
                place = box & 127
                planar.append(
                    jnp.where(
                        box < 128,
                        jnp.take_along_axis(low_table, place, axis=1),
                        jnp.take_along_axis(high_table, place, axis=1),
                    )
                )
            logits = logits + linear_term + jnp.concatenate(planar, axis=1)
            top = jnp.max(logits, axis=-1, keepdims=True)
            shifted = jnp.exp(logits - top)
            probs = shifted / jnp.sum(shifted, axis=-1, keepdims=True)
            probs_ref[stream, inner] = probs
            part = dot_nn(probs.astype(jnp.bfloat16), pieces[2])
            total = part if total is None else total + part
        mixed[inner] = total
    merged_ref[...] = jnp.where(lane_head == 0, mixed[0], mixed[1]).astype(jnp.bfloat16)


def attend(proj, linear_ext, planar_rows, anchor_rows, anchor_cols):
    return pl.pallas_call(
        attend_kernel,
        grid=(PAIRS,),
        in_specs=[
            pl.BlockSpec(proj.shape, lambda i: (0, 0)),
            pl.BlockSpec(linear_ext.shape, lambda i: (0, 0, 0)),
            pl.BlockSpec(planar_rows.shape, lambda i: (0, 0, 0)),
            pl.BlockSpec(anchor_rows.shape, lambda i: (0, 0)),
            pl.BlockSpec(anchor_cols.shape, lambda i: (0, 0)),
        ],
        out_specs=[
            pl.BlockSpec((PAGE_TOKENS, LANES), lambda i: (0, i)),
            pl.BlockSpec((2, 2, PAGE_TOKENS, PAGE_TOKENS), lambda i: (0, i, 0, 0)),
        ],
        out_shape=[
            jax.ShapeDtypeStruct((PAGE_TOKENS, MODEL_WIDTH), jnp.bfloat16),
            jax.ShapeDtypeStruct((2, HEADS, PAGE_TOKENS, PAGE_TOKENS), jnp.float32),
        ],
        scratch_shapes=[pltpu.VMEM((2, PAGE_TOKENS, PAGE_TOKENS), jnp.int32)],
        compiler_params=pltpu.CompilerParams(vmem_limit_bytes=48 << 20),
        name="attend",
    )(proj, linear_ext, planar_rows, anchor_rows, anchor_cols)


def attend_back_kernel(
    proj_ref, probs_ref, upstream_ref, rows_ref, cols_ref, grad_ref, linear_ref, planar_ref,
    place_ref, turned_ref, mask_ref, flip_ref,
):
    pair = pl.program_id(0)

    @pl.when(pair == 0)
    def _():
        lanes = lax.broadcasted_iota(jnp.int32, (PAGE_TOKENS, SP_B), 1)
        rows = lax.broadcasted_iota(jnp.int32, (PAGE_TOKENS, SP_B), 0)
        flip_ref[...] = (lanes + rows == PAGE_TOKENS - 1).astype(jnp.bfloat16)
        for stream in range(2):
            x_row = rows_ref[2 * stream : 2 * stream + 1, :]
            y_row = rows_ref[2 * stream + 1 : 2 * stream + 2, :]
            x_col = cols_ref[:, 2 * stream : 2 * stream + 1]
            y_col = cols_ref[:, 2 * stream + 1 : 2 * stream + 2]
            cell_row = (x_row >> 7) * SP_SIDE + (y_row >> 7)
            cell_col = (x_col >> 7) * SP_SIDE + (y_col >> 7)
            x_less = ((x_row & 127) < (x_col & 127)).astype(jnp.float32)
            y_less = ((y_row & 127) < (y_col & 127)).astype(jnp.float32)
            for x_side in range(2):
                for y_side in range(2):
                    side = 2 * x_side + y_side
                    place_ref[stream, side * PAGE_TOKENS : (side + 1) * PAGE_TOKENS, :] = (
                        lanes == cell_col + (SP_SIDE + 1 - SP_SIDE * x_side - y_side)
                    ).astype(jnp.bfloat16)
                    mask_ref[stream, side] = (
                        (x_less if x_side else 1.0 - x_less) * (y_less if y_side else 1.0 - y_less)
                    ).astype(jnp.bfloat16)
            turned_ref[stream] = (rows[:128] == 127 - cell_row).astype(jnp.bfloat16)

    lane_head = lax.broadcasted_iota(jnp.int32, (PAGE_TOKENS, LANES), 1) // HEAD_DIM
    wide_head = jnp.concatenate([lane_head, lane_head], axis=1)
    upstream = upstream_ref[...]
    scale = HEAD_DIM ** (-0.5)
    diagonal = [None, None]
    for stream in range(2):
        pieces = [proj_ref[:, head_columns(stream, kind, pair)] for kind in range(5)]
        queries = jnp.concatenate([pieces[0], pieces[3]], axis=1)
        keys = jnp.concatenate([pieces[1], pieces[4]], axis=1)
        grads = []
        for inner in range(2):
            head = 2 * pair + inner
            mine = lane_head == inner
            grad_probs = dot_nt(jnp.where(mine, upstream, jnp.zeros_like(upstream)), pieces[2])
            probs = probs_ref[stream, inner]
            weighted = probs * grad_probs
            grad_logits = (weighted - probs * jnp.sum(weighted, axis=-1, keepdims=True)).astype(jnp.bfloat16)
            grads.append(
                (
                    dot_nn(grad_logits, keys) * scale,
                    dot_tn(grad_logits, queries) * scale,
                    dot_tn(probs.astype(jnp.bfloat16), upstream),
                )
            )
            parts = jnp.concatenate([grad_logits * mask_ref[stream, side] for side in range(4)], axis=1)
            placed = dot_nn(parts, place_ref[stream])
            placed_high = placed.astype(jnp.bfloat16)
            placed_low = (placed - placed_high.astype(jnp.float32)).astype(jnp.bfloat16)
            turned = turned_ref[stream]
            cells = dot_nn(turned, placed_high) + dot_nn(turned, placed_low)
            sums = jnp.sum(
                pltpu.roll(cells, SP_B - SP_SIDE // 2, 1, stride=1, stride_axis=0), axis=0, keepdims=True
            )
            if stream == 0:
                planar_ref[head] = sums
            else:
                planar_ref[head] += sums
            turned_over = dot_nn(flip_ref[...], grad_logits)
            diagonal[inner] = turned_over if stream == 0 else diagonal[inner] + turned_over
        query_grad, key_grad = (jnp.where(wide_head == 0, grads[0][k], grads[1][k]) for k in range(2))
        value_grad = jnp.where(lane_head == 0, grads[0][2], grads[1][2])
        for kind, value in enumerate(
            (query_grad[:, :LANES], key_grad[:, :LANES], value_grad, query_grad[:, LANES:], key_grad[:, LANES:])
        ):
            grad_ref[:, head_columns(stream, kind, pair)] = value.astype(jnp.bfloat16)
    for inner in range(2):
        padded = jnp.concatenate([diagonal[inner], jnp.zeros_like(diagonal[inner])], axis=1)
        linear_ref[2 * pair + inner] = jnp.sum(
            pltpu.roll(padded, 0, 1, stride=1, stride_axis=0), axis=0, keepdims=True
        )


def attend_back(proj, probs, upstream, anchor_rows, anchor_cols):
    return pl.pallas_call(
        attend_back_kernel,
        grid=(PAIRS,),
        in_specs=[
            pl.BlockSpec(proj.shape, lambda i: (0, 0)),
            pl.BlockSpec((2, 2, PAGE_TOKENS, PAGE_TOKENS), lambda i: (0, i, 0, 0)),
            pl.BlockSpec((PAGE_TOKENS, LANES), lambda i: (0, i)),
            pl.BlockSpec(anchor_rows.shape, lambda i: (0, 0)),
            pl.BlockSpec(anchor_cols.shape, lambda i: (0, 0)),
        ],
        out_specs=[
            pl.BlockSpec(proj.shape, lambda i: (0, 0)),
            pl.BlockSpec((HEADS, 1, 2 * PAGE_TOKENS), lambda i: (0, 0, 0)),
            pl.BlockSpec((HEADS, 1, SP_B), lambda i: (0, 0, 0)),
        ],
        out_shape=[
            jax.ShapeDtypeStruct(proj.shape, jnp.bfloat16),
            jax.ShapeDtypeStruct((HEADS, 1, 2 * PAGE_TOKENS), jnp.float32),
            jax.ShapeDtypeStruct((HEADS, 1, SP_B), jnp.float32),
        ],
        scratch_shapes=[
            pltpu.VMEM((2, 4 * PAGE_TOKENS, SP_B), jnp.bfloat16),
            pltpu.VMEM((2, 128, PAGE_TOKENS), jnp.bfloat16),
            pltpu.VMEM((2, 4, PAGE_TOKENS, PAGE_TOKENS), jnp.bfloat16),
            pltpu.VMEM((PAGE_TOKENS, PAGE_TOKENS), jnp.bfloat16),
        ],
        compiler_params=pltpu.CompilerParams(vmem_limit_bytes=48 << 20),
        name="attend_back",
    )(proj, probs, upstream, anchor_rows, anchor_cols)


def linear_extended(linear_bias):
    rows = linear_bias.astype(jnp.float32).T
    low = jnp.broadcast_to(rows[:, :1], (HEADS, PAGE_TOKENS - 1 - REL_B // 2))
    high = jnp.broadcast_to(rows[:, -1:], (HEADS, PAGE_TOKENS - REL_B // 2 + 1))
    return jnp.concatenate([low, rows, high], axis=1)[:, None, :]


def linear_folded(sums):
    first = REL_B // 2
    last = PAGE_TOKENS - 1 + REL_B // 2 - 1
    return jnp.concatenate(
        [
            jnp.sum(sums[:, :first], axis=1, keepdims=True),
            sums[:, first:last],
            jnp.sum(sums[:, last : 2 * PAGE_TOKENS - 1], axis=1, keepdims=True),
        ],
        axis=1,
    )


MESH = pl.DeviceIdType.MESH
RING = 4


def place():
    dp = lax.axis_index("dp")
    return dp // RING, lax.rem(dp, RING), lax.axis_index("pair")


def across(q, bit):
    other = lax.rem(q // bit, 2)
    return q + bit - 2 * bit * other


def greet(line):
    z, q, c = place()
    barrier = pltpu.get_barrier_semaphore()

    def signal(zz, qq, cc):
        pl.semaphore_signal(barrier, inc=1, device_id={"dp": zz * RING + qq, "pair": cc}, device_id_type=MESH)

    signal(z, across(q, 1), c)
    signal(z, across(q, 2), c)
    signal(z, q, 1 - c)

    @pl.when(z > 0)
    def _():
        signal(z - 1, q, c)

    @pl.when(z < line - 1)
    def _():
        signal(z + 1, q, c)

    ends = (z > 0).astype(jnp.int32) + (z < line - 1).astype(jnp.int32)
    pl.semaphore_wait(barrier, 3 + ends)


def gather_kernel(line, count, *refs):
    ins, outs = refs[:count], refs[count : 2 * count]
    (own_sem, z_send, z_recv, xy_send, xy_recv, d_send, d_recv, c_send, c_recv) = refs[2 * count :]
    z, q, c = place()
    beside = (across(q, 1), across(q, 2))
    corner = across(across(q, 1), 2)

    def slot(zz, qq):
        return (zz * RING + qq) * 2 + c

    def remote(src, dst, send, recv, zz, qq, cc):
        return pltpu.make_async_remote_copy(
            src_ref=src, dst_ref=dst, send_sem=send, recv_sem=recv,
            device_id={"dp": zz * RING + qq, "pair": cc}, device_id_type=MESH,
        )

    def block(a, zz, qq):
        return outs[a].at[slot(zz, qq)]

    def halves(a):
        width = ins[a].shape[-1]
        cut = width // 2 if width % 256 == 0 else width
        return (0, cut), (cut, width - cut)

    def own(a):
        return pltpu.make_async_copy(ins[a], block(a, z, q), own_sem.at[a])

    def z_copy(a, way, step, first):
        zz = z - step if way == 0 else z + step
        target = z + 1 if way == 0 else z - 1
        src = ins[a] if first else block(a, zz, q)
        return remote(src, block(a, zz, q), z_send.at[way, a, step], z_recv.at[way, a, step], target, q, c)

    def xy_copy(a, axis, zz, first):
        src = ins[a] if first else block(a, zz, q)
        return remote(src, block(a, zz, q), xy_send.at[axis, a, zz], xy_recv.at[axis, a, zz], z, beside[axis], c)

    def d_copy(a, axis, zz):
        start, width = halves(a)[axis]
        part = outs[a].at[slot(zz, beside[axis]), :, pl.ds(start, width)]
        return remote(part, part, d_send.at[axis, a, zz], d_recv.at[axis, a, zz], z, beside[1 - axis], c)

    def c_copy(a, zz, qq, first):
        src = ins[a] if first else block(a, zz, qq)
        return remote(
            src, block(a, zz, qq), c_send.at[a, zz * RING + qq], c_recv.at[a, zz * RING + qq], z, q, 1 - c
        )

    greet(line)

    for a in range(count):
        own(a).start()
        for way in range(2):
            @pl.when(z < line - 1 if way == 0 else z > 0)
            def _():
                z_copy(a, way, 0, True).start()
        for axis in range(2):
            xy_copy(a, axis, z, True).start()
        c_copy(a, z, q, True).start()

    def arrived(a, zz):
        for axis in range(2):
            xy_copy(a, axis, zz, False).start()
        c_copy(a, zz, q, False).start()

    def passed_on(a, zz):
        for axis in range(2):
            start, width = halves(a)[axis]
            got = block(a, zz, beside[axis])
            remote(got, got, xy_send.at[axis, a, zz], xy_recv.at[axis, a, zz], z, beside[axis], c).wait_recv()
            if width:
                d_copy(a, axis, zz).start()
            c_copy(a, zz, beside[axis], False).start()

    def finished(a, zz):
        for axis in range(2):
            start, width = halves(a)[axis]
            if width:
                part = outs[a].at[slot(zz, corner), :, pl.ds(start, width)]
                remote(part, part, d_send.at[axis, a, zz], d_recv.at[axis, a, zz], z, beside[1 - axis], c).wait_recv()
        c_copy(a, zz, corner, False).start()

    def both_ways(g, work):
        @pl.when(z - g >= 0)
        def _():
            work(z - g)

        @pl.when(jnp.logical_and(z + g <= line - 1, g > 0))
        def _():
            work(z + g)

    def generation(g, unused):
        @pl.when(jnp.logical_and(g >= 1, g <= line - 1))
        def _():
            for a in range(count):
                @pl.when(z - g >= 0)
                def _():
                    got = block(a, z - g, q)
                    remote(got, got, z_send.at[0, a, g - 1], z_recv.at[0, a, g - 1], z, q, 1 - c).wait_recv()

                    @pl.when(z < line - 1)
                    def _():
                        z_copy(a, 0, g, False).start()

                    arrived(a, z - g)

                @pl.when(z + g <= line - 1)
                def _():
                    got = block(a, z + g, q)
                    remote(got, got, z_send.at[1, a, g - 1], z_recv.at[1, a, g - 1], z, q, 1 - c).wait_recv()

                    @pl.when(z > 0)
                    def _():
                        z_copy(a, 1, g, False).start()

                    arrived(a, z + g)

        @pl.when(jnp.logical_and(g >= 1, g <= line))
        def _():
            for a in range(count):
                both_ways(g - 1, partial(passed_on, a))

        @pl.when(g >= 2)
        def _():
            for a in range(count):
                both_ways(g - 2, partial(finished, a))

        return unused

    lax.fori_loop(1, line + 2, generation, 0)

    for a in range(count):
        own(a).wait()

    def drain(zz, unused):
        for a in range(count):
            for axis in range(2):
                xy_copy(a, axis, zz, False).wait_send()
                if halves(a)[axis][1]:
                    d_copy(a, axis, zz).wait_send()
            for qq in range(RING):
                c_copy(a, zz, qq, False).wait_send()
                got = outs[a].at[(zz * RING + qq) * 2 + 1 - c]
                remote(
                    got, got, c_send.at[a, zz * RING + qq], c_recv.at[a, zz * RING + qq], z, q, 1 - c
                ).wait_recv()

            @pl.when(jnp.logical_and(z < line - 1, zz <= z))
            def _():
                z_copy(a, 0, z - zz, False).wait_send()

            @pl.when(jnp.logical_and(z > 0, zz >= z))
            def _():
                z_copy(a, 1, zz - z, False).wait_send()
        return unused

    lax.fori_loop(0, line, drain, 0)


def gather_all(shards, collective_id):
    dp = lax.axis_size("dp")
    line = dp // RING
    devices = 2 * dp
    count = len(shards)
    dma = pltpu.SemaphoreType.DMA
    return pl.pallas_call(
        partial(gather_kernel, line, count),
        in_specs=[pl.BlockSpec(memory_space=pl.ANY)] * count,
        out_specs=[pl.BlockSpec(memory_space=pl.ANY)] * count,
        out_shape=[jax.ShapeDtypeStruct((devices, *shard.shape), shard.dtype) for shard in shards],
        scratch_shapes=[
            dma((count,)),
            dma((2, count, line)),
            dma((2, count, line)),
            dma((2, count, line)),
            dma((2, count, line)),
            dma((2, count, line)),
            dma((2, count, line)),
            dma((count, line * RING)),
            dma((count, line * RING)),
        ],
        compiler_params=pltpu.CompilerParams(collective_id=collective_id, has_side_effects=True),
        name="gather_all",
    )(*shards)


def scatter_kernel(line, count, *refs):
    ins, outs = refs[:count], refs[count : 2 * count]
    groups = [refs[(2 + k) * count : (3 + k) * count] for k in range(5)]
    mine, beside_sum, half_in, full_in, line_in = groups
    (own_sem, c_send, c_recv, d_send, d_recv, xy_send, xy_recv, z_send, z_recv) = refs[7 * count :]
    z, q, c = place()
    beside = (across(q, 1), across(q, 2))
    corner = across(across(q, 1), 2)

    def remote(src, dst, send, recv, zz, qq, cc):
        return pltpu.make_async_remote_copy(
            src_ref=src, dst_ref=dst, send_sem=send, recv_sem=recv,
            device_id={"dp": zz * RING + qq, "pair": cc}, device_id_type=MESH,
        )

    def halves(a):
        width = outs[a].shape[-1]
        cut = width // 2 if width % 256 == 0 else width
        return (0, cut), (cut, width - cut)

    def wide(value):
        return value.astype(jnp.float32)

    def group(zz):
        return pl.ds(zz * RING, RING)

    def own(a, zz):
        return pltpu.make_async_copy(ins[a].at[group(zz), c], mine[a].at[group(zz)], own_sem.at[a, zz])

    def c_copy(a, zz):
        return remote(
            ins[a].at[group(zz), 1 - c], beside_sum[a].at[group(zz)], c_send.at[a, zz], c_recv.at[a, zz], z, q, 1 - c
        )

    def d_copy(a, axis, zz):
        start, width = halves(a)[axis]
        return remote(
            mine[a].at[zz * RING + corner, :, pl.ds(start, width)],
            half_in[a].at[zz, :, pl.ds(start, width)],
            d_send.at[axis, a, zz], d_recv.at[axis, a, zz], z, beside[axis], c,
        )

    def xy_copy(a, axis, zz):
        return remote(
            mine[a].at[zz * RING + beside[axis]], full_in[a].at[axis, zz],
            xy_send.at[axis, a, zz], xy_recv.at[axis, a, zz], z, beside[axis], c,
        )

    def z_copy(a, way, zz):
        return remote(
            mine[a].at[zz * RING + q], line_in[a].at[way, zz],
            z_send.at[way, a, zz], z_recv.at[way, a, zz], z + 1 if way == 0 else z - 1, q, c,
        )

    greet(line)

    def both_ways(g, work):
        @pl.when(z - g >= 0)
        def _():
            work(z - g)

        @pl.when(jnp.logical_and(z + g <= line - 1, g > 0))
        def _():
            work(z + g)

    def begin(zz):
        for a in range(count):
            c_copy(a, zz).start()
            own(a, zz).start()

    def first(zz):
        for a in range(count):
            own(a, zz).wait()
            c_copy(a, zz).wait_recv()

            def one(qq, unused):
                k = zz * RING + qq
                mine[a][k] = mine[a][k] + beside_sum[a][k]
                return unused

            lax.fori_loop(0, RING, one, 0)
            for axis in range(2):
                if halves(a)[axis][1]:
                    d_copy(a, axis, zz).start()

    def second(zz):
        for a in range(count):
            for axis in range(2):
                start, width = halves(a)[axis]
                k = zz * RING + beside[1 - axis]
                if width:
                    d_copy(a, axis, zz).wait_recv()
                    mine[a][k, :, start : start + width] = (
                        mine[a][k, :, start : start + width] + half_in[a][zz, :, start : start + width]
                    )
                xy_copy(a, 1 - axis, zz).start()

    def third(zz):
        for a in range(count):
            k = zz * RING + q
            for axis in range(2):
                xy_copy(a, axis, zz).wait_recv()
            mine[a][k] = (
                wide(mine[a][k]) + wide(full_in[a][0, zz]) + wide(full_in[a][1, zz])
            ).astype(mine[a].dtype)
            for way in range(2):
                @pl.when(zz > z if way == 0 else zz < z)
                def _():
                    @pl.when(z > 0 if way == 0 else z < line - 1)
                    def _():
                        z_copy(a, way, zz).wait_recv()
                        mine[a][k] = mine[a][k] + line_in[a][way, zz]

                    z_copy(a, way, zz).start()

            @pl.when(zz == z)
            def _():
                outs[a][...] = wide(mine[a][k])
                for way in range(2):
                    @pl.when(z > 0 if way == 0 else z < line - 1)
                    def _():
                        z_copy(a, way, zz).wait_recv()
                        outs[a][...] += wide(line_in[a][way, zz])

    def start_all(step, unused):
        both_ways(line - 1 - step, begin)
        return unused

    lax.fori_loop(0, line, start_all, 0)

    def generation(step, unused):
        g = line - 1 - step

        @pl.when(g >= 0)
        def _():
            both_ways(g, first)

        @pl.when(jnp.logical_and(g + 1 >= 0, g + 1 <= line - 1))
        def _():
            both_ways(g + 1, second)

        @pl.when(g + 2 <= line - 1)
        def _():
            both_ways(g + 2, third)

        return unused

    lax.fori_loop(0, line + 2, generation, 0)

    def drain(zz, unused):
        for a in range(count):
            for axis in range(2):
                xy_copy(a, axis, zz).wait_send()
                if halves(a)[axis][1]:
                    d_copy(a, axis, zz).wait_send()
            c_copy(a, zz).wait_send()
            for way in range(2):
                @pl.when(zz > z if way == 0 else zz < z)
                def _():
                    z_copy(a, way, zz).wait_send()
        return unused

    lax.fori_loop(0, line, drain, 0)


def scatter_all(grads, collective_id):
    dp = lax.axis_size("dp")
    line = dp // RING
    count = len(grads)
    dma = pltpu.SemaphoreType.DMA
    blocks = [(grad.shape[1:], grad.dtype) for grad in grads]
    return pl.pallas_call(
        partial(scatter_kernel, line, count),
        in_specs=[pl.BlockSpec(memory_space=pl.ANY)] * count,
        out_specs=[pl.BlockSpec(memory_space=pltpu.VMEM)] * count,
        out_shape=[jax.ShapeDtypeStruct(shape, jnp.float32) for shape, kind in blocks],
        scratch_shapes=[
            *(pltpu.VMEM((line * RING, *shape), kind) for shape, kind in blocks),
            *(pltpu.VMEM((line * RING, *shape), kind) for shape, kind in blocks),
            *(pltpu.VMEM((line, *shape), kind) for shape, kind in blocks),
            *(pltpu.VMEM((2, line, *shape), kind) for shape, kind in blocks),
            *(pltpu.VMEM((2, line, *shape), kind) for shape, kind in blocks),
            *(dma((count, line)) for k in range(3)),
            *(dma((2, count, line)) for k in range(6)),
        ],
        compiler_params=pltpu.CompilerParams(
            collective_id=collective_id, has_side_effects=True, vmem_limit_bytes=63 << 20
        ),
        name="scatter_all",
    )(*(grad.reshape(line * RING, 2, *grad.shape[1:]) for grad in grads))


def exchange_kernel(line, combine, value_ref, total_ref, near_ref, part_ref, far_ref, n_send, n_recv, f_send, f_recv):
    z, q, c = place()
    cell = q * 2 + c
    near = RING * 2
    barrier = pltpu.get_barrier_semaphore()

    def near_place(k):
        other = lax.rem(cell + k, near)
        return other, {"dp": z * RING + other // 2, "pair": lax.rem(other, 2)}

    def far_place(k):
        other = lax.rem(z + k, line)
        return other, {"dp": other * RING + q, "pair": c}

    def each(places, stop, work):
        def one(k, unused):
            work(*places(k))
            return unused

        lax.fori_loop(1, stop, one, 0)

    def signal(other, device):
        pl.semaphore_signal(barrier, inc=1, device_id=device, device_id_type=MESH)

    each(near_place, near, signal)
    each(far_place, line, signal)
    pl.semaphore_wait(barrier, near + line - 2)

    def near_copy(other, device, source):
        return pltpu.make_async_remote_copy(
            src_ref=value_ref, dst_ref=near_ref.at[source], send_sem=n_send.at[other], recv_sem=n_recv.at[source],
            device_id=device, device_id_type=MESH,
        )

    def far_copy(other, device, source):
        return pltpu.make_async_remote_copy(
            src_ref=part_ref, dst_ref=far_ref.at[source], send_sem=f_send.at[other], recv_sem=f_recv.at[source],
            device_id=device, device_id_type=MESH,
        )

    each(near_place, near, lambda other, device: near_copy(other, device, cell).start())
    near_ref[cell] = value_ref[...]
    each(near_place, near, lambda other, device: near_copy(other, device, other).wait_recv())
    part_ref[...] = combine(near_ref, near, 1)
    each(far_place, line, lambda other, device: far_copy(other, device, z).start())
    far_ref[z] = part_ref[...]
    each(far_place, line, lambda other, device: far_copy(other, device, other).wait_recv())
    total_ref[...] = combine(far_ref, line, near)
    each(near_place, near, lambda other, device: near_copy(other, device, cell).wait_send())
    each(far_place, line, lambda other, device: far_copy(other, device, z).wait_send())


def add_up(parts, count, weight):
    return lax.fori_loop(1, count, lambda k, total: total + parts[k], parts[0])


def pool_statistics(rows, parts, count, weight):
    mean = lax.fori_loop(1, count, lambda k, total: total + parts[k, 0], parts[0, 0]) / count

    def squares(k, total):
        offset = parts[k, 0] - mean
        return total + parts[k, 1] + (rows * weight) * (offset * offset)

    return jnp.stack([mean, lax.fori_loop(0, count, squares, jnp.zeros_like(mean))])


def exchange(value, combine, collective_id, name):
    line = lax.axis_size("dp") // RING
    near = RING * 2
    dma = pltpu.SemaphoreType.DMA
    vmem = pl.BlockSpec(memory_space=pltpu.VMEM)
    return pl.pallas_call(
        partial(exchange_kernel, line, combine),
        in_specs=[vmem],
        out_specs=vmem,
        out_shape=jax.ShapeDtypeStruct(value.shape, value.dtype),
        scratch_shapes=[
            pltpu.VMEM((near, *value.shape), value.dtype),
            pltpu.VMEM(value.shape, value.dtype),
            pltpu.VMEM((line, *value.shape), value.dtype),
            dma((near,)),
            dma((near,)),
            dma((line,)),
            dma((line,)),
        ],
        compiler_params=pltpu.CompilerParams(collective_id=collective_id, has_side_effects=True),
        name=name,
    )(value)

AXES = ("dp", "pair")
SMALL = 1024
norm_epsilon = 1e-05
batch_epsilon = 1e-05


def folded(vectors):
    whole = jnp.stack([vector.reshape(-1, 128) for vector in vectors])
    return jnp.pad(whole, ((0, 0), (0, 8 - whole.shape[1]), (0, 0)))


def blocks_of(grad, devices):
    blocks = grad.astype(jnp.bfloat16).reshape(devices, grad.shape[0] // devices, grad.shape[1])
    return blocks if blocks.shape[1] % 8 == 0 else blocks.reshape(devices, -1, 128)


def normal_parts(values):
    center = values - jnp.mean(values, axis=-1, keepdims=True)
    inverse = lax.rsqrt(jnp.mean(center * center, axis=-1, keepdims=True) + norm_epsilon)
    return center * inverse, inverse


def normal_back(normal, inverse, gain, grad):
    scaled = grad * gain
    return inverse * (
        scaled
        - jnp.mean(scaled, axis=-1, keepdims=True)
        - normal * jnp.mean(scaled * normal, axis=-1, keepdims=True)
    )


def place_onehot(anchor_rows):
    coords = jnp.arange(COORDS, dtype=jnp.int32)
    return (anchor_rows[:, None] == coords[None, :]).astype(jnp.bfloat16)


def per_device(
    text_inputs,
    region_features,
    text_masked,
    region_masked,
    text_anchors,
    region_anchors,
    backbone_weight,
    batch_gain,
    batch_shift,
    text_blank,
    region_blank,
    position_table,
    stream_weights,
    linear_bias,
    planar_bias,
    merge_weight,
    mixer_gain,
    mixer_shift,
    expand_weight,
    expand_bias,
    reduce_weight,
    reduce_bias,
    output_gain,
    output_shift,
    cotangent,
):
    devices = lax.axis_size(AXES)
    row_count = text_inputs.shape[0]
    token_total = row_count * devices
    share = MODEL_WIDTH // devices
    bias_share = REL_B // devices * HEADS
    vectors = (
        batch_gain, batch_shift, text_blank, region_blank, mixer_gain, mixer_shift, reduce_bias,
        output_gain, output_shift,
    )
    small = jnp.concatenate(
        [
            part.astype(jnp.float32).reshape(-1)
            for part in (*vectors, expand_bias, linear_bias, planar_bias)
        ]
    )
    small = jnp.pad(small, (0, SMALL - small.shape[0])).reshape(-1, 128)
    wide = jnp.concatenate([stream_weights, merge_weight, expand_weight], axis=1)
    packed, w_backbone, w_table, w_wide, w_reduce = (
        whole.reshape(-1, whole.shape[-1])
        for whole in gather_all((small, backbone_weight, position_table, wide, reduce_weight), 0)
    )
    w_merge = w_wide[:, 10 * MODEL_WIDTH : 11 * MODEL_WIDTH]
    w_expand = w_wide[:, 11 * MODEL_WIDTH :]
    packed = packed.reshape(devices, SMALL)
    whole_vectors = packed[:, : 9 * share].reshape(devices, 9, share).transpose(1, 0, 2).reshape(9, -1)
    (
        w_batch_gain, w_batch_shift, w_text_blank, w_region_blank, w_mixer_gain, w_mixer_shift,
        w_reduce_bias, w_output_gain, w_output_shift,
    ) = (whole_vectors[k] for k in range(9))
    start = 9 * share
    stop = start + expand_bias.shape[0]
    w_expand_bias = packed[:, start:stop].reshape(-1)
    w_linear = packed[:, stop : stop + bias_share].reshape(REL_B, HEADS)
    w_planar = packed[:, stop + bias_share : stop + 2 * bias_share].reshape(SP_B, HEADS)

    conv = jnp.dot(region_features, w_backbone, preferred_element_type=jnp.float32)
    local_mean = jnp.mean(conv, axis=0)
    local_center = conv - local_mean
    local_square = jnp.sum(local_center * local_center, axis=0)
    pooled = exchange(
        folded([local_mean, local_square]), partial(pool_statistics, float(row_count)), 2, "pool"
    ).reshape(2, -1)
    batch_mean = pooled[0, :MODEL_WIDTH]
    batch_var = pooled[1, :MODEL_WIDTH] / token_total
    inverse_std = lax.rsqrt(batch_var + batch_epsilon)
    normal_feat = (conv - batch_mean) * inverse_std
    region_hit = region_masked[:, None] == 1
    text_hit = text_masked[:, None] == 1
    region_start = jnp.where(region_hit, w_region_blank[None, :], normal_feat * w_batch_gain + w_batch_shift)
    text_start = jnp.where(text_hit, w_text_blank[None, :], text_inputs.astype(jnp.float32))
    text_low = text_start.astype(jnp.bfloat16)
    region_low = region_start.astype(jnp.bfloat16)
    onehot_x = place_onehot(jnp.concatenate([text_anchors[0], region_anchors[0]]))
    onehot_y = place_onehot(jnp.concatenate([text_anchors[1], region_anchors[1]]))
    space = (
        jnp.dot(onehot_x, w_table[:, :MODEL_WIDTH], preferred_element_type=jnp.float32)
        + jnp.dot(onehot_y, w_table[:, MODEL_WIDTH:], preferred_element_type=jnp.float32)
    ).astype(jnp.bfloat16)
    text_space = space[:row_count]
    region_space = space[row_count:]

    def project(left, first, last):
        return jnp.dot(
            left,
            w_wide[:, first * MODEL_WIDTH : last * MODEL_WIDTH],
            preferred_element_type=jnp.float32,
        ).astype(jnp.bfloat16)

    proj = jnp.concatenate(
        [project(text_low, 0, 3), project(text_space, 3, 5), project(region_low, 5, 8), project(region_space, 8, 10)],
        axis=1,
    )
    anchor_rows = jnp.concatenate([text_anchors, region_anchors], axis=0)
    anchor_cols = anchor_rows.T
    merged_low, probs = attend(
        proj, linear_extended(w_linear), w_planar.T[:, None, :], anchor_rows, anchor_cols
    )
    attended = jnp.dot(merged_low, w_merge, preferred_element_type=jnp.float32)
    mixer_normal, mixer_inverse = normal_parts(text_start + region_start + attended)
    hidden = mixer_normal * w_mixer_gain + w_mixer_shift
    hidden_low = hidden.astype(jnp.bfloat16)
    inner = jnp.dot(hidden_low, w_expand, preferred_element_type=jnp.float32) + w_expand_bias
    activated_low = jax.nn.gelu(inner, approximate=False).astype(jnp.bfloat16)
    dense = jnp.dot(activated_low, w_reduce, preferred_element_type=jnp.float32) + w_reduce_bias
    output_normal, output_inverse = normal_parts(hidden + dense)
    layer_output = (output_normal * w_output_gain + w_output_shift).astype(jnp.bfloat16)

    upstream = cotangent.astype(jnp.float32)
    output_in_grad = normal_back(output_normal, output_inverse, w_output_gain, upstream)
    output_gain_grad = jnp.sum(upstream * output_normal, axis=0)
    output_shift_grad = jnp.sum(upstream, axis=0)
    dense_low = output_in_grad.astype(jnp.bfloat16)
    reduce_bias_grad = jnp.sum(output_in_grad, axis=0)
    reduce_weight_grad = (jnp.dot(activated_low.T, dense_low, preferred_element_type=jnp.float32))
    activated_grad = jnp.dot(dense_low, w_reduce.T, preferred_element_type=jnp.float32)
    unused, gelu_pull = jax.vjp(partial(jax.nn.gelu, approximate=False), inner)
    inner_low = gelu_pull(activated_grad)[0].astype(jnp.bfloat16)
    expand_bias_grad = jnp.sum(inner_low.astype(jnp.float32), axis=0)
    expand_weight_grad = (jnp.dot(hidden_low.T, inner_low, preferred_element_type=jnp.float32))
    hidden_grad = output_in_grad + jnp.dot(inner_low, w_expand.T, preferred_element_type=jnp.float32)
    mixer_in_grad = normal_back(mixer_normal, mixer_inverse, w_mixer_gain, hidden_grad)
    mixer_gain_grad = jnp.sum(hidden_grad * mixer_normal, axis=0)
    mixer_shift_grad = jnp.sum(hidden_grad, axis=0)
    attended_low = mixer_in_grad.astype(jnp.bfloat16)
    merge_weight_grad = (jnp.dot(merged_low.T, attended_low, preferred_element_type=jnp.float32))
    merged_grad = jnp.dot(attended_low, w_merge.T, preferred_element_type=jnp.float32).astype(jnp.bfloat16)
    proj_grad, linear_sums, planar_sums = attend_back(proj, probs, merged_grad, anchor_rows, anchor_cols)

    def columns(first, last):
        return proj_grad[:, first * MODEL_WIDTH : last * MODEL_WIDTH]

    def weight_columns(left, first, last):
        return jnp.dot(left.T, columns(first, last), preferred_element_type=jnp.float32).astype(jnp.bfloat16)

    def input_columns(first, last):
        return jnp.dot(
            columns(first, last),
            w_wide[:, first * MODEL_WIDTH : last * MODEL_WIDTH].T,
            preferred_element_type=jnp.float32,
        )

    stream_weights_grad = (
        jnp.concatenate(
            [
                weight_columns(text_low, 0, 3),
                weight_columns(text_space, 3, 5),
                weight_columns(region_low, 5, 8),
                weight_columns(region_space, 8, 10),
            ],
            axis=1,
        )
    )
    text_start_grad = mixer_in_grad + input_columns(0, 3)
    region_start_grad = mixer_in_grad + input_columns(5, 8)
    space_grads = jnp.concatenate([input_columns(3, 5), input_columns(8, 10)], axis=0).astype(jnp.bfloat16)
    position_table_grad = jnp.concatenate(
        [
            jnp.dot(onehot.T, space_grads, preferred_element_type=jnp.float32).astype(jnp.bfloat16)
            for onehot in (onehot_x, onehot_y)
        ],
        axis=1,
    )
    text_gradient = jnp.where(text_hit, 0.0, text_start_grad)
    text_blank_grad = jnp.sum(jnp.where(text_hit, text_start_grad, 0.0), axis=0)
    region_blank_grad = jnp.sum(jnp.where(region_hit, region_start_grad, 0.0), axis=0)
    normal_grad = jnp.where(region_hit, 0.0, region_start_grad)
    totals = exchange(
        folded([jnp.sum(normal_grad, axis=0), jnp.sum(normal_grad * normal_feat, axis=0)]), add_up, 3, "total"
    ).reshape(2, -1)
    shift_total = totals[0, :MODEL_WIDTH]
    gain_total = totals[1, :MODEL_WIDTH]
    conv_grad = (
        w_batch_gain
        * inverse_std
        * (normal_grad - shift_total / token_total - normal_feat * gain_total / token_total)
    ).astype(jnp.bfloat16)
    feature_gradient = jnp.dot(conv_grad, w_backbone.T, preferred_element_type=jnp.float32)
    backbone_weight_grad = (
        jnp.dot(region_features.T, conv_grad, preferred_element_type=jnp.float32)
    )
    owner_start = lax.axis_index(AXES) * share
    batch_gain_gradient = lax.dynamic_slice_in_dim(gain_total, owner_start, share)
    batch_shift_gradient = lax.dynamic_slice_in_dim(shift_total, owner_start, share)
    vector_grads = jnp.stack(
        [
            text_blank_grad, region_blank_grad, mixer_gain_grad, mixer_shift_grad, reduce_bias_grad,
            output_gain_grad, output_shift_grad,
        ]
    )
    small_grads = jnp.concatenate(
        [
            vector_grads.reshape(7, devices, share).transpose(1, 0, 2).reshape(devices, -1),
            expand_bias_grad.reshape(devices, -1),
            linear_folded(linear_sums[:, 0]).T.reshape(devices, -1),
            planar_sums[:, 0].T.reshape(devices, -1),
        ],
        axis=1,
    )
    small_grads = jnp.pad(small_grads, ((0, 0), (0, SMALL - small_grads.shape[1]))).reshape(devices, -1, 128)
    weight_grads = (
        stream_weights_grad, expand_weight_grad, reduce_weight_grad, merge_weight_grad, position_table_grad,
        backbone_weight_grad,
    )
    small, *shares = scatter_all([small_grads, *(blocks_of(grad, devices) for grad in weight_grads)], 1)
    small = small.reshape(-1)
    (
        stream_weights_grad, expand_weight_grad, reduce_weight_grad, merge_weight_grad, position_table_grad,
        backbone_weight_grad,
    ) = (part.reshape(-1, grad.shape[1]) for part, grad in zip(shares, weight_grads))
    vector_shares = [small[k * share : (k + 1) * share] for k in range(7)]
    start = 7 * share
    stop = start + expand_bias.shape[0]
    return (
        layer_output,
        text_gradient,
        feature_gradient,
        backbone_weight_grad,
        batch_gain_gradient,
        batch_shift_gradient,
        vector_shares[0],
        vector_shares[1],
        position_table_grad,
        stream_weights_grad,
        small[stop : stop + bias_share].reshape(-1, HEADS),
        small[stop + bias_share : stop + 2 * bias_share].reshape(-1, HEADS),
        merge_weight_grad,
        vector_shares[2],
        vector_shares[3],
        expand_weight_grad,
        small[start:stop],
        reduce_weight_grad,
        vector_shares[4],
        vector_shares[5],
        vector_shares[6],
    )


def solution(mesh):
    in_specs = (
        P(("dp", "pair"), None),
        P(("dp", "pair"), None),
        P(("dp", "pair")),
        P(("dp", "pair")),
        P(None, ("dp", "pair")),
        P(None, ("dp", "pair")),
        P(("dp", "pair"), None),
        P(("dp", "pair")),
        P(("dp", "pair")),
        P(("dp", "pair")),
        P(("dp", "pair")),
        P(("dp", "pair"), None),
        P(("dp", "pair"), None),
        P(("dp", "pair"), None),
        P(("dp", "pair"), None),
        P(("dp", "pair"), None),
        P(("dp", "pair")),
        P(("dp", "pair")),
        P(("dp", "pair"), None),
        P(("dp", "pair")),
        P(("dp", "pair"), None),
        P(("dp", "pair")),
        P(("dp", "pair")),
        P(("dp", "pair")),
        P(("dp", "pair"), None),
    )
    out_specs = (
        P(("dp", "pair"), None),
        P(("dp", "pair"), None),
        P(("dp", "pair"), None),
        P(("dp", "pair"), None),
        P(("dp", "pair")),
        P(("dp", "pair")),
        P(("dp", "pair")),
        P(("dp", "pair")),
        P(("dp", "pair"), None),
        P(("dp", "pair"), None),
        P(("dp", "pair"), None),
        P(("dp", "pair"), None),
        P(("dp", "pair"), None),
        P(("dp", "pair")),
        P(("dp", "pair")),
        P(("dp", "pair"), None),
        P(("dp", "pair")),
        P(("dp", "pair"), None),
        P(("dp", "pair")),
        P(("dp", "pair")),
        P(("dp", "pair")),
    )
    return jax.shard_map(
        per_device, mesh=mesh, in_specs=in_specs, out_specs=out_specs, check_vma=False
    )
```

```python
from functools import partial
from types import SimpleNamespace

import jax
import jax.numpy as jnp
from jax import lax
from jax.experimental import pallas as pl
from jax.experimental.pallas import tpu as pltpu
from jax.sharding import PartitionSpec as P

HEADS = 12
HEAD_DIM = 64
COORDS = 1024
REL_B = 256
SP_SIDE = 16
PAGE_TOKENS = 256
MODEL_WIDTH = 768
SP_B = 256
COORD_STEP = 128
PAIRS = HEADS // 2
LANES = 2 * HEAD_DIM


def dot_nt(left, right):
    return lax.dot_general(left, right, (((1,), (1,)), ((), ())), preferred_element_type=jnp.float32)


def dot_tn(left, right):
    return lax.dot_general(left, right, (((0,), (0,)), ((), ())), preferred_element_type=jnp.float32)


def dot_nn(left, right):
    return lax.dot_general(left, right, (((1,), (0,)), ((), ())), preferred_element_type=jnp.float32)


def head_columns(stream, kind, pair):
    return pl.ds(pl.multiple_of(((5 * stream + kind) * PAIRS + pair) * LANES, LANES), LANES)


def make_boxes(rows_ref, cols_ref, box_ref):
    for stream in range(2):
        part = []
        for axis in range(2):
            along = rows_ref[2 * stream + axis : 2 * stream + axis + 1, :]
            down = cols_ref[:, 2 * stream + axis : 2 * stream + axis + 1]
            part.append(((along - down) >> 7) + SP_SIDE // 2)
        box_ref[stream] = part[0] * SP_SIDE + part[1]


def attend_pair(pair, proj_ref, linear_ref, planar_ref, box_ref, merged_ref, probs_ref):
    lane_head = lax.broadcasted_iota(jnp.int32, (PAGE_TOKENS, LANES), 1) // HEAD_DIM
    mixed = [None, None]
    for inner in range(2):
        head = 2 * pair + inner
        mine = lane_head == inner
        spread = jnp.broadcast_to(linear_ref[head], (PAGE_TOKENS, 2 * PAGE_TOKENS))
        linear_term = pltpu.roll(spread, PAGE_TOKENS + 1, 1, stride=1, stride_axis=0)[:, :PAGE_TOKENS]
        low_table = jnp.broadcast_to(planar_ref[head, :, :128], (PAGE_TOKENS, 128))
        high_table = jnp.broadcast_to(planar_ref[head, :, 128:], (PAGE_TOKENS, 128))
        total = None
        for stream in range(2):
            pieces = [proj_ref[:, head_columns(stream, kind, pair)] for kind in range(5)]
            zero = jnp.zeros_like(pieces[0])
            left = jnp.concatenate([jnp.where(mine, pieces[0], zero), jnp.where(mine, pieces[3], zero)], axis=1)
            right = jnp.concatenate([pieces[1], pieces[4]], axis=1)
            logits = dot_nt(left, right) * HEAD_DIM ** (-0.5)
            planar = []
            for half in range(2):
                box = box_ref[stream, :, 128 * half : 128 * half + 128]
                place = box & 127
                planar.append(
                    jnp.where(
                        box < 128,
                        jnp.take_along_axis(low_table, place, axis=1),
                        jnp.take_along_axis(high_table, place, axis=1),
                    )
                )
            logits = logits + linear_term + jnp.concatenate(planar, axis=1)
            top = jnp.max(logits, axis=-1, keepdims=True)
            shifted = jnp.exp(logits - top)
            probs = shifted / jnp.sum(shifted, axis=-1, keepdims=True)
            probs_ref[stream, inner] = probs
            part = dot_nn(probs.astype(jnp.bfloat16), pieces[2])
            total = part if total is None else total + part
        mixed[inner] = total
    merged_ref[...] = jnp.where(lane_head == 0, mixed[0], mixed[1]).astype(jnp.bfloat16)


def make_places(rows_ref, cols_ref, place_ref, turned_ref, mask_ref, flip_ref):
    lanes = lax.broadcasted_iota(jnp.int32, (PAGE_TOKENS, SP_B), 1)
    rows = lax.broadcasted_iota(jnp.int32, (PAGE_TOKENS, SP_B), 0)
    flip_ref[...] = (lanes + rows == PAGE_TOKENS - 1).astype(jnp.bfloat16)
    for stream in range(2):
        x_row = rows_ref[2 * stream : 2 * stream + 1, :]
        y_row = rows_ref[2 * stream + 1 : 2 * stream + 2, :]
        x_col = cols_ref[:, 2 * stream : 2 * stream + 1]
        y_col = cols_ref[:, 2 * stream + 1 : 2 * stream + 2]
        cell_row = (x_row >> 7) * SP_SIDE + (y_row >> 7)
        cell_col = (x_col >> 7) * SP_SIDE + (y_col >> 7)
        x_less = ((x_row & 127) < (x_col & 127)).astype(jnp.float32)
        y_less = ((y_row & 127) < (y_col & 127)).astype(jnp.float32)
        for x_side in range(2):
            for y_side in range(2):
                side = 2 * x_side + y_side
                place_ref[stream, side * PAGE_TOKENS : (side + 1) * PAGE_TOKENS, :] = (
                    lanes == cell_col + (SP_SIDE + 1 - SP_SIDE * x_side - y_side)
                ).astype(jnp.bfloat16)
                mask_ref[stream, side] = (
                    (x_less if x_side else 1.0 - x_less) * (y_less if y_side else 1.0 - y_less)
                ).astype(jnp.bfloat16)
        turned_ref[stream] = (rows[:128] == 127 - cell_row).astype(jnp.bfloat16)


def attend_back_pair(
    pair, proj_ref, probs_ref, upstream_ref, grad_ref, linear_ref, planar_ref,
    place_ref, turned_ref, mask_ref, flip_ref,
):
    lane_head = lax.broadcasted_iota(jnp.int32, (PAGE_TOKENS, LANES), 1) // HEAD_DIM
    wide_head = jnp.concatenate([lane_head, lane_head], axis=1)
    upstream = upstream_ref[...]
    scale = HEAD_DIM ** (-0.5)
    diagonal = [None, None]
    for stream in range(2):
        pieces = [proj_ref[:, head_columns(stream, kind, pair)] for kind in range(5)]
        queries = jnp.concatenate([pieces[0], pieces[3]], axis=1)
        keys = jnp.concatenate([pieces[1], pieces[4]], axis=1)
        grads = []
        for inner in range(2):
            head = 2 * pair + inner
            mine = lane_head == inner
            grad_probs = dot_nt(jnp.where(mine, upstream, jnp.zeros_like(upstream)), pieces[2])
            probs = probs_ref[stream, inner]
            weighted = probs * grad_probs
            grad_logits = (weighted - probs * jnp.sum(weighted, axis=-1, keepdims=True)).astype(jnp.bfloat16)
            grads.append(
                (
                    dot_nn(grad_logits, keys) * scale,
                    dot_tn(grad_logits, queries) * scale,
                    dot_tn(probs.astype(jnp.bfloat16), upstream),
                )
            )
            parts = jnp.concatenate([grad_logits * mask_ref[stream, side] for side in range(4)], axis=1)
            placed = dot_nn(parts, place_ref[stream])
            placed_high = placed.astype(jnp.bfloat16)
            placed_low = (placed - placed_high.astype(jnp.float32)).astype(jnp.bfloat16)
            turned = turned_ref[stream]
            cells = dot_nn(turned, placed_high) + dot_nn(turned, placed_low)
            sums = jnp.sum(
                pltpu.roll(cells, SP_B - SP_SIDE // 2, 1, stride=1, stride_axis=0), axis=0, keepdims=True
            )
            if stream == 0:
                planar_ref[head] = sums
            else:
                planar_ref[head] += sums
            turned_over = dot_nn(flip_ref[...], grad_logits)
            diagonal[inner] = turned_over if stream == 0 else diagonal[inner] + turned_over
        query_grad, key_grad = (jnp.where(wide_head == 0, grads[0][k], grads[1][k]) for k in range(2))
        value_grad = jnp.where(lane_head == 0, grads[0][2], grads[1][2])
        for kind, value in enumerate(
            (query_grad[:, :LANES], key_grad[:, :LANES], value_grad, query_grad[:, LANES:], key_grad[:, LANES:])
        ):
            grad_ref[:, head_columns(stream, kind, pair)] = value.astype(jnp.bfloat16)
    for inner in range(2):
        padded = jnp.concatenate([diagonal[inner], jnp.zeros_like(diagonal[inner])], axis=1)
        linear_ref[2 * pair + inner] = jnp.sum(
            pltpu.roll(padded, 0, 1, stride=1, stride_axis=0), axis=0, keepdims=True
        )


def linear_extended(linear_bias):
    rows = linear_bias.astype(jnp.float32).T
    low = jnp.broadcast_to(rows[:, :1], (HEADS, PAGE_TOKENS - 1 - REL_B // 2))
    high = jnp.broadcast_to(rows[:, -1:], (HEADS, PAGE_TOKENS - REL_B // 2 + 1))
    return jnp.concatenate([low, rows, high], axis=1)[:, None, :]


def linear_folded(sums):
    first = REL_B // 2
    last = PAGE_TOKENS - 1 + REL_B // 2 - 1
    return jnp.concatenate(
        [
            jnp.sum(sums[:, :first], axis=1, keepdims=True),
            sums[:, first:last],
            jnp.sum(sums[:, last : 2 * PAGE_TOKENS - 1], axis=1, keepdims=True),
        ],
        axis=1,
    )


MESH = pl.DeviceIdType.MESH
RING = 4


def place():
    dp = lax.axis_index("dp")
    return dp // RING, lax.rem(dp, RING), lax.axis_index("pair")


def across(q, bit):
    other = lax.rem(q // bit, 2)
    return q + bit - 2 * bit * other


def greet(line):
    z, q, c = place()
    barrier = pltpu.get_barrier_semaphore()

    def signal(zz, qq, cc):
        pl.semaphore_signal(barrier, inc=1, device_id={"dp": zz * RING + qq, "pair": cc}, device_id_type=MESH)

    signal(z, across(q, 1), c)
    signal(z, across(q, 2), c)
    signal(z, q, 1 - c)

    @pl.when(z > 0)
    def _():
        signal(z - 1, q, c)

    @pl.when(z < line - 1)
    def _():
        signal(z + 1, q, c)

    ends = (z > 0).astype(jnp.int32) + (z < line - 1).astype(jnp.int32)
    pl.semaphore_wait(barrier, 3 + ends)


def spread(line, pumps, pump, first, work):
    total = line - first
    low, high = (first + total * (pump + k) // pumps for k in range(2))
    if high == low + 1:
        work(low)
    elif high > low:
        lax.fori_loop(low, high, lambda g, unused: (work(g), unused)[1], 0)


def gather_stages(line, ins, outs, sems):
    count = len(ins)
    (own_sem, z_send, z_recv, xy_send, xy_recv, d_send, d_recv, c_send, c_recv) = sems
    z, q, c = place()
    beside = (across(q, 1), across(q, 2))
    corner = across(across(q, 1), 2)

    def slot(zz, qq):
        return (zz * RING + qq) * 2 + c

    def remote(src, dst, send, recv, zz, qq, cc):
        return pltpu.make_async_remote_copy(
            src_ref=src, dst_ref=dst, send_sem=send, recv_sem=recv,
            device_id={"dp": zz * RING + qq, "pair": cc}, device_id_type=MESH,
        )

    def block(a, zz, qq):
        return outs[a].at[slot(zz, qq)]

    def halves(a):
        width = ins[a].shape[-1]
        cut = width // 2 if width % 256 == 0 else width
        return (0, cut), (cut, width - cut)

    def own(a):
        return pltpu.make_async_copy(ins[a], block(a, z, q), own_sem.at[a])

    def z_copy(a, way, step, first):
        zz = z - step if way == 0 else z + step
        target = z + 1 if way == 0 else z - 1
        src = ins[a] if first else block(a, zz, q)
        return remote(src, block(a, zz, q), z_send.at[way, a, step], z_recv.at[way, a, step], target, q, c)

    def xy_copy(a, axis, zz, first):
        src = ins[a] if first else block(a, zz, q)
        return remote(src, block(a, zz, q), xy_send.at[axis, a, zz], xy_recv.at[axis, a, zz], z, beside[axis], c)

    def d_copy(a, axis, zz):
        start, width = halves(a)[axis]
        part = outs[a].at[slot(zz, beside[axis]), :, pl.ds(start, width)]
        return remote(part, part, d_send.at[axis, a, zz], d_recv.at[axis, a, zz], z, beside[1 - axis], c)

    def c_copy(a, zz, qq, first):
        src = ins[a] if first else block(a, zz, qq)
        return remote(
            src, block(a, zz, qq), c_send.at[a, zz * RING + qq], c_recv.at[a, zz * RING + qq], z, q, 1 - c
        )

    def start():
        for a in range(count):
            own(a).start()
            for way in range(2):
                @pl.when(z < line - 1 if way == 0 else z > 0)
                def _():
                    z_copy(a, way, 0, True).start()
            for axis in range(2):
                xy_copy(a, axis, z, True).start()
            c_copy(a, z, q, True).start()

    def arrived(a, zz):
        for axis in range(2):
            xy_copy(a, axis, zz, False).start()
        c_copy(a, zz, q, False).start()

    def passed_on(a, zz):
        for axis in range(2):
            start, width = halves(a)[axis]
            got = block(a, zz, beside[axis])
            remote(got, got, xy_send.at[axis, a, zz], xy_recv.at[axis, a, zz], z, beside[axis], c).wait_recv()
            if width:
                d_copy(a, axis, zz).start()
            c_copy(a, zz, beside[axis], False).start()

    def finished(a, zz):
        for axis in range(2):
            start, width = halves(a)[axis]
            if width:
                part = outs[a].at[slot(zz, corner), :, pl.ds(start, width)]
                remote(part, part, d_send.at[axis, a, zz], d_recv.at[axis, a, zz], z, beside[1 - axis], c).wait_recv()
        c_copy(a, zz, corner, False).start()

    def both_ways(g, work):
        @pl.when(z - g >= 0)
        def _():
            work(z - g)

        @pl.when(jnp.logical_and(z + g <= line - 1, g > 0))
        def _():
            work(z + g)

    def along(g):
        for a in range(count):
            @pl.when(z - g >= 0)
            def _():
                got = block(a, z - g, q)
                remote(got, got, z_send.at[0, a, g - 1], z_recv.at[0, a, g - 1], z, q, 1 - c).wait_recv()

                @pl.when(z < line - 1)
                def _():
                    z_copy(a, 0, g, False).start()

                arrived(a, z - g)

            @pl.when(z + g <= line - 1)
            def _():
                got = block(a, z + g, q)
                remote(got, got, z_send.at[1, a, g - 1], z_recv.at[1, a, g - 1], z, q, 1 - c).wait_recv()

                @pl.when(z > 0)
                def _():
                    z_copy(a, 1, g, False).start()

                arrived(a, z + g)

    def around(g):
        for a in range(count):
            both_ways(g, partial(passed_on, a))

    def home(g):
        for a in range(count):
            both_ways(g, partial(finished, a))

    def drain(zz, unused):
        for a in range(count):
            for axis in range(2):
                xy_copy(a, axis, zz, False).wait_send()
                if halves(a)[axis][1]:
                    d_copy(a, axis, zz).wait_send()
            for qq in range(RING):
                c_copy(a, zz, qq, False).wait_send()
                got = outs[a].at[(zz * RING + qq) * 2 + 1 - c]
                remote(
                    got, got, c_send.at[a, zz * RING + qq], c_recv.at[a, zz * RING + qq], z, q, 1 - c
                ).wait_recv()

            @pl.when(jnp.logical_and(z < line - 1, zz <= z))
            def _():
                z_copy(a, 0, z - zz, False).wait_send()

            @pl.when(jnp.logical_and(z > 0, zz >= z))
            def _():
                z_copy(a, 1, zz - z, False).wait_send()
        return unused

    def end():
        for a in range(count):
            own(a).wait()
        lax.fori_loop(0, line, drain, 0)

    return SimpleNamespace(start=start, along=along, around=around, home=home, end=end)


def gather_sems(line, count):
    dma = pltpu.SemaphoreType.DMA
    return [
        dma((count,)),
        *(dma((2, count, line)) for k in range(6)),
        dma((count, line * RING)),
        dma((count, line * RING)),
    ]


def gather_kernel(line, count, *refs):
    stages = gather_stages(line, refs[:count], refs[count : 2 * count], refs[2 * count :])
    greet(line)
    stages.start()

    def generation(g, unused):
        @pl.when(g <= line - 1)
        def _():
            stages.along(g)

        @pl.when(g <= line)
        def _():
            stages.around(g - 1)

        @pl.when(g >= 2)
        def _():
            stages.home(g - 2)

        return unused

    lax.fori_loop(1, line + 2, generation, 0)
    stages.end()


def gather_all(shards, collective_id):
    dp = lax.axis_size("dp")
    line = dp // RING
    devices = 2 * dp
    count = len(shards)
    return pl.pallas_call(
        partial(gather_kernel, line, count),
        in_specs=[pl.BlockSpec(memory_space=pl.ANY)] * count,
        out_specs=[pl.BlockSpec(memory_space=pl.ANY)] * count,
        out_shape=[jax.ShapeDtypeStruct((devices, *shard.shape), shard.dtype) for shard in shards],
        scratch_shapes=gather_sems(line, count),
        compiler_params=pltpu.CompilerParams(collective_id=collective_id, has_side_effects=True),
        name="gather_all",
    )(*shards)


def scatter_stages(line, ins, outs, scratch):
    count = len(ins)
    groups = [scratch[k * count : (k + 1) * count] for k in range(5)]
    mine, beside_sum, half_in, full_in, line_in = groups
    (own_sem, c_send, c_recv, d_send, d_recv, xy_send, xy_recv, z_send, z_recv) = scratch[5 * count :]
    z, q, c = place()
    beside = (across(q, 1), across(q, 2))
    corner = across(across(q, 1), 2)

    def remote(src, dst, send, recv, zz, qq, cc):
        return pltpu.make_async_remote_copy(
            src_ref=src, dst_ref=dst, send_sem=send, recv_sem=recv,
            device_id={"dp": zz * RING + qq, "pair": cc}, device_id_type=MESH,
        )

    def halves(a):
        width = outs[a].shape[-1]
        cut = width // 2 if width % 256 == 0 else width
        return (0, cut), (cut, width - cut)

    def wide(value):
        return value.astype(jnp.float32)

    def group(zz):
        return pl.ds(zz * RING, RING)

    def own(a, zz):
        return pltpu.make_async_copy(ins[a].at[group(zz), c], mine[a].at[group(zz)], own_sem.at[a, zz])

    def c_copy(a, zz):
        return remote(
            ins[a].at[group(zz), 1 - c], beside_sum[a].at[group(zz)], c_send.at[a, zz], c_recv.at[a, zz], z, q, 1 - c
        )

    def d_copy(a, axis, zz):
        start, width = halves(a)[axis]
        return remote(
            mine[a].at[zz * RING + corner, :, pl.ds(start, width)],
            half_in[a].at[zz, :, pl.ds(start, width)],
            d_send.at[axis, a, zz], d_recv.at[axis, a, zz], z, beside[axis], c,
        )

    def xy_copy(a, axis, zz):
        return remote(
            mine[a].at[zz * RING + beside[axis]], full_in[a].at[axis, zz],
            xy_send.at[axis, a, zz], xy_recv.at[axis, a, zz], z, beside[axis], c,
        )

    def z_copy(a, way, zz):
        return remote(
            mine[a].at[zz * RING + q], line_in[a].at[way, zz],
            z_send.at[way, a, zz], z_recv.at[way, a, zz], z + 1 if way == 0 else z - 1, q, c,
        )

    def both_ways(g, work):
        @pl.when(z - g >= 0)
        def _():
            work(z - g)

        @pl.when(jnp.logical_and(z + g <= line - 1, g > 0))
        def _():
            work(z + g)

    def begin(zz):
        for a in range(count):
            c_copy(a, zz).start()
            own(a, zz).start()

    def first(zz):
        for a in range(count):
            own(a, zz).wait()
            c_copy(a, zz).wait_recv()

            def one(qq, unused):
                k = zz * RING + qq
                mine[a][k] = mine[a][k] + beside_sum[a][k]
                return unused

            lax.fori_loop(0, RING, one, 0)
            for axis in range(2):
                if halves(a)[axis][1]:
                    d_copy(a, axis, zz).start()

    def second(zz):
        for a in range(count):
            for axis in range(2):
                start, width = halves(a)[axis]
                k = zz * RING + beside[1 - axis]
                if width:
                    d_copy(a, axis, zz).wait_recv()
                    mine[a][k, :, start : start + width] = (
                        mine[a][k, :, start : start + width] + half_in[a][zz, :, start : start + width]
                    )
                xy_copy(a, 1 - axis, zz).start()

    def third(zz):
        for a in range(count):
            k = zz * RING + q
            for axis in range(2):
                xy_copy(a, axis, zz).wait_recv()
            mine[a][k] = (
                wide(mine[a][k]) + wide(full_in[a][0, zz]) + wide(full_in[a][1, zz])
            ).astype(mine[a].dtype)
            for way in range(2):
                @pl.when(zz > z if way == 0 else zz < z)
                def _():
                    @pl.when(z > 0 if way == 0 else z < line - 1)
                    def _():
                        z_copy(a, way, zz).wait_recv()
                        mine[a][k] = mine[a][k] + line_in[a][way, zz]

                    z_copy(a, way, zz).start()

            @pl.when(zz == z)
            def _():
                outs[a][...] = wide(mine[a][k])
                for way in range(2):
                    @pl.when(z > 0 if way == 0 else z < line - 1)
                    def _():
                        z_copy(a, way, zz).wait_recv()
                        outs[a][...] += wide(line_in[a][way, zz])

    def start():
        def begin_all(step, unused):
            both_ways(line - 1 - step, begin)
            return unused

        lax.fori_loop(0, line, begin_all, 0)

    def drain(zz, unused):
        for a in range(count):
            for axis in range(2):
                xy_copy(a, axis, zz).wait_send()
                if halves(a)[axis][1]:
                    d_copy(a, axis, zz).wait_send()
            c_copy(a, zz).wait_send()
            for way in range(2):
                @pl.when(zz > z if way == 0 else zz < z)
                def _():
                    z_copy(a, way, zz).wait_send()
        return unused

    def end():
        lax.fori_loop(0, line, drain, 0)

    return SimpleNamespace(
        start=start,
        first=lambda step: both_ways(line - 1 - step, first),
        second=lambda step: both_ways(line - 1 - step, second),
        third=lambda step: both_ways(line - 1 - step, third),
        end=end,
    )


def scatter_scratch(line, blocks):
    dma = pltpu.SemaphoreType.DMA
    count = len(blocks)
    return [
        *(pltpu.VMEM((line * RING, *shape), kind) for shape, kind in blocks),
        *(pltpu.VMEM((line * RING, *shape), kind) for shape, kind in blocks),
        *(pltpu.VMEM((line, *shape), kind) for shape, kind in blocks),
        *(pltpu.VMEM((2, line, *shape), kind) for shape, kind in blocks),
        *(pltpu.VMEM((2, line, *shape), kind) for shape, kind in blocks),
        *(dma((count, line)) for k in range(3)),
        *(dma((2, count, line)) for k in range(6)),
    ]


def scatter_kernel(line, count, *refs):
    stages = scatter_stages(line, refs[:count], refs[count : 2 * count], refs[2 * count :])
    greet(line)
    stages.start()

    def generation(step, unused):
        @pl.when(step < line)
        def _():
            stages.first(step)

        @pl.when(jnp.logical_and(step >= 1, step <= line))
        def _():
            stages.second(step - 1)

        @pl.when(step >= 2)
        def _():
            stages.third(step - 2)

        return unused

    lax.fori_loop(0, line + 2, generation, 0)
    stages.end()


def scatter_all(grads, collective_id):
    dp = lax.axis_size("dp")
    line = dp // RING
    count = len(grads)
    blocks = [(grad.shape[1:], grad.dtype) for grad in grads]
    return pl.pallas_call(
        partial(scatter_kernel, line, count),
        in_specs=[pl.BlockSpec(memory_space=pl.ANY)] * count,
        out_specs=[pl.BlockSpec(memory_space=pltpu.VMEM)] * count,
        out_shape=[jax.ShapeDtypeStruct(shape, jnp.float32) for shape, kind in blocks],
        scratch_shapes=scatter_scratch(line, blocks),
        compiler_params=pltpu.CompilerParams(
            collective_id=collective_id, has_side_effects=True, vmem_limit_bytes=63 << 20
        ),
        name="scatter_all",
    )(*(grad.reshape(line * RING, 2, *grad.shape[1:]) for grad in grads))


def exchange_kernel(line, combine, value_ref, total_ref, near_ref, part_ref, far_ref, n_send, n_recv, f_send, f_recv):
    z, q, c = place()
    cell = q * 2 + c
    near = RING * 2
    barrier = pltpu.get_barrier_semaphore()

    def near_place(k):
        other = lax.rem(cell + k, near)
        return other, {"dp": z * RING + other // 2, "pair": lax.rem(other, 2)}

    def far_place(k):
        other = lax.rem(z + k, line)
        return other, {"dp": other * RING + q, "pair": c}

    def each(places, stop, work):
        def one(k, unused):
            work(*places(k))
            return unused

        lax.fori_loop(1, stop, one, 0)

    def signal(other, device):
        pl.semaphore_signal(barrier, inc=1, device_id=device, device_id_type=MESH)

    each(near_place, near, signal)
    each(far_place, line, signal)
    pl.semaphore_wait(barrier, near + line - 2)

    def near_copy(other, device, source):
        return pltpu.make_async_remote_copy(
            src_ref=value_ref, dst_ref=near_ref.at[source], send_sem=n_send.at[other], recv_sem=n_recv.at[source],
            device_id=device, device_id_type=MESH,
        )

    def far_copy(other, device, source):
        return pltpu.make_async_remote_copy(
            src_ref=part_ref, dst_ref=far_ref.at[source], send_sem=f_send.at[other], recv_sem=f_recv.at[source],
            device_id=device, device_id_type=MESH,
        )

    each(near_place, near, lambda other, device: near_copy(other, device, cell).start())
    near_ref[cell] = value_ref[...]
    each(near_place, near, lambda other, device: near_copy(other, device, other).wait_recv())
    part_ref[...] = combine(near_ref, near, 1)
    each(far_place, line, lambda other, device: far_copy(other, device, z).start())
    far_ref[z] = part_ref[...]
    each(far_place, line, lambda other, device: far_copy(other, device, other).wait_recv())
    total_ref[...] = combine(far_ref, line, near)
    each(near_place, near, lambda other, device: near_copy(other, device, cell).wait_send())
    each(far_place, line, lambda other, device: far_copy(other, device, z).wait_send())


def add_up(parts, count, weight):
    return lax.fori_loop(1, count, lambda k, total: total + parts[k], parts[0])


def pool_statistics(rows, parts, count, weight):
    mean = lax.fori_loop(1, count, lambda k, total: total + parts[k, 0], parts[0, 0]) / count

    def squares(k, total):
        offset = parts[k, 0] - mean
        return total + parts[k, 1] + (rows * weight) * (offset * offset)

    return jnp.stack([mean, lax.fori_loop(0, count, squares, jnp.zeros_like(mean))])


def exchange(value, combine, collective_id, name):
    line = lax.axis_size("dp") // RING
    near = RING * 2
    dma = pltpu.SemaphoreType.DMA
    vmem = pl.BlockSpec(memory_space=pltpu.VMEM)
    return pl.pallas_call(
        partial(exchange_kernel, line, combine),
        in_specs=[vmem],
        out_specs=vmem,
        out_shape=jax.ShapeDtypeStruct(value.shape, value.dtype),
        scratch_shapes=[
            pltpu.VMEM((near, *value.shape), value.dtype),
            pltpu.VMEM(value.shape, value.dtype),
            pltpu.VMEM((line, *value.shape), value.dtype),
            dma((near,)),
            dma((near,)),
            dma((line,)),
            dma((line,)),
        ],
        compiler_params=pltpu.CompilerParams(collective_id=collective_id, has_side_effects=True),
        name=name,
    )(value)


KINDS = 10


def source_of(column):
    stream = column // 5
    return 2 * stream + (column - 5 * stream) // 3


def once(shape):
    return pl.BlockSpec(shape, lambda i: (0,) * len(shape), pipeline_mode=pl.Buffered(1))


def at_steps(schedule):
    step = pl.program_id(0)
    for when, work in schedule:
        @pl.when(step == when)
        def _():
            for one in work:
                one()


def forward_kernel(line, count, *refs):
    lefts_ref, weight_ref, linear_ref, planar_ref, rows_ref, cols_ref = refs[:6]
    ins = refs[6 : 6 + count]
    proj_ref, merged_ref, probs_ref = refs[6 + count : 9 + count]
    outs = refs[9 + count : 9 + 2 * count]
    box_ref = refs[9 + 2 * count]
    stages = gather_stages(line, ins, outs, refs[10 + 2 * count :])
    step = pl.program_id(0)

    @pl.when(step == 0)
    def _():
        greet(line)
        stages.start()
        make_boxes(rows_ref, cols_ref, box_ref)

    @pl.when(step < KINDS)
    def _():
        columns = pl.ds(pl.multiple_of(step * MODEL_WIDTH, MODEL_WIDTH), MODEL_WIDTH)
        proj_ref[:, columns] = dot_nn(lefts_ref[source_of(step)], weight_ref[...]).astype(jnp.bfloat16)

    @pl.when(step >= KINDS)
    def _():
        attend_pair(step - KINDS, proj_ref, linear_ref, planar_ref, box_ref, merged_ref, probs_ref)

    def along(k):
        return lambda: spread(line, 3, k, 1, stages.along)

    def around(k):
        return lambda: spread(line, 4, k, 0, stages.around)

    def home(k):
        return lambda: spread(line, 4, k, 0, stages.home)

    at_steps(
        [
            (3, [along(0)]),
            (6, [along(1)]),
            (9, [along(2), around(0)]),
            (12, [around(1), home(0)]),
            (14, [around(2), home(1)]),
            (15, [around(3), home(2), home(3), stages.end]),
        ]
    )


def forward_layer(lefts, weights, linear_ext, planar_rows, anchor_rows, anchor_cols, shards, collective_id):
    dp = lax.axis_size("dp")
    line = dp // RING
    count = len(shards)
    anywhere = pl.BlockSpec(memory_space=pl.ANY)
    width = weights.shape[1]
    return pl.pallas_call(
        partial(forward_kernel, line, count),
        grid=(KINDS + PAIRS,),
        in_specs=[
            once(lefts.shape),
            pl.BlockSpec((MODEL_WIDTH, MODEL_WIDTH), lambda i: (0, jnp.minimum(i, KINDS - 1))),
            once(linear_ext.shape),
            once(planar_rows.shape),
            once(anchor_rows.shape),
            once(anchor_cols.shape),
            *[anywhere] * count,
        ],
        out_specs=[
            pl.BlockSpec((PAGE_TOKENS, width), lambda i: (0, 0)),
            pl.BlockSpec((PAGE_TOKENS, LANES), lambda i: (0, jnp.maximum(i - KINDS, 0))),
            pl.BlockSpec((2, 2, PAGE_TOKENS, PAGE_TOKENS), lambda i: (0, jnp.maximum(i - KINDS, 0), 0, 0)),
            *[anywhere] * count,
        ],
        out_shape=[
            jax.ShapeDtypeStruct((PAGE_TOKENS, width), jnp.bfloat16),
            jax.ShapeDtypeStruct((PAGE_TOKENS, MODEL_WIDTH), jnp.bfloat16),
            jax.ShapeDtypeStruct((2, HEADS, PAGE_TOKENS, PAGE_TOKENS), jnp.float32),
            *(jax.ShapeDtypeStruct((2 * dp, *shard.shape), shard.dtype) for shard in shards),
        ],
        scratch_shapes=[pltpu.VMEM((2, PAGE_TOKENS, PAGE_TOKENS), jnp.int32), *gather_sems(line, count)],
        compiler_params=pltpu.CompilerParams(
            collective_id=collective_id, has_side_effects=True, vmem_limit_bytes=60 << 20
        ),
        name="forward_layer",
    )(lefts, weights, linear_ext, planar_rows, anchor_rows, anchor_cols, *shards)


def backward_kernel(line, count, *refs):
    proj_ref, probs_ref, upstream_ref, rows_ref, cols_ref, lefts_ref, weight_ref = refs[:7]
    ins = refs[7 : 7 + count]
    linear_ref, planar_ref, weight_grad_ref, input_grad_ref = refs[7 + count : 11 + count]
    outs = refs[11 + count : 11 + 2 * count]
    grad_ref, turned_left_ref = refs[11 + 2 * count : 13 + 2 * count]
    helpers = refs[13 + 2 * count : 17 + 2 * count]
    stages = scatter_stages(line, ins, outs, refs[17 + 2 * count :])
    step = pl.program_id(0)

    @pl.when(step == 0)
    def _():
        greet(line)
        stages.start()
        make_places(rows_ref, cols_ref, *helpers)

    @pl.when(step < PAIRS)
    def _():
        attend_back_pair(step, proj_ref, probs_ref, upstream_ref, grad_ref, linear_ref, planar_ref, *helpers)

    @pl.when(step >= PAIRS)
    def _():
        column = step - PAIRS
        source = source_of(column)
        fresh = jnp.logical_or(column == 0, source != source_of(jnp.maximum(column - 1, 0)))
        grads = grad_ref[:, pl.ds(pl.multiple_of(column * MODEL_WIDTH, MODEL_WIDTH), MODEL_WIDTH)]

        @pl.when(fresh)
        def _():
            turned_left_ref[...] = lefts_ref[source].T

        weight_grad_ref[...] = dot_nn(turned_left_ref[...], grads).astype(jnp.bfloat16)
        back = dot_nt(grads, weight_ref[...])

        @pl.when(fresh)
        def _():
            input_grad_ref[source] = back

        @pl.when(jnp.logical_not(fresh))
        def _():
            input_grad_ref[source] += back

    def first(k):
        return lambda: spread(line, 4, k, 0, stages.first)

    def second(k):
        return lambda: spread(line, 4, k, 0, stages.second)

    def third(k):
        return lambda: spread(line, 4, k, 0, stages.third)

    at_steps(
        [
            (1, [first(0)]),
            (2, [second(0), first(1)]),
            (3, [second(1), first(2)]),
            (4, [second(2), first(3), third(0)]),
            (5, [second(3), third(1)]),
            (9, [third(2)]),
            (15, [third(3), stages.end]),
        ]
    )


def backward_layer(proj, probs, upstream, anchor_rows, anchor_cols, lefts, weights, grads, collective_id):
    dp = lax.axis_size("dp")
    line = dp // RING
    count = len(grads)
    blocks = [(grad.shape[1:], grad.dtype) for grad in grads]
    anywhere = pl.BlockSpec(memory_space=pl.ANY)

    def pair_at(i):
        return jnp.minimum(i, PAIRS - 1)

    def column_at(i):
        return jnp.maximum(i - PAIRS, 0)

    return pl.pallas_call(
        partial(backward_kernel, line, count),
        grid=(PAIRS + KINDS,),
        in_specs=[
            once(proj.shape),
            pl.BlockSpec((2, 2, PAGE_TOKENS, PAGE_TOKENS), lambda i: (0, pair_at(i), 0, 0)),
            pl.BlockSpec((PAGE_TOKENS, LANES), lambda i: (0, pair_at(i))),
            once(anchor_rows.shape),
            once(anchor_cols.shape),
            once(lefts.shape),
            pl.BlockSpec((MODEL_WIDTH, MODEL_WIDTH), lambda i: (0, column_at(i))),
            *[anywhere] * count,
        ],
        out_specs=[
            pl.BlockSpec((HEADS, 1, 2 * PAGE_TOKENS), lambda i: (0, 0, 0)),
            pl.BlockSpec((HEADS, 1, SP_B), lambda i: (0, 0, 0)),
            pl.BlockSpec((MODEL_WIDTH, MODEL_WIDTH), lambda i: (0, column_at(i))),
            pl.BlockSpec(lefts.shape, lambda i: (0, 0, 0)),
            *(pl.BlockSpec(shape, lambda i: (0, 0)) for shape, kind in blocks),
        ],
        out_shape=[
            jax.ShapeDtypeStruct((HEADS, 1, 2 * PAGE_TOKENS), jnp.float32),
            jax.ShapeDtypeStruct((HEADS, 1, SP_B), jnp.float32),
            jax.ShapeDtypeStruct(weights.shape, jnp.bfloat16),
            jax.ShapeDtypeStruct(lefts.shape, jnp.float32),
            *(jax.ShapeDtypeStruct(shape, jnp.float32) for shape, kind in blocks),
        ],
        scratch_shapes=[
            pltpu.VMEM(proj.shape, jnp.bfloat16),
            pltpu.VMEM((MODEL_WIDTH, PAGE_TOKENS), jnp.bfloat16),
            pltpu.VMEM((2, 4 * PAGE_TOKENS, SP_B), jnp.bfloat16),
            pltpu.VMEM((2, 128, PAGE_TOKENS), jnp.bfloat16),
            pltpu.VMEM((2, 4, PAGE_TOKENS, PAGE_TOKENS), jnp.bfloat16),
            pltpu.VMEM((PAGE_TOKENS, PAGE_TOKENS), jnp.bfloat16),
            *scatter_scratch(line, blocks),
        ],
        compiler_params=pltpu.CompilerParams(
            collective_id=collective_id, has_side_effects=True, vmem_limit_bytes=63 << 20
        ),
        name="backward_layer",
    )(
        proj, probs, upstream, anchor_rows, anchor_cols, lefts, weights,
        *(grad.reshape(line * RING, 2, *grad.shape[1:]) for grad in grads),
    )

AXES = ("dp", "pair")
norm_epsilon = 1e-05
batch_epsilon = 1e-05


def folded(vectors):
    whole = jnp.stack([vector.reshape(-1, 128) for vector in vectors])
    return jnp.pad(whole, ((0, 0), (0, 8 - whole.shape[1]), (0, 0)))


def padded_rows(pieces):
    rows = [jnp.pad(piece.astype(jnp.float32), ((0, 0), (0, 128 - piece.shape[1]))) for piece in pieces]
    total = sum(piece.shape[0] for piece in pieces)
    rows.append(jnp.zeros((-total % 8, 128), jnp.float32))
    return jnp.concatenate(rows, axis=0)


def blocks_of(grad, devices):
    blocks = grad.astype(jnp.bfloat16).reshape(devices, grad.shape[0] // devices, grad.shape[1])
    return blocks if blocks.shape[1] % 8 == 0 else blocks.reshape(devices, -1, 128)


def normal_parts(values):
    center = values - jnp.mean(values, axis=-1, keepdims=True)
    inverse = lax.rsqrt(jnp.mean(center * center, axis=-1, keepdims=True) + norm_epsilon)
    return center * inverse, inverse


def normal_back(normal, inverse, gain, grad):
    scaled = grad * gain
    return inverse * (
        scaled
        - jnp.mean(scaled, axis=-1, keepdims=True)
        - normal * jnp.mean(scaled * normal, axis=-1, keepdims=True)
    )


def place_onehot(anchor_rows):
    coords = jnp.arange(COORDS, dtype=jnp.int32)
    return (anchor_rows[:, None] == coords[None, :]).astype(jnp.bfloat16)


def per_device(
    text_inputs,
    region_features,
    text_masked,
    region_masked,
    text_anchors,
    region_anchors,
    backbone_weight,
    batch_gain,
    batch_shift,
    text_blank,
    region_blank,
    position_table,
    stream_weights,
    linear_bias,
    planar_bias,
    merge_weight,
    mixer_gain,
    mixer_shift,
    expand_weight,
    expand_bias,
    reduce_weight,
    reduce_bias,
    output_gain,
    output_shift,
    cotangent,
):
    devices = lax.axis_size(AXES)
    row_count = text_inputs.shape[0]
    token_total = row_count * devices
    share = MODEL_WIDTH // devices
    expand_share = expand_bias.shape[0]
    bias_rows = REL_B // devices
    vectors = jnp.stack(
        [
            batch_gain, batch_shift, text_blank, region_blank, mixer_gain, mixer_shift, reduce_bias,
            output_gain, output_shift,
        ]
    )
    small = padded_rows([linear_bias, planar_bias, vectors, expand_bias[None, :]])
    packed, w_backbone, w_table, w_stream = gather_all(
        (small, backbone_weight, position_table, stream_weights), 0
    )
    w_linear = packed[:, :bias_rows, :HEADS].reshape(REL_B, HEADS)
    w_planar = packed[:, bias_rows : 2 * bias_rows, :HEADS].reshape(SP_B, HEADS)
    w_vectors = packed[:, 2 * bias_rows : 2 * bias_rows + 9, :share].transpose(1, 0, 2).reshape(9, -1)
    w_expand_bias = packed[:, 2 * bias_rows + 9, :expand_share].reshape(-1)
    (
        w_batch_gain, w_batch_shift, w_text_blank, w_region_blank, w_mixer_gain, w_mixer_shift,
        w_reduce_bias, w_output_gain, w_output_shift,
    ) = (w_vectors[k] for k in range(9))
    w_backbone, w_table, w_stream = (
        whole.reshape(-1, whole.shape[-1]) for whole in (w_backbone, w_table, w_stream)
    )

    conv = jnp.dot(region_features, w_backbone, preferred_element_type=jnp.float32)
    local_mean = jnp.mean(conv, axis=0)
    local_center = conv - local_mean
    local_square = jnp.sum(local_center * local_center, axis=0)
    pooled = exchange(
        folded([local_mean, local_square]), partial(pool_statistics, float(row_count)), 2, "pool"
    ).reshape(2, -1)
    batch_mean = pooled[0, :MODEL_WIDTH]
    batch_var = pooled[1, :MODEL_WIDTH] / token_total
    inverse_std = lax.rsqrt(batch_var + batch_epsilon)
    normal_feat = (conv - batch_mean) * inverse_std
    region_hit = region_masked[:, None] == 1
    text_hit = text_masked[:, None] == 1
    region_start = jnp.where(region_hit, w_region_blank[None, :], normal_feat * w_batch_gain + w_batch_shift)
    text_start = jnp.where(text_hit, w_text_blank[None, :], text_inputs.astype(jnp.float32))
    onehot_x = place_onehot(jnp.concatenate([text_anchors[0], region_anchors[0]]))
    onehot_y = place_onehot(jnp.concatenate([text_anchors[1], region_anchors[1]]))
    space = (
        jnp.dot(onehot_x, w_table[:, :MODEL_WIDTH], preferred_element_type=jnp.float32)
        + jnp.dot(onehot_y, w_table[:, MODEL_WIDTH:], preferred_element_type=jnp.float32)
    ).astype(jnp.bfloat16)
    lefts = jnp.stack(
        [
            text_start.astype(jnp.bfloat16), space[:row_count], region_start.astype(jnp.bfloat16),
            space[row_count:],
        ]
    )
    anchor_rows = jnp.concatenate([text_anchors, region_anchors], axis=0)
    anchor_cols = anchor_rows.T
    proj, merged_low, probs, *wholes = forward_layer(
        lefts, w_stream, linear_extended(w_linear), w_planar.T[:, None, :], anchor_rows, anchor_cols,
        (merge_weight, expand_weight, reduce_weight), 4,
    )
    w_merge, w_expand, w_reduce = (whole.reshape(-1, whole.shape[-1]) for whole in wholes)
    attended = jnp.dot(merged_low, w_merge, preferred_element_type=jnp.float32)
    mixer_normal, mixer_inverse = normal_parts(text_start + region_start + attended)
    hidden = mixer_normal * w_mixer_gain + w_mixer_shift
    hidden_low = hidden.astype(jnp.bfloat16)
    inner = jnp.dot(hidden_low, w_expand, preferred_element_type=jnp.float32) + w_expand_bias
    activated_low = jax.nn.gelu(inner, approximate=False).astype(jnp.bfloat16)
    dense = jnp.dot(activated_low, w_reduce, preferred_element_type=jnp.float32) + w_reduce_bias
    output_normal, output_inverse = normal_parts(hidden + dense)
    layer_output = (output_normal * w_output_gain + w_output_shift).astype(jnp.bfloat16)

    upstream = cotangent.astype(jnp.float32)
    output_in_grad = normal_back(output_normal, output_inverse, w_output_gain, upstream)
    output_gain_grad = jnp.sum(upstream * output_normal, axis=0)
    output_shift_grad = jnp.sum(upstream, axis=0)
    dense_low = output_in_grad.astype(jnp.bfloat16)
    reduce_bias_grad = jnp.sum(output_in_grad, axis=0)
    reduce_weight_grad = jnp.dot(activated_low.T, dense_low, preferred_element_type=jnp.float32)
    activated_grad = jnp.dot(dense_low, w_reduce.T, preferred_element_type=jnp.float32)
    unused, gelu_pull = jax.vjp(partial(jax.nn.gelu, approximate=False), inner)
    inner_low = gelu_pull(activated_grad)[0].astype(jnp.bfloat16)
    expand_bias_grad = jnp.sum(inner_low.astype(jnp.float32), axis=0)
    expand_weight_grad = jnp.dot(hidden_low.T, inner_low, preferred_element_type=jnp.float32)
    hidden_grad = output_in_grad + jnp.dot(inner_low, w_expand.T, preferred_element_type=jnp.float32)
    mixer_in_grad = normal_back(mixer_normal, mixer_inverse, w_mixer_gain, hidden_grad)
    mixer_gain_grad = jnp.sum(hidden_grad * mixer_normal, axis=0)
    mixer_shift_grad = jnp.sum(hidden_grad, axis=0)
    attended_low = mixer_in_grad.astype(jnp.bfloat16)
    merge_weight_grad = jnp.dot(merged_low.T, attended_low, preferred_element_type=jnp.float32)
    merged_grad = jnp.dot(attended_low, w_merge.T, preferred_element_type=jnp.float32).astype(jnp.bfloat16)
    early = (expand_weight_grad, reduce_weight_grad, merge_weight_grad)
    linear_sums, planar_sums, stream_weights_grad, input_grads, *early_shares = backward_layer(
        proj, probs, merged_grad, anchor_rows, anchor_cols, lefts, w_stream,
        [blocks_of(grad, devices) for grad in early], 5,
    )
    expand_weight_grad, reduce_weight_grad, merge_weight_grad = (
        part.reshape(-1, grad.shape[1]) for part, grad in zip(early_shares, early)
    )
    text_start_grad = mixer_in_grad + input_grads[0]
    region_start_grad = mixer_in_grad + input_grads[2]
    space_grads = jnp.concatenate([input_grads[1], input_grads[3]], axis=0).astype(jnp.bfloat16)
    position_table_grad = jnp.concatenate(
        [
            jnp.dot(onehot.T, space_grads, preferred_element_type=jnp.float32).astype(jnp.bfloat16)
            for onehot in (onehot_x, onehot_y)
        ],
        axis=1,
    )
    text_gradient = jnp.where(text_hit, 0.0, text_start_grad)
    text_blank_grad = jnp.sum(jnp.where(text_hit, text_start_grad, 0.0), axis=0)
    region_blank_grad = jnp.sum(jnp.where(region_hit, region_start_grad, 0.0), axis=0)
    normal_grad = jnp.where(region_hit, 0.0, region_start_grad)
    totals = exchange(
        folded([jnp.sum(normal_grad, axis=0), jnp.sum(normal_grad * normal_feat, axis=0)]), add_up, 3, "total"
    ).reshape(2, -1)
    shift_total = totals[0, :MODEL_WIDTH]
    gain_total = totals[1, :MODEL_WIDTH]
    conv_grad = (
        w_batch_gain
        * inverse_std
        * (normal_grad - shift_total / token_total - normal_feat * gain_total / token_total)
    ).astype(jnp.bfloat16)
    feature_gradient = jnp.dot(conv_grad, w_backbone.T, preferred_element_type=jnp.float32)
    backbone_weight_grad = jnp.dot(region_features.T, conv_grad, preferred_element_type=jnp.float32)
    owner_start = lax.axis_index(AXES) * share
    batch_gain_gradient = lax.dynamic_slice_in_dim(gain_total, owner_start, share)
    batch_shift_gradient = lax.dynamic_slice_in_dim(shift_total, owner_start, share)
    vector_grads = jnp.stack(
        [
            text_blank_grad, region_blank_grad, mixer_gain_grad, mixer_shift_grad, reduce_bias_grad,
            output_gain_grad, output_shift_grad,
        ]
    )
    pieces = [
        linear_folded(linear_sums[:, 0]).T.reshape(devices, bias_rows, HEADS),
        planar_sums[:, 0].T.reshape(devices, bias_rows, HEADS),
        vector_grads.reshape(7, devices, share).transpose(1, 0, 2),
        expand_bias_grad.reshape(devices, 1, expand_share),
    ]
    small_grads = jax.vmap(lambda *parts: padded_rows(parts))(*pieces)
    late = (stream_weights_grad, position_table_grad, backbone_weight_grad)
    small, *shares = scatter_all([small_grads, *(blocks_of(grad, devices) for grad in late)], 1)
    stream_weights_grad, position_table_grad, backbone_weight_grad = (
        part.reshape(-1, grad.shape[1]) for part, grad in zip(shares, late)
    )
    vector_shares = small[2 * bias_rows : 2 * bias_rows + 7, :share]
    return (
        layer_output,
        text_gradient,
        feature_gradient,
        backbone_weight_grad,
        batch_gain_gradient,
        batch_shift_gradient,
        vector_shares[0],
        vector_shares[1],
        position_table_grad,
        stream_weights_grad,
        small[:bias_rows, :HEADS],
        small[bias_rows : 2 * bias_rows, :HEADS],
        merge_weight_grad,
        vector_shares[2],
        vector_shares[3],
        expand_weight_grad,
        small[2 * bias_rows + 7, :expand_share],
        reduce_weight_grad,
        vector_shares[4],
        vector_shares[5],
        vector_shares[6],
    )


def solution(mesh):
    in_specs = (
        P(("dp", "pair"), None),
        P(("dp", "pair"), None),
        P(("dp", "pair")),
        P(("dp", "pair")),
        P(None, ("dp", "pair")),
        P(None, ("dp", "pair")),
        P(("dp", "pair"), None),
        P(("dp", "pair")),
        P(("dp", "pair")),
        P(("dp", "pair")),
        P(("dp", "pair")),
        P(("dp", "pair"), None),
        P(("dp", "pair"), None),
        P(("dp", "pair"), None),
        P(("dp", "pair"), None),
        P(("dp", "pair"), None),
        P(("dp", "pair")),
        P(("dp", "pair")),
        P(("dp", "pair"), None),
        P(("dp", "pair")),
        P(("dp", "pair"), None),
        P(("dp", "pair")),
        P(("dp", "pair")),
        P(("dp", "pair")),
        P(("dp", "pair"), None),
    )
    out_specs = (
        P(("dp", "pair"), None),
        P(("dp", "pair"), None),
        P(("dp", "pair"), None),
        P(("dp", "pair"), None),
        P(("dp", "pair")),
        P(("dp", "pair")),
        P(("dp", "pair")),
        P(("dp", "pair")),
        P(("dp", "pair"), None),
        P(("dp", "pair"), None),
        P(("dp", "pair"), None),
        P(("dp", "pair"), None),
        P(("dp", "pair"), None),
        P(("dp", "pair")),
        P(("dp", "pair")),
        P(("dp", "pair"), None),
        P(("dp", "pair")),
        P(("dp", "pair"), None),
        P(("dp", "pair")),
        P(("dp", "pair")),
        P(("dp", "pair")),
    )
    return jax.shard_map(
        per_device, mesh=mesh, in_specs=in_specs, out_specs=out_specs, check_vma=False
    )
```

```python
from functools import partial
from types import SimpleNamespace

import jax
import jax.numpy as jnp
from jax import lax
from jax.experimental import pallas as pl
from jax.experimental.pallas import tpu as pltpu
from jax.sharding import PartitionSpec as P

HEADS = 12
HEAD_DIM = 64
COORDS = 1024
REL_B = 256
SP_SIDE = 16
PAGE_TOKENS = 256
MODEL_WIDTH = 768
SP_B = 256
COORD_STEP = 128
PAIRS = HEADS // 2
LANES = 2 * HEAD_DIM


def dot_nt(left, right):
    return lax.dot_general(left, right, (((1,), (1,)), ((), ())), preferred_element_type=jnp.float32)


def dot_tn(left, right):
    return lax.dot_general(left, right, (((0,), (0,)), ((), ())), preferred_element_type=jnp.float32)


def dot_nn(left, right):
    return lax.dot_general(left, right, (((1,), (0,)), ((), ())), preferred_element_type=jnp.float32)


def head_columns(stream, kind, pair):
    return pl.ds(pl.multiple_of(((5 * stream + kind) * PAIRS + pair) * LANES, LANES), LANES)


def make_boxes(rows_ref, cols_ref, box_ref):
    for stream in range(2):
        part = []
        for axis in range(2):
            along = rows_ref[2 * stream + axis : 2 * stream + axis + 1, :]
            down = cols_ref[:, 2 * stream + axis : 2 * stream + axis + 1]
            part.append(((along - down) >> 7) + SP_SIDE // 2)
        box_ref[stream] = part[0] * SP_SIDE + part[1]


def attend_pair(pair, proj_ref, linear_ref, planar_ref, box_ref, merged_ref, probs_ref):
    lane_head = lax.broadcasted_iota(jnp.int32, (PAGE_TOKENS, LANES), 1) // HEAD_DIM
    mixed = [None, None]
    for inner in range(2):
        head = 2 * pair + inner
        mine = lane_head == inner
        spread = jnp.broadcast_to(linear_ref[head], (PAGE_TOKENS, 2 * PAGE_TOKENS))
        linear_term = pltpu.roll(spread, PAGE_TOKENS + 1, 1, stride=1, stride_axis=0)[:, :PAGE_TOKENS]
        low_table = jnp.broadcast_to(planar_ref[head, :, :128], (PAGE_TOKENS, 128))
        high_table = jnp.broadcast_to(planar_ref[head, :, 128:], (PAGE_TOKENS, 128))
        total = None
        for stream in range(2):
            pieces = [proj_ref[:, head_columns(stream, kind, pair)] for kind in range(5)]
            zero = jnp.zeros_like(pieces[0])
            left = jnp.concatenate([jnp.where(mine, pieces[0], zero), jnp.where(mine, pieces[3], zero)], axis=1)
            right = jnp.concatenate([pieces[1], pieces[4]], axis=1)
            logits = dot_nt(left, right) * HEAD_DIM ** (-0.5)
            planar = []
            for half in range(2):
                box = box_ref[stream, :, 128 * half : 128 * half + 128]
                place = box & 127
                planar.append(
                    jnp.where(
                        box < 128,
                        jnp.take_along_axis(low_table, place, axis=1),
                        jnp.take_along_axis(high_table, place, axis=1),
                    )
                )
            logits = logits + linear_term + jnp.concatenate(planar, axis=1)
            top = jnp.max(logits, axis=-1, keepdims=True)
            shifted = jnp.exp(logits - top)
            probs = shifted / jnp.sum(shifted, axis=-1, keepdims=True)
            probs_ref[stream, inner] = probs
            part = dot_nn(probs.astype(jnp.bfloat16), pieces[2])
            total = part if total is None else total + part
        mixed[inner] = total
    merged_ref[...] = jnp.where(lane_head == 0, mixed[0], mixed[1]).astype(jnp.bfloat16)


def make_places(rows_ref, cols_ref, place_ref, turned_ref, mask_ref, flip_ref):
    lanes = lax.broadcasted_iota(jnp.int32, (PAGE_TOKENS, SP_B), 1)
    rows = lax.broadcasted_iota(jnp.int32, (PAGE_TOKENS, SP_B), 0)
    flip_ref[...] = (lanes + rows == PAGE_TOKENS - 1).astype(jnp.bfloat16)
    for stream in range(2):
        x_row = rows_ref[2 * stream : 2 * stream + 1, :]
        y_row = rows_ref[2 * stream + 1 : 2 * stream + 2, :]
        x_col = cols_ref[:, 2 * stream : 2 * stream + 1]
        y_col = cols_ref[:, 2 * stream + 1 : 2 * stream + 2]
        cell_row = (x_row >> 7) * SP_SIDE + (y_row >> 7)
        cell_col = (x_col >> 7) * SP_SIDE + (y_col >> 7)
        x_less = ((x_row & 127) < (x_col & 127)).astype(jnp.float32)
        y_less = ((y_row & 127) < (y_col & 127)).astype(jnp.float32)
        for x_side in range(2):
            for y_side in range(2):
                side = 2 * x_side + y_side
                place_ref[stream, side * PAGE_TOKENS : (side + 1) * PAGE_TOKENS, :] = (
                    lanes == cell_col + (SP_SIDE + 1 - SP_SIDE * x_side - y_side)
                ).astype(jnp.bfloat16)
                mask_ref[stream, side] = (
                    (x_less if x_side else 1.0 - x_less) * (y_less if y_side else 1.0 - y_less)
                ).astype(jnp.bfloat16)
        turned_ref[stream] = (rows[:128] == 127 - cell_row).astype(jnp.bfloat16)


def attend_back_pair(
    pair, pump, proj_ref, probs_ref, upstream_ref, grad_ref, linear_ref, planar_ref,
    place_ref, turned_ref, mask_ref, flip_ref,
):
    lane_head = lax.broadcasted_iota(jnp.int32, (PAGE_TOKENS, LANES), 1) // HEAD_DIM
    wide_head = jnp.concatenate([lane_head, lane_head], axis=1)
    upstream = upstream_ref[...]
    scale = HEAD_DIM ** (-0.5)
    diagonal = [None, None]
    for stream in range(2):
        pieces = [proj_ref[:, head_columns(stream, kind, pair)] for kind in range(5)]
        queries = jnp.concatenate([pieces[0], pieces[3]], axis=1)
        keys = jnp.concatenate([pieces[1], pieces[4]], axis=1)
        grads = []
        for inner in range(2):
            head = 2 * pair + inner
            mine = lane_head == inner
            grad_probs = dot_nt(jnp.where(mine, upstream, jnp.zeros_like(upstream)), pieces[2])
            probs = probs_ref[stream, inner]
            weighted = probs * grad_probs
            grad_logits = (weighted - probs * jnp.sum(weighted, axis=-1, keepdims=True)).astype(jnp.bfloat16)
            grads.append(
                (
                    dot_nn(grad_logits, keys) * scale,
                    dot_tn(grad_logits, queries) * scale,
                    dot_tn(probs.astype(jnp.bfloat16), upstream),
                )
            )
            parts = jnp.concatenate([grad_logits * mask_ref[stream, side] for side in range(4)], axis=1)
            placed = dot_nn(parts, place_ref[stream])
            placed_high = placed.astype(jnp.bfloat16)
            placed_low = (placed - placed_high.astype(jnp.float32)).astype(jnp.bfloat16)
            turned = turned_ref[stream]
            cells = dot_nn(turned, placed_high) + dot_nn(turned, placed_low)
            sums = jnp.sum(
                pltpu.roll(cells, SP_B - SP_SIDE // 2, 1, stride=1, stride_axis=0), axis=0, keepdims=True
            )
            if stream == 0:
                planar_ref[head] = sums
            else:
                planar_ref[head] += sums
            turned_over = dot_nn(flip_ref[...], grad_logits)
            diagonal[inner] = turned_over if stream == 0 else diagonal[inner] + turned_over
            pump(2 * stream + inner)
        query_grad, key_grad = (jnp.where(wide_head == 0, grads[0][k], grads[1][k]) for k in range(2))
        value_grad = jnp.where(lane_head == 0, grads[0][2], grads[1][2])
        for kind, value in enumerate(
            (query_grad[:, :LANES], key_grad[:, :LANES], value_grad, query_grad[:, LANES:], key_grad[:, LANES:])
        ):
            grad_ref[:, head_columns(stream, kind, pair)] = value.astype(jnp.bfloat16)
    for inner in range(2):
        padded = jnp.concatenate([diagonal[inner], jnp.zeros_like(diagonal[inner])], axis=1)
        linear_ref[2 * pair + inner] = jnp.sum(
            pltpu.roll(padded, 0, 1, stride=1, stride_axis=0), axis=0, keepdims=True
        )


def linear_extended(linear_bias):
    rows = linear_bias.astype(jnp.float32).T
    low = jnp.broadcast_to(rows[:, :1], (HEADS, PAGE_TOKENS - 1 - REL_B // 2))
    high = jnp.broadcast_to(rows[:, -1:], (HEADS, PAGE_TOKENS - REL_B // 2 + 1))
    return jnp.concatenate([low, rows, high], axis=1)[:, None, :]


def linear_folded(sums):
    first = REL_B // 2
    last = PAGE_TOKENS - 1 + REL_B // 2 - 1
    return jnp.concatenate(
        [
            jnp.sum(sums[:, :first], axis=1, keepdims=True),
            sums[:, first:last],
            jnp.sum(sums[:, last : 2 * PAGE_TOKENS - 1], axis=1, keepdims=True),
        ],
        axis=1,
    )


MESH = pl.DeviceIdType.MESH
RING = 4


def place():
    dp = lax.axis_index("dp")
    return dp // RING, lax.rem(dp, RING), lax.axis_index("pair")


def across(q, bit):
    other = lax.rem(q // bit, 2)
    return q + bit - 2 * bit * other


def greet(line):
    z, q, c = place()
    barrier = pltpu.get_barrier_semaphore()

    def signal(zz, qq, cc):
        pl.semaphore_signal(barrier, inc=1, device_id={"dp": zz * RING + qq, "pair": cc}, device_id_type=MESH)

    signal(z, across(q, 1), c)
    signal(z, across(q, 2), c)
    signal(z, q, 1 - c)

    @pl.when(z > 0)
    def _():
        signal(z - 1, q, c)

    @pl.when(z < line - 1)
    def _():
        signal(z + 1, q, c)

    ends = (z > 0).astype(jnp.int32) + (z < line - 1).astype(jnp.int32)
    pl.semaphore_wait(barrier, 3 + ends)


def spread(line, pumps, pump, first, work):
    total = line - first
    low, high = (first + total * (pump + k) // pumps for k in range(2))
    if high == low + 1:
        work(low)
    elif high > low:
        lax.fori_loop(low, high, lambda g, unused: (work(g), unused)[1], 0)


def gather_stages(line, ins, outs, sems):
    count = len(ins)
    (own_sem, z_send, z_recv, xy_send, xy_recv, d_send, d_recv, c_send, c_recv) = sems
    z, q, c = place()
    beside = (across(q, 1), across(q, 2))
    corner = across(across(q, 1), 2)

    def slot(zz, qq):
        return (zz * RING + qq) * 2 + c

    def remote(src, dst, send, recv, zz, qq, cc):
        return pltpu.make_async_remote_copy(
            src_ref=src, dst_ref=dst, send_sem=send, recv_sem=recv,
            device_id={"dp": zz * RING + qq, "pair": cc}, device_id_type=MESH,
        )

    def block(a, zz, qq):
        return outs[a].at[slot(zz, qq)]

    def halves(a):
        width = ins[a].shape[-1]
        cut = width // 2 if width % 256 == 0 else width
        return (0, cut), (cut, width - cut)

    def own(a):
        return pltpu.make_async_copy(ins[a], block(a, z, q), own_sem.at[a])

    def z_copy(a, way, step, first):
        zz = z - step if way == 0 else z + step
        target = z + 1 if way == 0 else z - 1
        src = ins[a] if first else block(a, zz, q)
        return remote(src, block(a, zz, q), z_send.at[way, a, step], z_recv.at[way, a, step], target, q, c)

    def xy_copy(a, axis, zz, first):
        src = ins[a] if first else block(a, zz, q)
        return remote(src, block(a, zz, q), xy_send.at[axis, a, zz], xy_recv.at[axis, a, zz], z, beside[axis], c)

    def d_copy(a, axis, zz):
        start, width = halves(a)[axis]
        part = outs[a].at[slot(zz, beside[axis]), :, pl.ds(start, width)]
        return remote(part, part, d_send.at[axis, a, zz], d_recv.at[axis, a, zz], z, beside[1 - axis], c)

    def c_copy(a, zz, qq, first):
        src = ins[a] if first else block(a, zz, qq)
        return remote(
            src, block(a, zz, qq), c_send.at[a, zz * RING + qq], c_recv.at[a, zz * RING + qq], z, q, 1 - c
        )

    def start():
        for a in range(count):
            own(a).start()
            for way in range(2):
                @pl.when(z < line - 1 if way == 0 else z > 0)
                def _():
                    z_copy(a, way, 0, True).start()
            for axis in range(2):
                xy_copy(a, axis, z, True).start()
            c_copy(a, z, q, True).start()

    def arrived(a, zz):
        for axis in range(2):
            xy_copy(a, axis, zz, False).start()
        c_copy(a, zz, q, False).start()

    def passed_on(a, zz):
        for axis in range(2):
            start, width = halves(a)[axis]
            got = block(a, zz, beside[axis])
            remote(got, got, xy_send.at[axis, a, zz], xy_recv.at[axis, a, zz], z, beside[axis], c).wait_recv()
            if width:
                d_copy(a, axis, zz).start()
            c_copy(a, zz, beside[axis], False).start()

    def finished(a, zz):
        for axis in range(2):
            start, width = halves(a)[axis]
            if width:
                part = outs[a].at[slot(zz, corner), :, pl.ds(start, width)]
                remote(part, part, d_send.at[axis, a, zz], d_recv.at[axis, a, zz], z, beside[1 - axis], c).wait_recv()
        c_copy(a, zz, corner, False).start()

    def both_ways(g, work):
        @pl.when(z - g >= 0)
        def _():
            work(z - g)

        @pl.when(jnp.logical_and(z + g <= line - 1, g > 0))
        def _():
            work(z + g)

    def along(g):
        for a in range(count):
            @pl.when(z - g >= 0)
            def _():
                got = block(a, z - g, q)
                remote(got, got, z_send.at[0, a, g - 1], z_recv.at[0, a, g - 1], z, q, 1 - c).wait_recv()

                @pl.when(z < line - 1)
                def _():
                    z_copy(a, 0, g, False).start()

                arrived(a, z - g)

            @pl.when(z + g <= line - 1)
            def _():
                got = block(a, z + g, q)
                remote(got, got, z_send.at[1, a, g - 1], z_recv.at[1, a, g - 1], z, q, 1 - c).wait_recv()

                @pl.when(z > 0)
                def _():
                    z_copy(a, 1, g, False).start()

                arrived(a, z + g)

    def around(g):
        for a in range(count):
            both_ways(g, partial(passed_on, a))

    def home(g):
        for a in range(count):
            both_ways(g, partial(finished, a))

    def drain(zz, unused):
        for a in range(count):
            for axis in range(2):
                xy_copy(a, axis, zz, False).wait_send()
                if halves(a)[axis][1]:
                    d_copy(a, axis, zz).wait_send()
            for qq in range(RING):
                c_copy(a, zz, qq, False).wait_send()
                got = outs[a].at[(zz * RING + qq) * 2 + 1 - c]
                remote(
                    got, got, c_send.at[a, zz * RING + qq], c_recv.at[a, zz * RING + qq], z, q, 1 - c
                ).wait_recv()

            @pl.when(jnp.logical_and(z < line - 1, zz <= z))
            def _():
                z_copy(a, 0, z - zz, False).wait_send()

            @pl.when(jnp.logical_and(z > 0, zz >= z))
            def _():
                z_copy(a, 1, zz - z, False).wait_send()
        return unused

    def end():
        for a in range(count):
            own(a).wait()
        lax.fori_loop(0, line, drain, 0)

    return SimpleNamespace(start=start, along=along, around=around, home=home, end=end)


def gather_sems(line, count):
    dma = pltpu.SemaphoreType.DMA
    return [
        dma((count,)),
        *(dma((2, count, line)) for k in range(6)),
        dma((count, line * RING)),
        dma((count, line * RING)),
    ]


def gather_kernel(line, count, *refs):
    stages = gather_stages(line, refs[:count], refs[count : 2 * count], refs[2 * count :])
    greet(line)
    stages.start()

    def generation(g, unused):
        @pl.when(g <= line - 1)
        def _():
            stages.along(g)

        @pl.when(g <= line)
        def _():
            stages.around(g - 1)

        @pl.when(g >= 2)
        def _():
            stages.home(g - 2)

        return unused

    lax.fori_loop(1, line + 2, generation, 0)
    stages.end()


def gather_all(shards, collective_id):
    dp = lax.axis_size("dp")
    line = dp // RING
    devices = 2 * dp
    count = len(shards)
    return pl.pallas_call(
        partial(gather_kernel, line, count),
        in_specs=[pl.BlockSpec(memory_space=pl.ANY)] * count,
        out_specs=[pl.BlockSpec(memory_space=pl.ANY)] * count,
        out_shape=[jax.ShapeDtypeStruct((devices, *shard.shape), shard.dtype) for shard in shards],
        scratch_shapes=gather_sems(line, count),
        compiler_params=pltpu.CompilerParams(collective_id=collective_id, has_side_effects=True),
        name="gather_all",
    )(*shards)


def scatter_stages(line, ins, outs, scratch):
    count = len(ins)
    groups = [scratch[k * count : (k + 1) * count] for k in range(5)]
    mine, beside_sum, half_in, full_in, line_in = groups
    (own_sem, c_send, c_recv, d_send, d_recv, xy_send, xy_recv, z_send, z_recv) = scratch[5 * count :]
    z, q, c = place()
    beside = (across(q, 1), across(q, 2))
    corner = across(across(q, 1), 2)

    def remote(src, dst, send, recv, zz, qq, cc):
        return pltpu.make_async_remote_copy(
            src_ref=src, dst_ref=dst, send_sem=send, recv_sem=recv,
            device_id={"dp": zz * RING + qq, "pair": cc}, device_id_type=MESH,
        )

    def halves(a):
        width = outs[a].shape[-1]
        cut = width // 2 if width % 256 == 0 else width
        return (0, cut), (cut, width - cut)

    def wide(value):
        return value.astype(jnp.float32)

    def group(zz):
        return pl.ds(zz * RING, RING)

    def own(a, zz):
        return pltpu.make_async_copy(ins[a].at[group(zz), c], mine[a].at[group(zz)], own_sem.at[a, zz])

    def c_copy(a, zz):
        return remote(
            ins[a].at[group(zz), 1 - c], beside_sum[a].at[group(zz)], c_send.at[a, zz], c_recv.at[a, zz], z, q, 1 - c
        )

    def d_copy(a, axis, zz):
        start, width = halves(a)[axis]
        return remote(
            mine[a].at[zz * RING + corner, :, pl.ds(start, width)],
            half_in[a].at[zz, :, pl.ds(start, width)],
            d_send.at[axis, a, zz], d_recv.at[axis, a, zz], z, beside[axis], c,
        )

    def xy_copy(a, axis, zz):
        return remote(
            mine[a].at[zz * RING + beside[axis]], full_in[a].at[axis, zz],
            xy_send.at[axis, a, zz], xy_recv.at[axis, a, zz], z, beside[axis], c,
        )

    def z_copy(a, way, zz):
        return remote(
            mine[a].at[zz * RING + q], line_in[a].at[way, zz],
            z_send.at[way, a, zz], z_recv.at[way, a, zz], z + 1 if way == 0 else z - 1, q, c,
        )

    def both_ways(g, work):
        @pl.when(z - g >= 0)
        def _():
            work(z - g)

        @pl.when(jnp.logical_and(z + g <= line - 1, g > 0))
        def _():
            work(z + g)

    def begin(zz):
        for a in range(count):
            c_copy(a, zz).start()
            own(a, zz).start()

    def first(zz):
        for a in range(count):
            own(a, zz).wait()
            c_copy(a, zz).wait_recv()

            def one(qq, unused):
                k = zz * RING + qq
                mine[a][k] = mine[a][k] + beside_sum[a][k]
                return unused

            lax.fori_loop(0, RING, one, 0)
            for axis in range(2):
                if halves(a)[axis][1]:
                    d_copy(a, axis, zz).start()

    def second(zz):
        for a in range(count):
            for axis in range(2):
                start, width = halves(a)[axis]
                k = zz * RING + beside[1 - axis]
                if width:
                    d_copy(a, axis, zz).wait_recv()
                    mine[a][k, :, start : start + width] = (
                        mine[a][k, :, start : start + width] + half_in[a][zz, :, start : start + width]
                    )
                xy_copy(a, 1 - axis, zz).start()

    def third(zz):
        for a in range(count):
            k = zz * RING + q
            for axis in range(2):
                xy_copy(a, axis, zz).wait_recv()
            mine[a][k] = (
                wide(mine[a][k]) + wide(full_in[a][0, zz]) + wide(full_in[a][1, zz])
            ).astype(mine[a].dtype)
            for way in range(2):
                @pl.when(zz > z if way == 0 else zz < z)
                def _():
                    @pl.when(z > 0 if way == 0 else z < line - 1)
                    def _():
                        z_copy(a, way, zz).wait_recv()
                        mine[a][k] = mine[a][k] + line_in[a][way, zz]

                    z_copy(a, way, zz).start()

            @pl.when(zz == z)
            def _():
                outs[a][...] = wide(mine[a][k])
                for way in range(2):
                    @pl.when(z > 0 if way == 0 else z < line - 1)
                    def _():
                        z_copy(a, way, zz).wait_recv()
                        outs[a][...] += wide(line_in[a][way, zz])

    def start():
        def begin_all(step, unused):
            both_ways(line - 1 - step, begin)
            return unused

        lax.fori_loop(0, line, begin_all, 0)

    def drain(zz, unused):
        for a in range(count):
            for axis in range(2):
                xy_copy(a, axis, zz).wait_send()
                if halves(a)[axis][1]:
                    d_copy(a, axis, zz).wait_send()
            c_copy(a, zz).wait_send()
            for way in range(2):
                @pl.when(zz > z if way == 0 else zz < z)
                def _():
                    z_copy(a, way, zz).wait_send()
        return unused

    def end():
        lax.fori_loop(0, line, drain, 0)

    return SimpleNamespace(
        start=start,
        first=lambda step: both_ways(line - 1 - step, first),
        second=lambda step: both_ways(line - 1 - step, second),
        third=lambda step: both_ways(line - 1 - step, third),
        end=end,
    )


def scatter_scratch(line, blocks):
    dma = pltpu.SemaphoreType.DMA
    count = len(blocks)
    return [
        *(pltpu.VMEM((line * RING, *shape), kind) for shape, kind in blocks),
        *(pltpu.VMEM((line * RING, *shape), kind) for shape, kind in blocks),
        *(pltpu.VMEM((line, *shape), kind) for shape, kind in blocks),
        *(pltpu.VMEM((2, line, *shape), kind) for shape, kind in blocks),
        *(pltpu.VMEM((2, line, *shape), kind) for shape, kind in blocks),
        *(dma((count, line)) for k in range(3)),
        *(dma((2, count, line)) for k in range(6)),
    ]


def scatter_kernel(line, count, *refs):
    stages = scatter_stages(line, refs[:count], refs[count : 2 * count], refs[2 * count :])
    greet(line)
    stages.start()

    def generation(step, unused):
        @pl.when(step < line)
        def _():
            stages.first(step)

        @pl.when(jnp.logical_and(step >= 1, step <= line))
        def _():
            stages.second(step - 1)

        @pl.when(step >= 2)
        def _():
            stages.third(step - 2)

        return unused

    lax.fori_loop(0, line + 2, generation, 0)
    stages.end()


def scatter_all(grads, collective_id):
    dp = lax.axis_size("dp")
    line = dp // RING
    count = len(grads)
    blocks = [(grad.shape[1:], grad.dtype) for grad in grads]
    return pl.pallas_call(
        partial(scatter_kernel, line, count),
        in_specs=[pl.BlockSpec(memory_space=pl.ANY)] * count,
        out_specs=[pl.BlockSpec(memory_space=pltpu.VMEM)] * count,
        out_shape=[jax.ShapeDtypeStruct(shape, jnp.float32) for shape, kind in blocks],
        scratch_shapes=scatter_scratch(line, blocks),
        compiler_params=pltpu.CompilerParams(
            collective_id=collective_id, has_side_effects=True, vmem_limit_bytes=63 << 20
        ),
        name="scatter_all",
    )(*(grad.reshape(line * RING, 2, *grad.shape[1:]) for grad in grads))


def peers(line):
    z, q, c = place()
    cell = q * 2 + c
    near = RING * 2

    def near_place(k):
        other = lax.rem(cell + k, near)
        return other, {"dp": z * RING + other // 2, "pair": lax.rem(other, 2)}

    def far_place(k):
        other = lax.rem(z + k, line)
        return other, {"dp": other * RING + q, "pair": c}

    def each(places, stop, work):
        def one(k, unused):
            work(*places(k))
            return unused

        lax.fori_loop(1, stop, one, 0)

    return partial(each, near_place, near), partial(each, far_place, line)


def greet_peers(line):
    barrier = pltpu.get_barrier_semaphore()
    for each in peers(line):
        each(
            lambda other, device: pl.semaphore_signal(barrier, inc=1, device_id=device, device_id_type=MESH)
        )
    pl.semaphore_wait(barrier, 2 * RING + line - 2)


def exchange_stages(line, combine, value_ref, total_ref, scratch):
    near_ref, part_ref, far_ref, n_send, n_recv, f_send, f_recv = scratch
    z, q, c = place()
    cell = q * 2 + c
    each_near, each_far = peers(line)

    def near_copy(other, device, source):
        return pltpu.make_async_remote_copy(
            src_ref=value_ref, dst_ref=near_ref.at[source], send_sem=n_send.at[other], recv_sem=n_recv.at[source],
            device_id=device, device_id_type=MESH,
        )

    def far_copy(other, device, source):
        return pltpu.make_async_remote_copy(
            src_ref=part_ref, dst_ref=far_ref.at[source], send_sem=f_send.at[other], recv_sem=f_recv.at[source],
            device_id=device, device_id_type=MESH,
        )

    def near():
        each_near(lambda other, device: near_copy(other, device, cell).start())
        near_ref[cell] = value_ref[...]

    def far():
        each_near(lambda other, device: near_copy(other, device, other).wait_recv())
        part_ref[...] = combine(near_ref, 2 * RING, 1)
        each_far(lambda other, device: far_copy(other, device, z).start())
        far_ref[z] = part_ref[...]

    def total():
        each_far(lambda other, device: far_copy(other, device, other).wait_recv())
        total_ref[...] = combine(far_ref, line, 2 * RING)

    def end():
        each_near(lambda other, device: near_copy(other, device, cell).wait_send())
        each_far(lambda other, device: far_copy(other, device, z).wait_send())

    return SimpleNamespace(near=near, far=far, total=total, end=end)


def exchange_scratch(line, shape):
    dma = pltpu.SemaphoreType.DMA
    near = 2 * RING
    return [
        pltpu.VMEM((near, *shape), jnp.float32),
        pltpu.VMEM(shape, jnp.float32),
        pltpu.VMEM((line, *shape), jnp.float32),
        dma((near,)),
        dma((near,)),
        dma((line,)),
        dma((line,)),
    ]


def exchange_kernel(line, combine, value_ref, total_ref, *scratch):
    stages = exchange_stages(line, combine, value_ref, total_ref, scratch)
    greet_peers(line)
    stages.near()
    stages.far()
    stages.total()
    stages.end()


def add_up(parts, count, weight):
    return lax.fori_loop(1, count, lambda k, total: total + parts[k], parts[0])


def pool_statistics(rows, parts, count, weight):
    mean = lax.fori_loop(1, count, lambda k, total: total + parts[k, 0], parts[0, 0]) / count

    def squares(k, total):
        offset = parts[k, 0] - mean
        return total + parts[k, 1] + (rows * weight) * (offset * offset)

    return jnp.stack([mean, lax.fori_loop(0, count, squares, jnp.zeros_like(mean))])


def exchange(value, combine, collective_id, name):
    line = lax.axis_size("dp") // RING
    vmem = pl.BlockSpec(memory_space=pltpu.VMEM)
    return pl.pallas_call(
        partial(exchange_kernel, line, combine),
        in_specs=[vmem],
        out_specs=vmem,
        out_shape=jax.ShapeDtypeStruct(value.shape, value.dtype),
        scratch_shapes=exchange_scratch(line, value.shape),
        compiler_params=pltpu.CompilerParams(collective_id=collective_id, has_side_effects=True),
        name=name,
    )(value)


KINDS = 10


def source_of(column):
    stream = column // 5
    return 2 * stream + (column - 5 * stream) // 3


def once(shape):
    return pl.BlockSpec(shape, lambda i: (0,) * len(shape), pipeline_mode=pl.Buffered(1))


def at_steps(schedule):
    step = pl.program_id(0)
    for when, work in schedule:
        @pl.when(step == when)
        def _():
            for one in work:
                one()


def forward_kernel(line, count, *refs):
    lefts_ref, weight_ref, linear_ref, planar_ref, rows_ref, cols_ref = refs[:6]
    ins = refs[6 : 6 + count]
    proj_ref, merged_ref, probs_ref = refs[6 + count : 9 + count]
    outs = refs[9 + count : 9 + 2 * count]
    box_ref = refs[9 + 2 * count]
    stages = gather_stages(line, ins, outs, refs[10 + 2 * count :])
    step = pl.program_id(0)

    @pl.when(step == 0)
    def _():
        greet(line)
        stages.start()
        make_boxes(rows_ref, cols_ref, box_ref)

    @pl.when(step < KINDS)
    def _():
        columns = pl.ds(pl.multiple_of(step * MODEL_WIDTH, MODEL_WIDTH), MODEL_WIDTH)
        proj_ref[:, columns] = dot_nn(lefts_ref[source_of(step)], weight_ref[...]).astype(jnp.bfloat16)

    @pl.when(step >= KINDS)
    def _():
        attend_pair(step - KINDS, proj_ref, linear_ref, planar_ref, box_ref, merged_ref, probs_ref)

    def along(k):
        return lambda: spread(line, 3, k, 1, stages.along)

    def around(k):
        return lambda: spread(line, 4, k, 0, stages.around)

    def home(k):
        return lambda: spread(line, 4, k, 0, stages.home)

    at_steps(
        [
            (7, [along(0), around(0)]),
            (11, [along(1)]),
            (12, [around(1)]),
            (14, [along(2), home(0)]),
            (15, [around(2), home(1), around(3), home(2), home(3), stages.end]),
        ]
    )


def forward_layer(lefts, weights, linear_ext, planar_rows, anchor_rows, anchor_cols, shards, collective_id):
    dp = lax.axis_size("dp")
    line = dp // RING
    count = len(shards)
    anywhere = pl.BlockSpec(memory_space=pl.ANY)
    width = weights.shape[1]
    return pl.pallas_call(
        partial(forward_kernel, line, count),
        grid=(KINDS + PAIRS,),
        in_specs=[
            once(lefts.shape),
            pl.BlockSpec((MODEL_WIDTH, MODEL_WIDTH), lambda i: (0, jnp.minimum(i, KINDS - 1))),
            once(linear_ext.shape),
            once(planar_rows.shape),
            once(anchor_rows.shape),
            once(anchor_cols.shape),
            *[anywhere] * count,
        ],
        out_specs=[
            pl.BlockSpec((PAGE_TOKENS, width), lambda i: (0, 0)),
            pl.BlockSpec((PAGE_TOKENS, LANES), lambda i: (0, jnp.maximum(i - KINDS, 0))),
            pl.BlockSpec((2, 2, PAGE_TOKENS, PAGE_TOKENS), lambda i: (0, jnp.maximum(i - KINDS, 0), 0, 0)),
            *[anywhere] * count,
        ],
        out_shape=[
            jax.ShapeDtypeStruct((PAGE_TOKENS, width), jnp.bfloat16),
            jax.ShapeDtypeStruct((PAGE_TOKENS, MODEL_WIDTH), jnp.bfloat16),
            jax.ShapeDtypeStruct((2, HEADS, PAGE_TOKENS, PAGE_TOKENS), jnp.float32),
            *(jax.ShapeDtypeStruct((2 * dp, *shard.shape), shard.dtype) for shard in shards),
        ],
        scratch_shapes=[pltpu.VMEM((2, PAGE_TOKENS, PAGE_TOKENS), jnp.int32), *gather_sems(line, count)],
        compiler_params=pltpu.CompilerParams(
            collective_id=collective_id, has_side_effects=True, vmem_limit_bytes=60 << 20
        ),
        name="forward_layer",
    )(lefts, weights, linear_ext, planar_rows, anchor_rows, anchor_cols, *shards)


TABLE_STEP = PAIRS + KINDS


def backward_kernel(line, count, *refs):
    (
        proj_ref, probs_ref, upstream_ref, rows_ref, cols_ref, lefts_ref, weight_ref, mixer_grad_ref, normal_ref,
        hits_ref,
    ) = refs[:10]
    ins = refs[10 : 10 + count]
    (
        linear_ref, planar_ref, weight_grad_ref, table_grad_ref, text_grad_ref, region_grad_ref, sums_ref,
    ) = refs[10 + count : 17 + count]
    outs = refs[17 + count : 17 + 2 * count]
    grad_ref, turned_left_ref, input_grad_ref = refs[17 + 2 * count : 20 + 2 * count]
    helpers = refs[20 + 2 * count : 24 + 2 * count]
    stages = scatter_stages(line, ins, outs, refs[24 + 2 * count :])
    step = pl.program_id(0)

    @pl.when(step == 0)
    def _():
        greet(line)
        stages.start()
        make_places(rows_ref, cols_ref, *helpers)

    def first(k):
        return lambda: spread(line, 4, k, 0, stages.first)

    def second(k):
        return lambda: spread(line, 4, k, 0, stages.second)

    def third(k):
        return lambda: spread(line, 4, k, 0, stages.third)

    slots = {
        1: [first(0)],
        3: [first(1)],
        7: [second(0)],
        8: [first(2)],
        10: [first(3)],
        12: [second(1)],
        17: [third(0)],
        22: [second(2), second(3)],
    }

    def pump(sub):
        at_steps([(slot // 4, work) for slot, work in slots.items() if slot % 4 == sub])

    @pl.when(step < PAIRS)
    def _():
        attend_back_pair(step, pump, proj_ref, probs_ref, upstream_ref, grad_ref, linear_ref, planar_ref, *helpers)

    @pl.when(jnp.logical_and(step >= PAIRS, step < TABLE_STEP))
    def _():
        column = step - PAIRS
        source = source_of(column)
        fresh = jnp.logical_or(column == 0, source != source_of(jnp.maximum(column - 1, 0)))
        grads = grad_ref[:, pl.ds(pl.multiple_of(column * MODEL_WIDTH, MODEL_WIDTH), MODEL_WIDTH)]

        @pl.when(fresh)
        def _():
            turned_left_ref[...] = lefts_ref[source].T

        weight_grad_ref[...] = dot_nn(turned_left_ref[...], grads).astype(jnp.bfloat16)
        back = dot_nt(grads, weight_ref[...])

        @pl.when(fresh)
        def _():
            input_grad_ref[source] = back

        @pl.when(jnp.logical_not(fresh))
        def _():
            input_grad_ref[source] += back

    @pl.when(step >= TABLE_STEP)
    def _():
        axis = step - TABLE_STEP
        coords = lax.broadcasted_iota(jnp.int32, (COORDS, PAGE_TOKENS), 0)
        total = None
        for stream in range(2):
            hit = (coords == rows_ref[pl.ds(2 * stream + axis, 1), :]).astype(jnp.bfloat16)
            part = dot_nn(hit, input_grad_ref[2 * stream + 1].astype(jnp.bfloat16))
            total = part if total is None else total + part
        table_grad_ref[...] = total.astype(jnp.bfloat16)

    @pl.when(step == TABLE_STEP + 1)
    def _():
        mixer_grad = mixer_grad_ref[...]
        sums_ref[...] = jnp.zeros_like(sums_ref)
        for stream, out_ref in enumerate((text_grad_ref, region_grad_ref)):
            grad = mixer_grad + input_grad_ref[2 * stream]
            hit = jnp.broadcast_to(hits_ref[:, stream : stream + 1] == 1, grad.shape)
            zero = jnp.zeros_like(grad)
            kept = jnp.where(hit, zero, grad)
            out_ref[...] = kept
            sums_ref[stream : stream + 1, :] = jnp.sum(jnp.where(hit, grad, zero), axis=0, keepdims=True)
            if stream == 1:
                sums_ref[2:3, :] = jnp.sum(kept, axis=0, keepdims=True)
                sums_ref[3:4, :] = jnp.sum(kept * normal_ref[...], axis=0, keepdims=True)

    at_steps(
        [(PAIRS + 3, [third(1)]), (PAIRS + 8, [third(2)]), (TABLE_STEP + 1, [third(3), stages.end])]
    )


def backward_layer(
    proj, probs, upstream, anchor_rows, anchor_cols, lefts, weights, mixer_grad, normal, hits, grads, collective_id
):
    dp = lax.axis_size("dp")
    line = dp // RING
    count = len(grads)
    blocks = [(grad.shape[1:], grad.dtype) for grad in grads]
    anywhere = pl.BlockSpec(memory_space=pl.ANY)
    page = (PAGE_TOKENS, MODEL_WIDTH)

    def pair_at(i):
        return jnp.minimum(i, PAIRS - 1)

    def column_at(i):
        return jnp.clip(i - PAIRS, 0, KINDS - 1)

    return pl.pallas_call(
        partial(backward_kernel, line, count),
        grid=(TABLE_STEP + 2,),
        in_specs=[
            once(proj.shape),
            pl.BlockSpec((2, 2, PAGE_TOKENS, PAGE_TOKENS), lambda i: (0, pair_at(i), 0, 0)),
            pl.BlockSpec((PAGE_TOKENS, LANES), lambda i: (0, pair_at(i))),
            once(anchor_rows.shape),
            once(anchor_cols.shape),
            once(lefts.shape),
            pl.BlockSpec((MODEL_WIDTH, MODEL_WIDTH), lambda i: (0, column_at(i))),
            once(page),
            once(page),
            once(hits.shape),
            *[anywhere] * count,
        ],
        out_specs=[
            pl.BlockSpec((HEADS, 1, 2 * PAGE_TOKENS), lambda i: (0, 0, 0)),
            pl.BlockSpec((HEADS, 1, SP_B), lambda i: (0, 0, 0)),
            pl.BlockSpec((MODEL_WIDTH, MODEL_WIDTH), lambda i: (0, column_at(i))),
            pl.BlockSpec((COORDS, MODEL_WIDTH), lambda i: (0, jnp.maximum(i - TABLE_STEP, 0))),
            pl.BlockSpec(page, lambda i: (0, 0)),
            pl.BlockSpec(page, lambda i: (0, 0)),
            pl.BlockSpec((8, MODEL_WIDTH), lambda i: (0, 0)),
            *(pl.BlockSpec(shape, lambda i: (0, 0)) for shape, kind in blocks),
        ],
        out_shape=[
            jax.ShapeDtypeStruct((HEADS, 1, 2 * PAGE_TOKENS), jnp.float32),
            jax.ShapeDtypeStruct((HEADS, 1, SP_B), jnp.float32),
            jax.ShapeDtypeStruct(weights.shape, jnp.bfloat16),
            jax.ShapeDtypeStruct((COORDS, 2 * MODEL_WIDTH), jnp.bfloat16),
            jax.ShapeDtypeStruct(page, jnp.float32),
            jax.ShapeDtypeStruct(page, jnp.float32),
            jax.ShapeDtypeStruct((8, MODEL_WIDTH), jnp.float32),
            *(jax.ShapeDtypeStruct(shape, jnp.float32) for shape, kind in blocks),
        ],
        scratch_shapes=[
            pltpu.VMEM(proj.shape, jnp.bfloat16),
            pltpu.VMEM((MODEL_WIDTH, PAGE_TOKENS), jnp.bfloat16),
            pltpu.VMEM((4, *page), jnp.float32),
            pltpu.VMEM((2, 4 * PAGE_TOKENS, SP_B), jnp.bfloat16),
            pltpu.VMEM((2, 128, PAGE_TOKENS), jnp.bfloat16),
            pltpu.VMEM((2, 4, PAGE_TOKENS, PAGE_TOKENS), jnp.bfloat16),
            pltpu.VMEM((PAGE_TOKENS, PAGE_TOKENS), jnp.bfloat16),
            *scatter_scratch(line, blocks),
        ],
        compiler_params=pltpu.CompilerParams(
            collective_id=collective_id, has_side_effects=True, vmem_limit_bytes=63 << 20
        ),
        name="backward_layer",
    )(
        proj, probs, upstream, anchor_rows, anchor_cols, lefts, weights, mixer_grad, normal, hits,
        *(grad.reshape(line * RING, 2, *grad.shape[1:]) for grad in grads),
    )


def last_kernel(line, count, token_total, *refs):
    sums_ref, kept_ref, normal_ref, scale_ref, features_ref, backbone_ref = refs[:6]
    ins = refs[6 : 6 + count]
    feature_grad_ref, total_ref = refs[6 + count : 8 + count]
    outs = refs[8 + count : 9 + 2 * count]
    turned_ref, conv_grad_ref, late_ref = refs[9 + 2 * count : 12 + 2 * count]
    rest = refs[12 + 2 * count :]
    sums = exchange_stages(line, add_up, sums_ref, total_ref, rest[:7])
    early_scratch = 5 * count + 9
    early = scatter_stages(line, ins, outs[:count], rest[7 : 7 + early_scratch])
    late = scatter_stages(line, [late_ref], outs[count:], rest[7 + early_scratch :])
    share = late_ref.shape[2]

    def first(stages, k):
        spread(line, 4, k, 0, stages.first)

    def second(stages, k):
        spread(line, 4, k, 0, stages.second)

    def third(stages, k):
        spread(line, 4, k, 0, stages.third)

    greet_peers(line)
    sums.near()
    early.start()
    first(early, 0)
    sums.far()
    first(early, 1)
    sums.total()
    conv_grad_ref[...] = (
        scale_ref[...]
        * (kept_ref[...] - total_ref[0:1, :] / token_total - normal_ref[...] * (total_ref[1:2, :] / token_total))
    ).astype(jnp.bfloat16)
    second(early, 0)
    first(early, 2)
    first(early, 3)

    def turn(k, unused):
        columns = pl.ds(pl.multiple_of(k * 512, 512), 512)
        turned_ref[columns, :] = features_ref[:, columns].T
        return unused

    lax.fori_loop(0, features_ref.shape[1] // 512, turn, 0)
    width = min(512, 2 * share * line * RING)

    def backbone(k, unused):
        rows = pl.ds(pl.multiple_of(k * width, width), width)
        block = dot_nn(turned_ref[rows, :], conv_grad_ref[...])
        places = width // (2 * share)
        late_ref[pl.ds(k * places, places)] = block.reshape(places, 2, share, MODEL_WIDTH).astype(jnp.bfloat16)
        return unused

    lax.fori_loop(0, features_ref.shape[1] // width, backbone, 0)
    late.start()
    for k in range(4):
        first(late, k)
    second(early, 1)
    third(early, 0)

    def feature(k, unused):
        columns = pl.ds(pl.multiple_of(k * 512, 512), 512)
        feature_grad_ref[:, columns] = dot_nt(conv_grad_ref[...], backbone_ref[columns, :])
        return unused

    lax.fori_loop(0, features_ref.shape[1] // 512, feature, 0)
    second(early, 2)
    for k in range(4):
        second(late, k)
    second(early, 3)
    third(early, 1)
    third(early, 2)
    for k in range(3):
        third(late, k)
    third(early, 3)
    third(late, 3)
    sums.end()
    early.end()
    late.end()


def last_layer(sums, kept, normal, scale, features, backbone, grads, token_total, collective_id):
    dp = lax.axis_size("dp")
    line = dp // RING
    count = len(grads)
    blocks = [(grad.shape[1:], grad.dtype) for grad in grads]
    channels = backbone.shape[0]
    late = [((channels // (2 * dp), MODEL_WIDTH), jnp.bfloat16)]
    anywhere = pl.BlockSpec(memory_space=pl.ANY)
    vmem = pl.BlockSpec(memory_space=pltpu.VMEM)
    return pl.pallas_call(
        partial(last_kernel, line, count, float(token_total)),
        in_specs=[*[vmem] * 6, *[anywhere] * count],
        out_specs=[vmem] * (3 + count),
        out_shape=[
            jax.ShapeDtypeStruct(features.shape, jnp.float32),
            jax.ShapeDtypeStruct(sums.shape, jnp.float32),
            *(jax.ShapeDtypeStruct(shape, jnp.float32) for shape, kind in blocks + late),
        ],
        scratch_shapes=[
            pltpu.VMEM((channels, PAGE_TOKENS), jnp.bfloat16),
            pltpu.VMEM(kept.shape, jnp.bfloat16),
            pltpu.VMEM((dp, 2, *late[0][0]), jnp.bfloat16),
            *exchange_scratch(line, sums.shape),
            *scatter_scratch(line, blocks),
            *scatter_scratch(line, late),
        ],
        compiler_params=pltpu.CompilerParams(
            collective_id=collective_id, has_side_effects=True, vmem_limit_bytes=63 << 20
        ),
        name="last_layer",
    )(
        sums, kept, normal, scale, features, backbone,
        *(grad.reshape(line * RING, 2, *grad.shape[1:]) for grad in grads),
    )


norm_epsilon = 1e-05


def normal_parts(values):
    center = values - jnp.mean(values, axis=-1, keepdims=True)
    inverse = lax.rsqrt(jnp.mean(center * center, axis=-1, keepdims=True) + norm_epsilon)
    return center * inverse, inverse


def normal_back(normal, inverse, gain, grad):
    scaled = grad * gain
    return inverse * (
        scaled
        - jnp.mean(scaled, axis=-1, keepdims=True)
        - normal * jnp.mean(scaled * normal, axis=-1, keepdims=True)
    )


CHUNKS = 4


def mixer_kernel(
    merged_ref, start_ref, cotangent_ref, vectors_ref, bias_ref, merge_ref, expand_ref, reduce_ref,
    output_ref, mixer_grad_ref, merged_grad_ref, merge_grad_ref, expand_grad_ref, reduce_grad_ref, sums_ref,
    bias_grad_ref,
    hidden_ref, normal_ref, inverse_ref, low_ref, active_ref, slope_ref, dense_ref, grad_ref, grad_low_ref,
    turned_ref,
):
    step = pl.program_id(0)
    chunk = lax.rem(step, CHUNKS)

    def vector(k):
        return vectors_ref[k : k + 1, :]

    def column_sum(values):
        return jnp.sum(values, axis=0, keepdims=True)

    @pl.when(step == 0)
    def _():
        normal, inverse = normal_parts(start_ref[...] + dot_nn(merged_ref[...], merge_ref[...]))
        normal_ref[...] = normal
        inverse_ref[...] = jnp.broadcast_to(inverse, inverse_ref.shape)
        hidden = normal * vector(4) + vector(5)
        hidden_ref[...] = hidden
        low_ref[...] = hidden.astype(jnp.bfloat16)
        dense_ref[...] = jnp.zeros_like(dense_ref)

    @pl.when(step < CHUNKS)
    def _():
        inner = dot_nn(low_ref[...], expand_ref[...]) + bias_ref[chunk]
        share = 0.5 + 0.5 * lax.erf(inner * (0.5**0.5))
        active = (inner * share).astype(jnp.bfloat16)
        active_ref[chunk] = active
        slope_ref[chunk] = share + inner * jnp.exp(-0.5 * inner * inner) * (2.0 * jnp.pi) ** -0.5
        dense_ref[...] += dot_nn(active, reduce_ref[...])

    @pl.when(step == CHUNKS - 1)
    def _():
        normal, inverse = normal_parts(hidden_ref[...] + (dense_ref[...] + vector(6)))
        output_ref[...] = (normal * vector(7) + vector(8)).astype(jnp.bfloat16)
        upstream = cotangent_ref[...].astype(jnp.float32)
        grad = normal_back(normal, inverse, vector(7), upstream)
        grad_ref[...] = grad
        grad_low_ref[...] = grad.astype(jnp.bfloat16)
        sums_ref[2:3, :] = column_sum(grad)
        sums_ref[3:4, :] = column_sum(upstream * normal)
        sums_ref[4:5, :] = column_sum(upstream)
        turned_ref[...] = low_ref[...].T

    @pl.when(step >= CHUNKS)
    def _():
        grad_low = grad_low_ref[...]
        reduce_grad_ref[...] = dot_tn(active_ref[chunk], grad_low).astype(jnp.bfloat16)
        inner_low = (dot_nt(grad_low, reduce_ref[...]) * slope_ref[chunk]).astype(jnp.bfloat16)
        bias_grad_ref[chunk] = column_sum(inner_low.astype(jnp.float32))
        expand_grad_ref[...] = dot_nn(turned_ref[...], inner_low).astype(jnp.bfloat16)
        grad_ref[...] += dot_nt(inner_low, expand_ref[...])

    @pl.when(step == 2 * CHUNKS - 1)
    def _():
        grad = grad_ref[...]
        normal = normal_ref[...]
        mixer_grad = normal_back(normal, inverse_ref[:, :1], vector(4), grad)
        mixer_grad_ref[...] = mixer_grad
        sums_ref[0:1, :] = column_sum(grad * normal)
        sums_ref[1:2, :] = column_sum(grad)
        low = mixer_grad.astype(jnp.bfloat16)
        merge_grad_ref[...] = dot_tn(merged_ref[...], low).astype(jnp.bfloat16)
        merged_grad_ref[...] = dot_nt(low, merge_ref[...]).astype(jnp.bfloat16)


def mixer_layer(merged, start, cotangent, vectors, bias, w_merge, w_expand, w_reduce):
    rows = merged.shape[0]
    inner = w_expand.shape[1]
    width = inner // CHUNKS
    page = (rows, MODEL_WIDTH)

    def back_at(i):
        return jnp.maximum(i - CHUNKS, 0)

    def whole(shape):
        return pl.BlockSpec(shape, lambda i: (0,) * len(shape))

    f32, bf16 = jnp.float32, jnp.bfloat16
    outs = [
        (page, bf16, whole(page)),
        (page, f32, whole(page)),
        (page, bf16, whole(page)),
        ((MODEL_WIDTH, MODEL_WIDTH), bf16, whole((MODEL_WIDTH, MODEL_WIDTH))),
        ((MODEL_WIDTH, inner), bf16, pl.BlockSpec((MODEL_WIDTH, width), lambda i: (0, back_at(i)))),
        ((inner, MODEL_WIDTH), bf16, pl.BlockSpec((width, MODEL_WIDTH), lambda i: (back_at(i), 0))),
        ((8, MODEL_WIDTH), f32, whole((8, MODEL_WIDTH))),
        ((CHUNKS, 1, width), f32, whole((CHUNKS, 1, width))),
    ]
    return pl.pallas_call(
        mixer_kernel,
        grid=(2 * CHUNKS,),
        in_specs=[
            once(page),
            once(page),
            once(page),
            once(vectors.shape),
            once(bias.shape),
            once(w_merge.shape),
            pl.BlockSpec((MODEL_WIDTH, width), lambda i: (0, lax.rem(i, CHUNKS))),
            pl.BlockSpec((width, MODEL_WIDTH), lambda i: (lax.rem(i, CHUNKS), 0)),
        ],
        out_specs=[spec for shape, kind, spec in outs],
        out_shape=[jax.ShapeDtypeStruct(shape, kind) for shape, kind, spec in outs],
        scratch_shapes=[
            pltpu.VMEM(page, f32),
            pltpu.VMEM(page, f32),
            pltpu.VMEM((rows, 128), f32),
            pltpu.VMEM(page, bf16),
            pltpu.VMEM((CHUNKS, rows, width), bf16),
            pltpu.VMEM((CHUNKS, rows, width), f32),
            pltpu.VMEM(page, f32),
            pltpu.VMEM(page, f32),
            pltpu.VMEM(page, bf16),
            pltpu.VMEM((MODEL_WIDTH, rows), bf16),
        ],
        compiler_params=pltpu.CompilerParams(vmem_limit_bytes=48 << 20),
        name="mixer_layer",
    )(merged, start, cotangent, vectors, bias, w_merge, w_expand, w_reduce)

AXES = ("dp", "pair")
batch_epsilon = 1e-05


def folded(vectors):
    whole = jnp.stack([vector.reshape(-1, 128) for vector in vectors])
    return jnp.pad(whole, ((0, 0), (0, 8 - whole.shape[1]), (0, 0)))


def padded_rows(pieces):
    rows = [jnp.pad(piece.astype(jnp.float32), ((0, 0), (0, 128 - piece.shape[1]))) for piece in pieces]
    total = sum(piece.shape[0] for piece in pieces)
    rows.append(jnp.zeros((-total % 8, 128), jnp.float32))
    return jnp.concatenate(rows, axis=0)


def blocks_of(grad, devices):
    blocks = grad.astype(jnp.bfloat16).reshape(devices, grad.shape[0] // devices, grad.shape[1])
    return blocks if blocks.shape[1] % 8 == 0 else blocks.reshape(devices, -1, 128)


def place_onehot(anchor_rows):
    coords = jnp.arange(COORDS, dtype=jnp.int32)
    return (anchor_rows[:, None] == coords[None, :]).astype(jnp.bfloat16)


def per_device(
    text_inputs,
    region_features,
    text_masked,
    region_masked,
    text_anchors,
    region_anchors,
    backbone_weight,
    batch_gain,
    batch_shift,
    text_blank,
    region_blank,
    position_table,
    stream_weights,
    linear_bias,
    planar_bias,
    merge_weight,
    mixer_gain,
    mixer_shift,
    expand_weight,
    expand_bias,
    reduce_weight,
    reduce_bias,
    output_gain,
    output_shift,
    cotangent,
):
    devices = lax.axis_size(AXES)
    row_count = text_inputs.shape[0]
    token_total = row_count * devices
    share = MODEL_WIDTH // devices
    expand_share = expand_bias.shape[0]
    bias_rows = REL_B // devices
    vectors = jnp.stack(
        [
            batch_gain, batch_shift, text_blank, region_blank, mixer_gain, mixer_shift, reduce_bias,
            output_gain, output_shift,
        ]
    )
    small = padded_rows([linear_bias, planar_bias, vectors, expand_bias[None, :]])
    packed, w_backbone, w_table, w_stream = gather_all(
        (small, backbone_weight, position_table, stream_weights), 0
    )
    w_linear = packed[:, :bias_rows, :HEADS].reshape(REL_B, HEADS)
    w_planar = packed[:, bias_rows : 2 * bias_rows, :HEADS].reshape(SP_B, HEADS)
    w_vectors = packed[:, 2 * bias_rows : 2 * bias_rows + 9, :share].transpose(1, 0, 2).reshape(9, -1)
    w_expand_bias = packed[:, 2 * bias_rows + 9, :expand_share].reshape(-1)
    (
        w_batch_gain, w_batch_shift, w_text_blank, w_region_blank, w_mixer_gain, w_mixer_shift,
        w_reduce_bias, w_output_gain, w_output_shift,
    ) = (w_vectors[k] for k in range(9))
    w_backbone, w_table, w_stream = (
        whole.reshape(-1, whole.shape[-1]) for whole in (w_backbone, w_table, w_stream)
    )

    conv = jnp.dot(region_features, w_backbone, preferred_element_type=jnp.float32)
    local_mean = jnp.mean(conv, axis=0)
    local_center = conv - local_mean
    local_square = jnp.sum(local_center * local_center, axis=0)
    pooled = exchange(
        folded([local_mean, local_square]), partial(pool_statistics, float(row_count)), 2, "pool"
    ).reshape(2, -1)
    batch_mean = pooled[0, :MODEL_WIDTH]
    batch_var = pooled[1, :MODEL_WIDTH] / token_total
    inverse_std = lax.rsqrt(batch_var + batch_epsilon)
    normal_feat = (conv - batch_mean) * inverse_std
    region_hit = region_masked[:, None] == 1
    text_hit = text_masked[:, None] == 1
    region_start = jnp.where(region_hit, w_region_blank[None, :], normal_feat * w_batch_gain + w_batch_shift)
    text_start = jnp.where(text_hit, w_text_blank[None, :], text_inputs.astype(jnp.float32))
    onehot_x = place_onehot(jnp.concatenate([text_anchors[0], region_anchors[0]]))
    onehot_y = place_onehot(jnp.concatenate([text_anchors[1], region_anchors[1]]))
    space = (
        jnp.dot(onehot_x, w_table[:, :MODEL_WIDTH], preferred_element_type=jnp.float32)
        + jnp.dot(onehot_y, w_table[:, MODEL_WIDTH:], preferred_element_type=jnp.float32)
    ).astype(jnp.bfloat16)
    lefts = jnp.stack(
        [
            text_start.astype(jnp.bfloat16), space[:row_count], region_start.astype(jnp.bfloat16),
            space[row_count:],
        ]
    )
    anchor_rows = jnp.concatenate([text_anchors, region_anchors], axis=0)
    anchor_cols = anchor_rows.T
    proj, merged_low, probs, *wholes = forward_layer(
        lefts, w_stream, linear_extended(w_linear), w_planar.T[:, None, :], anchor_rows, anchor_cols,
        (merge_weight, expand_weight, reduce_weight), 4,
    )
    w_merge, w_expand, w_reduce = (whole.reshape(-1, whole.shape[-1]) for whole in wholes)
    (
        layer_output, mixer_in_grad, merged_grad, merge_weight_grad, expand_weight_grad, reduce_weight_grad,
        mixer_sums, expand_bias_grad,
    ) = mixer_layer(
        merged_low, text_start + region_start, cotangent, w_vectors, w_expand_bias.reshape(CHUNKS, 1, -1),
        w_merge, w_expand, w_reduce,
    )
    early = (expand_weight_grad, reduce_weight_grad, merge_weight_grad)
    hits = jnp.stack([text_masked, region_masked], axis=1)
    (
        linear_sums, planar_sums, stream_weights_grad, position_table_grad, text_gradient, region_kept,
        start_sums, *early_shares,
    ) = backward_layer(
        proj, probs, merged_grad, anchor_rows, anchor_cols, lefts, w_stream, mixer_in_grad, normal_feat, hits,
        [blocks_of(grad, devices) for grad in early], 5,
    )
    expand_weight_grad, reduce_weight_grad, merge_weight_grad = (
        part.reshape(-1, grad.shape[1]) for part, grad in zip(early_shares, early)
    )
    vector_grads = jnp.concatenate([start_sums[:2], mixer_sums[:5]], axis=0)
    pieces = [
        linear_folded(linear_sums[:, 0]).T.reshape(devices, bias_rows, HEADS),
        planar_sums[:, 0].T.reshape(devices, bias_rows, HEADS),
        vector_grads.reshape(7, devices, share).transpose(1, 0, 2),
        expand_bias_grad.reshape(devices, 1, expand_share),
    ]
    small_grads = jax.vmap(lambda *parts: padded_rows(parts))(*pieces)
    late = (stream_weights_grad, position_table_grad)
    feature_gradient, totals, small, *shares = last_layer(
        start_sums[2:4], region_kept, normal_feat, (w_batch_gain * inverse_std)[None, :], region_features,
        w_backbone, [small_grads, *(blocks_of(grad, devices) for grad in late)], token_total, 1,
    )
    stream_weights_grad, position_table_grad = (
        part.reshape(-1, grad.shape[1]) for part, grad in zip(shares, late)
    )
    backbone_weight_grad = shares[2]
    owned = lax.dynamic_slice_in_dim(totals, lax.axis_index(AXES) * share, share, axis=1)
    batch_shift_gradient = owned[0]
    batch_gain_gradient = owned[1]
    vector_shares = small[2 * bias_rows : 2 * bias_rows + 7, :share]
    return (
        layer_output,
        text_gradient,
        feature_gradient,
        backbone_weight_grad,
        batch_gain_gradient,
        batch_shift_gradient,
        vector_shares[0],
        vector_shares[1],
        position_table_grad,
        stream_weights_grad,
        small[:bias_rows, :HEADS],
        small[bias_rows : 2 * bias_rows, :HEADS],
        merge_weight_grad,
        vector_shares[2],
        vector_shares[3],
        expand_weight_grad,
        small[2 * bias_rows + 7, :expand_share],
        reduce_weight_grad,
        vector_shares[4],
        vector_shares[5],
        vector_shares[6],
    )


def solution(mesh):
    in_specs = (
        P(("dp", "pair"), None),
        P(("dp", "pair"), None),
        P(("dp", "pair")),
        P(("dp", "pair")),
        P(None, ("dp", "pair")),
        P(None, ("dp", "pair")),
        P(("dp", "pair"), None),
        P(("dp", "pair")),
        P(("dp", "pair")),
        P(("dp", "pair")),
        P(("dp", "pair")),
        P(("dp", "pair"), None),
        P(("dp", "pair"), None),
        P(("dp", "pair"), None),
        P(("dp", "pair"), None),
        P(("dp", "pair"), None),
        P(("dp", "pair")),
        P(("dp", "pair")),
        P(("dp", "pair"), None),
        P(("dp", "pair")),
        P(("dp", "pair"), None),
        P(("dp", "pair")),
        P(("dp", "pair")),
        P(("dp", "pair")),
        P(("dp", "pair"), None),
    )
    out_specs = (
        P(("dp", "pair"), None),
        P(("dp", "pair"), None),
        P(("dp", "pair"), None),
        P(("dp", "pair"), None),
        P(("dp", "pair")),
        P(("dp", "pair")),
        P(("dp", "pair")),
        P(("dp", "pair")),
        P(("dp", "pair"), None),
        P(("dp", "pair"), None),
        P(("dp", "pair"), None),
        P(("dp", "pair"), None),
        P(("dp", "pair"), None),
        P(("dp", "pair")),
        P(("dp", "pair")),
        P(("dp", "pair"), None),
        P(("dp", "pair")),
        P(("dp", "pair"), None),
        P(("dp", "pair")),
        P(("dp", "pair")),
        P(("dp", "pair")),
    )
    return jax.shard_map(
        per_device, mesh=mesh, in_specs=in_specs, out_specs=out_specs, check_vma=False
    )
```

```python
from functools import partial
from types import SimpleNamespace

import jax
import jax.numpy as jnp
from jax import lax
from jax.experimental import pallas as pl
from jax.experimental.pallas import tpu as pltpu
from jax.sharding import PartitionSpec as P

HEADS = 12
HEAD_DIM = 64
COORDS = 1024
REL_B = 256
SP_SIDE = 16
PAGE_TOKENS = 256
MODEL_WIDTH = 768
SP_B = 256
COORD_STEP = 128
PAIRS = HEADS // 2
LANES = 2 * HEAD_DIM


def dot_nt(left, right):
    return lax.dot_general(left, right, (((1,), (1,)), ((), ())), preferred_element_type=jnp.float32)


def dot_tn(left, right):
    return lax.dot_general(left, right, (((0,), (0,)), ((), ())), preferred_element_type=jnp.float32)


def dot_nn(left, right):
    return lax.dot_general(left, right, (((1,), (0,)), ((), ())), preferred_element_type=jnp.float32)


def head_columns(stream, kind, pair):
    return pl.ds(pl.multiple_of(((5 * stream + kind) * PAIRS + pair) * LANES, LANES), LANES)


def make_boxes(rows_ref, cols_ref, box_ref):
    for stream in range(2):
        part = []
        for axis in range(2):
            along = rows_ref[2 * stream + axis : 2 * stream + axis + 1, :]
            down = cols_ref[:, 2 * stream + axis : 2 * stream + axis + 1]
            part.append(((along - down) >> 7) + SP_SIDE // 2)
        box_ref[stream] = part[0] * SP_SIDE + part[1]


def attend_pair(pair, proj_ref, linear_ref, planar_ref, box_ref, merged_ref, probs_ref):
    lane_head = lax.broadcasted_iota(jnp.int32, (PAGE_TOKENS, LANES), 1) // HEAD_DIM
    mixed = [None, None]
    for inner in range(2):
        head = 2 * pair + inner
        mine = lane_head == inner
        spread = jnp.broadcast_to(linear_ref[head], (PAGE_TOKENS, 2 * PAGE_TOKENS))
        linear_term = pltpu.roll(spread, PAGE_TOKENS + 1, 1, stride=1, stride_axis=0)[:, :PAGE_TOKENS]
        low_table = jnp.broadcast_to(planar_ref[head, :, :128], (PAGE_TOKENS, 128))
        high_table = jnp.broadcast_to(planar_ref[head, :, 128:], (PAGE_TOKENS, 128))
        total = None
        for stream in range(2):
            pieces = [proj_ref[:, head_columns(stream, kind, pair)] for kind in range(5)]
            zero = jnp.zeros_like(pieces[0])
            left = jnp.concatenate([jnp.where(mine, pieces[0], zero), jnp.where(mine, pieces[3], zero)], axis=1)
            right = jnp.concatenate([pieces[1], pieces[4]], axis=1)
            logits = dot_nt(left, right) * HEAD_DIM ** (-0.5)
            planar = []
            for half in range(2):
                box = box_ref[stream, :, 128 * half : 128 * half + 128]
                place = box & 127
                planar.append(
                    jnp.where(
                        box < 128,
                        jnp.take_along_axis(low_table, place, axis=1),
                        jnp.take_along_axis(high_table, place, axis=1),
                    )
                )
            logits = logits + linear_term + jnp.concatenate(planar, axis=1)
            top = jnp.max(logits, axis=-1, keepdims=True)
            shifted = jnp.exp(logits - top)
            probs = shifted / jnp.sum(shifted, axis=-1, keepdims=True)
            probs_ref[stream, inner] = probs
            part = dot_nn(probs.astype(jnp.bfloat16), pieces[2])
            total = part if total is None else total + part
        mixed[inner] = total
    merged_ref[...] = jnp.where(lane_head == 0, mixed[0], mixed[1]).astype(jnp.bfloat16)


def make_places(rows_ref, cols_ref, place_ref, turned_ref, mask_ref, flip_ref):
    lanes = lax.broadcasted_iota(jnp.int32, (PAGE_TOKENS, SP_B), 1)
    rows = lax.broadcasted_iota(jnp.int32, (PAGE_TOKENS, SP_B), 0)
    flip_ref[...] = (lanes + rows == PAGE_TOKENS - 1).astype(jnp.bfloat16)
    for stream in range(2):
        x_row = rows_ref[2 * stream : 2 * stream + 1, :]
        y_row = rows_ref[2 * stream + 1 : 2 * stream + 2, :]
        x_col = cols_ref[:, 2 * stream : 2 * stream + 1]
        y_col = cols_ref[:, 2 * stream + 1 : 2 * stream + 2]
        cell_row = (x_row >> 7) * SP_SIDE + (y_row >> 7)
        cell_col = (x_col >> 7) * SP_SIDE + (y_col >> 7)
        x_less = ((x_row & 127) < (x_col & 127)).astype(jnp.float32)
        y_less = ((y_row & 127) < (y_col & 127)).astype(jnp.float32)
        for x_side in range(2):
            for y_side in range(2):
                side = 2 * x_side + y_side
                place_ref[stream, side * PAGE_TOKENS : (side + 1) * PAGE_TOKENS, :] = (
                    lanes == cell_col + (SP_SIDE + 1 - SP_SIDE * x_side - y_side)
                ).astype(jnp.bfloat16)
                mask_ref[stream, side] = (
                    (x_less if x_side else 1.0 - x_less) * (y_less if y_side else 1.0 - y_less)
                ).astype(jnp.bfloat16)
        turned_ref[stream] = (rows[:128] == 127 - cell_row).astype(jnp.bfloat16)


def attend_back_pair(
    pair, pump, proj_ref, probs_ref, upstream_ref, grad_ref, linear_ref, planar_ref,
    place_ref, turned_ref, mask_ref, flip_ref,
):
    lane_head = lax.broadcasted_iota(jnp.int32, (PAGE_TOKENS, LANES), 1) // HEAD_DIM
    wide_head = jnp.concatenate([lane_head, lane_head], axis=1)
    upstream = upstream_ref[...]
    scale = HEAD_DIM ** (-0.5)
    diagonal = [None, None]
    for stream in range(2):
        pieces = [proj_ref[:, head_columns(stream, kind, pair)] for kind in range(5)]
        queries = jnp.concatenate([pieces[0], pieces[3]], axis=1)
        keys = jnp.concatenate([pieces[1], pieces[4]], axis=1)
        grads = []
        for inner in range(2):
            head = 2 * pair + inner
            mine = lane_head == inner
            grad_probs = dot_nt(jnp.where(mine, upstream, jnp.zeros_like(upstream)), pieces[2])
            probs = probs_ref[stream, inner]
            weighted = probs * grad_probs
            grad_logits = (weighted - probs * jnp.sum(weighted, axis=-1, keepdims=True)).astype(jnp.bfloat16)
            grads.append(
                (
                    dot_nn(grad_logits, keys) * scale,
                    dot_tn(grad_logits, queries) * scale,
                    dot_tn(probs.astype(jnp.bfloat16), upstream),
                )
            )
            parts = jnp.concatenate([grad_logits * mask_ref[stream, side] for side in range(4)], axis=1)
            placed = dot_nn(parts, place_ref[stream])
            placed_high = placed.astype(jnp.bfloat16)
            placed_low = (placed - placed_high.astype(jnp.float32)).astype(jnp.bfloat16)
            turned = turned_ref[stream]
            cells = dot_nn(turned, placed_high) + dot_nn(turned, placed_low)
            sums = jnp.sum(
                pltpu.roll(cells, SP_B - SP_SIDE // 2, 1, stride=1, stride_axis=0), axis=0, keepdims=True
            )
            if stream == 0:
                planar_ref[head] = sums
            else:
                planar_ref[head] += sums
            turned_over = dot_nn(flip_ref[...], grad_logits)
            diagonal[inner] = turned_over if stream == 0 else diagonal[inner] + turned_over
            pump(2 * stream + inner)
        query_grad, key_grad = (jnp.where(wide_head == 0, grads[0][k], grads[1][k]) for k in range(2))
        value_grad = jnp.where(lane_head == 0, grads[0][2], grads[1][2])
        for kind, value in enumerate(
            (query_grad[:, :LANES], key_grad[:, :LANES], value_grad, query_grad[:, LANES:], key_grad[:, LANES:])
        ):
            grad_ref[:, head_columns(stream, kind, pair)] = value.astype(jnp.bfloat16)
    for inner in range(2):
        padded = jnp.concatenate([diagonal[inner], jnp.zeros_like(diagonal[inner])], axis=1)
        linear_ref[2 * pair + inner] = jnp.sum(
            pltpu.roll(padded, 0, 1, stride=1, stride_axis=0), axis=0, keepdims=True
        )


def linear_extended(linear_bias):
    rows = linear_bias.astype(jnp.float32).T
    low = jnp.broadcast_to(rows[:, :1], (HEADS, PAGE_TOKENS - 1 - REL_B // 2))
    high = jnp.broadcast_to(rows[:, -1:], (HEADS, PAGE_TOKENS - REL_B // 2 + 1))
    return jnp.concatenate([low, rows, high], axis=1)[:, None, :]


def linear_folded(sums):
    first = REL_B // 2
    last = PAGE_TOKENS - 1 + REL_B // 2 - 1
    return jnp.concatenate(
        [
            jnp.sum(sums[:, :first], axis=1, keepdims=True),
            sums[:, first:last],
            jnp.sum(sums[:, last : 2 * PAGE_TOKENS - 1], axis=1, keepdims=True),
        ],
        axis=1,
    )


MESH = pl.DeviceIdType.MESH
RING = 4


def place():
    dp = lax.axis_index("dp")
    return dp // RING, lax.rem(dp, RING), lax.axis_index("pair")


def across(q, bit):
    other = lax.rem(q // bit, 2)
    return q + bit - 2 * bit * other


def greet(line):
    z, q, c = place()
    barrier = pltpu.get_barrier_semaphore()

    def signal(zz, qq, cc):
        pl.semaphore_signal(barrier, inc=1, device_id={"dp": zz * RING + qq, "pair": cc}, device_id_type=MESH)

    signal(z, across(q, 1), c)
    signal(z, across(q, 2), c)
    signal(z, q, 1 - c)

    @pl.when(z > 0)
    def _():
        signal(z - 1, q, c)

    @pl.when(z < line - 1)
    def _():
        signal(z + 1, q, c)

    ends = (z > 0).astype(jnp.int32) + (z < line - 1).astype(jnp.int32)
    pl.semaphore_wait(barrier, 3 + ends)


def spread(line, pumps, pump, first, work):
    total = line - first
    low, high = (first + total * (pump + k) // pumps for k in range(2))
    if high == low + 1:
        work(low)
    elif high > low:
        lax.fori_loop(low, high, lambda g, unused: (work(g), unused)[1], 0)


def gather_stages(line, ins, outs, sems):
    count = len(ins)
    (own_sem, z_send, z_recv, xy_send, xy_recv, d_send, d_recv, c_send, c_recv) = sems
    z, q, c = place()
    beside = (across(q, 1), across(q, 2))
    corner = across(across(q, 1), 2)

    def slot(zz, qq):
        return (zz * RING + qq) * 2 + c

    def remote(src, dst, send, recv, zz, qq, cc):
        return pltpu.make_async_remote_copy(
            src_ref=src, dst_ref=dst, send_sem=send, recv_sem=recv,
            device_id={"dp": zz * RING + qq, "pair": cc}, device_id_type=MESH,
        )

    def block(a, zz, qq):
        return outs[a].at[slot(zz, qq)]

    def halves(a):
        width = ins[a].shape[-1]
        cut = width // 2 if width % 256 == 0 else width
        return (0, cut), (cut, width - cut)

    def own(a):
        return pltpu.make_async_copy(ins[a], block(a, z, q), own_sem.at[a])

    def z_copy(a, way, step, first):
        zz = z - step if way == 0 else z + step
        target = z + 1 if way == 0 else z - 1
        src = ins[a] if first else block(a, zz, q)
        return remote(src, block(a, zz, q), z_send.at[way, a, step], z_recv.at[way, a, step], target, q, c)

    def xy_copy(a, axis, zz, first):
        src = ins[a] if first else block(a, zz, q)
        return remote(src, block(a, zz, q), xy_send.at[axis, a, zz], xy_recv.at[axis, a, zz], z, beside[axis], c)

    def d_copy(a, axis, zz):
        start, width = halves(a)[axis]
        part = outs[a].at[slot(zz, beside[axis]), :, pl.ds(start, width)]
        return remote(part, part, d_send.at[axis, a, zz], d_recv.at[axis, a, zz], z, beside[1 - axis], c)

    def c_copy(a, zz, qq, first):
        src = ins[a] if first else block(a, zz, qq)
        return remote(
            src, block(a, zz, qq), c_send.at[a, zz * RING + qq], c_recv.at[a, zz * RING + qq], z, q, 1 - c
        )

    def start():
        for a in range(count):
            own(a).start()
            for way in range(2):
                @pl.when(z < line - 1 if way == 0 else z > 0)
                def _():
                    z_copy(a, way, 0, True).start()
            for axis in range(2):
                xy_copy(a, axis, z, True).start()
            c_copy(a, z, q, True).start()

    def arrived(a, zz):
        for axis in range(2):
            xy_copy(a, axis, zz, False).start()
        c_copy(a, zz, q, False).start()

    def passed_on(a, zz):
        for axis in range(2):
            start, width = halves(a)[axis]
            got = block(a, zz, beside[axis])
            remote(got, got, xy_send.at[axis, a, zz], xy_recv.at[axis, a, zz], z, beside[axis], c).wait_recv()
            if width:
                d_copy(a, axis, zz).start()
            c_copy(a, zz, beside[axis], False).start()

    def finished(a, zz):
        for axis in range(2):
            start, width = halves(a)[axis]
            if width:
                part = outs[a].at[slot(zz, corner), :, pl.ds(start, width)]
                remote(part, part, d_send.at[axis, a, zz], d_recv.at[axis, a, zz], z, beside[1 - axis], c).wait_recv()
        c_copy(a, zz, corner, False).start()

    def both_ways(g, work):
        @pl.when(z - g >= 0)
        def _():
            work(z - g)

        @pl.when(jnp.logical_and(z + g <= line - 1, g > 0))
        def _():
            work(z + g)

    def along(g):
        for a in range(count):
            @pl.when(z - g >= 0)
            def _():
                got = block(a, z - g, q)
                remote(got, got, z_send.at[0, a, g - 1], z_recv.at[0, a, g - 1], z, q, 1 - c).wait_recv()

                @pl.when(z < line - 1)
                def _():
                    z_copy(a, 0, g, False).start()

                arrived(a, z - g)

            @pl.when(z + g <= line - 1)
            def _():
                got = block(a, z + g, q)
                remote(got, got, z_send.at[1, a, g - 1], z_recv.at[1, a, g - 1], z, q, 1 - c).wait_recv()

                @pl.when(z > 0)
                def _():
                    z_copy(a, 1, g, False).start()

                arrived(a, z + g)

    def around(g):
        for a in range(count):
            both_ways(g, partial(passed_on, a))

    def home(g):
        for a in range(count):
            both_ways(g, partial(finished, a))

    def drain(zz, unused):
        for a in range(count):
            for axis in range(2):
                xy_copy(a, axis, zz, False).wait_send()
                if halves(a)[axis][1]:
                    d_copy(a, axis, zz).wait_send()
            for qq in range(RING):
                c_copy(a, zz, qq, False).wait_send()
                got = outs[a].at[(zz * RING + qq) * 2 + 1 - c]
                remote(
                    got, got, c_send.at[a, zz * RING + qq], c_recv.at[a, zz * RING + qq], z, q, 1 - c
                ).wait_recv()

            @pl.when(jnp.logical_and(z < line - 1, zz <= z))
            def _():
                z_copy(a, 0, z - zz, False).wait_send()

            @pl.when(jnp.logical_and(z > 0, zz >= z))
            def _():
                z_copy(a, 1, zz - z, False).wait_send()
        return unused

    def end():
        for a in range(count):
            own(a).wait()
        lax.fori_loop(0, line, drain, 0)

    return SimpleNamespace(start=start, along=along, around=around, home=home, end=end)


def gather_sems(line, count):
    dma = pltpu.SemaphoreType.DMA
    return [
        dma((count,)),
        *(dma((2, count, line)) for k in range(6)),
        dma((count, line * RING)),
        dma((count, line * RING)),
    ]


def gather_kernel(line, count, *refs):
    stages = gather_stages(line, refs[:count], refs[count : 2 * count], refs[2 * count :])
    greet(line)
    stages.start()

    def generation(g, unused):
        @pl.when(g <= line - 1)
        def _():
            stages.along(g)

        @pl.when(g <= line)
        def _():
            stages.around(g - 1)

        @pl.when(g >= 2)
        def _():
            stages.home(g - 2)

        return unused

    lax.fori_loop(1, line + 2, generation, 0)
    stages.end()


def gather_all(shards, collective_id):
    dp = lax.axis_size("dp")
    line = dp // RING
    devices = 2 * dp
    count = len(shards)
    return pl.pallas_call(
        partial(gather_kernel, line, count),
        in_specs=[pl.BlockSpec(memory_space=pl.ANY)] * count,
        out_specs=[pl.BlockSpec(memory_space=pl.ANY)] * count,
        out_shape=[jax.ShapeDtypeStruct((devices, *shard.shape), shard.dtype) for shard in shards],
        scratch_shapes=gather_sems(line, count),
        compiler_params=pltpu.CompilerParams(collective_id=collective_id, has_side_effects=True),
        name="gather_all",
    )(*shards)


def scatter_stages(line, ins, outs, scratch):
    count = len(ins)
    groups = [scratch[k * count : (k + 1) * count] for k in range(5)]
    mine, beside_sum, half_in, full_in, line_in = groups
    (own_sem, c_send, c_recv, d_send, d_recv, xy_send, xy_recv, z_send, z_recv) = scratch[5 * count :]
    z, q, c = place()
    beside = (across(q, 1), across(q, 2))
    corner = across(across(q, 1), 2)

    def remote(src, dst, send, recv, zz, qq, cc):
        return pltpu.make_async_remote_copy(
            src_ref=src, dst_ref=dst, send_sem=send, recv_sem=recv,
            device_id={"dp": zz * RING + qq, "pair": cc}, device_id_type=MESH,
        )

    def halves(a):
        width = outs[a].shape[-1]
        cut = width // 2 if width % 256 == 0 else width
        return (0, cut), (cut, width - cut)

    def wide(value):
        return value.astype(jnp.float32)

    def group(zz):
        return pl.ds(zz * RING, RING)

    def own(a, zz):
        return pltpu.make_async_copy(ins[a].at[group(zz), c], mine[a].at[group(zz)], own_sem.at[a, zz])

    def c_copy(a, zz):
        return remote(
            ins[a].at[group(zz), 1 - c], beside_sum[a].at[group(zz)], c_send.at[a, zz], c_recv.at[a, zz], z, q, 1 - c
        )

    def d_copy(a, axis, zz):
        start, width = halves(a)[axis]
        return remote(
            mine[a].at[zz * RING + corner, :, pl.ds(start, width)],
            half_in[a].at[zz, :, pl.ds(start, width)],
            d_send.at[axis, a, zz], d_recv.at[axis, a, zz], z, beside[axis], c,
        )

    def xy_copy(a, axis, zz):
        return remote(
            mine[a].at[zz * RING + beside[axis]], full_in[a].at[axis, zz],
            xy_send.at[axis, a, zz], xy_recv.at[axis, a, zz], z, beside[axis], c,
        )

    def z_copy(a, way, zz):
        return remote(
            mine[a].at[zz * RING + q], line_in[a].at[way, zz],
            z_send.at[way, a, zz], z_recv.at[way, a, zz], z + 1 if way == 0 else z - 1, q, c,
        )

    def both_ways(g, work):
        @pl.when(z - g >= 0)
        def _():
            work(z - g)

        @pl.when(jnp.logical_and(z + g <= line - 1, g > 0))
        def _():
            work(z + g)

    def begin(zz):
        for a in range(count):
            c_copy(a, zz).start()
            own(a, zz).start()

    def first(zz):
        for a in range(count):
            own(a, zz).wait()
            c_copy(a, zz).wait_recv()

            def one(qq, unused):
                k = zz * RING + qq
                mine[a][k] = mine[a][k] + beside_sum[a][k]
                return unused

            lax.fori_loop(0, RING, one, 0)
            for axis in range(2):
                if halves(a)[axis][1]:
                    d_copy(a, axis, zz).start()

    def second(zz):
        for a in range(count):
            for axis in range(2):
                start, width = halves(a)[axis]
                k = zz * RING + beside[1 - axis]
                if width:
                    d_copy(a, axis, zz).wait_recv()
                    mine[a][k, :, start : start + width] = (
                        mine[a][k, :, start : start + width] + half_in[a][zz, :, start : start + width]
                    )
                xy_copy(a, 1 - axis, zz).start()

    def third(zz):
        for a in range(count):
            k = zz * RING + q
            for axis in range(2):
                xy_copy(a, axis, zz).wait_recv()
            mine[a][k] = (
                wide(mine[a][k]) + wide(full_in[a][0, zz]) + wide(full_in[a][1, zz])
            ).astype(mine[a].dtype)
            for way in range(2):
                @pl.when(zz > z if way == 0 else zz < z)
                def _():
                    @pl.when(z > 0 if way == 0 else z < line - 1)
                    def _():
                        z_copy(a, way, zz).wait_recv()
                        mine[a][k] = mine[a][k] + line_in[a][way, zz]

                    z_copy(a, way, zz).start()

            @pl.when(zz == z)
            def _():
                outs[a][...] = wide(mine[a][k])
                for way in range(2):
                    @pl.when(z > 0 if way == 0 else z < line - 1)
                    def _():
                        z_copy(a, way, zz).wait_recv()
                        outs[a][...] += wide(line_in[a][way, zz])

    def start():
        def begin_all(step, unused):
            both_ways(line - 1 - step, begin)
            return unused

        lax.fori_loop(0, line, begin_all, 0)

    def drain(zz, unused):
        for a in range(count):
            for axis in range(2):
                xy_copy(a, axis, zz).wait_send()
                if halves(a)[axis][1]:
                    d_copy(a, axis, zz).wait_send()
            c_copy(a, zz).wait_send()
            for way in range(2):
                @pl.when(zz > z if way == 0 else zz < z)
                def _():
                    z_copy(a, way, zz).wait_send()
        return unused

    def end():
        lax.fori_loop(0, line, drain, 0)

    return SimpleNamespace(
        start=start,
        first=lambda step: both_ways(line - 1 - step, first),
        second=lambda step: both_ways(line - 1 - step, second),
        third=lambda step: both_ways(line - 1 - step, third),
        end=end,
    )


def scatter_scratch(line, blocks):
    dma = pltpu.SemaphoreType.DMA
    count = len(blocks)
    return [
        *(pltpu.VMEM((line * RING, *shape), kind) for shape, kind in blocks),
        *(pltpu.VMEM((line * RING, *shape), kind) for shape, kind in blocks),
        *(pltpu.VMEM((line, *shape), kind) for shape, kind in blocks),
        *(pltpu.VMEM((2, line, *shape), kind) for shape, kind in blocks),
        *(pltpu.VMEM((2, line, *shape), kind) for shape, kind in blocks),
        *(dma((count, line)) for k in range(3)),
        *(dma((2, count, line)) for k in range(6)),
    ]


def scatter_kernel(line, count, *refs):
    stages = scatter_stages(line, refs[:count], refs[count : 2 * count], refs[2 * count :])
    greet(line)
    stages.start()

    def generation(step, unused):
        @pl.when(step < line)
        def _():
            stages.first(step)

        @pl.when(jnp.logical_and(step >= 1, step <= line))
        def _():
            stages.second(step - 1)

        @pl.when(step >= 2)
        def _():
            stages.third(step - 2)

        return unused

    lax.fori_loop(0, line + 2, generation, 0)
    stages.end()


def scatter_all(grads, collective_id):
    dp = lax.axis_size("dp")
    line = dp // RING
    count = len(grads)
    blocks = [(grad.shape[1:], grad.dtype) for grad in grads]
    return pl.pallas_call(
        partial(scatter_kernel, line, count),
        in_specs=[pl.BlockSpec(memory_space=pl.ANY)] * count,
        out_specs=[pl.BlockSpec(memory_space=pltpu.VMEM)] * count,
        out_shape=[jax.ShapeDtypeStruct(shape, jnp.float32) for shape, kind in blocks],
        scratch_shapes=scatter_scratch(line, blocks),
        compiler_params=pltpu.CompilerParams(
            collective_id=collective_id, has_side_effects=True, vmem_limit_bytes=63 << 20
        ),
        name="scatter_all",
    )(*(grad.reshape(line * RING, 2, *grad.shape[1:]) for grad in grads))


def peers(line):
    z, q, c = place()
    cell = q * 2 + c
    near = RING * 2

    def near_place(k):
        other = lax.rem(cell + k, near)
        return other, {"dp": z * RING + other // 2, "pair": lax.rem(other, 2)}

    def far_place(k):
        other = lax.rem(z + k, line)
        return other, {"dp": other * RING + q, "pair": c}

    def each(places, stop, work):
        def one(k, unused):
            work(*places(k))
            return unused

        lax.fori_loop(1, stop, one, 0)

    return partial(each, near_place, near), partial(each, far_place, line)


def greet_peers(line):
    barrier = pltpu.get_barrier_semaphore()
    for each in peers(line):
        each(
            lambda other, device: pl.semaphore_signal(barrier, inc=1, device_id=device, device_id_type=MESH)
        )
    pl.semaphore_wait(barrier, 2 * RING + line - 2)


def exchange_stages(line, combine, value_ref, total_ref, scratch):
    near_ref, part_ref, far_ref, n_send, n_recv, f_send, f_recv = scratch
    z, q, c = place()
    cell = q * 2 + c
    each_near, each_far = peers(line)

    def near_copy(other, device, source):
        return pltpu.make_async_remote_copy(
            src_ref=value_ref, dst_ref=near_ref.at[source], send_sem=n_send.at[other], recv_sem=n_recv.at[source],
            device_id=device, device_id_type=MESH,
        )

    def far_copy(other, device, source):
        return pltpu.make_async_remote_copy(
            src_ref=part_ref, dst_ref=far_ref.at[source], send_sem=f_send.at[other], recv_sem=f_recv.at[source],
            device_id=device, device_id_type=MESH,
        )

    def near():
        each_near(lambda other, device: near_copy(other, device, cell).start())
        near_ref[cell] = value_ref[...]

    def far():
        each_near(lambda other, device: near_copy(other, device, other).wait_recv())
        part_ref[...] = combine(near_ref, 2 * RING, 1)
        each_far(lambda other, device: far_copy(other, device, z).start())
        far_ref[z] = part_ref[...]

    def total():
        each_far(lambda other, device: far_copy(other, device, other).wait_recv())
        total_ref[...] = combine(far_ref, line, 2 * RING)

    def end():
        each_near(lambda other, device: near_copy(other, device, cell).wait_send())
        each_far(lambda other, device: far_copy(other, device, z).wait_send())

    return SimpleNamespace(near=near, far=far, total=total, end=end)


def exchange_scratch(line, shape):
    dma = pltpu.SemaphoreType.DMA
    near = 2 * RING
    return [
        pltpu.VMEM((near, *shape), jnp.float32),
        pltpu.VMEM(shape, jnp.float32),
        pltpu.VMEM((line, *shape), jnp.float32),
        dma((near,)),
        dma((near,)),
        dma((line,)),
        dma((line,)),
    ]


def exchange_kernel(line, combine, value_ref, total_ref, *scratch):
    stages = exchange_stages(line, combine, value_ref, total_ref, scratch)
    greet_peers(line)
    stages.near()
    stages.far()
    stages.total()
    stages.end()


def add_up(parts, count, weight):
    return lax.fori_loop(1, count, lambda k, total: total + parts[k], parts[0])


def pool_statistics(rows, parts, count, weight):
    mean = lax.fori_loop(1, count, lambda k, total: total + parts[k, 0], parts[0, 0]) / count

    def squares(k, total):
        offset = parts[k, 0] - mean
        return total + parts[k, 1] + (rows * weight) * (offset * offset)

    return jnp.stack([mean, lax.fori_loop(0, count, squares, jnp.zeros_like(mean))])


def exchange(value, combine, collective_id, name):
    line = lax.axis_size("dp") // RING
    vmem = pl.BlockSpec(memory_space=pltpu.VMEM)
    return pl.pallas_call(
        partial(exchange_kernel, line, combine),
        in_specs=[vmem],
        out_specs=vmem,
        out_shape=jax.ShapeDtypeStruct(value.shape, value.dtype),
        scratch_shapes=exchange_scratch(line, value.shape),
        compiler_params=pltpu.CompilerParams(collective_id=collective_id, has_side_effects=True),
        name=name,
    )(value)


KINDS = 10


def source_of(column):
    stream = column // 5
    return 2 * stream + (column - 5 * stream) // 3


def once(shape):
    return pl.BlockSpec(shape, lambda i: (0,) * len(shape), pipeline_mode=pl.Buffered(1))


def at_steps(schedule):
    step = pl.program_id(0)
    for when, work in schedule:
        @pl.when(step == when)
        def _():
            for one in work:
                one()


batch_epsilon = 1e-05


def column_at_step(step):
    turn = jnp.clip(step - 1, 0, KINDS - 1)
    return jnp.where(turn >= 7, turn - 2, jnp.where(turn >= 5, turn + 3, turn))


def forward_kernel(line, count, token_total, *refs):
    (
        features_ref, backbone_ref, table_ref, text_ref, hits_ref, vectors_ref, weight_ref, linear_ref, planar_ref,
        rows_ref, cols_ref,
    ) = refs[:11]
    ins = refs[11 : 11 + count]
    proj_ref, merged_ref, probs_ref, lefts_ref, start_ref, normal_ref, scale_ref = refs[11 + count : 18 + count]
    outs = refs[18 + count : 18 + 2 * count]
    box_ref, conv_ref, local_ref, pooled_ref = refs[18 + 2 * count : 22 + 2 * count]
    rest = refs[22 + 2 * count :]
    rows = features_ref.shape[0]
    sums = exchange_stages(line, partial(pool_statistics, float(rows)), local_ref, pooled_ref, rest[:7])
    stages = gather_stages(line, ins, outs, rest[7:])
    step = pl.program_id(0)

    def vector(k):
        return vectors_ref[k : k + 1, :]

    def hit_rows(stream):
        return jnp.broadcast_to(hits_ref[:, stream : stream + 1] == 1, (rows, MODEL_WIDTH))

    @pl.when(step == 0)
    def _():
        greet_peers(line)
        conv = dot_nn(features_ref[...], backbone_ref[...])
        mean = jnp.mean(conv, axis=0, keepdims=True)
        center = conv - mean
        conv_ref[...] = conv
        local_ref[0] = mean
        local_ref[1] = jnp.sum(center * center, axis=0, keepdims=True)
        sums.near()
        stages.start()
        make_boxes(rows_ref, cols_ref, box_ref)
        text_start = jnp.where(hit_rows(0), vector(2), text_ref[...].astype(jnp.float32))
        start_ref[...] = text_start
        lefts_ref[0] = text_start.astype(jnp.bfloat16)
        coords = lax.broadcasted_iota(jnp.int32, (rows, COORDS), 1)
        for stream in range(2):
            space = None
            for axis in range(2):
                place = 2 * stream + axis
                hit = (coords == cols_ref[:, place : place + 1]).astype(jnp.bfloat16)
                part = dot_nn(hit, table_ref[:, axis * MODEL_WIDTH : (axis + 1) * MODEL_WIDTH])
                space = part if space is None else space + part
            lefts_ref[2 * stream + 1] = space.astype(jnp.bfloat16)
        sums.far()

    @pl.when(jnp.logical_and(step >= 1, step <= KINDS))
    def _():
        column = column_at_step(step)
        columns = pl.ds(pl.multiple_of(column * MODEL_WIDTH, MODEL_WIDTH), MODEL_WIDTH)
        proj_ref[:, columns] = dot_nn(lefts_ref[source_of(column)], weight_ref[...]).astype(jnp.bfloat16)

    @pl.when(step == 7)
    def _():
        sums.total()
        inverse = lax.rsqrt(pooled_ref[1] / token_total + batch_epsilon)
        normal = (conv_ref[...] - pooled_ref[0]) * inverse
        normal_ref[...] = normal
        scale_ref[...] = jnp.broadcast_to(vector(0) * inverse, scale_ref.shape)
        region_start = jnp.where(hit_rows(1), vector(3), normal * vector(0) + vector(1))
        start_ref[...] += region_start
        lefts_ref[2] = region_start.astype(jnp.bfloat16)

    @pl.when(step > KINDS)
    def _():
        attend_pair(step - 1 - KINDS, proj_ref, linear_ref, planar_ref, box_ref, merged_ref, probs_ref)

    def along(k):
        return lambda: spread(line, 3, k, 1, stages.along)

    def around(k):
        return lambda: spread(line, 4, k, 0, stages.around)

    def home(k):
        return lambda: spread(line, 4, k, 0, stages.home)

    at_steps(
        [
            (3, [along(0), around(0)]),
            (10, [along(1)]),
            (11, [around(1)]),
            (13, [along(2), home(0)]),
            (15, [around(2), home(1)]),
            (16, [around(3), home(2), home(3), sums.end, stages.end]),
        ]
    )


def forward_layer(
    features, backbone, table, text, hits, vectors, weights, linear_ext, planar_rows, anchor_rows, anchor_cols,
    shards, token_total, collective_id,
):
    dp = lax.axis_size("dp")
    line = dp // RING
    count = len(shards)
    anywhere = pl.BlockSpec(memory_space=pl.ANY)
    width = weights.shape[1]
    page = (PAGE_TOKENS, MODEL_WIDTH)
    f32, bf16 = jnp.float32, jnp.bfloat16

    def pair_at(i):
        return jnp.maximum(i - 1 - KINDS, 0)

    def whole(shape):
        return pl.BlockSpec(shape, lambda i: (0,) * len(shape))

    outs = [
        ((PAGE_TOKENS, width), bf16, whole((PAGE_TOKENS, width))),
        (page, bf16, pl.BlockSpec((PAGE_TOKENS, LANES), lambda i: (0, pair_at(i)))),
        (
            (2, HEADS, PAGE_TOKENS, PAGE_TOKENS), f32,
            pl.BlockSpec((2, 2, PAGE_TOKENS, PAGE_TOKENS), lambda i: (0, pair_at(i), 0, 0)),
        ),
        ((4, *page), bf16, whole((4, *page))),
        (page, f32, whole(page)),
        (page, f32, whole(page)),
        ((8, MODEL_WIDTH), f32, whole((8, MODEL_WIDTH))),
        *(((2 * dp, *shard.shape), shard.dtype, anywhere) for shard in shards),
    ]
    pool = (2, 1, MODEL_WIDTH)
    return pl.pallas_call(
        partial(forward_kernel, line, count, float(token_total)),
        grid=(1 + KINDS + PAIRS,),
        in_specs=[
            once(features.shape),
            once(backbone.shape),
            once(table.shape),
            once(text.shape),
            once(hits.shape),
            once(vectors.shape),
            pl.BlockSpec((MODEL_WIDTH, MODEL_WIDTH), lambda i: (0, column_at_step(i))),
            once(linear_ext.shape),
            once(planar_rows.shape),
            once(anchor_rows.shape),
            once(anchor_cols.shape),
            *[anywhere] * count,
        ],
        out_specs=[spec for shape, kind, spec in outs],
        out_shape=[jax.ShapeDtypeStruct(shape, kind) for shape, kind, spec in outs],
        scratch_shapes=[
            pltpu.VMEM((2, PAGE_TOKENS, PAGE_TOKENS), jnp.int32),
            pltpu.VMEM(page, f32),
            pltpu.VMEM(pool, f32),
            pltpu.VMEM(pool, f32),
            *exchange_scratch(line, pool),
            *gather_sems(line, count),
        ],
        compiler_params=pltpu.CompilerParams(
            collective_id=collective_id, has_side_effects=True, vmem_limit_bytes=62 << 20
        ),
        name="forward_layer",
    )(
        features, backbone, table, text, hits, vectors, weights, linear_ext, planar_rows, anchor_rows, anchor_cols,
        *shards,
    )


TABLE_STEP = PAIRS + KINDS


def backward_kernel(line, count, *refs):
    (
        proj_ref, probs_ref, upstream_ref, rows_ref, cols_ref, lefts_ref, weight_ref, mixer_grad_ref, normal_ref,
        hits_ref,
    ) = refs[:10]
    ins = refs[10 : 10 + count]
    (
        linear_ref, planar_ref, weight_grad_ref, table_grad_ref, text_grad_ref, region_grad_ref, sums_ref,
    ) = refs[10 + count : 17 + count]
    outs = refs[17 + count : 17 + 2 * count]
    grad_ref, turned_left_ref, input_grad_ref = refs[17 + 2 * count : 20 + 2 * count]
    helpers = refs[20 + 2 * count : 24 + 2 * count]
    stages = scatter_stages(line, ins, outs, refs[24 + 2 * count :])
    step = pl.program_id(0)

    @pl.when(step == 0)
    def _():
        greet(line)
        stages.start()
        make_places(rows_ref, cols_ref, *helpers)

    def first(k):
        return lambda: spread(line, 4, k, 0, stages.first)

    def second(k):
        return lambda: spread(line, 4, k, 0, stages.second)

    def third(k):
        return lambda: spread(line, 4, k, 0, stages.third)

    slots = {
        1: [first(0)],
        3: [first(1)],
        7: [second(0)],
        8: [first(2)],
        10: [first(3)],
        12: [second(1)],
        17: [third(0)],
        22: [second(2), second(3)],
    }

    def pump(sub):
        at_steps([(slot // 4, work) for slot, work in slots.items() if slot % 4 == sub])

    @pl.when(step < PAIRS)
    def _():
        attend_back_pair(step, pump, proj_ref, probs_ref, upstream_ref, grad_ref, linear_ref, planar_ref, *helpers)

    @pl.when(jnp.logical_and(step >= PAIRS, step < TABLE_STEP))
    def _():
        column = step - PAIRS
        source = source_of(column)
        fresh = jnp.logical_or(column == 0, source != source_of(jnp.maximum(column - 1, 0)))
        grads = grad_ref[:, pl.ds(pl.multiple_of(column * MODEL_WIDTH, MODEL_WIDTH), MODEL_WIDTH)]

        @pl.when(fresh)
        def _():
            turned_left_ref[...] = lefts_ref[source].T

        weight_grad_ref[...] = dot_nn(turned_left_ref[...], grads).astype(jnp.bfloat16)
        back = dot_nt(grads, weight_ref[...])

        @pl.when(fresh)
        def _():
            input_grad_ref[source] = back

        @pl.when(jnp.logical_not(fresh))
        def _():
            input_grad_ref[source] += back

    @pl.when(step >= TABLE_STEP)
    def _():
        axis = step - TABLE_STEP
        coords = lax.broadcasted_iota(jnp.int32, (COORDS, PAGE_TOKENS), 0)
        total = None
        for stream in range(2):
            hit = (coords == rows_ref[pl.ds(2 * stream + axis, 1), :]).astype(jnp.bfloat16)
            part = dot_nn(hit, input_grad_ref[2 * stream + 1].astype(jnp.bfloat16))
            total = part if total is None else total + part
        table_grad_ref[...] = total.astype(jnp.bfloat16)

    @pl.when(step == TABLE_STEP + 1)
    def _():
        mixer_grad = mixer_grad_ref[...]
        sums_ref[...] = jnp.zeros_like(sums_ref)
        for stream, out_ref in enumerate((text_grad_ref, region_grad_ref)):
            grad = mixer_grad + input_grad_ref[2 * stream]
            hit = jnp.broadcast_to(hits_ref[:, stream : stream + 1] == 1, grad.shape)
            zero = jnp.zeros_like(grad)
            kept = jnp.where(hit, zero, grad)
            out_ref[...] = kept
            sums_ref[stream : stream + 1, :] = jnp.sum(jnp.where(hit, grad, zero), axis=0, keepdims=True)
            if stream == 1:
                sums_ref[2:3, :] = jnp.sum(kept, axis=0, keepdims=True)
                sums_ref[3:4, :] = jnp.sum(kept * normal_ref[...], axis=0, keepdims=True)

    at_steps(
        [(PAIRS + 3, [third(1)]), (PAIRS + 8, [third(2)]), (TABLE_STEP + 1, [third(3), stages.end])]
    )


def backward_layer(
    proj, probs, upstream, anchor_rows, anchor_cols, lefts, weights, mixer_grad, normal, hits, grads, collective_id
):
    dp = lax.axis_size("dp")
    line = dp // RING
    count = len(grads)
    blocks = [(grad.shape[1:], grad.dtype) for grad in grads]
    anywhere = pl.BlockSpec(memory_space=pl.ANY)
    page = (PAGE_TOKENS, MODEL_WIDTH)

    def pair_at(i):
        return jnp.minimum(i, PAIRS - 1)

    def column_at(i):
        return jnp.clip(i - PAIRS, 0, KINDS - 1)

    return pl.pallas_call(
        partial(backward_kernel, line, count),
        grid=(TABLE_STEP + 2,),
        in_specs=[
            once(proj.shape),
            pl.BlockSpec((2, 2, PAGE_TOKENS, PAGE_TOKENS), lambda i: (0, pair_at(i), 0, 0)),
            pl.BlockSpec((PAGE_TOKENS, LANES), lambda i: (0, pair_at(i))),
            once(anchor_rows.shape),
            once(anchor_cols.shape),
            once(lefts.shape),
            pl.BlockSpec((MODEL_WIDTH, MODEL_WIDTH), lambda i: (0, column_at(i))),
            once(page),
            once(page),
            once(hits.shape),
            *[anywhere] * count,
        ],
        out_specs=[
            pl.BlockSpec((HEADS, 1, 2 * PAGE_TOKENS), lambda i: (0, 0, 0)),
            pl.BlockSpec((HEADS, 1, SP_B), lambda i: (0, 0, 0)),
            pl.BlockSpec((MODEL_WIDTH, MODEL_WIDTH), lambda i: (0, column_at(i))),
            pl.BlockSpec((COORDS, MODEL_WIDTH), lambda i: (0, jnp.maximum(i - TABLE_STEP, 0))),
            pl.BlockSpec(page, lambda i: (0, 0)),
            pl.BlockSpec(page, lambda i: (0, 0)),
            pl.BlockSpec((8, MODEL_WIDTH), lambda i: (0, 0)),
            *(pl.BlockSpec(shape, lambda i: (0, 0)) for shape, kind in blocks),
        ],
        out_shape=[
            jax.ShapeDtypeStruct((HEADS, 1, 2 * PAGE_TOKENS), jnp.float32),
            jax.ShapeDtypeStruct((HEADS, 1, SP_B), jnp.float32),
            jax.ShapeDtypeStruct(weights.shape, jnp.bfloat16),
            jax.ShapeDtypeStruct((COORDS, 2 * MODEL_WIDTH), jnp.bfloat16),
            jax.ShapeDtypeStruct(page, jnp.float32),
            jax.ShapeDtypeStruct(page, jnp.float32),
            jax.ShapeDtypeStruct((8, MODEL_WIDTH), jnp.float32),
            *(jax.ShapeDtypeStruct(shape, jnp.float32) for shape, kind in blocks),
        ],
        scratch_shapes=[
            pltpu.VMEM(proj.shape, jnp.bfloat16),
            pltpu.VMEM((MODEL_WIDTH, PAGE_TOKENS), jnp.bfloat16),
            pltpu.VMEM((4, *page), jnp.float32),
            pltpu.VMEM((2, 4 * PAGE_TOKENS, SP_B), jnp.bfloat16),
            pltpu.VMEM((2, 128, PAGE_TOKENS), jnp.bfloat16),
            pltpu.VMEM((2, 4, PAGE_TOKENS, PAGE_TOKENS), jnp.bfloat16),
            pltpu.VMEM((PAGE_TOKENS, PAGE_TOKENS), jnp.bfloat16),
            *scatter_scratch(line, blocks),
        ],
        compiler_params=pltpu.CompilerParams(
            collective_id=collective_id, has_side_effects=True, vmem_limit_bytes=63 << 20
        ),
        name="backward_layer",
    )(
        proj, probs, upstream, anchor_rows, anchor_cols, lefts, weights, mixer_grad, normal, hits,
        *(grad.reshape(line * RING, 2, *grad.shape[1:]) for grad in grads),
    )


def last_kernel(line, count, token_total, *refs):
    sums_ref, kept_ref, normal_ref, scale_ref, features_ref, backbone_ref = refs[:6]
    ins = refs[6 : 6 + count]
    feature_grad_ref, total_ref = refs[6 + count : 8 + count]
    outs = refs[8 + count : 9 + 2 * count]
    turned_ref, conv_grad_ref, late_ref = refs[9 + 2 * count : 12 + 2 * count]
    rest = refs[12 + 2 * count :]
    sums = exchange_stages(line, add_up, sums_ref, total_ref, rest[:7])
    early_scratch = 5 * count + 9
    early = scatter_stages(line, ins, outs[:count], rest[7 : 7 + early_scratch])
    late = scatter_stages(line, [late_ref], outs[count:], rest[7 + early_scratch :])
    share = late_ref.shape[2]

    def first(stages, k):
        spread(line, 4, k, 0, stages.first)

    def second(stages, k):
        spread(line, 4, k, 0, stages.second)

    def third(stages, k):
        spread(line, 4, k, 0, stages.third)

    greet_peers(line)
    sums.near()
    early.start()
    first(early, 0)
    sums.far()
    first(early, 1)
    sums.total()
    conv_grad_ref[...] = (
        scale_ref[...]
        * (kept_ref[...] - total_ref[0:1, :] / token_total - normal_ref[...] * (total_ref[1:2, :] / token_total))
    ).astype(jnp.bfloat16)
    second(early, 0)
    first(early, 2)
    first(early, 3)

    def turn(k, unused):
        columns = pl.ds(pl.multiple_of(k * 512, 512), 512)
        turned_ref[columns, :] = features_ref[:, columns].T
        return unused

    lax.fori_loop(0, features_ref.shape[1] // 512, turn, 0)
    width = min(512, 2 * share * line * RING)

    def backbone(k, unused):
        rows = pl.ds(pl.multiple_of(k * width, width), width)
        block = dot_nn(turned_ref[rows, :], conv_grad_ref[...])
        places = width // (2 * share)
        late_ref[pl.ds(k * places, places)] = block.reshape(places, 2, share, MODEL_WIDTH).astype(jnp.bfloat16)
        return unused

    lax.fori_loop(0, features_ref.shape[1] // width, backbone, 0)
    late.start()
    for k in range(4):
        first(late, k)
    second(early, 1)
    third(early, 0)

    def feature(k, unused):
        columns = pl.ds(pl.multiple_of(k * 512, 512), 512)
        feature_grad_ref[:, columns] = dot_nt(conv_grad_ref[...], backbone_ref[columns, :])
        return unused

    lax.fori_loop(0, features_ref.shape[1] // 512, feature, 0)
    second(early, 2)
    for k in range(4):
        second(late, k)
    second(early, 3)
    third(early, 1)
    third(early, 2)
    for k in range(3):
        third(late, k)
    third(early, 3)
    third(late, 3)
    sums.end()
    early.end()
    late.end()


def last_layer(sums, kept, normal, scale, features, backbone, grads, token_total, collective_id):
    dp = lax.axis_size("dp")
    line = dp // RING
    count = len(grads)
    blocks = [(grad.shape[1:], grad.dtype) for grad in grads]
    channels = backbone.shape[0]
    late = [((channels // (2 * dp), MODEL_WIDTH), jnp.bfloat16)]
    anywhere = pl.BlockSpec(memory_space=pl.ANY)
    vmem = pl.BlockSpec(memory_space=pltpu.VMEM)
    return pl.pallas_call(
        partial(last_kernel, line, count, float(token_total)),
        in_specs=[*[vmem] * 6, *[anywhere] * count],
        out_specs=[vmem] * (3 + count),
        out_shape=[
            jax.ShapeDtypeStruct(features.shape, jnp.float32),
            jax.ShapeDtypeStruct(sums.shape, jnp.float32),
            *(jax.ShapeDtypeStruct(shape, jnp.float32) for shape, kind in blocks + late),
        ],
        scratch_shapes=[
            pltpu.VMEM((channels, PAGE_TOKENS), jnp.bfloat16),
            pltpu.VMEM(kept.shape, jnp.bfloat16),
            pltpu.VMEM((dp, 2, *late[0][0]), jnp.bfloat16),
            *exchange_scratch(line, sums.shape),
            *scatter_scratch(line, blocks),
            *scatter_scratch(line, late),
        ],
        compiler_params=pltpu.CompilerParams(
            collective_id=collective_id, has_side_effects=True, vmem_limit_bytes=63 << 20
        ),
        name="last_layer",
    )(
        sums, kept, normal, scale, features, backbone,
        *(grad.reshape(line * RING, 2, *grad.shape[1:]) for grad in grads),
    )


norm_epsilon = 1e-05


def normal_parts(values):
    center = values - jnp.mean(values, axis=-1, keepdims=True)
    inverse = lax.rsqrt(jnp.mean(center * center, axis=-1, keepdims=True) + norm_epsilon)
    return center * inverse, inverse


def normal_back(normal, inverse, gain, grad):
    scaled = grad * gain
    return inverse * (
        scaled
        - jnp.mean(scaled, axis=-1, keepdims=True)
        - normal * jnp.mean(scaled * normal, axis=-1, keepdims=True)
    )


CHUNKS = 4


def mixer_kernel(
    merged_ref, start_ref, cotangent_ref, vectors_ref, bias_ref, merge_ref, expand_ref, reduce_ref,
    output_ref, mixer_grad_ref, merged_grad_ref, merge_grad_ref, expand_grad_ref, reduce_grad_ref, sums_ref,
    bias_grad_ref,
    hidden_ref, normal_ref, inverse_ref, low_ref, active_ref, slope_ref, dense_ref, grad_ref, grad_low_ref,
    turned_ref,
):
    step = pl.program_id(0)
    chunk = lax.rem(step, CHUNKS)
    width = expand_ref.shape[1] // CHUNKS
    part = pl.ds(pl.multiple_of(chunk * width, width), width)

    def vector(k):
        return vectors_ref[k : k + 1, :]

    def column_sum(values):
        return jnp.sum(values, axis=0, keepdims=True)

    @pl.when(step == 0)
    def _():
        normal, inverse = normal_parts(start_ref[...] + dot_nn(merged_ref[...], merge_ref[...]))
        normal_ref[...] = normal
        inverse_ref[...] = jnp.broadcast_to(inverse, inverse_ref.shape)
        hidden = normal * vector(4) + vector(5)
        hidden_ref[...] = hidden
        low_ref[...] = hidden.astype(jnp.bfloat16)
        dense_ref[...] = jnp.zeros_like(dense_ref)

    @pl.when(step < CHUNKS)
    def _():
        inner = dot_nn(low_ref[...], expand_ref[:, part]) + bias_ref[chunk]
        share = 0.5 + 0.5 * lax.erf(inner * (0.5**0.5))
        active = (inner * share).astype(jnp.bfloat16)
        active_ref[chunk] = active
        slope_ref[chunk] = share + inner * jnp.exp(-0.5 * inner * inner) * (2.0 * jnp.pi) ** -0.5
        dense_ref[...] += dot_nn(active, reduce_ref[part, :])

    @pl.when(step == CHUNKS - 1)
    def _():
        normal, inverse = normal_parts(hidden_ref[...] + (dense_ref[...] + vector(6)))
        output_ref[...] = (normal * vector(7) + vector(8)).astype(jnp.bfloat16)
        upstream = cotangent_ref[...].astype(jnp.float32)
        grad = normal_back(normal, inverse, vector(7), upstream)
        grad_ref[...] = grad
        grad_low_ref[...] = grad.astype(jnp.bfloat16)
        sums_ref[2:3, :] = column_sum(grad)
        sums_ref[3:4, :] = column_sum(upstream * normal)
        sums_ref[4:5, :] = column_sum(upstream)
        turned_ref[...] = low_ref[...].T

    @pl.when(step >= CHUNKS)
    def _():
        grad_low = grad_low_ref[...]
        reduce_grad_ref[...] = dot_tn(active_ref[chunk], grad_low).astype(jnp.bfloat16)
        inner_low = (dot_nt(grad_low, reduce_ref[part, :]) * slope_ref[chunk]).astype(jnp.bfloat16)
        bias_grad_ref[chunk] = column_sum(inner_low.astype(jnp.float32))
        expand_grad_ref[...] = dot_nn(turned_ref[...], inner_low).astype(jnp.bfloat16)
        grad_ref[...] += dot_nt(inner_low, expand_ref[:, part])

    @pl.when(step == 2 * CHUNKS - 1)
    def _():
        grad = grad_ref[...]
        normal = normal_ref[...]
        mixer_grad = normal_back(normal, inverse_ref[:, :1], vector(4), grad)
        mixer_grad_ref[...] = mixer_grad
        sums_ref[0:1, :] = column_sum(grad * normal)
        sums_ref[1:2, :] = column_sum(grad)
        low = mixer_grad.astype(jnp.bfloat16)
        merge_grad_ref[...] = dot_tn(merged_ref[...], low).astype(jnp.bfloat16)
        merged_grad_ref[...] = dot_nt(low, merge_ref[...]).astype(jnp.bfloat16)


def mixer_layer(merged, start, cotangent, vectors, bias, w_merge, w_expand, w_reduce):
    rows = merged.shape[0]
    inner = w_expand.shape[1]
    width = inner // CHUNKS
    page = (rows, MODEL_WIDTH)

    def back_at(i):
        return jnp.maximum(i - CHUNKS, 0)

    def whole(shape):
        return pl.BlockSpec(shape, lambda i: (0,) * len(shape))

    f32, bf16 = jnp.float32, jnp.bfloat16
    outs = [
        (page, bf16, whole(page)),
        (page, f32, whole(page)),
        (page, bf16, whole(page)),
        ((MODEL_WIDTH, MODEL_WIDTH), bf16, whole((MODEL_WIDTH, MODEL_WIDTH))),
        ((MODEL_WIDTH, inner), bf16, pl.BlockSpec((MODEL_WIDTH, width), lambda i: (0, back_at(i)))),
        ((inner, MODEL_WIDTH), bf16, pl.BlockSpec((width, MODEL_WIDTH), lambda i: (back_at(i), 0))),
        ((8, MODEL_WIDTH), f32, whole((8, MODEL_WIDTH))),
        ((CHUNKS, 1, width), f32, whole((CHUNKS, 1, width))),
    ]
    return pl.pallas_call(
        mixer_kernel,
        grid=(2 * CHUNKS,),
        in_specs=[
            once(page),
            once(page),
            once(page),
            once(vectors.shape),
            once(bias.shape),
            once(w_merge.shape),
            once(w_expand.shape),
            once(w_reduce.shape),
        ],
        out_specs=[spec for shape, kind, spec in outs],
        out_shape=[jax.ShapeDtypeStruct(shape, kind) for shape, kind, spec in outs],
        scratch_shapes=[
            pltpu.VMEM(page, f32),
            pltpu.VMEM(page, f32),
            pltpu.VMEM((rows, 128), f32),
            pltpu.VMEM(page, bf16),
            pltpu.VMEM((CHUNKS, rows, width), bf16),
            pltpu.VMEM((CHUNKS, rows, width), f32),
            pltpu.VMEM(page, f32),
            pltpu.VMEM(page, f32),
            pltpu.VMEM(page, bf16),
            pltpu.VMEM((MODEL_WIDTH, rows), bf16),
        ],
        compiler_params=pltpu.CompilerParams(vmem_limit_bytes=62 << 20),
        name="mixer_layer",
    )(merged, start, cotangent, vectors, bias, w_merge, w_expand, w_reduce)

AXES = ("dp", "pair")


def padded_rows(pieces):
    rows = [jnp.pad(piece.astype(jnp.float32), ((0, 0), (0, 128 - piece.shape[1]))) for piece in pieces]
    total = sum(piece.shape[0] for piece in pieces)
    rows.append(jnp.zeros((-total % 8, 128), jnp.float32))
    return jnp.concatenate(rows, axis=0)


def blocks_of(grad, devices):
    blocks = grad.astype(jnp.bfloat16).reshape(devices, grad.shape[0] // devices, grad.shape[1])
    return blocks if blocks.shape[1] % 8 == 0 else blocks.reshape(devices, -1, 128)


def per_device(
    text_inputs,
    region_features,
    text_masked,
    region_masked,
    text_anchors,
    region_anchors,
    backbone_weight,
    batch_gain,
    batch_shift,
    text_blank,
    region_blank,
    position_table,
    stream_weights,
    linear_bias,
    planar_bias,
    merge_weight,
    mixer_gain,
    mixer_shift,
    expand_weight,
    expand_bias,
    reduce_weight,
    reduce_bias,
    output_gain,
    output_shift,
    cotangent,
):
    devices = lax.axis_size(AXES)
    row_count = text_inputs.shape[0]
    token_total = row_count * devices
    share = MODEL_WIDTH // devices
    expand_share = expand_bias.shape[0]
    bias_rows = REL_B // devices
    vectors = jnp.stack(
        [
            batch_gain, batch_shift, text_blank, region_blank, mixer_gain, mixer_shift, reduce_bias,
            output_gain, output_shift,
        ]
    )
    small = padded_rows([linear_bias, planar_bias, vectors, expand_bias[None, :]])
    packed, w_backbone, w_table, w_stream = gather_all(
        (small, backbone_weight, position_table, stream_weights), 0
    )
    w_linear = packed[:, :bias_rows, :HEADS].reshape(REL_B, HEADS)
    w_planar = packed[:, bias_rows : 2 * bias_rows, :HEADS].reshape(SP_B, HEADS)
    w_vectors = packed[:, 2 * bias_rows : 2 * bias_rows + 9, :share].transpose(1, 0, 2).reshape(9, -1)
    w_expand_bias = packed[:, 2 * bias_rows + 9, :expand_share].reshape(-1)
    w_backbone, w_table, w_stream = (
        whole.reshape(-1, whole.shape[-1]) for whole in (w_backbone, w_table, w_stream)
    )

    anchor_rows = jnp.concatenate([text_anchors, region_anchors], axis=0)
    anchor_cols = anchor_rows.T
    hits = jnp.stack([text_masked, region_masked], axis=1)
    proj, merged_low, probs, lefts, start_sum, normal_feat, batch_scale, *wholes = forward_layer(
        region_features, w_backbone, w_table, text_inputs, hits, w_vectors, w_stream, linear_extended(w_linear),
        w_planar.T[:, None, :], anchor_rows, anchor_cols, (merge_weight, expand_weight, reduce_weight),
        token_total, 4,
    )
    w_merge, w_expand, w_reduce = (whole.reshape(-1, whole.shape[-1]) for whole in wholes)
    (
        layer_output, mixer_in_grad, merged_grad, merge_weight_grad, expand_weight_grad, reduce_weight_grad,
        mixer_sums, expand_bias_grad,
    ) = mixer_layer(
        merged_low, start_sum, cotangent, w_vectors, w_expand_bias.reshape(CHUNKS, 1, -1),
        w_merge, w_expand, w_reduce,
    )
    early = (expand_weight_grad, reduce_weight_grad, merge_weight_grad)
    (
        linear_sums, planar_sums, stream_weights_grad, position_table_grad, text_gradient, region_kept,
        start_sums, *early_shares,
    ) = backward_layer(
        proj, probs, merged_grad, anchor_rows, anchor_cols, lefts, w_stream, mixer_in_grad, normal_feat, hits,
        [blocks_of(grad, devices) for grad in early], 5,
    )
    expand_weight_grad, reduce_weight_grad, merge_weight_grad = (
        part.reshape(-1, grad.shape[1]) for part, grad in zip(early_shares, early)
    )
    vector_grads = jnp.concatenate([start_sums[:2], mixer_sums[:5]], axis=0)
    pieces = [
        linear_folded(linear_sums[:, 0]).T.reshape(devices, bias_rows, HEADS),
        planar_sums[:, 0].T.reshape(devices, bias_rows, HEADS),
        vector_grads.reshape(7, devices, share).transpose(1, 0, 2),
        expand_bias_grad.reshape(devices, 1, expand_share),
    ]
    small_grads = jax.vmap(lambda *parts: padded_rows(parts))(*pieces)
    late = (stream_weights_grad, position_table_grad)
    feature_gradient, totals, small, *shares = last_layer(
        start_sums[2:4], region_kept, normal_feat, batch_scale[:1], region_features,
        w_backbone, [small_grads, *(blocks_of(grad, devices) for grad in late)], token_total, 1,
    )
    stream_weights_grad, position_table_grad = (
        part.reshape(-1, grad.shape[1]) for part, grad in zip(shares, late)
    )
    backbone_weight_grad = shares[2]
    owned = lax.dynamic_slice_in_dim(totals, lax.axis_index(AXES) * share, share, axis=1)
    batch_shift_gradient = owned[0]
    batch_gain_gradient = owned[1]
    vector_shares = small[2 * bias_rows : 2 * bias_rows + 7, :share]
    return (
        layer_output,
        text_gradient,
        feature_gradient,
        backbone_weight_grad,
        batch_gain_gradient,
        batch_shift_gradient,
        vector_shares[0],
        vector_shares[1],
        position_table_grad,
        stream_weights_grad,
        small[:bias_rows, :HEADS],
        small[bias_rows : 2 * bias_rows, :HEADS],
        merge_weight_grad,
        vector_shares[2],
        vector_shares[3],
        expand_weight_grad,
        small[2 * bias_rows + 7, :expand_share],
        reduce_weight_grad,
        vector_shares[4],
        vector_shares[5],
        vector_shares[6],
    )


def solution(mesh):
    in_specs = (
        P(("dp", "pair"), None),
        P(("dp", "pair"), None),
        P(("dp", "pair")),
        P(("dp", "pair")),
        P(None, ("dp", "pair")),
        P(None, ("dp", "pair")),
        P(("dp", "pair"), None),
        P(("dp", "pair")),
        P(("dp", "pair")),
        P(("dp", "pair")),
        P(("dp", "pair")),
        P(("dp", "pair"), None),
        P(("dp", "pair"), None),
        P(("dp", "pair"), None),
        P(("dp", "pair"), None),
        P(("dp", "pair"), None),
        P(("dp", "pair")),
        P(("dp", "pair")),
        P(("dp", "pair"), None),
        P(("dp", "pair")),
        P(("dp", "pair"), None),
        P(("dp", "pair")),
        P(("dp", "pair")),
        P(("dp", "pair")),
        P(("dp", "pair"), None),
    )
    out_specs = (
        P(("dp", "pair"), None),
        P(("dp", "pair"), None),
        P(("dp", "pair"), None),
        P(("dp", "pair"), None),
        P(("dp", "pair")),
        P(("dp", "pair")),
        P(("dp", "pair")),
        P(("dp", "pair")),
        P(("dp", "pair"), None),
        P(("dp", "pair"), None),
        P(("dp", "pair"), None),
        P(("dp", "pair"), None),
        P(("dp", "pair"), None),
        P(("dp", "pair")),
        P(("dp", "pair")),
        P(("dp", "pair"), None),
        P(("dp", "pair")),
        P(("dp", "pair"), None),
        P(("dp", "pair")),
        P(("dp", "pair")),
        P(("dp", "pair")),
    )
    return jax.shard_map(
        per_device, mesh=mesh, in_specs=in_specs, out_specs=out_specs, check_vma=False
    )
```

```python
from functools import partial
from types import SimpleNamespace

import jax
import jax.numpy as jnp
from jax import lax
from jax.experimental import pallas as pl
from jax.experimental.pallas import tpu as pltpu
from jax.sharding import PartitionSpec as P

HEADS = 12
HEAD_DIM = 64
COORDS = 1024
REL_B = 256
SP_SIDE = 16
PAGE_TOKENS = 256
MODEL_WIDTH = 768
SP_B = 256
COORD_STEP = 128
PAIRS = HEADS // 2
LANES = 2 * HEAD_DIM


def dot_nt(left, right):
    return lax.dot_general(left, right, (((1,), (1,)), ((), ())), preferred_element_type=jnp.float32)


def dot_tn(left, right):
    return lax.dot_general(left, right, (((0,), (0,)), ((), ())), preferred_element_type=jnp.float32)


def dot_nn(left, right):
    return lax.dot_general(left, right, (((1,), (0,)), ((), ())), preferred_element_type=jnp.float32)


def head_columns(stream, kind, pair):
    return pl.ds(pl.multiple_of(((5 * stream + kind) * PAIRS + pair) * LANES, LANES), LANES)


def make_boxes(rows_ref, cols_ref, box_ref):
    for stream in range(2):
        part = []
        for axis in range(2):
            along = rows_ref[2 * stream + axis : 2 * stream + axis + 1, :]
            down = cols_ref[:, 2 * stream + axis : 2 * stream + axis + 1]
            part.append(((along - down) >> 7) + SP_SIDE // 2)
        box_ref[stream] = part[0] * SP_SIDE + part[1]


def attend_pair(pair, proj_ref, linear_ref, planar_ref, box_ref, merged_ref, probs_ref):
    lane_head = lax.broadcasted_iota(jnp.int32, (PAGE_TOKENS, LANES), 1) // HEAD_DIM
    mixed = [None, None]
    for inner in range(2):
        head = 2 * pair + inner
        mine = lane_head == inner
        spread = jnp.broadcast_to(linear_ref[head], (PAGE_TOKENS, 2 * PAGE_TOKENS))
        linear_term = pltpu.roll(spread, PAGE_TOKENS + 1, 1, stride=1, stride_axis=0)[:, :PAGE_TOKENS]
        low_table = jnp.broadcast_to(planar_ref[head, :, :128], (PAGE_TOKENS, 128))
        high_table = jnp.broadcast_to(planar_ref[head, :, 128:], (PAGE_TOKENS, 128))
        total = None
        for stream in range(2):
            pieces = [proj_ref[:, head_columns(stream, kind, pair)] for kind in range(5)]
            zero = jnp.zeros_like(pieces[0])
            left = jnp.concatenate([jnp.where(mine, pieces[0], zero), jnp.where(mine, pieces[3], zero)], axis=1)
            right = jnp.concatenate([pieces[1], pieces[4]], axis=1)
            logits = dot_nt(left, right) * HEAD_DIM ** (-0.5)
            planar = []
            for half in range(2):
                box = box_ref[stream, :, 128 * half : 128 * half + 128]
                place = box & 127
                planar.append(
                    jnp.where(
                        box < 128,
                        jnp.take_along_axis(low_table, place, axis=1),
                        jnp.take_along_axis(high_table, place, axis=1),
                    )
                )
            logits = logits + linear_term + jnp.concatenate(planar, axis=1)
            top = jnp.max(logits, axis=-1, keepdims=True)
            shifted = jnp.exp(logits - top)
            probs = shifted / jnp.sum(shifted, axis=-1, keepdims=True)
            probs_ref[stream, inner] = probs
            part = dot_nn(probs.astype(jnp.bfloat16), pieces[2])
            total = part if total is None else total + part
        mixed[inner] = total
    merged_ref[...] = jnp.where(lane_head == 0, mixed[0], mixed[1]).astype(jnp.bfloat16)


def make_places(rows_ref, cols_ref, place_ref, turned_ref, mask_ref, flip_ref):
    lanes = lax.broadcasted_iota(jnp.int32, (PAGE_TOKENS, SP_B), 1)
    rows = lax.broadcasted_iota(jnp.int32, (PAGE_TOKENS, SP_B), 0)
    flip_ref[...] = (lanes + rows == PAGE_TOKENS - 1).astype(jnp.bfloat16)
    for stream in range(2):
        x_row = rows_ref[2 * stream : 2 * stream + 1, :]
        y_row = rows_ref[2 * stream + 1 : 2 * stream + 2, :]
        x_col = cols_ref[:, 2 * stream : 2 * stream + 1]
        y_col = cols_ref[:, 2 * stream + 1 : 2 * stream + 2]
        cell_row = (x_row >> 7) * SP_SIDE + (y_row >> 7)
        cell_col = (x_col >> 7) * SP_SIDE + (y_col >> 7)
        x_less = ((x_row & 127) < (x_col & 127)).astype(jnp.float32)
        y_less = ((y_row & 127) < (y_col & 127)).astype(jnp.float32)
        for x_side in range(2):
            for y_side in range(2):
                side = 2 * x_side + y_side
                place_ref[stream, side * PAGE_TOKENS : (side + 1) * PAGE_TOKENS, :] = (
                    lanes == cell_col + (SP_SIDE + 1 - SP_SIDE * x_side - y_side)
                ).astype(jnp.bfloat16)
                mask_ref[stream, side] = (
                    (x_less if x_side else 1.0 - x_less) * (y_less if y_side else 1.0 - y_less)
                ).astype(jnp.bfloat16)
        turned_ref[stream] = (rows[:128] == 127 - cell_row).astype(jnp.bfloat16)


def attend_back_pair(
    pair, pump, proj_ref, probs_ref, upstream_ref, grad_ref, linear_ref, planar_ref,
    place_ref, turned_ref, mask_ref, flip_ref,
):
    lane_head = lax.broadcasted_iota(jnp.int32, (PAGE_TOKENS, LANES), 1) // HEAD_DIM
    wide_head = jnp.concatenate([lane_head, lane_head], axis=1)
    upstream = upstream_ref[...]
    scale = HEAD_DIM ** (-0.5)
    diagonal = [None, None]
    for stream in range(2):
        pieces = [proj_ref[:, head_columns(stream, kind, pair)] for kind in range(5)]
        queries = jnp.concatenate([pieces[0], pieces[3]], axis=1)
        keys = jnp.concatenate([pieces[1], pieces[4]], axis=1)
        grads = []
        for inner in range(2):
            head = 2 * pair + inner
            mine = lane_head == inner
            grad_probs = dot_nt(jnp.where(mine, upstream, jnp.zeros_like(upstream)), pieces[2])
            probs = probs_ref[stream, inner]
            weighted = probs * grad_probs
            grad_logits = (weighted - probs * jnp.sum(weighted, axis=-1, keepdims=True)).astype(jnp.bfloat16)
            grads.append(
                (
                    dot_nn(grad_logits, keys) * scale,
                    dot_tn(grad_logits, queries) * scale,
                    dot_tn(probs.astype(jnp.bfloat16), upstream),
                )
            )
            parts = jnp.concatenate([grad_logits * mask_ref[stream, side] for side in range(4)], axis=1)
            placed = dot_nn(parts, place_ref[stream])
            placed_high = placed.astype(jnp.bfloat16)
            placed_low = (placed - placed_high.astype(jnp.float32)).astype(jnp.bfloat16)
            turned = turned_ref[stream]
            cells = dot_nn(turned, placed_high) + dot_nn(turned, placed_low)
            sums = jnp.sum(
                pltpu.roll(cells, SP_B - SP_SIDE // 2, 1, stride=1, stride_axis=0), axis=0, keepdims=True
            )
            if stream == 0:
                planar_ref[head] = sums
            else:
                planar_ref[head] += sums
            turned_over = dot_nn(flip_ref[...], grad_logits)
            diagonal[inner] = turned_over if stream == 0 else diagonal[inner] + turned_over
            pump(2 * stream + inner)
        query_grad, key_grad = (jnp.where(wide_head == 0, grads[0][k], grads[1][k]) for k in range(2))
        value_grad = jnp.where(lane_head == 0, grads[0][2], grads[1][2])
        for kind, value in enumerate(
            (query_grad[:, :LANES], key_grad[:, :LANES], value_grad, query_grad[:, LANES:], key_grad[:, LANES:])
        ):
            grad_ref[:, head_columns(stream, kind, pair)] = value.astype(jnp.bfloat16)
    for inner in range(2):
        padded = jnp.concatenate([diagonal[inner], jnp.zeros_like(diagonal[inner])], axis=1)
        linear_ref[2 * pair + inner] = jnp.sum(
            pltpu.roll(padded, 0, 1, stride=1, stride_axis=0), axis=0, keepdims=True
        )


def linear_folded(sums):
    first = REL_B // 2
    last = PAGE_TOKENS - 1 + REL_B // 2 - 1
    return jnp.concatenate(
        [
            jnp.sum(sums[:, :first], axis=1, keepdims=True),
            sums[:, first:last],
            jnp.sum(sums[:, last : 2 * PAGE_TOKENS - 1], axis=1, keepdims=True),
        ],
        axis=1,
    )


MESH = pl.DeviceIdType.MESH
RING = 4


def place():
    dp = lax.axis_index("dp")
    return dp // RING, lax.rem(dp, RING), lax.axis_index("pair")


def across(q, bit):
    other = lax.rem(q // bit, 2)
    return q + bit - 2 * bit * other


def greet(line):
    z, q, c = place()
    barrier = pltpu.get_barrier_semaphore()

    def signal(zz, qq, cc):
        pl.semaphore_signal(barrier, inc=1, device_id={"dp": zz * RING + qq, "pair": cc}, device_id_type=MESH)

    signal(z, across(q, 1), c)
    signal(z, across(q, 2), c)
    signal(z, q, 1 - c)

    @pl.when(z > 0)
    def _():
        signal(z - 1, q, c)

    @pl.when(z < line - 1)
    def _():
        signal(z + 1, q, c)

    ends = (z > 0).astype(jnp.int32) + (z < line - 1).astype(jnp.int32)
    pl.semaphore_wait(barrier, 3 + ends)


def spread(line, pumps, pump, first, work):
    total = line - first
    low, high = (first + total * (pump + k) // pumps for k in range(2))
    if high == low + 1:
        work(low)
    elif high > low:
        lax.fori_loop(low, high, lambda g, unused: (work(g), unused)[1], 0)


def gather_stages(line, ins, outs, sems):
    count = len(ins)
    (own_sem, z_send, z_recv, xy_send, xy_recv, d_send, d_recv, c_send, c_recv) = sems
    z, q, c = place()
    beside = (across(q, 1), across(q, 2))
    corner = across(across(q, 1), 2)

    def slot(zz, qq):
        return (zz * RING + qq) * 2 + c

    def remote(src, dst, send, recv, zz, qq, cc):
        return pltpu.make_async_remote_copy(
            src_ref=src, dst_ref=dst, send_sem=send, recv_sem=recv,
            device_id={"dp": zz * RING + qq, "pair": cc}, device_id_type=MESH,
        )

    def block(a, zz, qq):
        return outs[a].at[slot(zz, qq)]

    def halves(a):
        width = ins[a].shape[-1]
        cut = width // 2 if width % 256 == 0 else width
        return (0, cut), (cut, width - cut)

    def own(a):
        return pltpu.make_async_copy(ins[a], block(a, z, q), own_sem.at[a])

    def z_copy(a, way, step, first):
        zz = z - step if way == 0 else z + step
        target = z + 1 if way == 0 else z - 1
        src = ins[a] if first else block(a, zz, q)
        return remote(src, block(a, zz, q), z_send.at[way, a, step], z_recv.at[way, a, step], target, q, c)

    def xy_copy(a, axis, zz, first):
        src = ins[a] if first else block(a, zz, q)
        return remote(src, block(a, zz, q), xy_send.at[axis, a, zz], xy_recv.at[axis, a, zz], z, beside[axis], c)

    def d_copy(a, axis, zz):
        start, width = halves(a)[axis]
        part = outs[a].at[slot(zz, beside[axis]), :, pl.ds(start, width)]
        return remote(part, part, d_send.at[axis, a, zz], d_recv.at[axis, a, zz], z, beside[1 - axis], c)

    def c_copy(a, zz, qq, first):
        src = ins[a] if first else block(a, zz, qq)
        return remote(
            src, block(a, zz, qq), c_send.at[a, zz * RING + qq], c_recv.at[a, zz * RING + qq], z, q, 1 - c
        )

    def start():
        for a in range(count):
            own(a).start()
            for way in range(2):
                @pl.when(z < line - 1 if way == 0 else z > 0)
                def _():
                    z_copy(a, way, 0, True).start()
            for axis in range(2):
                xy_copy(a, axis, z, True).start()
            c_copy(a, z, q, True).start()

    def arrived(a, zz):
        for axis in range(2):
            xy_copy(a, axis, zz, False).start()
        c_copy(a, zz, q, False).start()

    def passed_on(a, zz):
        for axis in range(2):
            start, width = halves(a)[axis]
            got = block(a, zz, beside[axis])
            remote(got, got, xy_send.at[axis, a, zz], xy_recv.at[axis, a, zz], z, beside[axis], c).wait_recv()
            if width:
                d_copy(a, axis, zz).start()
            c_copy(a, zz, beside[axis], False).start()

    def finished(a, zz):
        for axis in range(2):
            start, width = halves(a)[axis]
            if width:
                part = outs[a].at[slot(zz, corner), :, pl.ds(start, width)]
                remote(part, part, d_send.at[axis, a, zz], d_recv.at[axis, a, zz], z, beside[1 - axis], c).wait_recv()
        c_copy(a, zz, corner, False).start()

    def both_ways(g, work):
        @pl.when(z - g >= 0)
        def _():
            work(z - g)

        @pl.when(jnp.logical_and(z + g <= line - 1, g > 0))
        def _():
            work(z + g)

    def along(g):
        for a in range(count):
            @pl.when(z - g >= 0)
            def _():
                got = block(a, z - g, q)
                remote(got, got, z_send.at[0, a, g - 1], z_recv.at[0, a, g - 1], z, q, 1 - c).wait_recv()

                @pl.when(z < line - 1)
                def _():
                    z_copy(a, 0, g, False).start()

                arrived(a, z - g)

            @pl.when(z + g <= line - 1)
            def _():
                got = block(a, z + g, q)
                remote(got, got, z_send.at[1, a, g - 1], z_recv.at[1, a, g - 1], z, q, 1 - c).wait_recv()

                @pl.when(z > 0)
                def _():
                    z_copy(a, 1, g, False).start()

                arrived(a, z + g)

    def around(g):
        for a in range(count):
            both_ways(g, partial(passed_on, a))

    def home(g):
        for a in range(count):
            both_ways(g, partial(finished, a))

    def drain(zz, unused):
        for a in range(count):
            for axis in range(2):
                xy_copy(a, axis, zz, False).wait_send()
                if halves(a)[axis][1]:
                    d_copy(a, axis, zz).wait_send()
            for qq in range(RING):
                c_copy(a, zz, qq, False).wait_send()
                got = outs[a].at[(zz * RING + qq) * 2 + 1 - c]
                remote(
                    got, got, c_send.at[a, zz * RING + qq], c_recv.at[a, zz * RING + qq], z, q, 1 - c
                ).wait_recv()

            @pl.when(jnp.logical_and(z < line - 1, zz <= z))
            def _():
                z_copy(a, 0, z - zz, False).wait_send()

            @pl.when(jnp.logical_and(z > 0, zz >= z))
            def _():
                z_copy(a, 1, zz - z, False).wait_send()
        return unused

    def end():
        for a in range(count):
            own(a).wait()
        lax.fori_loop(0, line, drain, 0)

    return SimpleNamespace(start=start, along=along, around=around, home=home, end=end)


def gather_sems(line, count):
    dma = pltpu.SemaphoreType.DMA
    return [
        dma((count,)),
        *(dma((2, count, line)) for k in range(6)),
        dma((count, line * RING)),
        dma((count, line * RING)),
    ]


def group_of(zz):
    return pl.ds(zz * RING, RING)


def flat_gather_stages(line, ins, outs, sems):
    count = len(ins)
    own_sem, xy_send, xy_recv, d_send, d_recv, z_send, z_recv, c_send, c_recv = sems
    z, q, c = place()
    beside = (across(q, 1), across(q, 2))
    corner = across(across(q, 1), 2)

    def remote(src, dst, send, recv, zz, qq, cc):
        return pltpu.make_async_remote_copy(
            src_ref=src, dst_ref=dst, send_sem=send, recv_sem=recv,
            device_id={"dp": zz * RING + qq, "pair": cc}, device_id_type=MESH,
        )

    def block(a, qq):
        return outs[a].at[z * RING + qq, c]

    def halves(a):
        width = ins[a].shape[-1]
        return (0, width // 2), (width // 2, width // 2)

    def own(a):
        return pltpu.make_async_copy(ins[a], block(a, q), own_sem.at[a])

    def xy_copy(a, axis):
        return remote(ins[a], block(a, q), xy_send.at[axis, a], xy_recv.at[axis, a], z, beside[axis], c)

    def xy_got(a, axis):
        got = block(a, beside[axis])
        return remote(got, got, xy_send.at[axis, a], xy_recv.at[axis, a], z, beside[axis], c)

    def d_copy(a, axis, qq):
        start, width = halves(a)[axis]
        part = outs[a].at[z * RING + qq, c, :, pl.ds(start, width)]
        return remote(part, part, d_send.at[axis, a], d_recv.at[axis, a], z, beside[1 - axis], c)

    def z_copy(a, way, zz, target):
        part = outs[a].at[group_of(zz), c]
        return remote(part, part, z_send.at[way, a, zz], z_recv.at[way, a, zz], target, q, c)

    def c_copy(a, zz, cc):
        part = outs[a].at[group_of(zz), cc]
        return remote(part, part, c_send.at[a, zz], c_recv.at[a, zz], z, q, 1 - c)

    def ahead(way):
        return z < line - 1 if way == 0 else z > 0

    def start():
        for a in range(count):
            own(a).start()
            for axis in range(2):
                xy_copy(a, axis).start()

    def around():
        for a in range(count):
            for axis in range(2):
                xy_got(a, axis).wait_recv()
                d_copy(a, axis, beside[axis]).start()

    def home():
        for a in range(count):
            own(a).wait()
            for axis in range(2):
                d_copy(a, axis, corner).wait_recv()
            for way in range(2):
                @pl.when(ahead(way))
                def _():
                    z_copy(a, way, z, z + 1 - 2 * way).start()
            c_copy(a, z, c).start()

    def along(g):
        for a in range(count):
            for way in range(2):
                zz = z - g if way == 0 else z + g

                @pl.when(zz >= 0 if way == 0 else zz <= line - 1)
                def _():
                    z_copy(a, way, zz, z - 1 + 2 * way).wait_recv()

                    @pl.when(ahead(way))
                    def _():
                        z_copy(a, way, zz, z + 1 - 2 * way).start()

                    c_copy(a, zz, c).start()

    def end():
        for a in range(count):
            for axis in range(2):
                xy_copy(a, axis).wait_send()
                d_copy(a, axis, beside[axis]).wait_send()

            def drain(zz, unused):
                c_copy(a, zz, c).wait_send()
                c_copy(a, zz, 1 - c).wait_recv()
                for way in range(2):
                    @pl.when(jnp.logical_and(ahead(way), zz <= z if way == 0 else zz >= z))
                    def _():
                        z_copy(a, way, zz, z + 1 - 2 * way).wait_send()
                return unused

            lax.fori_loop(0, line, drain, 0)

    return SimpleNamespace(start=start, around=around, home=home, along=along, end=end)


def flat_gather_sems(line, count):
    dma = pltpu.SemaphoreType.DMA
    return [
        dma((count,)),
        *(dma((2, count)) for k in range(4)),
        *(dma((2, count, line)) for k in range(2)),
        *(dma((count, line)) for k in range(2)),
    ]


def gather_kernel(line, count, flat, *refs):
    both = count + flat
    ins, outs, sems = refs[:both], refs[both : 2 * both], refs[2 * both :]
    stages = gather_stages(line, ins[:count], outs[:count], sems[:9])
    plane = flat_gather_stages(line, ins[count:], outs[count:], sems[9:])
    greet(line)
    plane.start()
    stages.start()
    plane.around()
    plane.home()

    def generation(g, unused):
        @pl.when(jnp.logical_and(g >= 2, g <= line))
        def _():
            plane.along(g - 1)

        @pl.when(g <= line - 1)
        def _():
            stages.along(g)

        @pl.when(g <= line)
        def _():
            stages.around(g - 1)

        @pl.when(g >= 2)
        def _():
            stages.home(g - 2)

        return unused

    lax.fori_loop(1, line + 2, generation, 0)
    stages.end()
    plane.end()


def gather_all(shards, flat_shards, collective_id):
    dp = lax.axis_size("dp")
    line = dp // RING
    count, flat = len(shards), len(flat_shards)
    wholes = pl.pallas_call(
        partial(gather_kernel, line, count, flat),
        in_specs=[pl.BlockSpec(memory_space=pl.ANY)] * (count + flat),
        out_specs=[pl.BlockSpec(memory_space=pl.ANY)] * (count + flat),
        out_shape=[
            *(jax.ShapeDtypeStruct((2 * dp, *shard.shape), shard.dtype) for shard in shards),
            *(jax.ShapeDtypeStruct((dp, 2, *shard.shape), shard.dtype) for shard in flat_shards),
        ],
        scratch_shapes=[*gather_sems(line, count), *flat_gather_sems(line, flat)],
        compiler_params=pltpu.CompilerParams(collective_id=collective_id, has_side_effects=True),
        name="gather_all",
    )(*shards, *flat_shards)
    return [whole.reshape(2 * dp, *whole.shape[-2:]) for whole in wholes]


def scatter_stages(line, ins, outs, scratch):
    count = len(ins)
    groups = [scratch[k * count : (k + 1) * count] for k in range(5)]
    mine, beside_sum, half_in, full_in, line_in = groups
    (own_sem, c_send, c_recv, d_send, d_recv, xy_send, xy_recv, z_send, z_recv) = scratch[5 * count :]
    z, q, c = place()
    beside = (across(q, 1), across(q, 2))
    corner = across(across(q, 1), 2)

    def remote(src, dst, send, recv, zz, qq, cc):
        return pltpu.make_async_remote_copy(
            src_ref=src, dst_ref=dst, send_sem=send, recv_sem=recv,
            device_id={"dp": zz * RING + qq, "pair": cc}, device_id_type=MESH,
        )

    def halves(a):
        width = outs[a].shape[-1]
        cut = width // 2 if width % 256 == 0 else width
        return (0, cut), (cut, width - cut)

    def wide(value):
        return value.astype(jnp.float32)

    def group(zz):
        return pl.ds(zz * RING, RING)

    def own(a, zz):
        return pltpu.make_async_copy(ins[a].at[group(zz), c], mine[a].at[group(zz)], own_sem.at[a, zz])

    def c_copy(a, zz):
        return remote(
            ins[a].at[group(zz), 1 - c], beside_sum[a].at[group(zz)], c_send.at[a, zz], c_recv.at[a, zz], z, q, 1 - c
        )

    def d_copy(a, axis, zz):
        start, width = halves(a)[axis]
        return remote(
            mine[a].at[zz * RING + corner, :, pl.ds(start, width)],
            half_in[a].at[zz, :, pl.ds(start, width)],
            d_send.at[axis, a, zz], d_recv.at[axis, a, zz], z, beside[axis], c,
        )

    def xy_copy(a, axis, zz):
        return remote(
            mine[a].at[zz * RING + beside[axis]], full_in[a].at[axis, zz],
            xy_send.at[axis, a, zz], xy_recv.at[axis, a, zz], z, beside[axis], c,
        )

    def z_copy(a, way, zz):
        return remote(
            mine[a].at[zz * RING + q], line_in[a].at[way, zz],
            z_send.at[way, a, zz], z_recv.at[way, a, zz], z + 1 if way == 0 else z - 1, q, c,
        )

    def both_ways(g, work):
        @pl.when(z - g >= 0)
        def _():
            work(z - g)

        @pl.when(jnp.logical_and(z + g <= line - 1, g > 0))
        def _():
            work(z + g)

    def begin(zz):
        for a in range(count):
            c_copy(a, zz).start()
            own(a, zz).start()

    def first(zz):
        for a in range(count):
            own(a, zz).wait()
            c_copy(a, zz).wait_recv()

            def one(qq, unused):
                k = zz * RING + qq
                mine[a][k] = mine[a][k] + beside_sum[a][k]
                return unused

            lax.fori_loop(0, RING, one, 0)
            for axis in range(2):
                if halves(a)[axis][1]:
                    d_copy(a, axis, zz).start()

    def second(zz):
        for a in range(count):
            for axis in range(2):
                start, width = halves(a)[axis]
                k = zz * RING + beside[1 - axis]
                if width:
                    d_copy(a, axis, zz).wait_recv()
                    mine[a][k, :, start : start + width] = (
                        mine[a][k, :, start : start + width] + half_in[a][zz, :, start : start + width]
                    )
                xy_copy(a, 1 - axis, zz).start()

    def third(zz):
        for a in range(count):
            k = zz * RING + q
            for axis in range(2):
                xy_copy(a, axis, zz).wait_recv()
            mine[a][k] = (
                wide(mine[a][k]) + wide(full_in[a][0, zz]) + wide(full_in[a][1, zz])
            ).astype(mine[a].dtype)
            for way in range(2):
                @pl.when(zz > z if way == 0 else zz < z)
                def _():
                    @pl.when(z > 0 if way == 0 else z < line - 1)
                    def _():
                        z_copy(a, way, zz).wait_recv()
                        mine[a][k] = mine[a][k] + line_in[a][way, zz]

                    z_copy(a, way, zz).start()

            @pl.when(zz == z)
            def _():
                outs[a][...] = wide(mine[a][k])
                for way in range(2):
                    @pl.when(z > 0 if way == 0 else z < line - 1)
                    def _():
                        z_copy(a, way, zz).wait_recv()
                        outs[a][...] += wide(line_in[a][way, zz])

    def start():
        def begin_all(step, unused):
            both_ways(line - 1 - step, begin)
            return unused

        lax.fori_loop(0, line, begin_all, 0)

    def drain(zz, unused):
        for a in range(count):
            for axis in range(2):
                xy_copy(a, axis, zz).wait_send()
                if halves(a)[axis][1]:
                    d_copy(a, axis, zz).wait_send()
            c_copy(a, zz).wait_send()
            for way in range(2):
                @pl.when(zz > z if way == 0 else zz < z)
                def _():
                    z_copy(a, way, zz).wait_send()
        return unused

    def end():
        lax.fori_loop(0, line, drain, 0)

    return SimpleNamespace(
        start=start,
        first=lambda step: both_ways(line - 1 - step, first),
        second=lambda step: both_ways(line - 1 - step, second),
        third=lambda step: both_ways(line - 1 - step, third),
        end=end,
    )


def scatter_scratch(line, blocks):
    dma = pltpu.SemaphoreType.DMA
    count = len(blocks)
    return [
        *(pltpu.VMEM((line * RING, *shape), kind) for shape, kind in blocks),
        *(pltpu.VMEM((line * RING, *shape), kind) for shape, kind in blocks),
        *(pltpu.VMEM((line, *shape), kind) for shape, kind in blocks),
        *(pltpu.VMEM((2, line, *shape), kind) for shape, kind in blocks),
        *(pltpu.VMEM((2, line, *shape), kind) for shape, kind in blocks),
        *(dma((count, line)) for k in range(3)),
        *(dma((2, count, line)) for k in range(6)),
    ]


def flat_scatter_stages(line, ins, outs, scratch):
    count = len(ins)
    mine, beside_sum, line_in, half_in, full_in = (scratch[k * count : (k + 1) * count] for k in range(5))
    own_sem, c_send, c_recv, z_send, z_recv, d_send, d_recv, xy_send, xy_recv = scratch[5 * count :]
    z, q, c = place()
    beside = (across(q, 1), across(q, 2))
    corner = across(across(q, 1), 2)

    def remote(src, dst, send, recv, zz, qq, cc):
        return pltpu.make_async_remote_copy(
            src_ref=src, dst_ref=dst, send_sem=send, recv_sem=recv,
            device_id={"dp": zz * RING + qq, "pair": cc}, device_id_type=MESH,
        )

    def halves(a):
        width = outs[a].shape[-1]
        cut = width // 2 if width % 256 == 0 else width
        return (0, cut), (cut, width - cut)

    def own(a, zz):
        return pltpu.make_async_copy(ins[a].at[group_of(zz), c], mine[a].at[group_of(zz)], own_sem.at[a, zz])

    def c_copy(a, zz):
        return remote(
            ins[a].at[group_of(zz), 1 - c], beside_sum[a].at[group_of(zz)], c_send.at[a, zz], c_recv.at[a, zz],
            z, q, 1 - c,
        )

    def z_copy(a, way, zz):
        return remote(
            mine[a].at[group_of(zz)], line_in[a].at[way, group_of(zz)], z_send.at[way, a, zz],
            z_recv.at[way, a, zz], z + 1 - 2 * way, q, c,
        )

    def d_copy(a, axis):
        start, width = halves(a)[axis]
        return remote(
            mine[a].at[z * RING + corner, :, pl.ds(start, width)], half_in[a].at[:, pl.ds(start, width)],
            d_send.at[axis, a], d_recv.at[axis, a], z, beside[axis], c,
        )

    def xy_copy(a, axis):
        return remote(
            mine[a].at[z * RING + beside[axis]], full_in[a].at[axis], xy_send.at[axis, a], xy_recv.at[axis, a],
            z, beside[axis], c,
        )

    def behind(way):
        return z > 0 if way == 0 else z < line - 1

    def both_ways(g, work):
        @pl.when(z - g >= 0)
        def _():
            work(z - g)

        @pl.when(jnp.logical_and(z + g <= line - 1, g > 0))
        def _():
            work(z + g)

    def add(a, zz, part):
        def one(qq, unused):
            k = zz * RING + qq
            mine[a][k] = mine[a][k] + part[k]
            return unused

        lax.fori_loop(0, RING, one, 0)

    def begin(zz):
        for a in range(count):
            c_copy(a, zz).start()
            own(a, zz).start()

    def first(zz):
        for a in range(count):
            own(a, zz).wait()
            c_copy(a, zz).wait_recv()
            add(a, zz, beside_sum[a])
            for way in range(2):
                @pl.when(jnp.logical_and(behind(way), zz >= z if way == 0 else zz <= z))
                def _():
                    z_copy(a, way, zz).wait_recv()
                    add(a, zz, line_in[a].at[way])

                @pl.when(zz > z if way == 0 else zz < z)
                def _():
                    z_copy(a, way, zz).start()

            @pl.when(zz == z)
            def _():
                for axis in range(2):
                    if halves(a)[axis][1]:
                        d_copy(a, axis).start()

    def second():
        for a in range(count):
            for axis in range(2):
                start, width = halves(a)[axis]
                k = z * RING + beside[1 - axis]
                if width:
                    d_copy(a, axis).wait_recv()
                    mine[a][k, :, start : start + width] = (
                        mine[a][k, :, start : start + width] + half_in[a][:, start : start + width]
                    )
                xy_copy(a, 1 - axis).start()

    def third():
        for a in range(count):
            for axis in range(2):
                xy_copy(a, axis).wait_recv()
            outs[a][...] = sum(
                part.astype(jnp.float32) for part in (mine[a][z * RING + q], full_in[a][0], full_in[a][1])
            )

    def start():
        lax.fori_loop(0, line, lambda step, unused: (both_ways(line - 1 - step, begin), unused)[1], 0)

    def end():
        for a in range(count):
            for axis in range(2):
                if halves(a)[axis][1]:
                    d_copy(a, axis).wait_send()
                xy_copy(a, axis).wait_send()

            def drain(zz, unused):
                c_copy(a, zz).wait_send()
                for way in range(2):
                    @pl.when(zz > z if way == 0 else zz < z)
                    def _():
                        z_copy(a, way, zz).wait_send()
                return unused

            lax.fori_loop(0, line, drain, 0)

    return SimpleNamespace(
        start=start, first=lambda step: both_ways(line - 1 - step, first), second=second, third=third, end=end
    )


def flat_scatter_scratch(line, blocks):
    dma = pltpu.SemaphoreType.DMA
    count = len(blocks)
    return [
        *(pltpu.VMEM((line * RING, *shape), kind) for shape, kind in blocks),
        *(pltpu.VMEM((line * RING, *shape), kind) for shape, kind in blocks),
        *(pltpu.VMEM((2, line * RING, *shape), kind) for shape, kind in blocks),
        *(pltpu.VMEM(shape, kind) for shape, kind in blocks),
        *(pltpu.VMEM((2, *shape), kind) for shape, kind in blocks),
        *(dma((count, line)) for k in range(3)),
        *(dma((2, count, line)) for k in range(2)),
        *(dma((2, count)) for k in range(4)),
    ]


def peers(line):
    z, q, c = place()
    cell = q * 2 + c
    near = RING * 2

    def near_place(k):
        other = lax.rem(cell + k, near)
        return other, {"dp": z * RING + other // 2, "pair": lax.rem(other, 2)}

    def far_place(k):
        other = lax.rem(z + k, line)
        return other, {"dp": other * RING + q, "pair": c}

    def each(places, stop, work):
        def one(k, unused):
            work(*places(k))
            return unused

        lax.fori_loop(1, stop, one, 0)

    return partial(each, near_place, near), partial(each, far_place, line)


def greet_peers(line):
    barrier = pltpu.get_barrier_semaphore()
    for each in peers(line):
        each(
            lambda other, device: pl.semaphore_signal(barrier, inc=1, device_id=device, device_id_type=MESH)
        )
    pl.semaphore_wait(barrier, 2 * RING + line - 2)


def exchange_stages(line, combine, value_ref, total_ref, scratch):
    near_ref, part_ref, far_ref, n_send, n_recv, f_send, f_recv = scratch
    z, q, c = place()
    cell = q * 2 + c
    each_near, each_far = peers(line)

    def near_copy(other, device, source):
        return pltpu.make_async_remote_copy(
            src_ref=value_ref, dst_ref=near_ref.at[source], send_sem=n_send.at[other], recv_sem=n_recv.at[source],
            device_id=device, device_id_type=MESH,
        )

    def far_copy(other, device, source):
        return pltpu.make_async_remote_copy(
            src_ref=part_ref, dst_ref=far_ref.at[source], send_sem=f_send.at[other], recv_sem=f_recv.at[source],
            device_id=device, device_id_type=MESH,
        )

    def near():
        each_near(lambda other, device: near_copy(other, device, cell).start())
        near_ref[cell] = value_ref[...]

    def far():
        each_near(lambda other, device: near_copy(other, device, other).wait_recv())
        part_ref[...] = combine(near_ref, 2 * RING, 1)
        each_far(lambda other, device: far_copy(other, device, z).start())
        far_ref[z] = part_ref[...]

    def total():
        each_far(lambda other, device: far_copy(other, device, other).wait_recv())
        total_ref[...] = combine(far_ref, line, 2 * RING)

    def end():
        each_near(lambda other, device: near_copy(other, device, cell).wait_send())
        each_far(lambda other, device: far_copy(other, device, z).wait_send())

    return SimpleNamespace(near=near, far=far, total=total, end=end)


def exchange_scratch(line, shape):
    dma = pltpu.SemaphoreType.DMA
    near = 2 * RING
    return [
        pltpu.VMEM((near, *shape), jnp.float32),
        pltpu.VMEM(shape, jnp.float32),
        pltpu.VMEM((line, *shape), jnp.float32),
        dma((near,)),
        dma((near,)),
        dma((line,)),
        dma((line,)),
    ]


def exchange_kernel(line, combine, value_ref, total_ref, *scratch):
    stages = exchange_stages(line, combine, value_ref, total_ref, scratch)
    greet_peers(line)
    stages.near()
    stages.far()
    stages.total()
    stages.end()


def add_up(parts, count, weight):
    return lax.fori_loop(1, count, lambda k, total: total + parts[k], parts[0])


def pool_statistics(rows, parts, count, weight):
    mean = lax.fori_loop(1, count, lambda k, total: total + parts[k, 0], parts[0, 0]) / count

    def squares(k, total):
        offset = parts[k, 0] - mean
        return total + parts[k, 1] + (rows * weight) * (offset * offset)

    return jnp.stack([mean, lax.fori_loop(0, count, squares, jnp.zeros_like(mean))])


def exchange(value, combine, collective_id, name):
    line = lax.axis_size("dp") // RING
    vmem = pl.BlockSpec(memory_space=pltpu.VMEM)
    return pl.pallas_call(
        partial(exchange_kernel, line, combine),
        in_specs=[vmem],
        out_specs=vmem,
        out_shape=jax.ShapeDtypeStruct(value.shape, value.dtype),
        scratch_shapes=exchange_scratch(line, value.shape),
        compiler_params=pltpu.CompilerParams(collective_id=collective_id, has_side_effects=True),
        name=name,
    )(value)


KINDS = 10


def source_of(column):
    stream = column // 5
    return 2 * stream + (column - 5 * stream) // 3


def once(shape):
    return pl.BlockSpec(shape, lambda i: (0,) * len(shape), pipeline_mode=pl.Buffered(1))


def at_steps(schedule):
    step = pl.program_id(0)
    for when, work in schedule:
        @pl.when(step == when)
        def _():
            for one in work:
                one()


batch_epsilon = 1e-05


def column_at_step(step):
    turn = jnp.clip(step - 1, 0, KINDS - 1)
    return jnp.where(turn >= 7, turn - 2, jnp.where(turn >= 5, turn + 3, turn))


VECTORS = 9
CHUNKS = 4


def unpack(packed_ref, vectors_ref, bias_ref, linear_ref, planar_ref):
    devices = packed_ref.shape[0]
    bias_rows = REL_B // devices

    def row(k):
        return packed_ref[:, k, :].astype(jnp.bfloat16)

    def lined_up(k, share, first):
        lane = lax.broadcasted_iota(jnp.int32, (128, MODEL_WIDTH), 1)
        spread = (lax.broadcasted_iota(jnp.int32, (128, MODEL_WIDTH), 0) == lax.rem(lane, share)).astype(jnp.bfloat16)
        owner = lax.broadcasted_iota(jnp.int32, (devices, MODEL_WIDTH), 1) // share + first
        mine = lax.broadcasted_iota(jnp.int32, (devices, MODEL_WIDTH), 0) == owner
        whole = dot_nn(row(k), spread)
        return jnp.sum(jnp.where(mine, whole, jnp.zeros_like(whole)), axis=0, keepdims=True)

    def table(first, width, shift):
        bucket = jnp.clip(lax.broadcasted_iota(jnp.int32, (devices, width), 1) - shift, 0, REL_B - 1)
        start = lax.broadcasted_iota(jnp.int32, (devices, width), 0) * bias_rows
        total = None
        for k in range(bias_rows):
            part = dot_tn(row(first + k), (bucket == start + k).astype(jnp.bfloat16))
            total = part if total is None else total + part
        return total

    vectors_ref[...] = jnp.zeros_like(vectors_ref)
    for k in range(VECTORS):
        vectors_ref[k : k + 1, :] = lined_up(2 * bias_rows + k, MODEL_WIDTH // devices, 0)
    share = CHUNKS * MODEL_WIDTH // devices
    for k in range(CHUNKS):
        bias_ref[k] = lined_up(2 * bias_rows + VECTORS, share, k * (MODEL_WIDTH // share))
    linear = table(0, 2 * PAGE_TOKENS, PAGE_TOKENS - 1 - REL_B // 2)
    planar = table(bias_rows, SP_B, 0)
    for head in range(HEADS):
        linear_ref[head] = linear[head : head + 1, :]
        planar_ref[head] = planar[head : head + 1, :]


def forward_kernel(line, count, token_total, *refs):
    (
        features_ref, backbone_ref, table_ref, text_ref, hits_ref, packed_ref, weight_ref, rows_ref, cols_ref,
    ) = refs[:9]
    ins = refs[9 : 9 + count]
    (
        proj_ref, merged_ref, probs_ref, lefts_ref, start_ref, normal_ref, scale_ref, vectors_ref, bias_ref,
    ) = refs[9 + count : 18 + count]
    outs = refs[18 + count : 18 + 2 * count]
    box_ref, conv_ref, local_ref, pooled_ref, linear_ref, planar_ref = refs[18 + 2 * count : 24 + 2 * count]
    rest = refs[24 + 2 * count :]
    rows = features_ref.shape[0]
    sums = exchange_stages(line, partial(pool_statistics, float(rows)), local_ref, pooled_ref, rest[:7])
    stages = gather_stages(line, ins, outs, rest[7:])
    step = pl.program_id(0)

    def vector(k):
        return vectors_ref[k : k + 1, :]

    def hit_rows(stream):
        return jnp.broadcast_to(hits_ref[:, stream : stream + 1] == 1, (rows, MODEL_WIDTH))

    @pl.when(step == 0)
    def _():
        greet_peers(line)
        conv = dot_nn(features_ref[...], backbone_ref[...])
        mean = jnp.mean(conv, axis=0, keepdims=True)
        center = conv - mean
        conv_ref[...] = conv
        local_ref[0] = mean
        local_ref[1] = jnp.sum(center * center, axis=0, keepdims=True)
        sums.near()
        stages.start()
        unpack(packed_ref, vectors_ref, bias_ref, linear_ref, planar_ref)
        make_boxes(rows_ref, cols_ref, box_ref)
        text_start = jnp.where(hit_rows(0), vector(2), text_ref[...].astype(jnp.float32))
        start_ref[...] = text_start
        lefts_ref[0] = text_start.astype(jnp.bfloat16)
        coords = lax.broadcasted_iota(jnp.int32, (rows, COORDS), 1)
        for stream in range(2):
            space = None
            for axis in range(2):
                place = 2 * stream + axis
                hit = (coords == cols_ref[:, place : place + 1]).astype(jnp.bfloat16)
                part = dot_nn(hit, table_ref[:, axis * MODEL_WIDTH : (axis + 1) * MODEL_WIDTH])
                space = part if space is None else space + part
            lefts_ref[2 * stream + 1] = space.astype(jnp.bfloat16)
        sums.far()

    @pl.when(jnp.logical_and(step >= 1, step <= KINDS))
    def _():
        column = column_at_step(step)
        columns = pl.ds(pl.multiple_of(column * MODEL_WIDTH, MODEL_WIDTH), MODEL_WIDTH)
        proj_ref[:, columns] = dot_nn(lefts_ref[source_of(column)], weight_ref[...]).astype(jnp.bfloat16)

    @pl.when(step == 7)
    def _():
        sums.total()
        inverse = lax.rsqrt(pooled_ref[1] / token_total + batch_epsilon)
        normal = (conv_ref[...] - pooled_ref[0]) * inverse
        normal_ref[...] = normal
        scale_ref[...] = jnp.broadcast_to(vector(0) * inverse, scale_ref.shape)
        region_start = jnp.where(hit_rows(1), vector(3), normal * vector(0) + vector(1))
        start_ref[...] += region_start
        lefts_ref[2] = region_start.astype(jnp.bfloat16)

    @pl.when(step > KINDS)
    def _():
        attend_pair(step - 1 - KINDS, proj_ref, linear_ref, planar_ref, box_ref, merged_ref, probs_ref)

    def along(k):
        return lambda: spread(line, 3, k, 1, stages.along)

    def around(k):
        return lambda: spread(line, 4, k, 0, stages.around)

    def home(k):
        return lambda: spread(line, 4, k, 0, stages.home)

    at_steps(
        [
            (3, [along(0), around(0)]),
            (10, [along(1)]),
            (11, [around(1)]),
            (13, [along(2), home(0)]),
            (15, [around(2), home(1)]),
            (16, [around(3), home(2), home(3), sums.end, stages.end]),
        ]
    )


def forward_layer(
    features, backbone, table, text, hits, packed, weights, anchor_rows, anchor_cols, shards, token_total,
    collective_id,
):
    dp = lax.axis_size("dp")
    line = dp // RING
    count = len(shards)
    anywhere = pl.BlockSpec(memory_space=pl.ANY)
    width = weights.shape[1]
    page = (PAGE_TOKENS, MODEL_WIDTH)
    f32, bf16 = jnp.float32, jnp.bfloat16

    def pair_at(i):
        return jnp.maximum(i - 1 - KINDS, 0)

    def whole(shape):
        return pl.BlockSpec(shape, lambda i: (0,) * len(shape))

    outs = [
        ((PAGE_TOKENS, width), bf16, whole((PAGE_TOKENS, width))),
        (page, bf16, pl.BlockSpec((PAGE_TOKENS, LANES), lambda i: (0, pair_at(i)))),
        (
            (2, HEADS, PAGE_TOKENS, PAGE_TOKENS), f32,
            pl.BlockSpec((2, 2, PAGE_TOKENS, PAGE_TOKENS), lambda i: (0, pair_at(i), 0, 0)),
        ),
        ((4, *page), bf16, whole((4, *page))),
        (page, f32, whole(page)),
        (page, f32, whole(page)),
        ((8, MODEL_WIDTH), f32, whole((8, MODEL_WIDTH))),
        ((16, MODEL_WIDTH), f32, whole((16, MODEL_WIDTH))),
        ((CHUNKS, 1, MODEL_WIDTH), f32, whole((CHUNKS, 1, MODEL_WIDTH))),
        *(((2 * dp, *shard.shape), shard.dtype, anywhere) for shard in shards),
    ]
    pool = (2, 1, MODEL_WIDTH)
    return pl.pallas_call(
        partial(forward_kernel, line, count, float(token_total)),
        grid=(1 + KINDS + PAIRS,),
        in_specs=[
            once(features.shape),
            once(backbone.shape),
            once(table.shape),
            once(text.shape),
            once(hits.shape),
            once(packed.shape),
            pl.BlockSpec((MODEL_WIDTH, MODEL_WIDTH), lambda i: (0, column_at_step(i))),
            once(anchor_rows.shape),
            once(anchor_cols.shape),
            *[anywhere] * count,
        ],
        out_specs=[spec for shape, kind, spec in outs],
        out_shape=[jax.ShapeDtypeStruct(shape, kind) for shape, kind, spec in outs],
        scratch_shapes=[
            pltpu.VMEM((2, PAGE_TOKENS, PAGE_TOKENS), jnp.int32),
            pltpu.VMEM(page, f32),
            pltpu.VMEM(pool, f32),
            pltpu.VMEM(pool, f32),
            pltpu.VMEM((HEADS, 1, 2 * PAGE_TOKENS), f32),
            pltpu.VMEM((HEADS, 1, SP_B), f32),
            *exchange_scratch(line, pool),
            *gather_sems(line, count),
        ],
        compiler_params=pltpu.CompilerParams(
            collective_id=collective_id, has_side_effects=True, vmem_limit_bytes=62 << 20
        ),
        name="forward_layer",
    )(
        features, backbone, table, text, hits, packed, weights, anchor_rows, anchor_cols, *shards,
    )


TABLE_STEP = PAIRS + KINDS


def backward_kernel(line, count, *refs):
    (
        proj_ref, probs_ref, upstream_ref, rows_ref, cols_ref, lefts_ref, weight_ref, mixer_grad_ref, normal_ref,
        hits_ref,
    ) = refs[:10]
    ins = refs[10 : 10 + count]
    (
        linear_ref, planar_ref, weight_grad_ref, table_grad_ref, text_grad_ref, region_grad_ref, sums_ref,
    ) = refs[10 + count : 17 + count]
    outs = refs[17 + count : 17 + 2 * count]
    grad_ref, turned_left_ref, input_grad_ref = refs[17 + 2 * count : 20 + 2 * count]
    helpers = refs[20 + 2 * count : 24 + 2 * count]
    stages = scatter_stages(line, ins, outs, refs[24 + 2 * count :])
    step = pl.program_id(0)

    @pl.when(step == 0)
    def _():
        greet(line)
        stages.start()
        make_places(rows_ref, cols_ref, *helpers)

    def first(k):
        return lambda: spread(line, 4, k, 0, stages.first)

    def second(k):
        return lambda: spread(line, 4, k, 0, stages.second)

    def third(k):
        return lambda: spread(line, 4, k, 0, stages.third)

    slots = {
        1: [first(0)],
        3: [first(1)],
        7: [second(0)],
        8: [first(2)],
        10: [first(3)],
        12: [second(1)],
        17: [third(0)],
        22: [second(2), second(3)],
    }

    def pump(sub):
        at_steps([(slot // 4, work) for slot, work in slots.items() if slot % 4 == sub])

    @pl.when(step < PAIRS)
    def _():
        attend_back_pair(step, pump, proj_ref, probs_ref, upstream_ref, grad_ref, linear_ref, planar_ref, *helpers)

    @pl.when(jnp.logical_and(step >= PAIRS, step < TABLE_STEP))
    def _():
        column = step - PAIRS
        source = source_of(column)
        fresh = jnp.logical_or(column == 0, source != source_of(jnp.maximum(column - 1, 0)))
        grads = grad_ref[:, pl.ds(pl.multiple_of(column * MODEL_WIDTH, MODEL_WIDTH), MODEL_WIDTH)]

        @pl.when(fresh)
        def _():
            turned_left_ref[...] = lefts_ref[source].T

        weight_grad_ref[...] = dot_nn(turned_left_ref[...], grads).astype(jnp.bfloat16)
        back = dot_nt(grads, weight_ref[...])

        @pl.when(fresh)
        def _():
            input_grad_ref[source] = back

        @pl.when(jnp.logical_not(fresh))
        def _():
            input_grad_ref[source] += back

    @pl.when(step >= TABLE_STEP)
    def _():
        axis = step - TABLE_STEP
        coords = lax.broadcasted_iota(jnp.int32, (COORDS, PAGE_TOKENS), 0)
        total = None
        for stream in range(2):
            hit = (coords == rows_ref[pl.ds(2 * stream + axis, 1), :]).astype(jnp.bfloat16)
            part = dot_nn(hit, input_grad_ref[2 * stream + 1].astype(jnp.bfloat16))
            total = part if total is None else total + part
        table_grad_ref[...] = total.astype(jnp.bfloat16)

    @pl.when(step == TABLE_STEP + 1)
    def _():
        mixer_grad = mixer_grad_ref[...]
        sums_ref[...] = jnp.zeros_like(sums_ref)
        for stream, out_ref in enumerate((text_grad_ref, region_grad_ref)):
            grad = mixer_grad + input_grad_ref[2 * stream]
            hit = jnp.broadcast_to(hits_ref[:, stream : stream + 1] == 1, grad.shape)
            zero = jnp.zeros_like(grad)
            kept = jnp.where(hit, zero, grad)
            out_ref[...] = kept
            sums_ref[stream : stream + 1, :] = jnp.sum(jnp.where(hit, grad, zero), axis=0, keepdims=True)
            if stream == 1:
                sums_ref[2:3, :] = jnp.sum(kept, axis=0, keepdims=True)
                sums_ref[3:4, :] = jnp.sum(kept * normal_ref[...], axis=0, keepdims=True)

    at_steps(
        [(PAIRS + 3, [third(1)]), (PAIRS + 8, [third(2)]), (TABLE_STEP + 1, [third(3), stages.end])]
    )


def backward_layer(
    proj, probs, upstream, anchor_rows, anchor_cols, lefts, weights, mixer_grad, normal, hits, grads, collective_id
):
    dp = lax.axis_size("dp")
    line = dp // RING
    count = len(grads)
    blocks = [(grad.shape[1:], grad.dtype) for grad in grads]
    anywhere = pl.BlockSpec(memory_space=pl.ANY)
    page = (PAGE_TOKENS, MODEL_WIDTH)

    def pair_at(i):
        return jnp.minimum(i, PAIRS - 1)

    def column_at(i):
        return jnp.clip(i - PAIRS, 0, KINDS - 1)

    return pl.pallas_call(
        partial(backward_kernel, line, count),
        grid=(TABLE_STEP + 2,),
        in_specs=[
            once(proj.shape),
            pl.BlockSpec((2, 2, PAGE_TOKENS, PAGE_TOKENS), lambda i: (0, pair_at(i), 0, 0)),
            pl.BlockSpec((PAGE_TOKENS, LANES), lambda i: (0, pair_at(i))),
            once(anchor_rows.shape),
            once(anchor_cols.shape),
            once(lefts.shape),
            pl.BlockSpec((MODEL_WIDTH, MODEL_WIDTH), lambda i: (0, column_at(i))),
            once(page),
            once(page),
            once(hits.shape),
            *[anywhere] * count,
        ],
        out_specs=[
            pl.BlockSpec((HEADS, 1, 2 * PAGE_TOKENS), lambda i: (0, 0, 0)),
            pl.BlockSpec((HEADS, 1, SP_B), lambda i: (0, 0, 0)),
            pl.BlockSpec((MODEL_WIDTH, MODEL_WIDTH), lambda i: (0, column_at(i))),
            pl.BlockSpec((COORDS, MODEL_WIDTH), lambda i: (0, jnp.maximum(i - TABLE_STEP, 0))),
            pl.BlockSpec(page, lambda i: (0, 0)),
            pl.BlockSpec(page, lambda i: (0, 0)),
            pl.BlockSpec((8, MODEL_WIDTH), lambda i: (0, 0)),
            *(pl.BlockSpec(shape, lambda i: (0, 0)) for shape, kind in blocks),
        ],
        out_shape=[
            jax.ShapeDtypeStruct((HEADS, 1, 2 * PAGE_TOKENS), jnp.float32),
            jax.ShapeDtypeStruct((HEADS, 1, SP_B), jnp.float32),
            jax.ShapeDtypeStruct(weights.shape, jnp.bfloat16),
            jax.ShapeDtypeStruct((COORDS, 2 * MODEL_WIDTH), jnp.bfloat16),
            jax.ShapeDtypeStruct(page, jnp.float32),
            jax.ShapeDtypeStruct(page, jnp.float32),
            jax.ShapeDtypeStruct((8, MODEL_WIDTH), jnp.float32),
            *(jax.ShapeDtypeStruct(shape, jnp.float32) for shape, kind in blocks),
        ],
        scratch_shapes=[
            pltpu.VMEM(proj.shape, jnp.bfloat16),
            pltpu.VMEM((MODEL_WIDTH, PAGE_TOKENS), jnp.bfloat16),
            pltpu.VMEM((4, *page), jnp.float32),
            pltpu.VMEM((2, 4 * PAGE_TOKENS, SP_B), jnp.bfloat16),
            pltpu.VMEM((2, 128, PAGE_TOKENS), jnp.bfloat16),
            pltpu.VMEM((2, 4, PAGE_TOKENS, PAGE_TOKENS), jnp.bfloat16),
            pltpu.VMEM((PAGE_TOKENS, PAGE_TOKENS), jnp.bfloat16),
            *scatter_scratch(line, blocks),
        ],
        compiler_params=pltpu.CompilerParams(
            collective_id=collective_id, has_side_effects=True, vmem_limit_bytes=63 << 20
        ),
        name="backward_layer",
    )(
        proj, probs, upstream, anchor_rows, anchor_cols, lefts, weights, mixer_grad, normal, hits,
        *(grad.reshape(line * RING, 2, *grad.shape[1:]) for grad in grads),
    )


def last_kernel(line, count, token_total, *refs):
    sums_ref, kept_ref, normal_ref, scale_ref, features_ref, backbone_ref = refs[:6]
    ins = refs[6 : 7 + count]
    feature_grad_ref, total_ref = refs[7 + count : 9 + count]
    outs = refs[9 + count : 11 + 2 * count]
    turned_ref, conv_grad_ref, late_ref = refs[11 + 2 * count : 14 + 2 * count]
    rest = refs[14 + 2 * count :]
    local_ref, *rest = rest
    sums = exchange_stages(line, add_up, local_ref, total_ref, rest[:7])
    stop = 7 + 5 * count + 9
    early = scatter_stages(line, ins[:count], outs[:count], rest[7:stop])
    late = scatter_stages(line, [late_ref], outs[count : count + 1], rest[stop : stop + 14])
    flat = flat_scatter_stages(line, ins[count:], outs[count + 1 :], rest[stop + 14 :])
    share = late_ref.shape[2]

    def first(stages, k):
        spread(line, 4, k, 0, stages.first)

    def second(stages, k):
        spread(line, 4, k, 0, stages.second)

    def third(stages, k):
        spread(line, 4, k, 0, stages.third)

    greet_peers(line)
    local_ref[...] = sums_ref[2:4, :]
    sums.near()
    flat.start()
    early.start()
    sums.far()
    first(flat, 0)
    first(early, 0)
    first(early, 1)
    sums.total()
    conv_grad_ref[...] = (
        scale_ref[0:1, :]
        * (kept_ref[...] - total_ref[0:1, :] / token_total - normal_ref[...] * (total_ref[1:2, :] / token_total))
    ).astype(jnp.bfloat16)
    second(early, 0)
    first(flat, 1)
    first(early, 2)
    first(early, 3)

    def turn(k, unused):
        columns = pl.ds(pl.multiple_of(k * 512, 512), 512)
        turned_ref[columns, :] = features_ref[:, columns].T
        return unused

    lax.fori_loop(0, features_ref.shape[1] // 512, turn, 0)
    width = min(512, 2 * share * line * RING)

    def backbone(k, unused):
        rows = pl.ds(pl.multiple_of(k * width, width), width)
        block = dot_nn(turned_ref[rows, :], conv_grad_ref[...])
        places = width // (2 * share)
        late_ref[pl.ds(k * places, places)] = block.reshape(places, 2, share, MODEL_WIDTH).astype(jnp.bfloat16)
        return unused

    lax.fori_loop(0, features_ref.shape[1] // width, backbone, 0)
    late.start()
    for k in range(4):
        first(late, k)
    first(flat, 2)
    second(early, 1)
    third(early, 0)

    def feature(k, unused):
        columns = pl.ds(pl.multiple_of(k * 512, 512), 512)
        feature_grad_ref[:, columns] = dot_nt(conv_grad_ref[...], backbone_ref[columns, :])
        return unused

    lax.fori_loop(0, features_ref.shape[1] // 512, feature, 0)
    first(flat, 3)
    second(early, 2)
    for k in range(4):
        second(late, k)
    flat.second()
    second(early, 3)
    third(early, 1)
    third(early, 2)
    for k in range(3):
        third(late, k)
    flat.third()
    third(early, 3)
    third(late, 3)
    sums.end()
    early.end()
    late.end()
    flat.end()


def last_layer(
    sums, kept, normal, scale, features, backbone, grads, flat_grad, token_total, collective_id
):
    dp = lax.axis_size("dp")
    line = dp // RING
    count = len(grads)
    blocks = [(grad.shape[1:], grad.dtype) for grad in grads]
    flat = [(flat_grad.shape[1:], flat_grad.dtype)]
    pair = (2, MODEL_WIDTH)
    channels = backbone.shape[0]
    late = [((channels // (2 * dp), MODEL_WIDTH), jnp.bfloat16)]
    anywhere = pl.BlockSpec(memory_space=pl.ANY)
    vmem = pl.BlockSpec(memory_space=pltpu.VMEM)
    return pl.pallas_call(
        partial(last_kernel, line, count, float(token_total)),
        in_specs=[*[vmem] * 6, *[anywhere] * (count + 1)],
        out_specs=[vmem] * (4 + count),
        out_shape=[
            jax.ShapeDtypeStruct(features.shape, jnp.float32),
            jax.ShapeDtypeStruct(pair, jnp.float32),
            *(jax.ShapeDtypeStruct(shape, jnp.float32) for shape, kind in blocks + late + flat),
        ],
        scratch_shapes=[
            pltpu.VMEM((channels, PAGE_TOKENS), jnp.bfloat16),
            pltpu.VMEM(kept.shape, jnp.bfloat16),
            pltpu.VMEM((dp, 2, *late[0][0]), jnp.bfloat16),
            pltpu.VMEM(pair, jnp.float32),
            *exchange_scratch(line, pair),
            *scatter_scratch(line, blocks),
            *scatter_scratch(line, late),
            *flat_scatter_scratch(line, flat),
        ],
        compiler_params=pltpu.CompilerParams(
            collective_id=collective_id, has_side_effects=True, vmem_limit_bytes=63 << 20
        ),
        name="last_layer",
    )(
        sums, kept, normal, scale, features, backbone,
        *(grad.reshape(line * RING, 2, *grad.shape[1:]) for grad in [*grads, flat_grad]),
    )


def finish_kernel(count, share, expand_share, bias_rows, *refs):
    ins = refs[:count]
    small_ref, total_ref = refs[count : count + 2]
    outs = refs[count + 2 : 2 * count + 2]
    small_outs = refs[2 * count + 2 : 2 * count + 14]
    staged = refs[2 * count + 14 : 2 * count + 26]
    sems, small_sems = refs[2 * count + 26 :]
    copies = [pltpu.make_async_copy(ins[k], outs[k], sems.at[k]) for k in range(count)]
    for copy in copies:
        copy.start()
    staged[0][...] = small_ref[:bias_rows, :HEADS]
    staged[1][...] = small_ref[bias_rows : 2 * bias_rows, :HEADS]
    for k in range(7):
        staged[2 + k][...] = small_ref[2 * bias_rows + k : 2 * bias_rows + k + 1, :share]
    staged[9][...] = small_ref[2 * bias_rows + 7 : 2 * bias_rows + 8, :expand_share]
    owner = (lax.axis_index("dp") * 2 + lax.axis_index("pair")) * share
    chosen = lax.broadcasted_iota(jnp.int32, (MODEL_WIDTH, 128), 0) == (
        lax.broadcasted_iota(jnp.int32, (MODEL_WIDTH, 128), 1) + owner
    )
    owned = lax.dot_general(
        total_ref[...], chosen.astype(jnp.float32), (((1,), (0,)), ((), ())),
        precision=lax.Precision.HIGHEST, preferred_element_type=jnp.float32,
    )
    for k in range(2):
        staged[10 + k][...] = owned[k : k + 1, :share]
    small_copies = [pltpu.make_async_copy(staged[k], small_outs[k], small_sems.at[k]) for k in range(12)]
    for copy in small_copies:
        copy.start()
    for copy in copies + small_copies:
        copy.wait()


def finish(arrays, small, totals, share, expand_share, bias_rows):
    count = len(arrays)
    anywhere = pl.BlockSpec(memory_space=pl.ANY)
    vmem = pl.BlockSpec(memory_space=pltpu.VMEM)
    shapes = [(bias_rows, HEADS)] * 2 + [(1, share)] * 7 + [(1, expand_share)] + [(1, share)] * 2
    return pl.pallas_call(
        partial(finish_kernel, count, share, expand_share, bias_rows),
        in_specs=[vmem] * (count + 2),
        out_specs=[anywhere] * (count + 12),
        out_shape=[
            *(jax.ShapeDtypeStruct(array.shape, array.dtype) for array in arrays),
            *(jax.ShapeDtypeStruct(shape, jnp.float32) for shape in shapes),
        ],
        scratch_shapes=[
            *(pltpu.VMEM(shape, jnp.float32) for shape in shapes),
            pltpu.SemaphoreType.DMA((count,)),
            pltpu.SemaphoreType.DMA((12,)),
        ],
        name="finish",
    )(*arrays, small, totals)


norm_epsilon = 1e-05


def normal_parts(values):
    center = values - jnp.mean(values, axis=-1, keepdims=True)
    inverse = lax.rsqrt(jnp.mean(center * center, axis=-1, keepdims=True) + norm_epsilon)
    return center * inverse, inverse


def normal_back(normal, inverse, gain, grad):
    scaled = grad * gain
    return inverse * (
        scaled
        - jnp.mean(scaled, axis=-1, keepdims=True)
        - normal * jnp.mean(scaled * normal, axis=-1, keepdims=True)
    )


def mixer_kernel(
    merged_ref, start_ref, cotangent_ref, vectors_ref, bias_ref, merge_ref, expand_ref, reduce_ref,
    output_ref, mixer_grad_ref, merged_grad_ref, merge_grad_ref, expand_grad_ref, reduce_grad_ref, sums_ref,
    bias_grad_ref,
    hidden_ref, normal_ref, inverse_ref, low_ref, active_ref, slope_ref, dense_ref, grad_ref, grad_low_ref,
    turned_ref,
):
    step = pl.program_id(0)
    chunk = lax.rem(step, CHUNKS)
    width = expand_ref.shape[1] // CHUNKS
    part = pl.ds(pl.multiple_of(chunk * width, width), width)

    def vector(k):
        return vectors_ref[k : k + 1, :]

    def column_sum(values):
        return jnp.sum(values, axis=0, keepdims=True)

    @pl.when(step == 0)
    def _():
        normal, inverse = normal_parts(start_ref[...] + dot_nn(merged_ref[...], merge_ref[...]))
        normal_ref[...] = normal
        inverse_ref[...] = jnp.broadcast_to(inverse, inverse_ref.shape)
        hidden = normal * vector(4) + vector(5)
        hidden_ref[...] = hidden
        low_ref[...] = hidden.astype(jnp.bfloat16)
        dense_ref[...] = jnp.zeros_like(dense_ref)

    @pl.when(step < CHUNKS)
    def _():
        inner = dot_nn(low_ref[...], expand_ref[:, part]) + bias_ref[chunk]
        share = 0.5 + 0.5 * lax.erf(inner * (0.5**0.5))
        active = (inner * share).astype(jnp.bfloat16)
        active_ref[chunk] = active
        slope_ref[chunk] = share + inner * jnp.exp(-0.5 * inner * inner) * (2.0 * jnp.pi) ** -0.5
        dense_ref[...] += dot_nn(active, reduce_ref[part, :])

    @pl.when(step == CHUNKS - 1)
    def _():
        normal, inverse = normal_parts(hidden_ref[...] + (dense_ref[...] + vector(6)))
        output_ref[...] = (normal * vector(7) + vector(8)).astype(jnp.bfloat16)
        upstream = cotangent_ref[...].astype(jnp.float32)
        grad = normal_back(normal, inverse, vector(7), upstream)
        grad_ref[...] = grad
        grad_low_ref[...] = grad.astype(jnp.bfloat16)
        sums_ref[2:3, :] = column_sum(grad)
        sums_ref[3:4, :] = column_sum(upstream * normal)
        sums_ref[4:5, :] = column_sum(upstream)
        turned_ref[...] = low_ref[...].T

    @pl.when(step >= CHUNKS)
    def _():
        grad_low = grad_low_ref[...]
        reduce_grad_ref[...] = dot_tn(active_ref[chunk], grad_low).astype(jnp.bfloat16)
        inner_low = (dot_nt(grad_low, reduce_ref[part, :]) * slope_ref[chunk]).astype(jnp.bfloat16)
        bias_grad_ref[chunk] = column_sum(inner_low.astype(jnp.float32))
        expand_grad_ref[...] = dot_nn(turned_ref[...], inner_low).astype(jnp.bfloat16)
        grad_ref[...] += dot_nt(inner_low, expand_ref[:, part])

    @pl.when(step == 2 * CHUNKS - 1)
    def _():
        grad = grad_ref[...]
        normal = normal_ref[...]
        mixer_grad = normal_back(normal, inverse_ref[:, :1], vector(4), grad)
        mixer_grad_ref[...] = mixer_grad
        sums_ref[0:1, :] = column_sum(grad * normal)
        sums_ref[1:2, :] = column_sum(grad)
        low = mixer_grad.astype(jnp.bfloat16)
        merge_grad_ref[...] = dot_tn(merged_ref[...], low).astype(jnp.bfloat16)
        merged_grad_ref[...] = dot_nt(low, merge_ref[...]).astype(jnp.bfloat16)


def mixer_layer(merged, start, cotangent, vectors, bias, w_merge, w_expand, w_reduce):
    rows = merged.shape[0]
    inner = w_expand.shape[1]
    width = inner // CHUNKS
    page = (rows, MODEL_WIDTH)

    def back_at(i):
        return jnp.maximum(i - CHUNKS, 0)

    def whole(shape):
        return pl.BlockSpec(shape, lambda i: (0,) * len(shape))

    f32, bf16 = jnp.float32, jnp.bfloat16
    outs = [
        (page, bf16, whole(page)),
        (page, f32, whole(page)),
        (page, bf16, whole(page)),
        ((MODEL_WIDTH, MODEL_WIDTH), bf16, whole((MODEL_WIDTH, MODEL_WIDTH))),
        ((MODEL_WIDTH, inner), bf16, pl.BlockSpec((MODEL_WIDTH, width), lambda i: (0, back_at(i)))),
        ((inner, MODEL_WIDTH), bf16, pl.BlockSpec((width, MODEL_WIDTH), lambda i: (back_at(i), 0))),
        ((8, MODEL_WIDTH), f32, whole((8, MODEL_WIDTH))),
        ((CHUNKS, 1, width), f32, whole((CHUNKS, 1, width))),
    ]
    return pl.pallas_call(
        mixer_kernel,
        grid=(2 * CHUNKS,),
        in_specs=[
            once(page),
            once(page),
            once(page),
            once(vectors.shape),
            once(bias.shape),
            once(w_merge.shape),
            once(w_expand.shape),
            once(w_reduce.shape),
        ],
        out_specs=[spec for shape, kind, spec in outs],
        out_shape=[jax.ShapeDtypeStruct(shape, kind) for shape, kind, spec in outs],
        scratch_shapes=[
            pltpu.VMEM(page, f32),
            pltpu.VMEM(page, f32),
            pltpu.VMEM((rows, 128), f32),
            pltpu.VMEM(page, bf16),
            pltpu.VMEM((CHUNKS, rows, width), bf16),
            pltpu.VMEM((CHUNKS, rows, width), f32),
            pltpu.VMEM(page, f32),
            pltpu.VMEM(page, f32),
            pltpu.VMEM(page, bf16),
            pltpu.VMEM((MODEL_WIDTH, rows), bf16),
        ],
        compiler_params=pltpu.CompilerParams(vmem_limit_bytes=62 << 20),
        name="mixer_layer",
    )(merged, start, cotangent, vectors, bias, w_merge, w_expand, w_reduce)

AXES = ("dp", "pair")


def padded_rows(pieces):
    total = sum(piece.shape[0] for piece in pieces)
    rows = -(-total // 8) * 8
    whole = jnp.zeros((rows, 128), jnp.float32)
    start = 0
    for piece in pieces:
        stop = start + piece.shape[0]
        whole += jnp.pad(piece.astype(jnp.float32), ((start, rows - stop), (0, 128 - piece.shape[1])))
        start = stop
    return whole


def blocks_of(grad, devices):
    blocks = grad.astype(jnp.bfloat16).reshape(devices, grad.shape[0] // devices, grad.shape[1])
    return blocks if blocks.shape[1] % 8 == 0 else blocks.reshape(devices, -1, 128)


def per_device(
    text_inputs,
    region_features,
    text_masked,
    region_masked,
    text_anchors,
    region_anchors,
    backbone_weight,
    batch_gain,
    batch_shift,
    text_blank,
    region_blank,
    position_table,
    stream_weights,
    linear_bias,
    planar_bias,
    merge_weight,
    mixer_gain,
    mixer_shift,
    expand_weight,
    expand_bias,
    reduce_weight,
    reduce_bias,
    output_gain,
    output_shift,
    cotangent,
):
    devices = lax.axis_size(AXES)
    row_count = text_inputs.shape[0]
    token_total = row_count * devices
    share = MODEL_WIDTH // devices
    expand_share = expand_bias.shape[0]
    bias_rows = REL_B // devices
    vectors = (
        batch_gain, batch_shift, text_blank, region_blank, mixer_gain, mixer_shift, reduce_bias,
        output_gain, output_shift, expand_bias,
    )
    small = padded_rows([linear_bias, planar_bias, *(vector[None, :] for vector in vectors)])
    packed, w_backbone, w_stream, w_table = gather_all(
        (small, backbone_weight, stream_weights), (position_table,), 0
    )
    w_backbone, w_table, w_stream = (
        whole.reshape(-1, whole.shape[-1]) for whole in (w_backbone, w_table, w_stream)
    )

    anchor_rows = jnp.concatenate([text_anchors, region_anchors], axis=0)
    anchor_cols = anchor_rows.T
    hits = jnp.stack([text_masked, region_masked], axis=1)
    proj, merged_low, probs, lefts, start_sum, normal_feat, batch_scale, w_vectors, w_expand_bias, *wholes = forward_layer(
        region_features, w_backbone, w_table, text_inputs, hits, packed, w_stream, anchor_rows, anchor_cols,
        (merge_weight, expand_weight, reduce_weight), token_total, 4,
    )
    w_merge, w_expand, w_reduce = (whole.reshape(-1, whole.shape[-1]) for whole in wholes)
    (
        layer_output, mixer_in_grad, merged_grad, merge_weight_grad, expand_weight_grad, reduce_weight_grad,
        mixer_sums, expand_bias_grad,
    ) = mixer_layer(
        merged_low, start_sum, cotangent, w_vectors, w_expand_bias,
        w_merge, w_expand, w_reduce,
    )
    early = (expand_weight_grad, reduce_weight_grad, merge_weight_grad)
    (
        linear_sums, planar_sums, stream_weights_grad, position_table_grad, text_gradient, region_kept,
        start_sums, *early_shares,
    ) = backward_layer(
        proj, probs, merged_grad, anchor_rows, anchor_cols, lefts, w_stream, mixer_in_grad, normal_feat, hits,
        [blocks_of(grad, devices) for grad in early], 5,
    )
    vector_grads = jnp.concatenate([start_sums[:2], mixer_sums[:5]], axis=0)
    pieces = [
        linear_folded(linear_sums[:, 0]).T.reshape(devices, bias_rows, HEADS),
        planar_sums[:, 0].T.reshape(devices, bias_rows, HEADS),
        vector_grads.reshape(7, devices, share).transpose(1, 0, 2),
        expand_bias_grad.reshape(devices, 1, expand_share),
    ]
    rows = sum(piece.shape[1] for piece in pieces)
    pieces = [jnp.pad(piece, ((0, 0), (0, 0), (0, 128 - piece.shape[2]))) for piece in pieces]
    small_grads = jnp.pad(jnp.concatenate(pieces, axis=1), ((0, 0), (0, -rows % 8), (0, 0)))
    feature_gradient, totals, small, stream_share, backbone_weight_grad, table_share = last_layer(
        start_sums, region_kept, normal_feat, batch_scale, region_features, w_backbone,
        [small_grads, blocks_of(stream_weights_grad, devices)], blocks_of(position_table_grad, devices),
        token_total, 1,
    )
    arrays = (
        text_gradient, feature_gradient, backbone_weight_grad, table_share, stream_share, *early_shares,
    )
    (
        text_gradient, feature_gradient, backbone_weight_grad, table_share, stream_share, expand_share_grad,
        reduce_share_grad, merge_share_grad, linear_grad, planar_grad, *vector_grads,
    ) = finish(arrays, small, totals, share, expand_share, bias_rows)
    vector_grads = [grad.reshape(-1) for grad in vector_grads]
    return (
        layer_output,
        text_gradient,
        feature_gradient,
        backbone_weight_grad,
        vector_grads[9],
        vector_grads[8],
        vector_grads[0],
        vector_grads[1],
        table_share.reshape(-1, position_table.shape[1]),
        stream_share.reshape(-1, stream_weights.shape[1]),
        linear_grad,
        planar_grad,
        merge_share_grad.reshape(-1, MODEL_WIDTH),
        vector_grads[2],
        vector_grads[3],
        expand_share_grad.reshape(-1, expand_weight.shape[1]),
        vector_grads[7],
        reduce_share_grad.reshape(-1, MODEL_WIDTH),
        vector_grads[4],
        vector_grads[5],
        vector_grads[6],
    )

def solution(mesh):
    in_specs = (
        P(("dp", "pair"), None),
        P(("dp", "pair"), None),
        P(("dp", "pair")),
        P(("dp", "pair")),
        P(None, ("dp", "pair")),
        P(None, ("dp", "pair")),
        P(("dp", "pair"), None),
        P(("dp", "pair")),
        P(("dp", "pair")),
        P(("dp", "pair")),
        P(("dp", "pair")),
        P(("dp", "pair"), None),
        P(("dp", "pair"), None),
        P(("dp", "pair"), None),
        P(("dp", "pair"), None),
        P(("dp", "pair"), None),
        P(("dp", "pair")),
        P(("dp", "pair")),
        P(("dp", "pair"), None),
        P(("dp", "pair")),
        P(("dp", "pair"), None),
        P(("dp", "pair")),
        P(("dp", "pair")),
        P(("dp", "pair")),
        P(("dp", "pair"), None),
    )
    out_specs = (
        P(("dp", "pair"), None),
        P(("dp", "pair"), None),
        P(("dp", "pair"), None),
        P(("dp", "pair"), None),
        P(("dp", "pair")),
        P(("dp", "pair")),
        P(("dp", "pair")),
        P(("dp", "pair")),
        P(("dp", "pair"), None),
        P(("dp", "pair"), None),
        P(("dp", "pair"), None),
        P(("dp", "pair"), None),
        P(("dp", "pair"), None),
        P(("dp", "pair")),
        P(("dp", "pair")),
        P(("dp", "pair"), None),
        P(("dp", "pair")),
        P(("dp", "pair"), None),
        P(("dp", "pair")),
        P(("dp", "pair")),
        P(("dp", "pair")),
    )
    return jax.shard_map(
        per_device, mesh=mesh, in_specs=in_specs, out_specs=out_specs, check_vma=False
    )
```

```python
from functools import partial
from types import SimpleNamespace

import jax
import jax.numpy as jnp
from jax import lax
from jax.experimental import pallas as pl
from jax.experimental.pallas import tpu as pltpu
from jax.sharding import PartitionSpec as P

HEADS = 12
HEAD_DIM = 64
COORDS = 1024
REL_B = 256
SP_SIDE = 16
PAGE_TOKENS = 256
MODEL_WIDTH = 768
SP_B = 256
COORD_STEP = 128
PAIRS = HEADS // 2
LANES = 2 * HEAD_DIM


def dot_nt(left, right):
    return lax.dot_general(left, right, (((1,), (1,)), ((), ())), preferred_element_type=jnp.float32)


def dot_tn(left, right):
    return lax.dot_general(left, right, (((0,), (0,)), ((), ())), preferred_element_type=jnp.float32)


def dot_nn(left, right):
    return lax.dot_general(left, right, (((1,), (0,)), ((), ())), preferred_element_type=jnp.float32)


def head_columns(stream, kind, pair):
    return pl.ds(pl.multiple_of(((5 * stream + kind) * PAIRS + pair) * LANES, LANES), LANES)


def make_boxes(rows_ref, cols_ref, box_ref):
    for stream in range(2):
        part = []
        for axis in range(2):
            along = rows_ref[2 * stream + axis : 2 * stream + axis + 1, :]
            down = cols_ref[:, 2 * stream + axis : 2 * stream + axis + 1]
            part.append(((along - down) >> 7) + SP_SIDE // 2)
        box_ref[stream] = part[0] * SP_SIDE + part[1]


def attend_pair(pair, proj_ref, linear_ref, planar_ref, box_ref, merged_ref, probs_ref):
    lane_head = lax.broadcasted_iota(jnp.int32, (PAGE_TOKENS, LANES), 1) // HEAD_DIM
    mixed = [None, None]
    for inner in range(2):
        head = 2 * pair + inner
        mine = lane_head == inner
        spread = jnp.broadcast_to(linear_ref[head], (PAGE_TOKENS, 2 * PAGE_TOKENS))
        linear_term = pltpu.roll(spread, PAGE_TOKENS + 1, 1, stride=1, stride_axis=0)[:, :PAGE_TOKENS]
        low_table = jnp.broadcast_to(planar_ref[head, :, :128], (PAGE_TOKENS, 128))
        high_table = jnp.broadcast_to(planar_ref[head, :, 128:], (PAGE_TOKENS, 128))
        total = None
        for stream in range(2):
            pieces = [proj_ref[:, head_columns(stream, kind, pair)] for kind in range(5)]
            zero = jnp.zeros_like(pieces[0])
            left = jnp.concatenate([jnp.where(mine, pieces[0], zero), jnp.where(mine, pieces[3], zero)], axis=1)
            right = jnp.concatenate([pieces[1], pieces[4]], axis=1)
            logits = dot_nt(left, right) * HEAD_DIM ** (-0.5)
            planar = []
            for half in range(2):
                box = box_ref[stream, :, 128 * half : 128 * half + 128]
                place = box & 127
                planar.append(
                    jnp.where(
                        box < 128,
                        jnp.take_along_axis(low_table, place, axis=1),
                        jnp.take_along_axis(high_table, place, axis=1),
                    )
                )
            logits = logits + linear_term + jnp.concatenate(planar, axis=1)
            top = jnp.max(logits, axis=-1, keepdims=True)
            shifted = jnp.exp(logits - top)
            probs = shifted / jnp.sum(shifted, axis=-1, keepdims=True)
            probs_ref[stream, inner] = probs
            part = dot_nn(probs.astype(jnp.bfloat16), pieces[2])
            total = part if total is None else total + part
        mixed[inner] = total
    merged_ref[...] = jnp.where(lane_head == 0, mixed[0], mixed[1]).astype(jnp.bfloat16)


def make_places(rows_ref, cols_ref, place_ref, turned_ref, mask_ref, flip_ref):
    lanes = lax.broadcasted_iota(jnp.int32, (PAGE_TOKENS, SP_B), 1)
    rows = lax.broadcasted_iota(jnp.int32, (PAGE_TOKENS, SP_B), 0)
    flip_ref[...] = (lanes + rows == PAGE_TOKENS - 1).astype(jnp.bfloat16)
    for stream in range(2):
        x_row = rows_ref[2 * stream : 2 * stream + 1, :]
        y_row = rows_ref[2 * stream + 1 : 2 * stream + 2, :]
        x_col = cols_ref[:, 2 * stream : 2 * stream + 1]
        y_col = cols_ref[:, 2 * stream + 1 : 2 * stream + 2]
        cell_row = (x_row >> 7) * SP_SIDE + (y_row >> 7)
        cell_col = (x_col >> 7) * SP_SIDE + (y_col >> 7)
        x_less = ((x_row & 127) < (x_col & 127)).astype(jnp.float32)
        y_less = ((y_row & 127) < (y_col & 127)).astype(jnp.float32)
        for x_side in range(2):
            for y_side in range(2):
                side = 2 * x_side + y_side
                place_ref[stream, side * PAGE_TOKENS : (side + 1) * PAGE_TOKENS, :] = (
                    lanes == cell_col + (SP_SIDE + 1 - SP_SIDE * x_side - y_side)
                ).astype(jnp.bfloat16)
                mask_ref[stream, side] = (
                    (x_less if x_side else 1.0 - x_less) * (y_less if y_side else 1.0 - y_less)
                ).astype(jnp.bfloat16)
        turned_ref[stream] = (rows[:128] == 127 - cell_row).astype(jnp.bfloat16)


def attend_back_pair(
    pair, pump, proj_ref, probs_ref, upstream_ref, grad_ref, linear_ref, planar_ref,
    place_ref, turned_ref, mask_ref, flip_ref,
):
    lane_head = lax.broadcasted_iota(jnp.int32, (PAGE_TOKENS, LANES), 1) // HEAD_DIM
    wide_head = jnp.concatenate([lane_head, lane_head], axis=1)
    upstream = upstream_ref[...]
    scale = HEAD_DIM ** (-0.5)
    diagonal = [None, None]
    for stream in range(2):
        pieces = [proj_ref[:, head_columns(stream, kind, pair)] for kind in range(5)]
        queries = jnp.concatenate([pieces[0], pieces[3]], axis=1)
        keys = jnp.concatenate([pieces[1], pieces[4]], axis=1)
        grads = []
        for inner in range(2):
            head = 2 * pair + inner
            mine = lane_head == inner
            grad_probs = dot_nt(jnp.where(mine, upstream, jnp.zeros_like(upstream)), pieces[2])
            probs = probs_ref[stream, inner]
            weighted = probs * grad_probs
            grad_logits = (weighted - probs * jnp.sum(weighted, axis=-1, keepdims=True)).astype(jnp.bfloat16)
            grads.append(
                (
                    dot_nn(grad_logits, keys) * scale,
                    dot_tn(grad_logits, queries) * scale,
                    dot_tn(probs.astype(jnp.bfloat16), upstream),
                )
            )
            parts = jnp.concatenate([grad_logits * mask_ref[stream, side] for side in range(4)], axis=1)
            placed = dot_nn(parts, place_ref[stream]).astype(jnp.bfloat16)
            cells = dot_nn(turned_ref[stream], placed)
            sums = jnp.sum(
                pltpu.roll(cells, SP_B - SP_SIDE // 2, 1, stride=1, stride_axis=0), axis=0, keepdims=True
            )
            if stream == 0:
                planar_ref[head] = sums
            else:
                planar_ref[head] += sums
            turned_over = dot_nn(flip_ref[...], grad_logits)
            diagonal[inner] = turned_over if stream == 0 else diagonal[inner] + turned_over
            pump(2 * stream + inner)
        query_grad, key_grad = (jnp.where(wide_head == 0, grads[0][k], grads[1][k]) for k in range(2))
        value_grad = jnp.where(lane_head == 0, grads[0][2], grads[1][2])
        for kind, value in enumerate(
            (query_grad[:, :LANES], key_grad[:, :LANES], value_grad, query_grad[:, LANES:], key_grad[:, LANES:])
        ):
            grad_ref[:, head_columns(stream, kind, pair)] = value.astype(jnp.bfloat16)
    for inner in range(2):
        padded = jnp.concatenate([diagonal[inner], jnp.zeros_like(diagonal[inner])], axis=1)
        linear_ref[2 * pair + inner] = jnp.sum(
            pltpu.roll(padded, 0, 1, stride=1, stride_axis=0), axis=0, keepdims=True
        )


def linear_folded(sums):
    first = REL_B // 2
    last = PAGE_TOKENS - 1 + REL_B // 2 - 1
    return jnp.concatenate(
        [
            jnp.sum(sums[:, :first], axis=1, keepdims=True),
            sums[:, first:last],
            jnp.sum(sums[:, last : 2 * PAGE_TOKENS - 1], axis=1, keepdims=True),
        ],
        axis=1,
    )


MESH = pl.DeviceIdType.MESH
RING = 4


def place():
    dp = lax.axis_index("dp")
    return dp // RING, lax.rem(dp, RING), lax.axis_index("pair")


def across(q, bit):
    other = lax.rem(q // bit, 2)
    return q + bit - 2 * bit * other


def greet(line):
    z, q, c = place()
    barrier = pltpu.get_barrier_semaphore()

    def signal(zz, qq, cc):
        pl.semaphore_signal(barrier, inc=1, device_id={"dp": zz * RING + qq, "pair": cc}, device_id_type=MESH)

    signal(z, across(q, 1), c)
    signal(z, across(q, 2), c)
    signal(z, q, 1 - c)

    @pl.when(z > 0)
    def _():
        signal(z - 1, q, c)

    @pl.when(z < line - 1)
    def _():
        signal(z + 1, q, c)

    ends = (z > 0).astype(jnp.int32) + (z < line - 1).astype(jnp.int32)
    pl.semaphore_wait(barrier, 3 + ends)


def spread(line, pumps, pump, first, work):
    total = line - first
    low, high = (first + total * (pump + k) // pumps for k in range(2))
    if high == low + 1:
        work(low)
    elif high > low:
        lax.fori_loop(low, high, lambda g, unused: (work(g), unused)[1], 0)


def gather_stages(line, ins, outs, sems):
    count = len(ins)
    (own_sem, z_send, z_recv, xy_send, xy_recv, d_send, d_recv, c_send, c_recv) = sems
    z, q, c = place()
    beside = (across(q, 1), across(q, 2))
    corner = across(across(q, 1), 2)

    def slot(zz, qq):
        return (zz * RING + qq) * 2 + c

    def remote(src, dst, send, recv, zz, qq, cc):
        return pltpu.make_async_remote_copy(
            src_ref=src, dst_ref=dst, send_sem=send, recv_sem=recv,
            device_id={"dp": zz * RING + qq, "pair": cc}, device_id_type=MESH,
        )

    def block(a, zz, qq):
        return outs[a].at[slot(zz, qq)]

    def halves(a):
        width = ins[a].shape[-1]
        cut = width // 2 if width % 256 == 0 else width
        return (0, cut), (cut, width - cut)

    def own(a):
        return pltpu.make_async_copy(ins[a], block(a, z, q), own_sem.at[a])

    def z_copy(a, way, step, first):
        zz = z - step if way == 0 else z + step
        target = z + 1 if way == 0 else z - 1
        src = ins[a] if first else block(a, zz, q)
        return remote(src, block(a, zz, q), z_send.at[way, a, step], z_recv.at[way, a, step], target, q, c)

    def xy_copy(a, axis, zz, first):
        src = ins[a] if first else block(a, zz, q)
        return remote(src, block(a, zz, q), xy_send.at[axis, a, zz], xy_recv.at[axis, a, zz], z, beside[axis], c)

    def d_copy(a, axis, zz):
        start, width = halves(a)[axis]
        part = outs[a].at[slot(zz, beside[axis]), :, pl.ds(start, width)]
        return remote(part, part, d_send.at[axis, a, zz], d_recv.at[axis, a, zz], z, beside[1 - axis], c)

    def c_copy(a, zz, qq, first):
        src = ins[a] if first else block(a, zz, qq)
        return remote(
            src, block(a, zz, qq), c_send.at[a, zz * RING + qq], c_recv.at[a, zz * RING + qq], z, q, 1 - c
        )

    def start_line():
        for a in range(count):
            own(a).start()
            for way in range(2):
                @pl.when(z < line - 1 if way == 0 else z > 0)
                def _():
                    z_copy(a, way, 0, True).start()
            c_copy(a, z, q, True).start()

    def start_ring():
        for a in range(count):
            for axis in range(2):
                xy_copy(a, axis, z, True).start()

    def arrived(a, zz):
        for axis in range(2):
            xy_copy(a, axis, zz, False).start()
        c_copy(a, zz, q, False).start()

    def passed_on(a, zz):
        for axis in range(2):
            start, width = halves(a)[axis]
            got = block(a, zz, beside[axis])
            remote(got, got, xy_send.at[axis, a, zz], xy_recv.at[axis, a, zz], z, beside[axis], c).wait_recv()
            if width:
                d_copy(a, axis, zz).start()
            c_copy(a, zz, beside[axis], False).start()

    def finished(a, zz):
        for axis in range(2):
            start, width = halves(a)[axis]
            if width:
                part = outs[a].at[slot(zz, corner), :, pl.ds(start, width)]
                remote(part, part, d_send.at[axis, a, zz], d_recv.at[axis, a, zz], z, beside[1 - axis], c).wait_recv()
        c_copy(a, zz, corner, False).start()

    def both_ways(g, work):
        @pl.when(z - g >= 0)
        def _():
            work(z - g)

        @pl.when(jnp.logical_and(z + g <= line - 1, g > 0))
        def _():
            work(z + g)

    def along(g):
        for a in range(count):
            @pl.when(z - g >= 0)
            def _():
                got = block(a, z - g, q)
                remote(got, got, z_send.at[0, a, g - 1], z_recv.at[0, a, g - 1], z, q, 1 - c).wait_recv()

                @pl.when(z < line - 1)
                def _():
                    z_copy(a, 0, g, False).start()

                arrived(a, z - g)

            @pl.when(z + g <= line - 1)
            def _():
                got = block(a, z + g, q)
                remote(got, got, z_send.at[1, a, g - 1], z_recv.at[1, a, g - 1], z, q, 1 - c).wait_recv()

                @pl.when(z > 0)
                def _():
                    z_copy(a, 1, g, False).start()

                arrived(a, z + g)

    def around(g):
        for a in range(count):
            both_ways(g, partial(passed_on, a))

    def home(g):
        for a in range(count):
            both_ways(g, partial(finished, a))

    def drain(zz, unused):
        for a in range(count):
            for axis in range(2):
                xy_copy(a, axis, zz, False).wait_send()
                if halves(a)[axis][1]:
                    d_copy(a, axis, zz).wait_send()
            for qq in range(RING):
                c_copy(a, zz, qq, False).wait_send()
                got = outs[a].at[(zz * RING + qq) * 2 + 1 - c]
                remote(
                    got, got, c_send.at[a, zz * RING + qq], c_recv.at[a, zz * RING + qq], z, q, 1 - c
                ).wait_recv()

            @pl.when(jnp.logical_and(z < line - 1, zz <= z))
            def _():
                z_copy(a, 0, z - zz, False).wait_send()

            @pl.when(jnp.logical_and(z > 0, zz >= z))
            def _():
                z_copy(a, 1, zz - z, False).wait_send()
        return unused

    def end():
        for a in range(count):
            own(a).wait()
        lax.fori_loop(0, line, drain, 0)

    return SimpleNamespace(
        start_line=start_line, start_ring=start_ring, along=along, around=around, home=home, end=end
    )


def gather_sems(line, count):
    dma = pltpu.SemaphoreType.DMA
    return [
        dma((count,)),
        *(dma((2, count, line)) for k in range(6)),
        dma((count, line * RING)),
        dma((count, line * RING)),
    ]


def group_of(zz):
    return pl.ds(zz * RING, RING)


def flat_gather_stages(line, ins, outs, sems):
    count = len(ins)
    own_sem, xy_send, xy_recv, d_send, d_recv, z_send, z_recv, c_send, c_recv = sems
    z, q, c = place()
    beside = (across(q, 1), across(q, 2))
    corner = across(across(q, 1), 2)

    def remote(src, dst, send, recv, zz, qq, cc):
        return pltpu.make_async_remote_copy(
            src_ref=src, dst_ref=dst, send_sem=send, recv_sem=recv,
            device_id={"dp": zz * RING + qq, "pair": cc}, device_id_type=MESH,
        )

    def block(a, qq):
        return outs[a].at[z * RING + qq, c]

    def halves(a):
        width = ins[a].shape[-1]
        return (0, width // 2), (width // 2, width // 2)

    def own(a):
        return pltpu.make_async_copy(ins[a], block(a, q), own_sem.at[a])

    def xy_copy(a, axis):
        return remote(ins[a], block(a, q), xy_send.at[axis, a], xy_recv.at[axis, a], z, beside[axis], c)

    def xy_got(a, axis):
        got = block(a, beside[axis])
        return remote(got, got, xy_send.at[axis, a], xy_recv.at[axis, a], z, beside[axis], c)

    def d_copy(a, axis, qq):
        start, width = halves(a)[axis]
        part = outs[a].at[z * RING + qq, c, :, pl.ds(start, width)]
        return remote(part, part, d_send.at[axis, a], d_recv.at[axis, a], z, beside[1 - axis], c)

    def z_copy(a, way, zz, target):
        part = outs[a].at[group_of(zz), c]
        return remote(part, part, z_send.at[way, a, zz], z_recv.at[way, a, zz], target, q, c)

    def c_copy(a, zz, cc):
        part = outs[a].at[group_of(zz), cc]
        return remote(part, part, c_send.at[a, zz], c_recv.at[a, zz], z, q, 1 - c)

    def ahead(way):
        return z < line - 1 if way == 0 else z > 0

    def start():
        for a in range(count):
            own(a).start()
            for axis in range(2):
                xy_copy(a, axis).start()

    def around():
        for a in range(count):
            for axis in range(2):
                xy_got(a, axis).wait_recv()
                d_copy(a, axis, beside[axis]).start()

    def home():
        for a in range(count):
            own(a).wait()
            for axis in range(2):
                d_copy(a, axis, corner).wait_recv()
            for way in range(2):
                @pl.when(ahead(way))
                def _():
                    z_copy(a, way, z, z + 1 - 2 * way).start()
            c_copy(a, z, c).start()

    def along(g):
        for a in range(count):
            for way in range(2):
                zz = z - g if way == 0 else z + g

                @pl.when(zz >= 0 if way == 0 else zz <= line - 1)
                def _():
                    z_copy(a, way, zz, z - 1 + 2 * way).wait_recv()

                    @pl.when(ahead(way))
                    def _():
                        z_copy(a, way, zz, z + 1 - 2 * way).start()

                    c_copy(a, zz, c).start()

    def end():
        for a in range(count):
            for axis in range(2):
                xy_copy(a, axis).wait_send()
                d_copy(a, axis, beside[axis]).wait_send()

            def drain(zz, unused):
                c_copy(a, zz, c).wait_send()
                c_copy(a, zz, 1 - c).wait_recv()
                for way in range(2):
                    @pl.when(jnp.logical_and(ahead(way), zz <= z if way == 0 else zz >= z))
                    def _():
                        z_copy(a, way, zz, z + 1 - 2 * way).wait_send()
                return unused

            lax.fori_loop(0, line, drain, 0)

    return SimpleNamespace(start=start, around=around, home=home, along=along, end=end)


def flat_gather_sems(line, count):
    dma = pltpu.SemaphoreType.DMA
    return [
        dma((count,)),
        *(dma((2, count)) for k in range(4)),
        *(dma((2, count, line)) for k in range(2)),
        *(dma((count, line)) for k in range(2)),
    ]


def gather_kernel(line, count, flat, *refs):
    both = count + flat
    ins, outs, sems = refs[:both], refs[both : 2 * both], refs[2 * both :]
    stages = gather_stages(line, ins[:count], outs[:count], sems[:9])
    plane = flat_gather_stages(line, ins[count:], outs[count:], sems[9:])
    greet(line)
    plane.start()
    stages.start_line()
    stages.start_ring()

    def generation(g, unused):
        stages.along(g)
        stages.around(g - 1)

        @pl.when(g == 1)
        def _():
            plane.around()

        @pl.when(g == 2)
        def _():
            plane.home()

        @pl.when(g >= 3)
        def _():
            stages.home(g - 3)

        return unused

    lax.fori_loop(1, line, generation, 0)
    if line == 2:
        plane.home()

    def rest(g, unused):
        @pl.when(g <= line - 1)
        def _():
            plane.along(g)

        @pl.when(g == 1)
        def _():
            stages.around(line - 1)

        @pl.when(g + line - 4 >= 0)
        def _():
            stages.home(g + line - 4)

        return unused

    lax.fori_loop(1, 4, rest, 0)
    lax.fori_loop(4, line, lambda g, unused: (plane.along(g), unused)[1], 0)
    stages.end()
    plane.end()


def gather_all(shards, flat_shards, collective_id):
    dp = lax.axis_size("dp")
    line = dp // RING
    count, flat = len(shards), len(flat_shards)
    wholes = pl.pallas_call(
        partial(gather_kernel, line, count, flat),
        in_specs=[pl.BlockSpec(memory_space=pl.ANY)] * (count + flat),
        out_specs=[pl.BlockSpec(memory_space=pl.ANY)] * (count + flat),
        out_shape=[
            *(jax.ShapeDtypeStruct((2 * dp, *shard.shape), shard.dtype) for shard in shards),
            *(jax.ShapeDtypeStruct((dp, 2, *shard.shape), shard.dtype) for shard in flat_shards),
        ],
        scratch_shapes=[*gather_sems(line, count), *flat_gather_sems(line, flat)],
        compiler_params=pltpu.CompilerParams(collective_id=collective_id, has_side_effects=True),
        name="gather_all",
    )(*shards, *flat_shards)
    return [whole.reshape(2 * dp, *whole.shape[-2:]) for whole in wholes]


def scatter_stages(line, ins, outs, scratch):
    count = len(ins)
    groups = [scratch[k * count : (k + 1) * count] for k in range(5)]
    mine, beside_sum, half_in, full_in, line_in = groups
    (own_sem, c_send, c_recv, d_send, d_recv, xy_send, xy_recv, z_send, z_recv) = scratch[5 * count :]
    z, q, c = place()
    beside = (across(q, 1), across(q, 2))
    corner = across(across(q, 1), 2)

    def remote(src, dst, send, recv, zz, qq, cc):
        return pltpu.make_async_remote_copy(
            src_ref=src, dst_ref=dst, send_sem=send, recv_sem=recv,
            device_id={"dp": zz * RING + qq, "pair": cc}, device_id_type=MESH,
        )

    def halves(a):
        width = outs[a].shape[-1]
        cut = width // 2 if width % 256 == 0 else width
        return (0, cut), (cut, width - cut)

    def wide(value):
        return value.astype(jnp.float32)

    def group(zz):
        return pl.ds(zz * RING, RING)

    def own(a, zz):
        return pltpu.make_async_copy(ins[a].at[group(zz), c], mine[a].at[group(zz)], own_sem.at[a, zz])

    def c_copy(a, zz):
        return remote(
            ins[a].at[group(zz), 1 - c], beside_sum[a].at[group(zz)], c_send.at[a, zz], c_recv.at[a, zz], z, q, 1 - c
        )

    def d_copy(a, axis, zz):
        start, width = halves(a)[axis]
        return remote(
            mine[a].at[zz * RING + corner, :, pl.ds(start, width)],
            half_in[a].at[zz, :, pl.ds(start, width)],
            d_send.at[axis, a, zz], d_recv.at[axis, a, zz], z, beside[axis], c,
        )

    def xy_copy(a, axis, zz):
        return remote(
            mine[a].at[zz * RING + beside[axis]], full_in[a].at[axis, zz],
            xy_send.at[axis, a, zz], xy_recv.at[axis, a, zz], z, beside[axis], c,
        )

    def z_copy(a, way, zz):
        return remote(
            mine[a].at[zz * RING + q], line_in[a].at[way, zz],
            z_send.at[way, a, zz], z_recv.at[way, a, zz], z + 1 if way == 0 else z - 1, q, c,
        )

    def both_ways(g, work):
        @pl.when(z - g >= 0)
        def _():
            work(z - g)

        @pl.when(jnp.logical_and(z + g <= line - 1, g > 0))
        def _():
            work(z + g)

    def begin(zz):
        for a in range(count):
            c_copy(a, zz).start()
            own(a, zz).start()

    def first(zz):
        for a in range(count):
            own(a, zz).wait()
            c_copy(a, zz).wait_recv()

            def one(qq, unused):
                k = zz * RING + qq
                mine[a][k] = mine[a][k] + beside_sum[a][k]
                return unused

            lax.fori_loop(0, RING, one, 0)
            for axis in range(2):
                if halves(a)[axis][1]:
                    d_copy(a, axis, zz).start()

    def second(zz):
        for a in range(count):
            for axis in range(2):
                start, width = halves(a)[axis]
                k = zz * RING + beside[1 - axis]
                if width:
                    d_copy(a, axis, zz).wait_recv()
                    mine[a][k, :, start : start + width] = (
                        mine[a][k, :, start : start + width] + half_in[a][zz, :, start : start + width]
                    )
                xy_copy(a, 1 - axis, zz).start()

    def third(zz):
        for a in range(count):
            k = zz * RING + q
            for axis in range(2):
                xy_copy(a, axis, zz).wait_recv()
            mine[a][k] = (
                wide(mine[a][k]) + wide(full_in[a][0, zz]) + wide(full_in[a][1, zz])
            ).astype(mine[a].dtype)
            for way in range(2):
                @pl.when(zz > z if way == 0 else zz < z)
                def _():
                    @pl.when(z > 0 if way == 0 else z < line - 1)
                    def _():
                        z_copy(a, way, zz).wait_recv()
                        mine[a][k] = mine[a][k] + line_in[a][way, zz]

                    z_copy(a, way, zz).start()

            @pl.when(zz == z)
            def _():
                outs[a][...] = wide(mine[a][k])
                for way in range(2):
                    @pl.when(z > 0 if way == 0 else z < line - 1)
                    def _():
                        z_copy(a, way, zz).wait_recv()
                        outs[a][...] += wide(line_in[a][way, zz])

    def start():
        def begin_all(step, unused):
            both_ways(line - 1 - step, begin)
            return unused

        lax.fori_loop(0, line, begin_all, 0)

    def drain(zz, unused):
        for a in range(count):
            for axis in range(2):
                xy_copy(a, axis, zz).wait_send()
                if halves(a)[axis][1]:
                    d_copy(a, axis, zz).wait_send()
            c_copy(a, zz).wait_send()
            for way in range(2):
                @pl.when(zz > z if way == 0 else zz < z)
                def _():
                    z_copy(a, way, zz).wait_send()
        return unused

    def end():
        lax.fori_loop(0, line, drain, 0)

    return SimpleNamespace(
        start=start,
        first=lambda step: both_ways(line - 1 - step, first),
        second=lambda step: both_ways(line - 1 - step, second),
        third=lambda step: both_ways(line - 1 - step, third),
        end=end,
    )


def scatter_scratch(line, blocks):
    dma = pltpu.SemaphoreType.DMA
    count = len(blocks)
    return [
        *(pltpu.VMEM((line * RING, *shape), kind) for shape, kind in blocks),
        *(pltpu.VMEM((line * RING, *shape), kind) for shape, kind in blocks),
        *(pltpu.VMEM((line, *shape), kind) for shape, kind in blocks),
        *(pltpu.VMEM((2, line, *shape), kind) for shape, kind in blocks),
        *(pltpu.VMEM((2, line, *shape), kind) for shape, kind in blocks),
        *(dma((count, line)) for k in range(3)),
        *(dma((2, count, line)) for k in range(6)),
    ]


def flat_scatter_stages(line, ins, outs, scratch):
    count = len(ins)
    mine, beside_sum, line_in, half_in, full_in = (scratch[k * count : (k + 1) * count] for k in range(5))
    own_sem, c_send, c_recv, z_send, z_recv, d_send, d_recv, xy_send, xy_recv = scratch[5 * count :]
    z, q, c = place()
    beside = (across(q, 1), across(q, 2))
    corner = across(across(q, 1), 2)

    def remote(src, dst, send, recv, zz, qq, cc):
        return pltpu.make_async_remote_copy(
            src_ref=src, dst_ref=dst, send_sem=send, recv_sem=recv,
            device_id={"dp": zz * RING + qq, "pair": cc}, device_id_type=MESH,
        )

    def halves(a):
        width = outs[a].shape[-1]
        cut = width // 2 if width % 256 == 0 else width
        return (0, cut), (cut, width - cut)

    def own(a, zz):
        return pltpu.make_async_copy(ins[a].at[group_of(zz), c], mine[a].at[group_of(zz)], own_sem.at[a, zz])

    def c_copy(a, zz):
        return remote(
            ins[a].at[group_of(zz), 1 - c], beside_sum[a].at[group_of(zz)], c_send.at[a, zz], c_recv.at[a, zz],
            z, q, 1 - c,
        )

    def z_copy(a, way, zz):
        return remote(
            mine[a].at[group_of(zz)], line_in[a].at[way, group_of(zz)], z_send.at[way, a, zz],
            z_recv.at[way, a, zz], z + 1 - 2 * way, q, c,
        )

    def d_copy(a, axis):
        start, width = halves(a)[axis]
        return remote(
            mine[a].at[z * RING + corner, :, pl.ds(start, width)], half_in[a].at[:, pl.ds(start, width)],
            d_send.at[axis, a], d_recv.at[axis, a], z, beside[axis], c,
        )

    def xy_copy(a, axis):
        return remote(
            mine[a].at[z * RING + beside[axis]], full_in[a].at[axis], xy_send.at[axis, a], xy_recv.at[axis, a],
            z, beside[axis], c,
        )

    def behind(way):
        return z > 0 if way == 0 else z < line - 1

    def both_ways(g, work):
        @pl.when(z - g >= 0)
        def _():
            work(z - g)

        @pl.when(jnp.logical_and(z + g <= line - 1, g > 0))
        def _():
            work(z + g)

    def add(a, zz, part):
        def one(qq, unused):
            k = zz * RING + qq
            mine[a][k] = mine[a][k] + part[k]
            return unused

        lax.fori_loop(0, RING, one, 0)

    def begin(zz):
        for a in range(count):
            c_copy(a, zz).start()
            own(a, zz).start()

    def first(zz):
        for a in range(count):
            own(a, zz).wait()
            c_copy(a, zz).wait_recv()
            add(a, zz, beside_sum[a])
            for way in range(2):
                @pl.when(jnp.logical_and(behind(way), zz >= z if way == 0 else zz <= z))
                def _():
                    z_copy(a, way, zz).wait_recv()
                    add(a, zz, line_in[a].at[way])

                @pl.when(zz > z if way == 0 else zz < z)
                def _():
                    z_copy(a, way, zz).start()

            @pl.when(zz == z)
            def _():
                for axis in range(2):
                    if halves(a)[axis][1]:
                        d_copy(a, axis).start()

    def second():
        for a in range(count):
            for axis in range(2):
                start, width = halves(a)[axis]
                k = z * RING + beside[1 - axis]
                if width:
                    d_copy(a, axis).wait_recv()
                    mine[a][k, :, start : start + width] = (
                        mine[a][k, :, start : start + width] + half_in[a][:, start : start + width]
                    )
                xy_copy(a, 1 - axis).start()

    def third():
        for a in range(count):
            for axis in range(2):
                xy_copy(a, axis).wait_recv()
            outs[a][...] = sum(
                part.astype(jnp.float32) for part in (mine[a][z * RING + q], full_in[a][0], full_in[a][1])
            )

    def start():
        lax.fori_loop(0, line, lambda step, unused: (both_ways(line - 1 - step, begin), unused)[1], 0)

    def end():
        for a in range(count):
            for axis in range(2):
                if halves(a)[axis][1]:
                    d_copy(a, axis).wait_send()
                xy_copy(a, axis).wait_send()

            def drain(zz, unused):
                c_copy(a, zz).wait_send()
                for way in range(2):
                    @pl.when(zz > z if way == 0 else zz < z)
                    def _():
                        z_copy(a, way, zz).wait_send()
                return unused

            lax.fori_loop(0, line, drain, 0)

    return SimpleNamespace(
        start=start, first=lambda step: both_ways(line - 1 - step, first), second=second, third=third, end=end
    )


def flat_scatter_scratch(line, blocks):
    dma = pltpu.SemaphoreType.DMA
    count = len(blocks)
    return [
        *(pltpu.VMEM((line * RING, *shape), kind) for shape, kind in blocks),
        *(pltpu.VMEM((line * RING, *shape), kind) for shape, kind in blocks),
        *(pltpu.VMEM((2, line * RING, *shape), kind) for shape, kind in blocks),
        *(pltpu.VMEM(shape, kind) for shape, kind in blocks),
        *(pltpu.VMEM((2, *shape), kind) for shape, kind in blocks),
        *(dma((count, line)) for k in range(3)),
        *(dma((2, count, line)) for k in range(2)),
        *(dma((2, count)) for k in range(4)),
    ]


def peers(line):
    z, q, c = place()
    cell = q * 2 + c
    near = RING * 2

    def near_place(k):
        other = lax.rem(cell + k, near)
        return other, {"dp": z * RING + other // 2, "pair": lax.rem(other, 2)}

    def far_place(k):
        other = lax.rem(z + k, line)
        return other, {"dp": other * RING + q, "pair": c}

    def each(places, stop, work):
        def one(k, unused):
            work(*places(k))
            return unused

        lax.fori_loop(1, stop, one, 0)

    return partial(each, near_place, near), partial(each, far_place, line)


def greet_peers(line):
    barrier = pltpu.get_barrier_semaphore()
    for each in peers(line):
        each(
            lambda other, device: pl.semaphore_signal(barrier, inc=1, device_id=device, device_id_type=MESH)
        )
    pl.semaphore_wait(barrier, 2 * RING + line - 2)


def exchange_stages(line, combine, value_ref, total_ref, scratch):
    near_ref, part_ref, far_ref, n_send, n_recv, f_send, f_recv = scratch
    z, q, c = place()
    cell = q * 2 + c
    each_near, each_far = peers(line)

    def near_copy(other, device, source):
        return pltpu.make_async_remote_copy(
            src_ref=value_ref, dst_ref=near_ref.at[source], send_sem=n_send.at[other], recv_sem=n_recv.at[source],
            device_id=device, device_id_type=MESH,
        )

    def far_copy(other, device, source):
        return pltpu.make_async_remote_copy(
            src_ref=part_ref, dst_ref=far_ref.at[source], send_sem=f_send.at[other], recv_sem=f_recv.at[source],
            device_id=device, device_id_type=MESH,
        )

    def near():
        each_near(lambda other, device: near_copy(other, device, cell).start())
        near_ref[cell] = value_ref[...]

    def far():
        each_near(lambda other, device: near_copy(other, device, other).wait_recv())
        part_ref[...] = combine(near_ref, 2 * RING, 1)
        each_far(lambda other, device: far_copy(other, device, z).start())
        far_ref[z] = part_ref[...]

    def total():
        each_far(lambda other, device: far_copy(other, device, other).wait_recv())
        total_ref[...] = combine(far_ref, line, 2 * RING)

    def end():
        each_near(lambda other, device: near_copy(other, device, cell).wait_send())
        each_far(lambda other, device: far_copy(other, device, z).wait_send())

    return SimpleNamespace(near=near, far=far, total=total, end=end)


def exchange_scratch(line, shape):
    dma = pltpu.SemaphoreType.DMA
    near = 2 * RING
    return [
        pltpu.VMEM((near, *shape), jnp.float32),
        pltpu.VMEM(shape, jnp.float32),
        pltpu.VMEM((line, *shape), jnp.float32),
        dma((near,)),
        dma((near,)),
        dma((line,)),
        dma((line,)),
    ]


def exchange_kernel(line, combine, value_ref, total_ref, *scratch):
    stages = exchange_stages(line, combine, value_ref, total_ref, scratch)
    greet_peers(line)
    stages.near()
    stages.far()
    stages.total()
    stages.end()


def add_up(parts, count, weight):
    return lax.fori_loop(1, count, lambda k, total: total + parts[k], parts[0])


def pool_statistics(rows, parts, count, weight):
    mean = lax.fori_loop(1, count, lambda k, total: total + parts[k, 0], parts[0, 0]) / count

    def squares(k, total):
        offset = parts[k, 0] - mean
        return total + parts[k, 1] + (rows * weight) * (offset * offset)

    return jnp.stack([mean, lax.fori_loop(0, count, squares, jnp.zeros_like(mean))])


def exchange(value, combine, collective_id, name):
    line = lax.axis_size("dp") // RING
    vmem = pl.BlockSpec(memory_space=pltpu.VMEM)
    return pl.pallas_call(
        partial(exchange_kernel, line, combine),
        in_specs=[vmem],
        out_specs=vmem,
        out_shape=jax.ShapeDtypeStruct(value.shape, value.dtype),
        scratch_shapes=exchange_scratch(line, value.shape),
        compiler_params=pltpu.CompilerParams(collective_id=collective_id, has_side_effects=True),
        name=name,
    )(value)


KINDS = 10


def source_of(column):
    stream = column // 5
    return 2 * stream + (column - 5 * stream) // 3


def once(shape):
    return pl.BlockSpec(shape, lambda i: (0,) * len(shape), pipeline_mode=pl.Buffered(1))


def at_steps(schedule):
    step = pl.program_id(0)
    for when, work in schedule:
        @pl.when(step == when)
        def _():
            for one in work:
                one()


batch_epsilon = 1e-05


def column_at_step(step):
    turn = jnp.clip(step - 1, 0, KINDS - 1)
    return jnp.where(turn >= 7, turn - 2, jnp.where(turn >= 5, turn + 3, turn))


VECTORS = 9
CHUNKS = 4


def unpack(packed_ref, vectors_ref, bias_ref, linear_ref, planar_ref):
    devices = packed_ref.shape[0]
    bias_rows = REL_B // devices

    def row(k):
        return packed_ref[:, k, :].astype(jnp.bfloat16)

    def lined_up(k, share, first):
        lane = lax.broadcasted_iota(jnp.int32, (128, MODEL_WIDTH), 1)
        spread = (lax.broadcasted_iota(jnp.int32, (128, MODEL_WIDTH), 0) == lax.rem(lane, share)).astype(jnp.bfloat16)
        owner = lax.broadcasted_iota(jnp.int32, (devices, MODEL_WIDTH), 1) // share + first
        mine = lax.broadcasted_iota(jnp.int32, (devices, MODEL_WIDTH), 0) == owner
        whole = dot_nn(row(k), spread)
        return jnp.sum(jnp.where(mine, whole, jnp.zeros_like(whole)), axis=0, keepdims=True)

    def table(first, width, shift):
        bucket = jnp.clip(lax.broadcasted_iota(jnp.int32, (devices, width), 1) - shift, 0, REL_B - 1)
        start = lax.broadcasted_iota(jnp.int32, (devices, width), 0) * bias_rows
        total = None
        for k in range(bias_rows):
            part = dot_tn(row(first + k), (bucket == start + k).astype(jnp.bfloat16))
            total = part if total is None else total + part
        return total

    vectors_ref[...] = jnp.zeros_like(vectors_ref)
    for k in range(VECTORS):
        vectors_ref[k : k + 1, :] = lined_up(2 * bias_rows + k, MODEL_WIDTH // devices, 0)
    share = CHUNKS * MODEL_WIDTH // devices
    for k in range(CHUNKS):
        bias_ref[k] = lined_up(2 * bias_rows + VECTORS, share, k * (MODEL_WIDTH // share))
    linear = table(0, 2 * PAGE_TOKENS, PAGE_TOKENS - 1 - REL_B // 2)
    planar = table(bias_rows, SP_B, 0)
    for head in range(HEADS):
        linear_ref[head] = linear[head : head + 1, :]
        planar_ref[head] = planar[head : head + 1, :]


def forward_kernel(line, count, token_total, *refs):
    (
        features_ref, backbone_hbm, table_hbm, text_ref, hits_ref, packed_ref, weight_ref, rows_ref, cols_ref,
    ) = refs[:9]
    ins = refs[9 : 9 + count]
    (
        proj_ref, merged_ref, probs_ref, lefts_ref, start_ref, normal_ref, scale_ref, vectors_ref, bias_ref,
    ) = refs[9 + count : 18 + count]
    outs = refs[18 + count : 18 + 2 * count]
    box_ref, conv_ref, local_ref, pooled_ref, linear_ref, planar_ref = refs[18 + 2 * count : 24 + 2 * count]
    backbone_ref, table_ref, fetch_sem, *rest = refs[24 + 2 * count :]
    rows = features_ref.shape[0]
    sums = exchange_stages(line, partial(pool_statistics, float(rows)), local_ref, pooled_ref, rest[:7])
    stages = gather_stages(line, ins, outs, rest[7:])
    step = pl.program_id(0)

    def vector(k):
        return vectors_ref[k : k + 1, :]

    def hit_rows(stream):
        return jnp.broadcast_to(hits_ref[:, stream : stream + 1] == 1, (rows, MODEL_WIDTH))

    @pl.when(step == 0)
    def _():
        fetches = [
            pltpu.make_async_copy(source, target, fetch_sem.at[k])
            for k, (source, target) in enumerate(((backbone_hbm, backbone_ref), (table_hbm, table_ref)))
        ]
        for fetch in fetches:
            fetch.start()
        greet_peers(line)
        stages.start_line()
        fetches[0].wait()
        conv = dot_nn(features_ref[...], backbone_ref[...])
        mean = jnp.mean(conv, axis=0, keepdims=True)
        center = conv - mean
        conv_ref[...] = conv
        local_ref[0] = mean
        local_ref[1] = jnp.sum(center * center, axis=0, keepdims=True)
        sums.near()
        stages.start_ring()
        unpack(packed_ref, vectors_ref, bias_ref, linear_ref, planar_ref)
        make_boxes(rows_ref, cols_ref, box_ref)
        text_start = jnp.where(hit_rows(0), vector(2), text_ref[...].astype(jnp.float32))
        start_ref[...] = text_start
        lefts_ref[0] = text_start.astype(jnp.bfloat16)
        coords = lax.broadcasted_iota(jnp.int32, (rows, COORDS), 1)
        fetches[1].wait()
        for stream in range(2):
            space = None
            for axis in range(2):
                place = 2 * stream + axis
                hit = (coords == cols_ref[:, place : place + 1]).astype(jnp.bfloat16)
                part = dot_nn(hit, table_ref[:, axis * MODEL_WIDTH : (axis + 1) * MODEL_WIDTH])
                space = part if space is None else space + part
            lefts_ref[2 * stream + 1] = space.astype(jnp.bfloat16)
        sums.far()

    @pl.when(jnp.logical_and(step >= 1, step <= KINDS))
    def _():
        column = column_at_step(step)
        columns = pl.ds(pl.multiple_of(column * MODEL_WIDTH, MODEL_WIDTH), MODEL_WIDTH)
        proj_ref[:, columns] = dot_nn(lefts_ref[source_of(column)], weight_ref[...]).astype(jnp.bfloat16)

    @pl.when(step == 7)
    def _():
        sums.total()
        inverse = lax.rsqrt(pooled_ref[1] / token_total + batch_epsilon)
        normal = (conv_ref[...] - pooled_ref[0]) * inverse
        normal_ref[...] = normal
        scale_ref[...] = jnp.broadcast_to(vector(0) * inverse, scale_ref.shape)
        region_start = jnp.where(hit_rows(1), vector(3), normal * vector(0) + vector(1))
        start_ref[...] += region_start
        lefts_ref[2] = region_start.astype(jnp.bfloat16)

    @pl.when(step > KINDS)
    def _():
        attend_pair(step - 1 - KINDS, proj_ref, linear_ref, planar_ref, box_ref, merged_ref, probs_ref)

    def along(k):
        return lambda: spread(line, 3, k, 1, stages.along)

    def around(k):
        return lambda: spread(line, 4, k, 0, stages.around)

    def home(k):
        return lambda: spread(line, 4, k, 0, stages.home)

    at_steps(
        [
            (1, [along(0), around(0)]),
            (8, [along(1)]),
            (11, [around(1)]),
            (13, [along(2), home(0)]),
            (15, [around(2), home(1)]),
            (16, [around(3), home(2), home(3), sums.end, stages.end]),
        ]
    )


def forward_layer(
    features, backbone, table, text, hits, packed, weights, anchor_rows, anchor_cols, shards, token_total,
    collective_id,
):
    dp = lax.axis_size("dp")
    line = dp // RING
    count = len(shards)
    anywhere = pl.BlockSpec(memory_space=pl.ANY)
    width = weights.shape[1]
    page = (PAGE_TOKENS, MODEL_WIDTH)
    f32, bf16 = jnp.float32, jnp.bfloat16

    def pair_at(i):
        return jnp.maximum(i - 1 - KINDS, 0)

    def whole(shape):
        return pl.BlockSpec(shape, lambda i: (0,) * len(shape))

    outs = [
        ((PAGE_TOKENS, width), bf16, whole((PAGE_TOKENS, width))),
        (page, bf16, pl.BlockSpec((PAGE_TOKENS, LANES), lambda i: (0, pair_at(i)))),
        (
            (2, HEADS, PAGE_TOKENS, PAGE_TOKENS), f32,
            pl.BlockSpec((2, 2, PAGE_TOKENS, PAGE_TOKENS), lambda i: (0, pair_at(i), 0, 0)),
        ),
        ((4, *page), bf16, whole((4, *page))),
        (page, f32, whole(page)),
        (page, f32, whole(page)),
        ((8, MODEL_WIDTH), f32, whole((8, MODEL_WIDTH))),
        ((16, MODEL_WIDTH), f32, whole((16, MODEL_WIDTH))),
        ((CHUNKS, 1, MODEL_WIDTH), f32, whole((CHUNKS, 1, MODEL_WIDTH))),
        *(((2 * dp, *shard.shape), shard.dtype, anywhere) for shard in shards),
    ]
    pool = (2, 1, MODEL_WIDTH)
    return pl.pallas_call(
        partial(forward_kernel, line, count, float(token_total)),
        grid=(1 + KINDS + PAIRS,),
        in_specs=[
            once(features.shape),
            anywhere,
            anywhere,
            once(text.shape),
            once(hits.shape),
            once(packed.shape),
            pl.BlockSpec((MODEL_WIDTH, MODEL_WIDTH), lambda i: (0, column_at_step(i))),
            once(anchor_rows.shape),
            once(anchor_cols.shape),
            *[anywhere] * count,
        ],
        out_specs=[spec for shape, kind, spec in outs],
        out_shape=[jax.ShapeDtypeStruct(shape, kind) for shape, kind, spec in outs],
        scratch_shapes=[
            pltpu.VMEM((2, PAGE_TOKENS, PAGE_TOKENS), jnp.int32),
            pltpu.VMEM(page, f32),
            pltpu.VMEM(pool, f32),
            pltpu.VMEM(pool, f32),
            pltpu.VMEM((HEADS, 1, 2 * PAGE_TOKENS), f32),
            pltpu.VMEM((HEADS, 1, SP_B), f32),
            pltpu.VMEM(backbone.shape, bf16),
            pltpu.VMEM(table.shape, bf16),
            pltpu.SemaphoreType.DMA((2,)),
            *exchange_scratch(line, pool),
            *gather_sems(line, count),
        ],
        compiler_params=pltpu.CompilerParams(
            collective_id=collective_id, has_side_effects=True, vmem_limit_bytes=62 << 20
        ),
        name="forward_layer",
    )(
        features, backbone, table, text, hits, packed, weights, anchor_rows, anchor_cols, *shards,
    )


TABLE_STEP = PAIRS + KINDS


def backward_kernel(line, count, *refs):
    (
        proj_ref, probs_ref, upstream_ref, rows_ref, cols_ref, lefts_ref, weight_ref, mixer_grad_ref, normal_ref,
        hits_ref,
    ) = refs[:10]
    ins = refs[10 : 10 + count]
    (
        linear_ref, planar_ref, weight_grad_ref, table_grad_ref, text_grad_ref, region_grad_ref, sums_ref,
    ) = refs[10 + count : 17 + count]
    outs = refs[17 + count : 17 + 2 * count]
    grad_ref, turned_left_ref, input_grad_ref = refs[17 + 2 * count : 20 + 2 * count]
    helpers = refs[20 + 2 * count : 24 + 2 * count]
    stages = scatter_stages(line, ins, outs, refs[24 + 2 * count :])
    step = pl.program_id(0)

    @pl.when(step == 0)
    def _():
        greet(line)
        stages.start()
        make_places(rows_ref, cols_ref, *helpers)
        spread(line, 4, 0, 0, stages.first)

    def first(k):
        return lambda: spread(line, 4, k, 0, stages.first)

    def second(k):
        return lambda: spread(line, 4, k, 0, stages.second)

    def third(k):
        return lambda: spread(line, 4, k, 0, stages.third)

    slots = {
        1: [first(1)],
        5: [second(0)],
        6: [first(2)],
        8: [first(3)],
        10: [second(1)],
        15: [third(0)],
        19: [second(2)],
        21: [second(3)],
    }

    def pump(sub):
        at_steps([(slot // 4, work) for slot, work in slots.items() if slot % 4 == sub])

    @pl.when(step < PAIRS)
    def _():
        attend_back_pair(step, pump, proj_ref, probs_ref, upstream_ref, grad_ref, linear_ref, planar_ref, *helpers)

    @pl.when(jnp.logical_and(step >= PAIRS, step < TABLE_STEP))
    def _():
        column = step - PAIRS
        source = source_of(column)
        fresh = jnp.logical_or(column == 0, source != source_of(jnp.maximum(column - 1, 0)))
        grads = grad_ref[:, pl.ds(pl.multiple_of(column * MODEL_WIDTH, MODEL_WIDTH), MODEL_WIDTH)]

        @pl.when(fresh)
        def _():
            turned_left_ref[...] = lefts_ref[source].T

        weight_grad_ref[...] = dot_nn(turned_left_ref[...], grads).astype(jnp.bfloat16)
        back = dot_nt(grads, weight_ref[...])

        @pl.when(fresh)
        def _():
            input_grad_ref[source] = back

        @pl.when(jnp.logical_not(fresh))
        def _():
            input_grad_ref[source] += back

    @pl.when(step >= TABLE_STEP)
    def _():
        axis = step - TABLE_STEP
        coords = lax.broadcasted_iota(jnp.int32, (COORDS, PAGE_TOKENS), 0)
        total = None
        for stream in range(2):
            hit = (coords == rows_ref[pl.ds(2 * stream + axis, 1), :]).astype(jnp.bfloat16)
            part = dot_nn(hit, input_grad_ref[2 * stream + 1].astype(jnp.bfloat16))
            total = part if total is None else total + part
        table_grad_ref[...] = total.astype(jnp.bfloat16)

    @pl.when(step == TABLE_STEP + 1)
    def _():
        mixer_grad = mixer_grad_ref[...]
        sums_ref[...] = jnp.zeros_like(sums_ref)
        for stream, out_ref in enumerate((text_grad_ref, region_grad_ref)):
            grad = mixer_grad + input_grad_ref[2 * stream]
            hit = jnp.broadcast_to(hits_ref[:, stream : stream + 1] == 1, grad.shape)
            zero = jnp.zeros_like(grad)
            kept = jnp.where(hit, zero, grad)
            out_ref[...] = kept
            sums_ref[stream : stream + 1, :] = jnp.sum(jnp.where(hit, grad, zero), axis=0, keepdims=True)
            if stream == 1:
                sums_ref[2:3, :] = jnp.sum(kept, axis=0, keepdims=True)
                sums_ref[3:4, :] = jnp.sum(kept * normal_ref[...], axis=0, keepdims=True)

    at_steps(
        [(PAIRS, [third(1)]), (PAIRS + 7, [third(2)]), (TABLE_STEP + 1, [third(3), stages.end])]
    )


def backward_layer(
    proj, probs, upstream, anchor_rows, anchor_cols, lefts, weights, mixer_grad, normal, hits, grads, collective_id
):
    dp = lax.axis_size("dp")
    line = dp // RING
    count = len(grads)
    blocks = [(grad.shape[1:], grad.dtype) for grad in grads]
    anywhere = pl.BlockSpec(memory_space=pl.ANY)
    page = (PAGE_TOKENS, MODEL_WIDTH)

    def pair_at(i):
        return jnp.minimum(i, PAIRS - 1)

    def column_at(i):
        return jnp.clip(i - PAIRS, 0, KINDS - 1)

    return pl.pallas_call(
        partial(backward_kernel, line, count),
        grid=(TABLE_STEP + 2,),
        in_specs=[
            once(proj.shape),
            pl.BlockSpec((2, 2, PAGE_TOKENS, PAGE_TOKENS), lambda i: (0, pair_at(i), 0, 0)),
            pl.BlockSpec((PAGE_TOKENS, LANES), lambda i: (0, pair_at(i))),
            once(anchor_rows.shape),
            once(anchor_cols.shape),
            once(lefts.shape),
            pl.BlockSpec((MODEL_WIDTH, MODEL_WIDTH), lambda i: (0, column_at(i))),
            once(page),
            once(page),
            once(hits.shape),
            *[anywhere] * count,
        ],
        out_specs=[
            pl.BlockSpec((HEADS, 1, 2 * PAGE_TOKENS), lambda i: (0, 0, 0)),
            pl.BlockSpec((HEADS, 1, SP_B), lambda i: (0, 0, 0)),
            pl.BlockSpec((MODEL_WIDTH, MODEL_WIDTH), lambda i: (0, column_at(i))),
            pl.BlockSpec((COORDS, MODEL_WIDTH), lambda i: (0, jnp.maximum(i - TABLE_STEP, 0))),
            pl.BlockSpec(page, lambda i: (0, 0)),
            pl.BlockSpec(page, lambda i: (0, 0)),
            pl.BlockSpec((8, MODEL_WIDTH), lambda i: (0, 0)),
            *(pl.BlockSpec(shape, lambda i: (0, 0)) for shape, kind in blocks),
        ],
        out_shape=[
            jax.ShapeDtypeStruct((HEADS, 1, 2 * PAGE_TOKENS), jnp.float32),
            jax.ShapeDtypeStruct((HEADS, 1, SP_B), jnp.float32),
            jax.ShapeDtypeStruct(weights.shape, jnp.bfloat16),
            jax.ShapeDtypeStruct((COORDS, 2 * MODEL_WIDTH), jnp.bfloat16),
            jax.ShapeDtypeStruct(page, jnp.float32),
            jax.ShapeDtypeStruct(page, jnp.float32),
            jax.ShapeDtypeStruct((8, MODEL_WIDTH), jnp.float32),
            *(jax.ShapeDtypeStruct(shape, jnp.float32) for shape, kind in blocks),
        ],
        scratch_shapes=[
            pltpu.VMEM(proj.shape, jnp.bfloat16),
            pltpu.VMEM((MODEL_WIDTH, PAGE_TOKENS), jnp.bfloat16),
            pltpu.VMEM((4, *page), jnp.float32),
            pltpu.VMEM((2, 4 * PAGE_TOKENS, SP_B), jnp.bfloat16),
            pltpu.VMEM((2, 128, PAGE_TOKENS), jnp.bfloat16),
            pltpu.VMEM((2, 4, PAGE_TOKENS, PAGE_TOKENS), jnp.bfloat16),
            pltpu.VMEM((PAGE_TOKENS, PAGE_TOKENS), jnp.bfloat16),
            *scatter_scratch(line, blocks),
        ],
        compiler_params=pltpu.CompilerParams(
            collective_id=collective_id, has_side_effects=True, vmem_limit_bytes=63 << 20
        ),
        name="backward_layer",
    )(
        proj, probs, upstream, anchor_rows, anchor_cols, lefts, weights, mixer_grad, normal, hits,
        *(grad.reshape(line * RING, 2, *grad.shape[1:]) for grad in grads),
    )


def last_kernel(line, count, token_total, *refs):
    sums_ref, kept_ref, normal_ref, scale_ref, features_hbm, backbone_hbm = refs[:6]
    ins = refs[6 : 7 + count]
    feature_grad_ref, total_ref = refs[7 + count : 9 + count]
    outs = refs[9 + count : 11 + 2 * count]
    turned_ref, conv_grad_ref, late_ref = refs[11 + 2 * count : 14 + 2 * count]
    rest = refs[14 + 2 * count :]
    features_ref, backbone_ref, fetch_sem, local_ref, *rest = rest
    sums = exchange_stages(line, add_up, local_ref, total_ref, rest[:7])
    stop = 7 + 5 * count + 9
    early = scatter_stages(line, ins[:count], outs[:count], rest[7:stop])
    late = scatter_stages(line, [late_ref], outs[count : count + 1], rest[stop : stop + 14])
    flat = flat_scatter_stages(line, ins[count:], outs[count + 1 :], rest[stop + 14 :])
    share = late_ref.shape[2]

    def first(stages, k):
        spread(line, 4, k, 0, stages.first)

    def second(stages, k):
        spread(line, 4, k, 0, stages.second)

    def third(stages, k):
        spread(line, 4, k, 0, stages.third)

    fetches = [
        pltpu.make_async_copy(source, target, fetch_sem.at[k])
        for k, (source, target) in enumerate(((features_hbm, features_ref), (backbone_hbm, backbone_ref)))
    ]
    greet_peers(line)
    local_ref[...] = sums_ref[2:4, :]
    sums.near()
    flat.start()
    early.start()
    for fetch in fetches:
        fetch.start()
    sums.far()
    first(flat, 0)
    first(early, 0)
    first(early, 1)
    sums.total()
    conv_grad_ref[...] = (
        scale_ref[0:1, :]
        * (kept_ref[...] - total_ref[0:1, :] / token_total - normal_ref[...] * (total_ref[1:2, :] / token_total))
    ).astype(jnp.bfloat16)
    second(early, 0)
    first(flat, 1)
    first(early, 2)
    first(early, 3)

    for fetch in fetches:
        fetch.wait()

    def turn(k, unused):
        columns = pl.ds(pl.multiple_of(k * 512, 512), 512)
        turned_ref[columns, :] = features_ref[:, columns].T
        return unused

    lax.fori_loop(0, features_ref.shape[1] // 512, turn, 0)
    width = min(512, 2 * share * line * RING)

    def backbone(k, unused):
        rows = pl.ds(pl.multiple_of(k * width, width), width)
        block = dot_nn(turned_ref[rows, :], conv_grad_ref[...])
        places = width // (2 * share)
        late_ref[pl.ds(k * places, places)] = block.reshape(places, 2, share, MODEL_WIDTH).astype(jnp.bfloat16)
        return unused

    lax.fori_loop(0, features_ref.shape[1] // width, backbone, 0)
    late.start()
    for k in range(4):
        first(late, k)
    first(flat, 2)
    second(early, 1)
    third(early, 0)

    def feature(k, unused):
        columns = pl.ds(pl.multiple_of(k * 512, 512), 512)
        feature_grad_ref[:, columns] = dot_nt(conv_grad_ref[...], backbone_ref[columns, :])
        return unused

    lax.fori_loop(0, features_ref.shape[1] // 512, feature, 0)
    first(flat, 3)
    for k in range(4):
        second(late, k)
    second(early, 2)
    flat.second()
    second(early, 3)
    third(early, 1)
    third(late, 0)
    third(late, 1)
    third(early, 2)
    third(late, 2)
    flat.third()
    third(early, 3)
    third(late, 3)
    sums.end()
    early.end()
    late.end()
    flat.end()


def last_layer(
    sums, kept, normal, scale, features, backbone, grads, flat_grad, token_total, collective_id
):
    dp = lax.axis_size("dp")
    line = dp // RING
    count = len(grads)
    blocks = [(grad.shape[1:], grad.dtype) for grad in grads]
    flat = [(flat_grad.shape[1:], flat_grad.dtype)]
    pair = (2, MODEL_WIDTH)
    channels = backbone.shape[0]
    late = [((channels // (2 * dp), MODEL_WIDTH), jnp.bfloat16)]
    anywhere = pl.BlockSpec(memory_space=pl.ANY)
    vmem = pl.BlockSpec(memory_space=pltpu.VMEM)
    return pl.pallas_call(
        partial(last_kernel, line, count, float(token_total)),
        in_specs=[*[vmem] * 4, *[anywhere] * (count + 3)],
        out_specs=[vmem] * (4 + count),
        out_shape=[
            jax.ShapeDtypeStruct(features.shape, jnp.float32),
            jax.ShapeDtypeStruct(pair, jnp.float32),
            *(jax.ShapeDtypeStruct(shape, jnp.float32) for shape, kind in blocks + late + flat),
        ],
        scratch_shapes=[
            pltpu.VMEM((channels, PAGE_TOKENS), jnp.bfloat16),
            pltpu.VMEM(kept.shape, jnp.bfloat16),
            pltpu.VMEM((dp, 2, *late[0][0]), jnp.bfloat16),
            pltpu.VMEM(features.shape, jnp.bfloat16),
            pltpu.VMEM(backbone.shape, jnp.bfloat16),
            pltpu.SemaphoreType.DMA((2,)),
            pltpu.VMEM(pair, jnp.float32),
            *exchange_scratch(line, pair),
            *scatter_scratch(line, blocks),
            *scatter_scratch(line, late),
            *flat_scatter_scratch(line, flat),
        ],
        compiler_params=pltpu.CompilerParams(
            collective_id=collective_id, has_side_effects=True, vmem_limit_bytes=63 << 20
        ),
        name="last_layer",
    )(
        sums, kept, normal, scale, features, backbone,
        *(grad.reshape(line * RING, 2, *grad.shape[1:]) for grad in [*grads, flat_grad]),
    )


def finish_kernel(count, share, expand_share, bias_rows, *refs):
    ins = refs[:count]
    small_ref, total_ref = refs[count : count + 2]
    outs = refs[count + 2 : 2 * count + 2]
    small_outs = refs[2 * count + 2 : 2 * count + 14]
    staged = refs[2 * count + 14 : 2 * count + 26]
    sems, small_sems = refs[2 * count + 26 :]
    copies = [pltpu.make_async_copy(ins[k], outs[k], sems.at[k]) for k in range(count)]
    for copy in copies:
        copy.start()
    staged[0][...] = small_ref[:bias_rows, :HEADS]
    staged[1][...] = small_ref[bias_rows : 2 * bias_rows, :HEADS]
    for k in range(7):
        staged[2 + k][...] = small_ref[2 * bias_rows + k : 2 * bias_rows + k + 1, :share]
    staged[9][...] = small_ref[2 * bias_rows + 7 : 2 * bias_rows + 8, :expand_share]
    owner = (lax.axis_index("dp") * 2 + lax.axis_index("pair")) * share
    chosen = lax.broadcasted_iota(jnp.int32, (MODEL_WIDTH, 128), 0) == (
        lax.broadcasted_iota(jnp.int32, (MODEL_WIDTH, 128), 1) + owner
    )
    owned = lax.dot_general(
        total_ref[...], chosen.astype(jnp.float32), (((1,), (0,)), ((), ())),
        precision=lax.Precision.HIGHEST, preferred_element_type=jnp.float32,
    )
    for k in range(2):
        staged[10 + k][...] = owned[k : k + 1, :share]
    small_copies = [pltpu.make_async_copy(staged[k], small_outs[k], small_sems.at[k]) for k in range(12)]
    for copy in small_copies:
        copy.start()
    for copy in copies + small_copies:
        copy.wait()


def finish(arrays, small, totals, share, expand_share, bias_rows):
    count = len(arrays)
    anywhere = pl.BlockSpec(memory_space=pl.ANY)
    vmem = pl.BlockSpec(memory_space=pltpu.VMEM)
    shapes = [(bias_rows, HEADS)] * 2 + [(1, share)] * 7 + [(1, expand_share)] + [(1, share)] * 2
    return pl.pallas_call(
        partial(finish_kernel, count, share, expand_share, bias_rows),
        in_specs=[vmem] * (count + 2),
        out_specs=[anywhere] * (count + 12),
        out_shape=[
            *(jax.ShapeDtypeStruct(array.shape, array.dtype) for array in arrays),
            *(jax.ShapeDtypeStruct(shape, jnp.float32) for shape in shapes),
        ],
        scratch_shapes=[
            *(pltpu.VMEM(shape, jnp.float32) for shape in shapes),
            pltpu.SemaphoreType.DMA((count,)),
            pltpu.SemaphoreType.DMA((12,)),
        ],
        name="finish",
    )(*arrays, small, totals)


norm_epsilon = 1e-05


def normal_parts(values):
    center = values - jnp.mean(values, axis=-1, keepdims=True)
    inverse = lax.rsqrt(jnp.mean(center * center, axis=-1, keepdims=True) + norm_epsilon)
    return center * inverse, inverse


def normal_back(normal, inverse, gain, grad):
    scaled = grad * gain
    return inverse * (
        scaled
        - jnp.mean(scaled, axis=-1, keepdims=True)
        - normal * jnp.mean(scaled * normal, axis=-1, keepdims=True)
    )


def mixer_kernel(
    merged_ref, start_ref, cotangent_ref, vectors_ref, bias_ref, merge_ref, expand_ref, reduce_ref,
    output_ref, mixer_grad_ref, merged_grad_ref, merge_grad_ref, expand_grad_ref, reduce_grad_ref, sums_ref,
    bias_grad_ref,
    hidden_ref, normal_ref, inverse_ref, low_ref, active_ref, slope_ref, dense_ref, grad_ref, grad_low_ref,
    turned_ref,
):
    step = pl.program_id(0)
    chunk = lax.rem(step, CHUNKS)
    width = expand_ref.shape[1] // CHUNKS
    part = pl.ds(pl.multiple_of(chunk * width, width), width)

    def vector(k):
        return vectors_ref[k : k + 1, :]

    def column_sum(values):
        return jnp.sum(values, axis=0, keepdims=True)

    @pl.when(step == 0)
    def _():
        normal, inverse = normal_parts(start_ref[...] + dot_nn(merged_ref[...], merge_ref[...]))
        normal_ref[...] = normal
        inverse_ref[...] = jnp.broadcast_to(inverse, inverse_ref.shape)
        hidden = normal * vector(4) + vector(5)
        hidden_ref[...] = hidden
        low_ref[...] = hidden.astype(jnp.bfloat16)
        dense_ref[...] = jnp.zeros_like(dense_ref)

    @pl.when(step < CHUNKS)
    def _():
        inner = dot_nn(low_ref[...], expand_ref[:, part]) + bias_ref[chunk]
        share = 0.5 + 0.5 * lax.erf(inner * (0.5**0.5))
        active = (inner * share).astype(jnp.bfloat16)
        active_ref[chunk] = active
        slope_ref[chunk] = share + inner * jnp.exp(-0.5 * inner * inner) * (2.0 * jnp.pi) ** -0.5
        dense_ref[...] += dot_nn(active, reduce_ref[part, :])

    @pl.when(step == CHUNKS - 1)
    def _():
        normal, inverse = normal_parts(hidden_ref[...] + (dense_ref[...] + vector(6)))
        output_ref[...] = (normal * vector(7) + vector(8)).astype(jnp.bfloat16)
        upstream = cotangent_ref[...].astype(jnp.float32)
        grad = normal_back(normal, inverse, vector(7), upstream)
        grad_ref[...] = grad
        grad_low_ref[...] = grad.astype(jnp.bfloat16)
        sums_ref[2:3, :] = column_sum(grad)
        sums_ref[3:4, :] = column_sum(upstream * normal)
        sums_ref[4:5, :] = column_sum(upstream)
        turned_ref[...] = low_ref[...].T

    @pl.when(step >= CHUNKS)
    def _():
        grad_low = grad_low_ref[...]
        reduce_grad_ref[...] = dot_tn(active_ref[chunk], grad_low).astype(jnp.bfloat16)
        inner_low = (dot_nt(grad_low, reduce_ref[part, :]) * slope_ref[chunk]).astype(jnp.bfloat16)
        bias_grad_ref[chunk] = column_sum(inner_low.astype(jnp.float32))
        expand_grad_ref[...] = dot_nn(turned_ref[...], inner_low).astype(jnp.bfloat16)
        grad_ref[...] += dot_nt(inner_low, expand_ref[:, part])

    @pl.when(step == 2 * CHUNKS - 1)
    def _():
        grad = grad_ref[...]
        normal = normal_ref[...]
        mixer_grad = normal_back(normal, inverse_ref[:, :1], vector(4), grad)
        mixer_grad_ref[...] = mixer_grad
        sums_ref[0:1, :] = column_sum(grad * normal)
        sums_ref[1:2, :] = column_sum(grad)
        low = mixer_grad.astype(jnp.bfloat16)
        merge_grad_ref[...] = dot_tn(merged_ref[...], low).astype(jnp.bfloat16)
        merged_grad_ref[...] = dot_nt(low, merge_ref[...]).astype(jnp.bfloat16)


def mixer_layer(merged, start, cotangent, vectors, bias, w_merge, w_expand, w_reduce):
    rows = merged.shape[0]
    inner = w_expand.shape[1]
    width = inner // CHUNKS
    page = (rows, MODEL_WIDTH)

    def back_at(i):
        return jnp.maximum(i - CHUNKS, 0)

    def whole(shape):
        return pl.BlockSpec(shape, lambda i: (0,) * len(shape))

    f32, bf16 = jnp.float32, jnp.bfloat16
    outs = [
        (page, bf16, whole(page)),
        (page, f32, whole(page)),
        (page, bf16, whole(page)),
        ((MODEL_WIDTH, MODEL_WIDTH), bf16, whole((MODEL_WIDTH, MODEL_WIDTH))),
        ((MODEL_WIDTH, inner), bf16, pl.BlockSpec((MODEL_WIDTH, width), lambda i: (0, back_at(i)))),
        ((inner, MODEL_WIDTH), bf16, pl.BlockSpec((width, MODEL_WIDTH), lambda i: (back_at(i), 0))),
        ((8, MODEL_WIDTH), f32, whole((8, MODEL_WIDTH))),
        ((CHUNKS, 1, width), f32, whole((CHUNKS, 1, width))),
    ]
    return pl.pallas_call(
        mixer_kernel,
        grid=(2 * CHUNKS,),
        in_specs=[
            once(page),
            once(page),
            once(page),
            once(vectors.shape),
            once(bias.shape),
            once(w_merge.shape),
            once(w_expand.shape),
            once(w_reduce.shape),
        ],
        out_specs=[spec for shape, kind, spec in outs],
        out_shape=[jax.ShapeDtypeStruct(shape, kind) for shape, kind, spec in outs],
        scratch_shapes=[
            pltpu.VMEM(page, f32),
            pltpu.VMEM(page, f32),
            pltpu.VMEM((rows, 128), f32),
            pltpu.VMEM(page, bf16),
            pltpu.VMEM((CHUNKS, rows, width), bf16),
            pltpu.VMEM((CHUNKS, rows, width), f32),
            pltpu.VMEM(page, f32),
            pltpu.VMEM(page, f32),
            pltpu.VMEM(page, bf16),
            pltpu.VMEM((MODEL_WIDTH, rows), bf16),
        ],
        compiler_params=pltpu.CompilerParams(vmem_limit_bytes=62 << 20),
        name="mixer_layer",
    )(merged, start, cotangent, vectors, bias, w_merge, w_expand, w_reduce)

AXES = ("dp", "pair")


def padded_rows(pieces):
    total = sum(piece.shape[0] for piece in pieces)
    rows = -(-total // 8) * 8
    whole = jnp.zeros((rows, 128), jnp.float32)
    start = 0
    for piece in pieces:
        stop = start + piece.shape[0]
        whole += jnp.pad(piece.astype(jnp.float32), ((start, rows - stop), (0, 128 - piece.shape[1])))
        start = stop
    return whole


def blocks_of(grad, devices):
    blocks = grad.astype(jnp.bfloat16).reshape(devices, grad.shape[0] // devices, grad.shape[1])
    return blocks if blocks.shape[1] % 8 == 0 else blocks.reshape(devices, -1, 128)


def per_device(
    text_inputs,
    region_features,
    text_masked,
    region_masked,
    text_anchors,
    region_anchors,
    backbone_weight,
    batch_gain,
    batch_shift,
    text_blank,
    region_blank,
    position_table,
    stream_weights,
    linear_bias,
    planar_bias,
    merge_weight,
    mixer_gain,
    mixer_shift,
    expand_weight,
    expand_bias,
    reduce_weight,
    reduce_bias,
    output_gain,
    output_shift,
    cotangent,
):
    devices = lax.axis_size(AXES)
    row_count = text_inputs.shape[0]
    token_total = row_count * devices
    share = MODEL_WIDTH // devices
    expand_share = expand_bias.shape[0]
    bias_rows = REL_B // devices
    vectors = (
        batch_gain, batch_shift, text_blank, region_blank, mixer_gain, mixer_shift, reduce_bias,
        output_gain, output_shift, expand_bias,
    )
    small = padded_rows([linear_bias, planar_bias, *(vector[None, :] for vector in vectors)])
    packed, w_backbone, w_stream, w_table = gather_all(
        (small, backbone_weight, stream_weights), (position_table,), 0
    )
    w_backbone, w_table, w_stream = (
        whole.reshape(-1, whole.shape[-1]) for whole in (w_backbone, w_table, w_stream)
    )

    anchor_rows = jnp.concatenate([text_anchors, region_anchors], axis=0)
    anchor_cols = anchor_rows.T
    hits = jnp.stack([text_masked, region_masked], axis=1)
    proj, merged_low, probs, lefts, start_sum, normal_feat, batch_scale, w_vectors, w_expand_bias, *wholes = forward_layer(
        region_features, w_backbone, w_table, text_inputs, hits, packed, w_stream, anchor_rows, anchor_cols,
        (merge_weight, expand_weight, reduce_weight), token_total, 4,
    )
    w_merge, w_expand, w_reduce = (whole.reshape(-1, whole.shape[-1]) for whole in wholes)
    (
        layer_output, mixer_in_grad, merged_grad, merge_weight_grad, expand_weight_grad, reduce_weight_grad,
        mixer_sums, expand_bias_grad,
    ) = mixer_layer(
        merged_low, start_sum, cotangent, w_vectors, w_expand_bias,
        w_merge, w_expand, w_reduce,
    )
    early = (expand_weight_grad, reduce_weight_grad, merge_weight_grad)
    (
        linear_sums, planar_sums, stream_weights_grad, position_table_grad, text_gradient, region_kept,
        start_sums, *early_shares,
    ) = backward_layer(
        proj, probs, merged_grad, anchor_rows, anchor_cols, lefts, w_stream, mixer_in_grad, normal_feat, hits,
        [blocks_of(grad, devices) for grad in early], 5,
    )
    vector_grads = jnp.concatenate([start_sums[:2], mixer_sums[:5]], axis=0)
    pieces = [
        linear_folded(linear_sums[:, 0]).T.reshape(devices, bias_rows, HEADS),
        planar_sums[:, 0].T.reshape(devices, bias_rows, HEADS),
        vector_grads.reshape(7, devices, share).transpose(1, 0, 2),
        expand_bias_grad.reshape(devices, 1, expand_share),
    ]
    rows = sum(piece.shape[1] for piece in pieces)
    pieces = [jnp.pad(piece, ((0, 0), (0, 0), (0, 128 - piece.shape[2]))) for piece in pieces]
    small_grads = jnp.pad(jnp.concatenate(pieces, axis=1), ((0, 0), (0, -rows % 8), (0, 0)))
    feature_gradient, totals, small, stream_share, backbone_weight_grad, table_share = last_layer(
        start_sums, region_kept, normal_feat, batch_scale, region_features, w_backbone,
        [small_grads, blocks_of(stream_weights_grad, devices)], blocks_of(position_table_grad, devices),
        token_total, 1,
    )
    arrays = (
        text_gradient, feature_gradient, backbone_weight_grad, table_share, stream_share, *early_shares,
    )
    (
        text_gradient, feature_gradient, backbone_weight_grad, table_share, stream_share, expand_share_grad,
        reduce_share_grad, merge_share_grad, linear_grad, planar_grad, *vector_grads,
    ) = finish(arrays, small, totals, share, expand_share, bias_rows)
    vector_grads = [grad.reshape(-1) for grad in vector_grads]
    return (
        layer_output,
        text_gradient,
        feature_gradient,
        backbone_weight_grad,
        vector_grads[9],
        vector_grads[8],
        vector_grads[0],
        vector_grads[1],
        table_share.reshape(-1, position_table.shape[1]),
        stream_share.reshape(-1, stream_weights.shape[1]),
        linear_grad,
        planar_grad,
        merge_share_grad.reshape(-1, MODEL_WIDTH),
        vector_grads[2],
        vector_grads[3],
        expand_share_grad.reshape(-1, expand_weight.shape[1]),
        vector_grads[7],
        reduce_share_grad.reshape(-1, MODEL_WIDTH),
        vector_grads[4],
        vector_grads[5],
        vector_grads[6],
    )

def solution(mesh):
    in_specs = (
        P(("dp", "pair"), None),
        P(("dp", "pair"), None),
        P(("dp", "pair")),
        P(("dp", "pair")),
        P(None, ("dp", "pair")),
        P(None, ("dp", "pair")),
        P(("dp", "pair"), None),
        P(("dp", "pair")),
        P(("dp", "pair")),
        P(("dp", "pair")),
        P(("dp", "pair")),
        P(("dp", "pair"), None),
        P(("dp", "pair"), None),
        P(("dp", "pair"), None),
        P(("dp", "pair"), None),
        P(("dp", "pair"), None),
        P(("dp", "pair")),
        P(("dp", "pair")),
        P(("dp", "pair"), None),
        P(("dp", "pair")),
        P(("dp", "pair"), None),
        P(("dp", "pair")),
        P(("dp", "pair")),
        P(("dp", "pair")),
        P(("dp", "pair"), None),
    )
    out_specs = (
        P(("dp", "pair"), None),
        P(("dp", "pair"), None),
        P(("dp", "pair"), None),
        P(("dp", "pair"), None),
        P(("dp", "pair")),
        P(("dp", "pair")),
        P(("dp", "pair")),
        P(("dp", "pair")),
        P(("dp", "pair"), None),
        P(("dp", "pair"), None),
        P(("dp", "pair"), None),
        P(("dp", "pair"), None),
        P(("dp", "pair"), None),
        P(("dp", "pair")),
        P(("dp", "pair")),
        P(("dp", "pair"), None),
        P(("dp", "pair")),
        P(("dp", "pair"), None),
        P(("dp", "pair")),
        P(("dp", "pair")),
        P(("dp", "pair")),
    )
    return jax.shard_map(
        per_device, mesh=mesh, in_specs=in_specs, out_specs=out_specs, check_vma=False
    )
```

```python
from functools import partial
from types import SimpleNamespace

import jax
import jax.numpy as jnp
from jax import lax
from jax.experimental import pallas as pl
from jax.experimental.pallas import tpu as pltpu
from jax.sharding import PartitionSpec as P

HEADS = 12
HEAD_DIM = 64
COORDS = 1024
REL_B = 256
SP_SIDE = 16
PAGE_TOKENS = 256
MODEL_WIDTH = 768
SP_B = 256
COORD_STEP = 128
PAIRS = HEADS // 2
LANES = 2 * HEAD_DIM


def dot_nt(left, right):
    return lax.dot_general(left, right, (((1,), (1,)), ((), ())), preferred_element_type=jnp.float32)


def dot_tn(left, right):
    return lax.dot_general(left, right, (((0,), (0,)), ((), ())), preferred_element_type=jnp.float32)


def dot_nn(left, right):
    return lax.dot_general(left, right, (((1,), (0,)), ((), ())), preferred_element_type=jnp.float32)


def head_columns(stream, kind, pair):
    return pl.ds(pl.multiple_of(((5 * stream + kind) * PAIRS + pair) * LANES, LANES), LANES)


def make_boxes(rows_ref, cols_ref, box_ref):
    for stream in range(2):
        part = []
        for axis in range(2):
            along = rows_ref[2 * stream + axis : 2 * stream + axis + 1, :]
            down = cols_ref[:, 2 * stream + axis : 2 * stream + axis + 1]
            part.append(((along - down) >> 7) + SP_SIDE // 2)
        box_ref[stream] = part[0] * SP_SIDE + part[1]


def attend_pair(pair, proj_ref, linear_ref, planar_ref, box_ref, merged_ref, probs_ref):
    lane_head = lax.broadcasted_iota(jnp.int32, (PAGE_TOKENS, LANES), 1) // HEAD_DIM
    mixed = [None, None]
    for inner in range(2):
        head = 2 * pair + inner
        mine = lane_head == inner
        spread = jnp.broadcast_to(linear_ref[head], (PAGE_TOKENS, 2 * PAGE_TOKENS))
        linear_term = pltpu.roll(spread, PAGE_TOKENS + 1, 1, stride=1, stride_axis=0)[:, :PAGE_TOKENS]
        low_table = jnp.broadcast_to(planar_ref[head, :, :128], (PAGE_TOKENS, 128))
        high_table = jnp.broadcast_to(planar_ref[head, :, 128:], (PAGE_TOKENS, 128))
        total = None
        for stream in range(2):
            pieces = [proj_ref[:, head_columns(stream, kind, pair)] for kind in range(5)]
            zero = jnp.zeros_like(pieces[0])
            left = jnp.concatenate([jnp.where(mine, pieces[0], zero), jnp.where(mine, pieces[3], zero)], axis=1)
            right = jnp.concatenate([pieces[1], pieces[4]], axis=1)
            logits = dot_nt(left, right) * HEAD_DIM ** (-0.5)
            planar = []
            for half in range(2):
                box = box_ref[stream, :, 128 * half : 128 * half + 128]
                place = box & 127
                planar.append(
                    jnp.where(
                        box < 128,
                        jnp.take_along_axis(low_table, place, axis=1),
                        jnp.take_along_axis(high_table, place, axis=1),
                    )
                )
            logits = logits + linear_term + jnp.concatenate(planar, axis=1)
            top = jnp.max(logits, axis=-1, keepdims=True)
            shifted = jnp.exp(logits - top)
            probs = shifted / jnp.sum(shifted, axis=-1, keepdims=True)
            probs_ref[stream, inner] = probs
            part = dot_nn(probs.astype(jnp.bfloat16), pieces[2])
            total = part if total is None else total + part
        mixed[inner] = total
    merged_ref[...] = jnp.where(lane_head == 0, mixed[0], mixed[1]).astype(jnp.bfloat16)


def make_places(rows_ref, cols_ref, place_ref, turned_ref, mask_ref, flip_ref):
    lanes = lax.broadcasted_iota(jnp.int32, (PAGE_TOKENS, SP_B), 1)
    rows = lax.broadcasted_iota(jnp.int32, (PAGE_TOKENS, SP_B), 0)
    flip_ref[...] = (lanes + rows == PAGE_TOKENS - 1).astype(jnp.bfloat16)
    for stream in range(2):
        x_row = rows_ref[2 * stream : 2 * stream + 1, :]
        y_row = rows_ref[2 * stream + 1 : 2 * stream + 2, :]
        x_col = cols_ref[:, 2 * stream : 2 * stream + 1]
        y_col = cols_ref[:, 2 * stream + 1 : 2 * stream + 2]
        cell_row = (x_row >> 7) * SP_SIDE + (y_row >> 7)
        cell_col = (x_col >> 7) * SP_SIDE + (y_col >> 7)
        x_less = ((x_row & 127) < (x_col & 127)).astype(jnp.float32)
        y_less = ((y_row & 127) < (y_col & 127)).astype(jnp.float32)
        for x_side in range(2):
            for y_side in range(2):
                side = 2 * x_side + y_side
                place_ref[stream, side * PAGE_TOKENS : (side + 1) * PAGE_TOKENS, :] = (
                    lanes == cell_col + (SP_SIDE + 1 - SP_SIDE * x_side - y_side)
                ).astype(jnp.bfloat16)
                mask_ref[stream, side] = (
                    (x_less if x_side else 1.0 - x_less) * (y_less if y_side else 1.0 - y_less)
                ).astype(jnp.bfloat16)
        turned_ref[stream] = (rows[:128] == 127 - cell_row).astype(jnp.bfloat16)


def attend_back_pair(
    pair, pump, proj_ref, probs_ref, upstream_ref, grad_ref, linear_ref, planar_ref,
    place_ref, turned_ref, mask_ref, flip_ref,
):
    lane_head = lax.broadcasted_iota(jnp.int32, (PAGE_TOKENS, LANES), 1) // HEAD_DIM
    wide_head = jnp.concatenate([lane_head, lane_head], axis=1)
    upstream = upstream_ref[...]
    scale = HEAD_DIM ** (-0.5)
    diagonal = [None, None]
    for stream in range(2):
        pieces = [proj_ref[:, head_columns(stream, kind, pair)] for kind in range(5)]
        queries = jnp.concatenate([pieces[0], pieces[3]], axis=1)
        keys = jnp.concatenate([pieces[1], pieces[4]], axis=1)
        grads = []
        for inner in range(2):
            head = 2 * pair + inner
            mine = lane_head == inner
            grad_probs = dot_nt(jnp.where(mine, upstream, jnp.zeros_like(upstream)), pieces[2])
            probs = probs_ref[stream, inner]
            weighted = probs * grad_probs
            grad_logits = (weighted - probs * jnp.sum(weighted, axis=-1, keepdims=True)).astype(jnp.bfloat16)
            grads.append(
                (
                    dot_nn(grad_logits, keys) * scale,
                    dot_tn(grad_logits, queries) * scale,
                    dot_tn(probs.astype(jnp.bfloat16), upstream),
                )
            )
            parts = jnp.concatenate([grad_logits * mask_ref[stream, side] for side in range(4)], axis=1)
            placed = dot_nn(parts, place_ref[stream]).astype(jnp.bfloat16)
            cells = dot_nn(turned_ref[stream], placed)
            sums = jnp.sum(
                pltpu.roll(cells, SP_B - SP_SIDE // 2, 1, stride=1, stride_axis=0), axis=0, keepdims=True
            )
            if stream == 0:
                planar_ref[head] = sums
            else:
                planar_ref[head] += sums
            turned_over = dot_nn(flip_ref[...], grad_logits)
            diagonal[inner] = turned_over if stream == 0 else diagonal[inner] + turned_over
            pump(2 * stream + inner)
        query_grad, key_grad = (jnp.where(wide_head == 0, grads[0][k], grads[1][k]) for k in range(2))
        value_grad = jnp.where(lane_head == 0, grads[0][2], grads[1][2])
        for kind, value in enumerate(
            (query_grad[:, :LANES], key_grad[:, :LANES], value_grad, query_grad[:, LANES:], key_grad[:, LANES:])
        ):
            grad_ref[:, head_columns(stream, kind, pair)] = value.astype(jnp.bfloat16)
    for inner in range(2):
        padded = jnp.concatenate([diagonal[inner], jnp.zeros_like(diagonal[inner])], axis=1)
        linear_ref[2 * pair + inner] = jnp.sum(
            pltpu.roll(padded, 0, 1, stride=1, stride_axis=0), axis=0, keepdims=True
        )


def linear_folded(sums):
    first = REL_B // 2
    last = PAGE_TOKENS - 1 + REL_B // 2 - 1
    return jnp.concatenate(
        [
            jnp.sum(sums[:, :first], axis=1, keepdims=True),
            sums[:, first:last],
            jnp.sum(sums[:, last : 2 * PAGE_TOKENS - 1], axis=1, keepdims=True),
        ],
        axis=1,
    )


MESH = pl.DeviceIdType.MESH
RING = 4


def place():
    dp = lax.axis_index("dp")
    return dp // RING, lax.rem(dp, RING), lax.axis_index("pair")


def across(q, bit):
    other = lax.rem(q // bit, 2)
    return q + bit - 2 * bit * other


def greet(line):
    z, q, c = place()
    barrier = pltpu.get_barrier_semaphore()

    def signal(zz, qq, cc):
        pl.semaphore_signal(barrier, inc=1, device_id={"dp": zz * RING + qq, "pair": cc}, device_id_type=MESH)

    signal(z, across(q, 1), c)
    signal(z, across(q, 2), c)
    signal(z, q, 1 - c)

    @pl.when(z > 0)
    def _():
        signal(z - 1, q, c)

    @pl.when(z < line - 1)
    def _():
        signal(z + 1, q, c)

    ends = (z > 0).astype(jnp.int32) + (z < line - 1).astype(jnp.int32)
    pl.semaphore_wait(barrier, 3 + ends)


def spread(line, pumps, pump, first, work):
    total = line - first
    low, high = (first + total * (pump + k) // pumps for k in range(2))
    if high == low + 1:
        work(low)
    elif high > low:
        lax.fori_loop(low, high, lambda g, unused: (work(g), unused)[1], 0)


def gather_stages(line, ins, outs, sems):
    count = len(ins)
    (own_sem, z_send, z_recv, xy_send, xy_recv, d_send, d_recv, c_send, c_recv) = sems
    z, q, c = place()
    beside = (across(q, 1), across(q, 2))
    corner = across(across(q, 1), 2)

    def slot(zz, qq):
        return (zz * RING + qq) * 2 + c

    def remote(src, dst, send, recv, zz, qq, cc):
        return pltpu.make_async_remote_copy(
            src_ref=src, dst_ref=dst, send_sem=send, recv_sem=recv,
            device_id={"dp": zz * RING + qq, "pair": cc}, device_id_type=MESH,
        )

    def block(a, zz, qq):
        return outs[a].at[slot(zz, qq)]

    def halves(a):
        width = ins[a].shape[-1]
        cut = width // 2 if width % 256 == 0 else width
        return (0, cut), (cut, width - cut)

    def own(a):
        return pltpu.make_async_copy(ins[a], block(a, z, q), own_sem.at[a])

    def z_copy(a, way, step, first):
        zz = z - step if way == 0 else z + step
        target = z + 1 if way == 0 else z - 1
        src = ins[a] if first else block(a, zz, q)
        return remote(src, block(a, zz, q), z_send.at[way, a, step], z_recv.at[way, a, step], target, q, c)

    def xy_copy(a, axis, zz, first):
        src = ins[a] if first else block(a, zz, q)
        return remote(src, block(a, zz, q), xy_send.at[axis, a, zz], xy_recv.at[axis, a, zz], z, beside[axis], c)

    def d_copy(a, axis, zz):
        start, width = halves(a)[axis]
        part = outs[a].at[slot(zz, beside[axis]), :, pl.ds(start, width)]
        return remote(part, part, d_send.at[axis, a, zz], d_recv.at[axis, a, zz], z, beside[1 - axis], c)

    def c_copy(a, zz, qq, first):
        src = ins[a] if first else block(a, zz, qq)
        return remote(
            src, block(a, zz, qq), c_send.at[a, zz * RING + qq], c_recv.at[a, zz * RING + qq], z, q, 1 - c
        )

    def start_line():
        for a in range(count):
            own(a).start()
            for way in range(2):
                @pl.when(z < line - 1 if way == 0 else z > 0)
                def _():
                    z_copy(a, way, 0, True).start()
            c_copy(a, z, q, True).start()

    def start_ring():
        for a in range(count):
            for axis in range(2):
                xy_copy(a, axis, z, True).start()

    def arrived(a, zz):
        for axis in range(2):
            xy_copy(a, axis, zz, False).start()
        c_copy(a, zz, q, False).start()

    def passed_on(a, zz):
        for axis in range(2):
            start, width = halves(a)[axis]
            got = block(a, zz, beside[axis])
            remote(got, got, xy_send.at[axis, a, zz], xy_recv.at[axis, a, zz], z, beside[axis], c).wait_recv()
            if width:
                d_copy(a, axis, zz).start()
            c_copy(a, zz, beside[axis], False).start()

    def finished(a, zz):
        for axis in range(2):
            start, width = halves(a)[axis]
            if width:
                part = outs[a].at[slot(zz, corner), :, pl.ds(start, width)]
                remote(part, part, d_send.at[axis, a, zz], d_recv.at[axis, a, zz], z, beside[1 - axis], c).wait_recv()
        c_copy(a, zz, corner, False).start()

    def both_ways(g, work):
        @pl.when(z - g >= 0)
        def _():
            work(z - g)

        @pl.when(jnp.logical_and(z + g <= line - 1, g > 0))
        def _():
            work(z + g)

    def along(g):
        for a in range(count):
            @pl.when(z - g >= 0)
            def _():
                got = block(a, z - g, q)
                remote(got, got, z_send.at[0, a, g - 1], z_recv.at[0, a, g - 1], z, q, 1 - c).wait_recv()

                @pl.when(z < line - 1)
                def _():
                    z_copy(a, 0, g, False).start()

                arrived(a, z - g)

            @pl.when(z + g <= line - 1)
            def _():
                got = block(a, z + g, q)
                remote(got, got, z_send.at[1, a, g - 1], z_recv.at[1, a, g - 1], z, q, 1 - c).wait_recv()

                @pl.when(z > 0)
                def _():
                    z_copy(a, 1, g, False).start()

                arrived(a, z + g)

    def around(g):
        for a in range(count):
            both_ways(g, partial(passed_on, a))

    def home(g):
        for a in range(count):
            both_ways(g, partial(finished, a))

    def drain(zz, unused):
        for a in range(count):
            for axis in range(2):
                xy_copy(a, axis, zz, False).wait_send()
                if halves(a)[axis][1]:
                    d_copy(a, axis, zz).wait_send()
            for qq in range(RING):
                c_copy(a, zz, qq, False).wait_send()
                got = outs[a].at[(zz * RING + qq) * 2 + 1 - c]
                remote(
                    got, got, c_send.at[a, zz * RING + qq], c_recv.at[a, zz * RING + qq], z, q, 1 - c
                ).wait_recv()

            @pl.when(jnp.logical_and(z < line - 1, zz <= z))
            def _():
                z_copy(a, 0, z - zz, False).wait_send()

            @pl.when(jnp.logical_and(z > 0, zz >= z))
            def _():
                z_copy(a, 1, zz - z, False).wait_send()
        return unused

    def end():
        for a in range(count):
            own(a).wait()
        lax.fori_loop(0, line, drain, 0)

    return SimpleNamespace(
        start_line=start_line, start_ring=start_ring, along=along, around=around, home=home, end=end
    )


def gather_sems(line, count):
    dma = pltpu.SemaphoreType.DMA
    return [
        dma((count,)),
        *(dma((2, count, line)) for k in range(6)),
        dma((count, line * RING)),
        dma((count, line * RING)),
    ]


def group_of(zz):
    return pl.ds(zz * RING, RING)


def flat_gather_stages(line, ins, outs, sems):
    count = len(ins)
    own_sem, xy_send, xy_recv, d_send, d_recv, z_send, z_recv, c_send, c_recv = sems
    z, q, c = place()
    beside = (across(q, 1), across(q, 2))
    corner = across(across(q, 1), 2)

    def remote(src, dst, send, recv, zz, qq, cc):
        return pltpu.make_async_remote_copy(
            src_ref=src, dst_ref=dst, send_sem=send, recv_sem=recv,
            device_id={"dp": zz * RING + qq, "pair": cc}, device_id_type=MESH,
        )

    def block(a, qq):
        return outs[a].at[z * RING + qq, c]

    def halves(a):
        width = ins[a].shape[-1]
        return (0, width // 2), (width // 2, width // 2)

    def own(a):
        return pltpu.make_async_copy(ins[a], block(a, q), own_sem.at[a])

    def xy_copy(a, axis):
        return remote(ins[a], block(a, q), xy_send.at[axis, a], xy_recv.at[axis, a], z, beside[axis], c)

    def xy_got(a, axis):
        got = block(a, beside[axis])
        return remote(got, got, xy_send.at[axis, a], xy_recv.at[axis, a], z, beside[axis], c)

    def d_copy(a, axis, qq):
        start, width = halves(a)[axis]
        part = outs[a].at[z * RING + qq, c, :, pl.ds(start, width)]
        return remote(part, part, d_send.at[axis, a], d_recv.at[axis, a], z, beside[1 - axis], c)

    def z_copy(a, way, zz, target):
        part = outs[a].at[group_of(zz), c]
        return remote(part, part, z_send.at[way, a, zz], z_recv.at[way, a, zz], target, q, c)

    def c_copy(a, zz, cc):
        part = outs[a].at[group_of(zz), cc]
        return remote(part, part, c_send.at[a, zz], c_recv.at[a, zz], z, q, 1 - c)

    def ahead(way):
        return z < line - 1 if way == 0 else z > 0

    def start():
        for a in range(count):
            own(a).start()
            for axis in range(2):
                xy_copy(a, axis).start()

    def around():
        for a in range(count):
            for axis in range(2):
                xy_got(a, axis).wait_recv()
                d_copy(a, axis, beside[axis]).start()

    def home():
        for a in range(count):
            own(a).wait()
            for axis in range(2):
                d_copy(a, axis, corner).wait_recv()
            for way in range(2):
                @pl.when(ahead(way))
                def _():
                    z_copy(a, way, z, z + 1 - 2 * way).start()
            c_copy(a, z, c).start()

    def along(g):
        for a in range(count):
            for way in range(2):
                zz = z - g if way == 0 else z + g

                @pl.when(zz >= 0 if way == 0 else zz <= line - 1)
                def _():
                    z_copy(a, way, zz, z - 1 + 2 * way).wait_recv()

                    @pl.when(ahead(way))
                    def _():
                        z_copy(a, way, zz, z + 1 - 2 * way).start()

                    c_copy(a, zz, c).start()

    def end():
        for a in range(count):
            for axis in range(2):
                xy_copy(a, axis).wait_send()
                d_copy(a, axis, beside[axis]).wait_send()

            def drain(zz, unused):
                c_copy(a, zz, c).wait_send()
                c_copy(a, zz, 1 - c).wait_recv()
                for way in range(2):
                    @pl.when(jnp.logical_and(ahead(way), zz <= z if way == 0 else zz >= z))
                    def _():
                        z_copy(a, way, zz, z + 1 - 2 * way).wait_send()
                return unused

            lax.fori_loop(0, line, drain, 0)

    return SimpleNamespace(start=start, around=around, home=home, along=along, end=end)


def flat_gather_sems(line, count):
    dma = pltpu.SemaphoreType.DMA
    return [
        dma((count,)),
        *(dma((2, count)) for k in range(4)),
        *(dma((2, count, line)) for k in range(2)),
        *(dma((count, line)) for k in range(2)),
    ]


def gather_kernel(line, count, flat, *refs):
    both = count + flat
    ins, outs, sems = refs[:both], refs[both : 2 * both], refs[2 * both :]
    stages = gather_stages(line, ins[:count], outs[:count], sems[:9])
    plane = flat_gather_stages(line, ins[count:], outs[count:], sems[9:])
    greet(line)
    plane.start()
    stages.start_line()
    stages.start_ring()

    def generation(g, unused):
        stages.along(g)
        stages.around(g - 1)

        @pl.when(g == 1)
        def _():
            plane.around()

        @pl.when(g == 2)
        def _():
            plane.home()

        @pl.when(g >= 3)
        def _():
            stages.home(g - 3)

        return unused

    lax.fori_loop(1, line, generation, 0)
    if line == 2:
        plane.home()

    def rest(g, unused):
        @pl.when(g <= line - 1)
        def _():
            plane.along(g)

        @pl.when(g == 1)
        def _():
            stages.around(line - 1)

        @pl.when(g + line - 4 >= 0)
        def _():
            stages.home(g + line - 4)

        return unused

    lax.fori_loop(1, 4, rest, 0)
    lax.fori_loop(4, line, lambda g, unused: (plane.along(g), unused)[1], 0)
    stages.end()
    plane.end()


def gather_all(shards, flat_shards, collective_id):
    dp = lax.axis_size("dp")
    line = dp // RING
    count, flat = len(shards), len(flat_shards)
    wholes = pl.pallas_call(
        partial(gather_kernel, line, count, flat),
        in_specs=[pl.BlockSpec(memory_space=pl.ANY)] * (count + flat),
        out_specs=[pl.BlockSpec(memory_space=pl.ANY)] * (count + flat),
        out_shape=[
            *(jax.ShapeDtypeStruct((2 * dp, *shard.shape), shard.dtype) for shard in shards),
            *(jax.ShapeDtypeStruct((dp, 2, *shard.shape), shard.dtype) for shard in flat_shards),
        ],
        scratch_shapes=[*gather_sems(line, count), *flat_gather_sems(line, flat)],
        compiler_params=pltpu.CompilerParams(collective_id=collective_id, has_side_effects=True),
        name="gather_all",
    )(*shards, *flat_shards)
    return [whole.reshape(2 * dp, *whole.shape[-2:]) for whole in wholes]


def scatter_stages(line, ins, outs, scratch):
    count = len(ins)
    groups = [scratch[k * count : (k + 1) * count] for k in range(5)]
    mine, beside_sum, half_in, full_in, line_in = groups
    (own_sem, c_send, c_recv, d_send, d_recv, xy_send, xy_recv, z_send, z_recv) = scratch[5 * count :]
    z, q, c = place()
    beside = (across(q, 1), across(q, 2))
    corner = across(across(q, 1), 2)

    def remote(src, dst, send, recv, zz, qq, cc):
        return pltpu.make_async_remote_copy(
            src_ref=src, dst_ref=dst, send_sem=send, recv_sem=recv,
            device_id={"dp": zz * RING + qq, "pair": cc}, device_id_type=MESH,
        )

    def halves(a):
        width = outs[a].shape[-1]
        cut = width // 2 if width % 256 == 0 else width
        return (0, cut), (cut, width - cut)

    def wide(value):
        return value.astype(jnp.float32)

    def group(zz):
        return pl.ds(zz * RING, RING)

    def own(a, zz):
        return pltpu.make_async_copy(ins[a].at[group(zz), c], mine[a].at[group(zz)], own_sem.at[a, zz])

    def c_copy(a, zz):
        return remote(
            ins[a].at[group(zz), 1 - c], beside_sum[a].at[group(zz)], c_send.at[a, zz], c_recv.at[a, zz], z, q, 1 - c
        )

    def d_copy(a, axis, zz):
        start, width = halves(a)[axis]
        return remote(
            mine[a].at[zz * RING + corner, :, pl.ds(start, width)],
            half_in[a].at[zz, :, pl.ds(start, width)],
            d_send.at[axis, a, zz], d_recv.at[axis, a, zz], z, beside[axis], c,
        )

    def xy_copy(a, axis, zz):
        return remote(
            mine[a].at[zz * RING + beside[axis]], full_in[a].at[axis, zz],
            xy_send.at[axis, a, zz], xy_recv.at[axis, a, zz], z, beside[axis], c,
        )

    def z_copy(a, way, zz):
        return remote(
            mine[a].at[zz * RING + q], line_in[a].at[way, zz],
            z_send.at[way, a, zz], z_recv.at[way, a, zz], z + 1 if way == 0 else z - 1, q, c,
        )

    def both_ways(g, work):
        @pl.when(z - g >= 0)
        def _():
            work(z - g)

        @pl.when(jnp.logical_and(z + g <= line - 1, g > 0))
        def _():
            work(z + g)

    def begin(zz):
        for a in range(count):
            c_copy(a, zz).start()
            own(a, zz).start()

    def first(zz):
        for a in range(count):
            own(a, zz).wait()
            c_copy(a, zz).wait_recv()

            def one(qq, unused):
                k = zz * RING + qq
                mine[a][k] = mine[a][k] + beside_sum[a][k]
                return unused

            lax.fori_loop(0, RING, one, 0)
            for axis in range(2):
                if halves(a)[axis][1]:
                    d_copy(a, axis, zz).start()

    def second(zz):
        for a in range(count):
            for axis in range(2):
                start, width = halves(a)[axis]
                k = zz * RING + beside[1 - axis]
                if width:
                    d_copy(a, axis, zz).wait_recv()
                    mine[a][k, :, start : start + width] = (
                        mine[a][k, :, start : start + width] + half_in[a][zz, :, start : start + width]
                    )
                xy_copy(a, 1 - axis, zz).start()

    def third(zz):
        for a in range(count):
            k = zz * RING + q
            for axis in range(2):
                xy_copy(a, axis, zz).wait_recv()
            mine[a][k] = (
                wide(mine[a][k]) + wide(full_in[a][0, zz]) + wide(full_in[a][1, zz])
            ).astype(mine[a].dtype)
            for way in range(2):
                @pl.when(zz > z if way == 0 else zz < z)
                def _():
                    @pl.when(z > 0 if way == 0 else z < line - 1)
                    def _():
                        z_copy(a, way, zz).wait_recv()
                        mine[a][k] = mine[a][k] + line_in[a][way, zz]

                    z_copy(a, way, zz).start()

            @pl.when(zz == z)
            def _():
                outs[a][...] = wide(mine[a][k])
                for way in range(2):
                    @pl.when(z > 0 if way == 0 else z < line - 1)
                    def _():
                        z_copy(a, way, zz).wait_recv()
                        outs[a][...] += wide(line_in[a][way, zz])

    def start():
        def begin_all(step, unused):
            both_ways(line - 1 - step, begin)
            return unused

        lax.fori_loop(0, line, begin_all, 0)

    def drain(zz, unused):
        for a in range(count):
            for axis in range(2):
                xy_copy(a, axis, zz).wait_send()
                if halves(a)[axis][1]:
                    d_copy(a, axis, zz).wait_send()
            c_copy(a, zz).wait_send()
            for way in range(2):
                @pl.when(zz > z if way == 0 else zz < z)
                def _():
                    z_copy(a, way, zz).wait_send()
        return unused

    def end():
        lax.fori_loop(0, line, drain, 0)

    return SimpleNamespace(
        start=start,
        first=lambda step: both_ways(line - 1 - step, first),
        second=lambda step: both_ways(line - 1 - step, second),
        third=lambda step: both_ways(line - 1 - step, third),
        end=end,
    )


def scatter_scratch(line, blocks):
    dma = pltpu.SemaphoreType.DMA
    count = len(blocks)
    return [
        *(pltpu.VMEM((line * RING, *shape), kind) for shape, kind in blocks),
        *(pltpu.VMEM((line * RING, *shape), kind) for shape, kind in blocks),
        *(pltpu.VMEM((line, *shape), kind) for shape, kind in blocks),
        *(pltpu.VMEM((2, line, *shape), kind) for shape, kind in blocks),
        *(pltpu.VMEM((2, line, *shape), kind) for shape, kind in blocks),
        *(dma((count, line)) for k in range(3)),
        *(dma((2, count, line)) for k in range(6)),
    ]


def flat_scatter_stages(line, ins, outs, scratch):
    count = len(ins)
    mine, beside_sum, line_in, half_in, full_in = (scratch[k * count : (k + 1) * count] for k in range(5))
    own_sem, c_send, c_recv, z_send, z_recv, d_send, d_recv, xy_send, xy_recv = scratch[5 * count :]
    z, q, c = place()
    beside = (across(q, 1), across(q, 2))
    corner = across(across(q, 1), 2)

    def remote(src, dst, send, recv, zz, qq, cc):
        return pltpu.make_async_remote_copy(
            src_ref=src, dst_ref=dst, send_sem=send, recv_sem=recv,
            device_id={"dp": zz * RING + qq, "pair": cc}, device_id_type=MESH,
        )

    def halves(a):
        width = outs[a].shape[-1]
        cut = width // 2 if width % 256 == 0 else width
        return (0, cut), (cut, width - cut)

    def own(a, zz):
        return pltpu.make_async_copy(ins[a].at[group_of(zz), c], mine[a].at[group_of(zz)], own_sem.at[a, zz])

    def c_copy(a, zz):
        return remote(
            ins[a].at[group_of(zz), 1 - c], beside_sum[a].at[group_of(zz)], c_send.at[a, zz], c_recv.at[a, zz],
            z, q, 1 - c,
        )

    def z_copy(a, way, zz):
        return remote(
            mine[a].at[group_of(zz)], line_in[a].at[way, group_of(zz)], z_send.at[way, a, zz],
            z_recv.at[way, a, zz], z + 1 - 2 * way, q, c,
        )

    def d_copy(a, axis):
        start, width = halves(a)[axis]
        return remote(
            mine[a].at[z * RING + corner, :, pl.ds(start, width)], half_in[a].at[:, pl.ds(start, width)],
            d_send.at[axis, a], d_recv.at[axis, a], z, beside[axis], c,
        )

    def xy_copy(a, axis):
        return remote(
            mine[a].at[z * RING + beside[axis]], full_in[a].at[axis], xy_send.at[axis, a], xy_recv.at[axis, a],
            z, beside[axis], c,
        )

    def behind(way):
        return z > 0 if way == 0 else z < line - 1

    def both_ways(g, work):
        @pl.when(z - g >= 0)
        def _():
            work(z - g)

        @pl.when(jnp.logical_and(z + g <= line - 1, g > 0))
        def _():
            work(z + g)

    def add(a, zz, part):
        def one(qq, unused):
            k = zz * RING + qq
            mine[a][k] = mine[a][k] + part[k]
            return unused

        lax.fori_loop(0, RING, one, 0)

    def begin(zz):
        for a in range(count):
            c_copy(a, zz).start()
            own(a, zz).start()

    def first(zz):
        for a in range(count):
            own(a, zz).wait()
            c_copy(a, zz).wait_recv()
            add(a, zz, beside_sum[a])
            for way in range(2):
                @pl.when(jnp.logical_and(behind(way), zz >= z if way == 0 else zz <= z))
                def _():
                    z_copy(a, way, zz).wait_recv()
                    add(a, zz, line_in[a].at[way])

                @pl.when(zz > z if way == 0 else zz < z)
                def _():
                    z_copy(a, way, zz).start()

            @pl.when(zz == z)
            def _():
                for axis in range(2):
                    if halves(a)[axis][1]:
                        d_copy(a, axis).start()

    def second():
        for a in range(count):
            for axis in range(2):
                start, width = halves(a)[axis]
                k = z * RING + beside[1 - axis]
                if width:
                    d_copy(a, axis).wait_recv()
                    mine[a][k, :, start : start + width] = (
                        mine[a][k, :, start : start + width] + half_in[a][:, start : start + width]
                    )
                xy_copy(a, 1 - axis).start()

    def third():
        for a in range(count):
            for axis in range(2):
                xy_copy(a, axis).wait_recv()
            outs[a][...] = sum(
                part.astype(jnp.float32) for part in (mine[a][z * RING + q], full_in[a][0], full_in[a][1])
            )

    def start():
        lax.fori_loop(0, line, lambda step, unused: (both_ways(line - 1 - step, begin), unused)[1], 0)

    def end():
        for a in range(count):
            for axis in range(2):
                if halves(a)[axis][1]:
                    d_copy(a, axis).wait_send()
                xy_copy(a, axis).wait_send()

            def drain(zz, unused):
                c_copy(a, zz).wait_send()
                for way in range(2):
                    @pl.when(zz > z if way == 0 else zz < z)
                    def _():
                        z_copy(a, way, zz).wait_send()
                return unused

            lax.fori_loop(0, line, drain, 0)

    return SimpleNamespace(
        start=start, first=lambda step: both_ways(line - 1 - step, first), second=second, third=third, end=end
    )


def flat_scatter_scratch(line, blocks):
    dma = pltpu.SemaphoreType.DMA
    count = len(blocks)
    return [
        *(pltpu.VMEM((line * RING, *shape), kind) for shape, kind in blocks),
        *(pltpu.VMEM((line * RING, *shape), kind) for shape, kind in blocks),
        *(pltpu.VMEM((2, line * RING, *shape), kind) for shape, kind in blocks),
        *(pltpu.VMEM(shape, kind) for shape, kind in blocks),
        *(pltpu.VMEM((2, *shape), kind) for shape, kind in blocks),
        *(dma((count, line)) for k in range(3)),
        *(dma((2, count, line)) for k in range(2)),
        *(dma((2, count)) for k in range(4)),
    ]


def peers(line):
    z, q, c = place()
    cell = q * 2 + c
    near = RING * 2

    def near_place(k):
        other = lax.rem(cell + k, near)
        return other, {"dp": z * RING + other // 2, "pair": lax.rem(other, 2)}

    def far_place(k):
        other = lax.rem(z + k, line)
        return other, {"dp": other * RING + q, "pair": c}

    def each(places, stop, work):
        def one(k, unused):
            work(*places(k))
            return unused

        lax.fori_loop(1, stop, one, 0)

    return partial(each, near_place, near), partial(each, far_place, line)


def greet_peers(line):
    barrier = pltpu.get_barrier_semaphore()
    for each in peers(line):
        each(
            lambda other, device: pl.semaphore_signal(barrier, inc=1, device_id=device, device_id_type=MESH)
        )
    pl.semaphore_wait(barrier, 2 * RING + line - 2)


def exchange_stages(line, combine, value_ref, total_ref, scratch):
    near_ref, part_ref, far_ref, n_send, n_recv, f_send, f_recv = scratch
    z, q, c = place()
    cell = q * 2 + c
    each_near, each_far = peers(line)

    def near_copy(other, device, source):
        return pltpu.make_async_remote_copy(
            src_ref=value_ref, dst_ref=near_ref.at[source], send_sem=n_send.at[other], recv_sem=n_recv.at[source],
            device_id=device, device_id_type=MESH,
        )

    def far_copy(other, device, source):
        return pltpu.make_async_remote_copy(
            src_ref=part_ref, dst_ref=far_ref.at[source], send_sem=f_send.at[other], recv_sem=f_recv.at[source],
            device_id=device, device_id_type=MESH,
        )

    def near():
        each_near(lambda other, device: near_copy(other, device, cell).start())
        near_ref[cell] = value_ref[...]

    def far():
        each_near(lambda other, device: near_copy(other, device, other).wait_recv())
        part_ref[...] = combine(near_ref, 2 * RING, 1)
        each_far(lambda other, device: far_copy(other, device, z).start())
        far_ref[z] = part_ref[...]

    def total():
        each_far(lambda other, device: far_copy(other, device, other).wait_recv())
        total_ref[...] = combine(far_ref, line, 2 * RING)

    def end():
        each_near(lambda other, device: near_copy(other, device, cell).wait_send())
        each_far(lambda other, device: far_copy(other, device, z).wait_send())

    return SimpleNamespace(near=near, far=far, total=total, end=end)


def exchange_scratch(line, shape):
    dma = pltpu.SemaphoreType.DMA
    near = 2 * RING
    return [
        pltpu.VMEM((near, *shape), jnp.float32),
        pltpu.VMEM(shape, jnp.float32),
        pltpu.VMEM((line, *shape), jnp.float32),
        dma((near,)),
        dma((near,)),
        dma((line,)),
        dma((line,)),
    ]


def exchange_kernel(line, combine, value_ref, total_ref, *scratch):
    stages = exchange_stages(line, combine, value_ref, total_ref, scratch)
    greet_peers(line)
    stages.near()
    stages.far()
    stages.total()
    stages.end()


def add_up(parts, count, weight):
    return lax.fori_loop(1, count, lambda k, total: total + parts[k], parts[0])


def pool_statistics(rows, parts, count, weight):
    mean = lax.fori_loop(1, count, lambda k, total: total + parts[k, 0], parts[0, 0]) / count

    def squares(k, total):
        offset = parts[k, 0] - mean
        return total + parts[k, 1] + (rows * weight) * (offset * offset)

    return jnp.stack([mean, lax.fori_loop(0, count, squares, jnp.zeros_like(mean))])


def exchange(value, combine, collective_id, name):
    line = lax.axis_size("dp") // RING
    vmem = pl.BlockSpec(memory_space=pltpu.VMEM)
    return pl.pallas_call(
        partial(exchange_kernel, line, combine),
        in_specs=[vmem],
        out_specs=vmem,
        out_shape=jax.ShapeDtypeStruct(value.shape, value.dtype),
        scratch_shapes=exchange_scratch(line, value.shape),
        compiler_params=pltpu.CompilerParams(collective_id=collective_id, has_side_effects=True),
        name=name,
    )(value)


KINDS = 10


def source_of(column):
    stream = column // 5
    return 2 * stream + (column - 5 * stream) // 3


def once(shape):
    return pl.BlockSpec(shape, lambda i: (0,) * len(shape), pipeline_mode=pl.Buffered(1))


def at_steps(schedule):
    step = pl.program_id(0)
    for when, work in schedule:
        @pl.when(step == when)
        def _():
            for one in work:
                one()


batch_epsilon = 1e-05


def column_at_step(step):
    turn = jnp.clip(step - 1, 0, KINDS - 1)
    return jnp.where(turn >= 7, turn - 2, jnp.where(turn >= 5, turn + 3, turn))


VECTORS = 9
CHUNKS = 4


def unpack(packed_ref, vectors_ref, bias_ref, linear_ref, planar_ref):
    devices = packed_ref.shape[0]
    bias_rows = REL_B // devices

    def row(k):
        return packed_ref[:, k, :].astype(jnp.bfloat16)

    def lined_up(k, share, first):
        lane = lax.broadcasted_iota(jnp.int32, (128, MODEL_WIDTH), 1)
        spread = (lax.broadcasted_iota(jnp.int32, (128, MODEL_WIDTH), 0) == lax.rem(lane, share)).astype(jnp.bfloat16)
        owner = lax.broadcasted_iota(jnp.int32, (devices, MODEL_WIDTH), 1) // share + first
        mine = lax.broadcasted_iota(jnp.int32, (devices, MODEL_WIDTH), 0) == owner
        whole = dot_nn(row(k), spread)
        return jnp.sum(jnp.where(mine, whole, jnp.zeros_like(whole)), axis=0, keepdims=True)

    def table(first, width, shift):
        bucket = jnp.clip(lax.broadcasted_iota(jnp.int32, (devices, width), 1) - shift, 0, REL_B - 1)
        start = lax.broadcasted_iota(jnp.int32, (devices, width), 0) * bias_rows
        total = None
        for k in range(bias_rows):
            part = dot_tn(row(first + k), (bucket == start + k).astype(jnp.bfloat16))
            total = part if total is None else total + part
        return total

    vectors_ref[...] = jnp.zeros_like(vectors_ref)
    for k in range(VECTORS):
        vectors_ref[k : k + 1, :] = lined_up(2 * bias_rows + k, MODEL_WIDTH // devices, 0)
    share = CHUNKS * MODEL_WIDTH // devices
    for k in range(CHUNKS):
        bias_ref[k] = lined_up(2 * bias_rows + VECTORS, share, k * (MODEL_WIDTH // share))
    linear = table(0, 2 * PAGE_TOKENS, PAGE_TOKENS - 1 - REL_B // 2)
    planar = table(bias_rows, SP_B, 0)
    for head in range(HEADS):
        linear_ref[head] = linear[head : head + 1, :]
        planar_ref[head] = planar[head : head + 1, :]


def forward_kernel(line, count, token_total, *refs):
    (
        features_ref, backbone_hbm, table_hbm, text_ref, hits_ref, packed_ref, weight_ref, rows_ref, cols_ref,
    ) = refs[:9]
    ins = refs[9 : 9 + count]
    (
        proj_ref, merged_ref, probs_ref, lefts_ref, start_ref, normal_ref, scale_ref, vectors_ref, bias_ref,
    ) = refs[9 + count : 18 + count]
    outs = refs[18 + count : 18 + 2 * count]
    box_ref, conv_ref, local_ref, pooled_ref, linear_ref, planar_ref = refs[18 + 2 * count : 24 + 2 * count]
    backbone_ref, table_ref, fetch_sem, *rest = refs[24 + 2 * count :]
    rows = features_ref.shape[0]
    sums = exchange_stages(line, partial(pool_statistics, float(rows)), local_ref, pooled_ref, rest[:7])
    stages = gather_stages(line, ins[:-1], outs[:-1], rest[7:16])
    plane = flat_gather_stages(line, ins[-1:], outs[-1:], rest[16:])
    step = pl.program_id(0)

    def vector(k):
        return vectors_ref[k : k + 1, :]

    def hit_rows(stream):
        return jnp.broadcast_to(hits_ref[:, stream : stream + 1] == 1, (rows, MODEL_WIDTH))

    @pl.when(step == 0)
    def _():
        fetches = [
            pltpu.make_async_copy(source, target, fetch_sem.at[k])
            for k, (source, target) in enumerate(((backbone_hbm, backbone_ref), (table_hbm, table_ref)))
        ]
        for fetch in fetches:
            fetch.start()
        greet_peers(line)
        stages.start_line()
        fetches[0].wait()
        conv = dot_nn(features_ref[...], backbone_ref[...])
        mean = jnp.mean(conv, axis=0, keepdims=True)
        center = conv - mean
        conv_ref[...] = conv
        local_ref[0] = mean
        local_ref[1] = jnp.sum(center * center, axis=0, keepdims=True)
        sums.near()
        plane.start()
        stages.start_ring()
        unpack(packed_ref, vectors_ref, bias_ref, linear_ref, planar_ref)
        make_boxes(rows_ref, cols_ref, box_ref)
        text_start = jnp.where(hit_rows(0), vector(2), text_ref[...].astype(jnp.float32))
        start_ref[...] = text_start
        lefts_ref[0] = text_start.astype(jnp.bfloat16)
        coords = lax.broadcasted_iota(jnp.int32, (rows, COORDS), 1)
        fetches[1].wait()
        for stream in range(2):
            space = None
            for axis in range(2):
                place = 2 * stream + axis
                hit = (coords == cols_ref[:, place : place + 1]).astype(jnp.bfloat16)
                part = dot_nn(hit, table_ref[:, axis * MODEL_WIDTH : (axis + 1) * MODEL_WIDTH])
                space = part if space is None else space + part
            lefts_ref[2 * stream + 1] = space.astype(jnp.bfloat16)
        sums.far()

    @pl.when(jnp.logical_and(step >= 1, step <= KINDS))
    def _():
        column = column_at_step(step)
        columns = pl.ds(pl.multiple_of(column * MODEL_WIDTH, MODEL_WIDTH), MODEL_WIDTH)
        proj_ref[:, columns] = dot_nn(lefts_ref[source_of(column)], weight_ref[...]).astype(jnp.bfloat16)

    @pl.when(step == 7)
    def _():
        sums.total()
        inverse = lax.rsqrt(pooled_ref[1] / token_total + batch_epsilon)
        normal = (conv_ref[...] - pooled_ref[0]) * inverse
        normal_ref[...] = normal
        scale_ref[...] = jnp.broadcast_to(vector(0) * inverse, scale_ref.shape)
        region_start = jnp.where(hit_rows(1), vector(3), normal * vector(0) + vector(1))
        start_ref[...] += region_start
        lefts_ref[2] = region_start.astype(jnp.bfloat16)

    @pl.when(step > KINDS)
    def _():
        attend_pair(step - 1 - KINDS, proj_ref, linear_ref, planar_ref, box_ref, merged_ref, probs_ref)

    def along(k):
        return lambda: spread(line, 3, k, 1, stages.along)

    def around(k):
        return lambda: spread(line, 4, k, 0, stages.around)

    def flat(k):
        return lambda: spread(line, 3, k, 1, plane.along)

    def home(k):
        return lambda: spread(line, 4, k, 0, stages.home)

    at_steps(
        [
            (1, [along(0), around(0)]),
            (5, [plane.around]),
            (8, [along(1)]),
            (11, [around(1), plane.home]),
            (13, [along(2), home(0)]),
            (14, [flat(0)]),
            (15, [around(2), home(1)]),
            (16, [flat(1), around(3), home(2), flat(2), home(3), sums.end, stages.end, plane.end]),
        ]
    )


def forward_layer(
    features, backbone, table, text, hits, packed, weights, anchor_rows, anchor_cols, shards, token_total,
    collective_id,
):
    dp = lax.axis_size("dp")
    line = dp // RING
    count = len(shards)
    anywhere = pl.BlockSpec(memory_space=pl.ANY)
    width = weights.shape[1]
    page = (PAGE_TOKENS, MODEL_WIDTH)
    f32, bf16 = jnp.float32, jnp.bfloat16

    def pair_at(i):
        return jnp.maximum(i - 1 - KINDS, 0)

    def whole(shape):
        return pl.BlockSpec(shape, lambda i: (0,) * len(shape))

    outs = [
        ((PAGE_TOKENS, width), bf16, whole((PAGE_TOKENS, width))),
        (page, bf16, pl.BlockSpec((PAGE_TOKENS, LANES), lambda i: (0, pair_at(i)))),
        (
            (2, HEADS, PAGE_TOKENS, PAGE_TOKENS), f32,
            pl.BlockSpec((2, 2, PAGE_TOKENS, PAGE_TOKENS), lambda i: (0, pair_at(i), 0, 0)),
        ),
        ((4, *page), bf16, whole((4, *page))),
        (page, f32, whole(page)),
        (page, f32, whole(page)),
        ((8, MODEL_WIDTH), f32, whole((8, MODEL_WIDTH))),
        ((16, MODEL_WIDTH), f32, whole((16, MODEL_WIDTH))),
        ((CHUNKS, 1, MODEL_WIDTH), f32, whole((CHUNKS, 1, MODEL_WIDTH))),
        *(((2 * dp, *shard.shape), shard.dtype, anywhere) for shard in shards[:-1]),
        ((dp, 2, *shards[-1].shape), shards[-1].dtype, anywhere),
    ]
    pool = (2, 1, MODEL_WIDTH)
    return pl.pallas_call(
        partial(forward_kernel, line, count, float(token_total)),
        grid=(1 + KINDS + PAIRS,),
        in_specs=[
            once(features.shape),
            anywhere,
            anywhere,
            once(text.shape),
            once(hits.shape),
            once(packed.shape),
            pl.BlockSpec((MODEL_WIDTH, MODEL_WIDTH), lambda i: (0, column_at_step(i))),
            once(anchor_rows.shape),
            once(anchor_cols.shape),
            *[anywhere] * count,
        ],
        out_specs=[spec for shape, kind, spec in outs],
        out_shape=[jax.ShapeDtypeStruct(shape, kind) for shape, kind, spec in outs],
        scratch_shapes=[
            pltpu.VMEM((2, PAGE_TOKENS, PAGE_TOKENS), jnp.int32),
            pltpu.VMEM(page, f32),
            pltpu.VMEM(pool, f32),
            pltpu.VMEM(pool, f32),
            pltpu.VMEM((HEADS, 1, 2 * PAGE_TOKENS), f32),
            pltpu.VMEM((HEADS, 1, SP_B), f32),
            pltpu.VMEM(backbone.shape, bf16),
            pltpu.VMEM(table.shape, bf16),
            pltpu.SemaphoreType.DMA((2,)),
            *exchange_scratch(line, pool),
            *gather_sems(line, count - 1),
            *flat_gather_sems(line, 1),
        ],
        compiler_params=pltpu.CompilerParams(
            collective_id=collective_id, has_side_effects=True, vmem_limit_bytes=62 << 20
        ),
        name="forward_layer",
    )(
        features, backbone, table, text, hits, packed, weights, anchor_rows, anchor_cols, *shards,
    )


TABLE_STEP = PAIRS + KINDS


def backward_kernel(line, count, *refs):
    (
        proj_ref, probs_ref, upstream_ref, rows_ref, cols_ref, lefts_hbm, weight_ref, mixer_grad_hbm, normal_hbm,
        hits_ref,
    ) = refs[:10]
    ins = refs[10 : 10 + count]
    (
        linear_ref, planar_ref, weight_grad_ref, table_grad_ref, text_grad_ref, region_grad_ref, sums_ref,
    ) = refs[10 + count : 17 + count]
    outs = refs[17 + count : 17 + 2 * count]
    grad_ref, turned_left_ref, input_grad_ref = refs[17 + 2 * count : 20 + 2 * count]
    helpers = refs[20 + 2 * count : 24 + 2 * count]
    lefts_ref, mixer_grad_ref, normal_ref, fetch_sem, *rest = refs[24 + 2 * count :]
    stages = scatter_stages(line, ins, outs, rest)
    step = pl.program_id(0)
    fetches = [
        pltpu.make_async_copy(source, target, fetch_sem.at[k])
        for k, (source, target) in enumerate(
            ((lefts_hbm, lefts_ref), (mixer_grad_hbm, mixer_grad_ref), (normal_hbm, normal_ref))
        )
    ]

    @pl.when(step == 0)
    def _():
        greet(line)
        stages.start()
        for fetch in fetches:
            fetch.start()
        make_places(rows_ref, cols_ref, *helpers)
        spread(line, 4, 0, 0, stages.first)

    def first(k):
        return lambda: spread(line, 4, k, 0, stages.first)

    def second(k):
        return lambda: spread(line, 4, k, 0, stages.second)

    def third(k):
        return lambda: spread(line, 4, k, 0, stages.third)

    slots = {
        1: [first(1)],
        5: [second(0), first(2)],
        9: [first(3), second(1)],
        17: [third(0), second(2)],
        21: [second(3)],
    }

    def pump(sub):
        at_steps([(slot // 4, work) for slot, work in slots.items() if slot % 4 == sub])

    @pl.when(step < PAIRS)
    def _():
        attend_back_pair(step, pump, proj_ref, probs_ref, upstream_ref, grad_ref, linear_ref, planar_ref, *helpers)

    @pl.when(jnp.logical_and(step >= PAIRS, step < TABLE_STEP))
    def _():
        column = step - PAIRS

        @pl.when(column == 0)
        def _():
            for fetch in fetches:
                fetch.wait()

        source = source_of(column)
        fresh = jnp.logical_or(column == 0, source != source_of(jnp.maximum(column - 1, 0)))
        grads = grad_ref[:, pl.ds(pl.multiple_of(column * MODEL_WIDTH, MODEL_WIDTH), MODEL_WIDTH)]

        @pl.when(fresh)
        def _():
            turned_left_ref[...] = lefts_ref[source].T

        weight_grad_ref[...] = dot_nn(turned_left_ref[...], grads).astype(jnp.bfloat16)
        back = dot_nt(grads, weight_ref[...])

        @pl.when(fresh)
        def _():
            input_grad_ref[source] = back

        @pl.when(jnp.logical_not(fresh))
        def _():
            input_grad_ref[source] += back

    @pl.when(step >= TABLE_STEP)
    def _():
        axis = step - TABLE_STEP
        coords = lax.broadcasted_iota(jnp.int32, (COORDS, PAGE_TOKENS), 0)
        total = None
        for stream in range(2):
            hit = (coords == rows_ref[pl.ds(2 * stream + axis, 1), :]).astype(jnp.bfloat16)
            part = dot_nn(hit, input_grad_ref[2 * stream + 1].astype(jnp.bfloat16))
            total = part if total is None else total + part
        table_grad_ref[...] = total.astype(jnp.bfloat16)

    @pl.when(step == TABLE_STEP + 1)
    def _():
        mixer_grad = mixer_grad_ref[...]
        sums_ref[...] = jnp.zeros_like(sums_ref)
        for stream, out_ref in enumerate((text_grad_ref, region_grad_ref)):
            grad = mixer_grad + input_grad_ref[2 * stream]
            hit = jnp.broadcast_to(hits_ref[:, stream : stream + 1] == 1, grad.shape)
            zero = jnp.zeros_like(grad)
            kept = jnp.where(hit, zero, grad)
            out_ref[...] = kept
            sums_ref[stream : stream + 1, :] = jnp.sum(jnp.where(hit, grad, zero), axis=0, keepdims=True)
            if stream == 1:
                sums_ref[2:3, :] = jnp.sum(kept, axis=0, keepdims=True)
                sums_ref[3:4, :] = jnp.sum(kept * normal_ref[...], axis=0, keepdims=True)

    at_steps(
        [(PAIRS, [third(1)]), (PAIRS + 7, [third(2)]), (TABLE_STEP + 1, [third(3), stages.end])]
    )


def backward_layer(
    proj, probs, upstream, anchor_rows, anchor_cols, lefts, weights, mixer_grad, normal, hits, grads, collective_id
):
    dp = lax.axis_size("dp")
    line = dp // RING
    count = len(grads)
    blocks = [(grad.shape[1:], grad.dtype) for grad in grads]
    anywhere = pl.BlockSpec(memory_space=pl.ANY)
    page = (PAGE_TOKENS, MODEL_WIDTH)

    def pair_at(i):
        return jnp.minimum(i, PAIRS - 1)

    def column_at(i):
        return jnp.clip(i - PAIRS, 0, KINDS - 1)

    return pl.pallas_call(
        partial(backward_kernel, line, count),
        grid=(TABLE_STEP + 2,),
        in_specs=[
            once(proj.shape),
            pl.BlockSpec((2, 2, PAGE_TOKENS, PAGE_TOKENS), lambda i: (0, pair_at(i), 0, 0)),
            pl.BlockSpec((PAGE_TOKENS, LANES), lambda i: (0, pair_at(i))),
            once(anchor_rows.shape),
            once(anchor_cols.shape),
            anywhere,
            pl.BlockSpec((MODEL_WIDTH, MODEL_WIDTH), lambda i: (0, column_at(i))),
            anywhere,
            anywhere,
            once(hits.shape),
            *[anywhere] * count,
        ],
        out_specs=[
            pl.BlockSpec((HEADS, 1, 2 * PAGE_TOKENS), lambda i: (0, 0, 0)),
            pl.BlockSpec((HEADS, 1, SP_B), lambda i: (0, 0, 0)),
            pl.BlockSpec((MODEL_WIDTH, MODEL_WIDTH), lambda i: (0, column_at(i))),
            pl.BlockSpec((COORDS, MODEL_WIDTH), lambda i: (0, jnp.maximum(i - TABLE_STEP, 0))),
            pl.BlockSpec(page, lambda i: (0, 0)),
            pl.BlockSpec(page, lambda i: (0, 0)),
            pl.BlockSpec((8, MODEL_WIDTH), lambda i: (0, 0)),
            *(pl.BlockSpec(shape, lambda i: (0, 0)) for shape, kind in blocks),
        ],
        out_shape=[
            jax.ShapeDtypeStruct((HEADS, 1, 2 * PAGE_TOKENS), jnp.float32),
            jax.ShapeDtypeStruct((HEADS, 1, SP_B), jnp.float32),
            jax.ShapeDtypeStruct(weights.shape, jnp.bfloat16),
            jax.ShapeDtypeStruct((COORDS, 2 * MODEL_WIDTH), jnp.bfloat16),
            jax.ShapeDtypeStruct(page, jnp.float32),
            jax.ShapeDtypeStruct(page, jnp.float32),
            jax.ShapeDtypeStruct((8, MODEL_WIDTH), jnp.float32),
            *(jax.ShapeDtypeStruct(shape, jnp.float32) for shape, kind in blocks),
        ],
        scratch_shapes=[
            pltpu.VMEM(proj.shape, jnp.bfloat16),
            pltpu.VMEM((MODEL_WIDTH, PAGE_TOKENS), jnp.bfloat16),
            pltpu.VMEM((4, *page), jnp.float32),
            pltpu.VMEM((2, 4 * PAGE_TOKENS, SP_B), jnp.bfloat16),
            pltpu.VMEM((2, 128, PAGE_TOKENS), jnp.bfloat16),
            pltpu.VMEM((2, 4, PAGE_TOKENS, PAGE_TOKENS), jnp.bfloat16),
            pltpu.VMEM((PAGE_TOKENS, PAGE_TOKENS), jnp.bfloat16),
            pltpu.VMEM(lefts.shape, jnp.bfloat16),
            pltpu.VMEM(page, jnp.float32),
            pltpu.VMEM(page, jnp.float32),
            pltpu.SemaphoreType.DMA((3,)),
            *scatter_scratch(line, blocks),
        ],
        compiler_params=pltpu.CompilerParams(
            collective_id=collective_id, has_side_effects=True, vmem_limit_bytes=63 << 20
        ),
        name="backward_layer",
    )(
        proj, probs, upstream, anchor_rows, anchor_cols, lefts, weights, mixer_grad, normal, hits,
        *(grad.reshape(line * RING, 2, *grad.shape[1:]) for grad in grads),
    )


def last_kernel(line, count, token_total, *refs):
    sums_ref, kept_ref, normal_ref, scale_ref, features_hbm, backbone_hbm = refs[:6]
    ins = refs[6 : 7 + count]
    feature_grad_ref, total_ref = refs[7 + count : 9 + count]
    outs = refs[9 + count : 11 + 2 * count]
    turned_ref, conv_grad_ref, late_ref = refs[11 + 2 * count : 14 + 2 * count]
    rest = refs[14 + 2 * count :]
    features_ref, backbone_ref, fetch_sem, local_ref, *rest = rest
    sums = exchange_stages(line, add_up, local_ref, total_ref, rest[:7])
    stop = 7 + 5 * count + 9
    early = scatter_stages(line, ins[:count], outs[:count], rest[7:stop])
    late = scatter_stages(line, [late_ref], outs[count : count + 1], rest[stop : stop + 14])
    flat = flat_scatter_stages(line, ins[count:], outs[count + 1 :], rest[stop + 14 :])
    share = late_ref.shape[2]

    def first(stages, k):
        spread(line, 4, k, 0, stages.first)

    def second(stages, k):
        spread(line, 4, k, 0, stages.second)

    def third(stages, k):
        spread(line, 4, k, 0, stages.third)

    fetches = [
        pltpu.make_async_copy(source, target, fetch_sem.at[k])
        for k, (source, target) in enumerate(((features_hbm, features_ref), (backbone_hbm, backbone_ref)))
    ]
    greet_peers(line)
    local_ref[...] = sums_ref[2:4, :]
    sums.near()
    flat.start()
    early.start()
    for fetch in fetches:
        fetch.start()
    sums.far()
    first(flat, 0)
    first(early, 0)
    first(early, 1)
    sums.total()
    conv_grad_ref[...] = (
        scale_ref[0:1, :]
        * (kept_ref[...] - total_ref[0:1, :] / token_total - normal_ref[...] * (total_ref[1:2, :] / token_total))
    ).astype(jnp.bfloat16)
    second(early, 0)
    first(flat, 1)
    first(early, 2)
    first(early, 3)

    for fetch in fetches:
        fetch.wait()

    def turn(k, unused):
        columns = pl.ds(pl.multiple_of(k * 512, 512), 512)
        turned_ref[columns, :] = features_ref[:, columns].T
        return unused

    lax.fori_loop(0, features_ref.shape[1] // 512, turn, 0)
    width = min(512, 2 * share * line * RING)

    def backbone(k, unused):
        rows = pl.ds(pl.multiple_of(k * width, width), width)
        block = dot_nn(turned_ref[rows, :], conv_grad_ref[...])
        places = width // (2 * share)
        late_ref[pl.ds(k * places, places)] = block.reshape(places, 2, share, MODEL_WIDTH).astype(jnp.bfloat16)
        return unused

    lax.fori_loop(0, features_ref.shape[1] // width, backbone, 0)
    late.start()
    for k in range(4):
        first(late, k)
    first(flat, 2)
    second(early, 1)
    third(early, 0)

    def feature(k, unused):
        columns = pl.ds(pl.multiple_of(k * 512, 512), 512)
        feature_grad_ref[:, columns] = dot_nt(conv_grad_ref[...], backbone_ref[columns, :])
        return unused

    lax.fori_loop(0, features_ref.shape[1] // 512, feature, 0)
    first(flat, 3)
    for k in range(4):
        second(late, k)
    second(early, 2)
    flat.second()
    second(early, 3)
    third(early, 1)
    third(late, 0)
    third(late, 1)
    third(early, 2)
    third(late, 2)
    flat.third()
    third(early, 3)
    third(late, 3)
    sums.end()
    early.end()
    late.end()
    flat.end()


def last_layer(
    sums, kept, normal, scale, features, backbone, grads, flat_grad, token_total, collective_id
):
    dp = lax.axis_size("dp")
    line = dp // RING
    count = len(grads)
    blocks = [(grad.shape[1:], grad.dtype) for grad in grads]
    flat = [(flat_grad.shape[1:], flat_grad.dtype)]
    pair = (2, MODEL_WIDTH)
    channels = backbone.shape[0]
    late = [((channels // (2 * dp), MODEL_WIDTH), jnp.bfloat16)]
    anywhere = pl.BlockSpec(memory_space=pl.ANY)
    vmem = pl.BlockSpec(memory_space=pltpu.VMEM)
    return pl.pallas_call(
        partial(last_kernel, line, count, float(token_total)),
        in_specs=[*[vmem] * 4, *[anywhere] * (count + 3)],
        out_specs=[vmem] * (4 + count),
        out_shape=[
            jax.ShapeDtypeStruct(features.shape, jnp.float32),
            jax.ShapeDtypeStruct(pair, jnp.float32),
            *(jax.ShapeDtypeStruct(shape, jnp.float32) for shape, kind in blocks + late + flat),
        ],
        scratch_shapes=[
            pltpu.VMEM((channels, PAGE_TOKENS), jnp.bfloat16),
            pltpu.VMEM(kept.shape, jnp.bfloat16),
            pltpu.VMEM((dp, 2, *late[0][0]), jnp.bfloat16),
            pltpu.VMEM(features.shape, jnp.bfloat16),
            pltpu.VMEM(backbone.shape, jnp.bfloat16),
            pltpu.SemaphoreType.DMA((2,)),
            pltpu.VMEM(pair, jnp.float32),
            *exchange_scratch(line, pair),
            *scatter_scratch(line, blocks),
            *scatter_scratch(line, late),
            *flat_scatter_scratch(line, flat),
        ],
        compiler_params=pltpu.CompilerParams(
            collective_id=collective_id, has_side_effects=True, vmem_limit_bytes=63 << 20
        ),
        name="last_layer",
    )(
        sums, kept, normal, scale, features, backbone,
        *(grad.reshape(line * RING, 2, *grad.shape[1:]) for grad in [*grads, flat_grad]),
    )


def finish_kernel(pieces, share, expand_share, bias_rows, *refs):
    given = pieces[-1][0] + 1
    count = len(pieces)
    ins = refs[:given]
    small_ref, total_ref = refs[given : given + 2]
    refs = refs[given + 2 :]
    outs, small_outs, staged = refs[:count], refs[count : count + 12], refs[count + 12 : count + 24]
    sems, small_sems = refs[count + 24 :]
    copies = [
        pltpu.make_async_copy(ins[k].at[:, pl.ds(start, width)], outs[place], sems.at[place])
        for place, (k, start, width) in enumerate(pieces)
    ]
    for copy in copies:
        copy.start()
    staged[0][...] = small_ref[:bias_rows, :HEADS]
    staged[1][...] = small_ref[bias_rows : 2 * bias_rows, :HEADS]
    for k in range(7):
        staged[2 + k][...] = small_ref[2 * bias_rows + k : 2 * bias_rows + k + 1, :share]
    staged[9][...] = small_ref[2 * bias_rows + 7 : 2 * bias_rows + 8, :expand_share]
    owner = (lax.axis_index("dp") * 2 + lax.axis_index("pair")) * share
    chosen = lax.broadcasted_iota(jnp.int32, (MODEL_WIDTH, 128), 0) == (
        lax.broadcasted_iota(jnp.int32, (MODEL_WIDTH, 128), 1) + owner
    )
    owned = lax.dot_general(
        total_ref[...], chosen.astype(jnp.float32), (((1,), (0,)), ((), ())),
        precision=lax.Precision.HIGHEST, preferred_element_type=jnp.float32,
    )
    for k in range(2):
        staged[10 + k][...] = owned[k : k + 1, :share]
    small_copies = [pltpu.make_async_copy(staged[k], small_outs[k], small_sems.at[k]) for k in range(12)]
    for copy in small_copies:
        copy.start()
    for copy in copies + small_copies:
        copy.wait()


def finish(arrays, cut, small, totals, share, expand_share, bias_rows):
    pieces = [(k, 0, array.shape[1]) for k, array in enumerate(arrays)]
    if cut:
        k, start, width = pieces.pop()
        pieces += [(k, 0, cut), (k, cut, width - cut)]
    count = len(pieces)
    anywhere = pl.BlockSpec(memory_space=pl.ANY)
    vmem = pl.BlockSpec(memory_space=pltpu.VMEM)
    shapes = [(bias_rows, HEADS)] * 2 + [(1, share)] * 7 + [(1, expand_share)] + [(1, share)] * 2
    return pl.pallas_call(
        partial(finish_kernel, tuple(pieces), share, expand_share, bias_rows),
        in_specs=[vmem] * (len(arrays) + 2),
        out_specs=[anywhere] * (count + 12),
        out_shape=[
            *(jax.ShapeDtypeStruct((arrays[k].shape[0], width), jnp.float32) for k, start, width in pieces),
            *(jax.ShapeDtypeStruct(shape, jnp.float32) for shape in shapes),
        ],
        scratch_shapes=[
            *(pltpu.VMEM(shape, jnp.float32) for shape in shapes),
            pltpu.SemaphoreType.DMA((count,)),
            pltpu.SemaphoreType.DMA((12,)),
        ],
        name="finish",
    )(*arrays, small, totals)


norm_epsilon = 1e-05


def normal_parts(values):
    center = values - jnp.mean(values, axis=-1, keepdims=True)
    inverse = lax.rsqrt(jnp.mean(center * center, axis=-1, keepdims=True) + norm_epsilon)
    return center * inverse, inverse


def normal_back(normal, inverse, gain, grad):
    scaled = grad * gain
    return inverse * (
        scaled
        - jnp.mean(scaled, axis=-1, keepdims=True)
        - normal * jnp.mean(scaled * normal, axis=-1, keepdims=True)
    )


def mixer_kernel(
    merged_ref, start_ref, cotangent_ref, vectors_ref, bias_ref, merge_ref, expand_hbm, reduce_hbm,
    output_ref, mixer_grad_ref, merged_grad_ref, wide_grad_ref, reduce_grad_ref, sums_ref, bias_grad_ref,
    hidden_ref, normal_ref, inverse_ref, low_ref, active_ref, slope_ref, dense_ref, grad_ref, grad_low_ref,
    turned_ref, expand_ref, reduce_ref, fetch_sem,
):
    step = pl.program_id(0)
    chunk = lax.rem(step, CHUNKS)
    width = expand_ref.shape[1] // CHUNKS
    part = pl.ds(pl.multiple_of(chunk * width, width), width)

    def vector(k):
        return vectors_ref[k : k + 1, :]

    def column_sum(values):
        return jnp.sum(values, axis=0, keepdims=True)

    fetches = [
        pltpu.make_async_copy(source, target, fetch_sem.at[k])
        for k, (source, target) in enumerate(((expand_hbm, expand_ref), (reduce_hbm, reduce_ref)))
    ]

    @pl.when(step == 0)
    def _():
        for fetch in fetches:
            fetch.start()
        normal, inverse = normal_parts(start_ref[...] + dot_nn(merged_ref[...], merge_ref[...]))
        normal_ref[...] = normal
        inverse_ref[...] = jnp.broadcast_to(inverse, inverse_ref.shape)
        hidden = normal * vector(4) + vector(5)
        hidden_ref[...] = hidden
        low_ref[...] = hidden.astype(jnp.bfloat16)
        dense_ref[...] = jnp.zeros_like(dense_ref)
        for fetch in fetches:
            fetch.wait()

    @pl.when(step < CHUNKS)
    def _():
        inner = dot_nn(low_ref[...], expand_ref[:, part]) + bias_ref[chunk]
        share = 0.5 + 0.5 * lax.erf(inner * (0.5**0.5))
        active = (inner * share).astype(jnp.bfloat16)
        active_ref[chunk] = active
        slope_ref[chunk] = share + inner * jnp.exp(-0.5 * inner * inner) * (2.0 * jnp.pi) ** -0.5
        dense_ref[...] += dot_nn(active, reduce_ref[part, :])

    @pl.when(step == CHUNKS - 1)
    def _():
        normal, inverse = normal_parts(hidden_ref[...] + (dense_ref[...] + vector(6)))
        output_ref[...] = (normal * vector(7) + vector(8)).astype(jnp.bfloat16)
        upstream = cotangent_ref[...].astype(jnp.float32)
        grad = normal_back(normal, inverse, vector(7), upstream)
        grad_ref[...] = grad
        grad_low_ref[...] = grad.astype(jnp.bfloat16)
        sums_ref[2:3, :] = column_sum(grad)
        sums_ref[3:4, :] = column_sum(upstream * normal)
        sums_ref[4:5, :] = column_sum(upstream)
        turned_ref[...] = low_ref[...].T

    @pl.when(jnp.logical_and(step >= CHUNKS, step < 2 * CHUNKS))
    def _():
        grad_low = grad_low_ref[...]
        reduce_grad_ref[...] = dot_tn(active_ref[chunk], grad_low).astype(jnp.bfloat16)
        inner_low = (dot_nt(grad_low, reduce_ref[part, :]) * slope_ref[chunk]).astype(jnp.bfloat16)
        bias_grad_ref[chunk] = column_sum(inner_low.astype(jnp.float32))
        wide_grad_ref[...] = dot_nn(turned_ref[...], inner_low).astype(jnp.bfloat16)
        grad_ref[...] += dot_nt(inner_low, expand_ref[:, part])

    @pl.when(step == 2 * CHUNKS)
    def _():
        grad = grad_ref[...]
        normal = normal_ref[...]
        mixer_grad = normal_back(normal, inverse_ref[:, :1], vector(4), grad)
        mixer_grad_ref[...] = mixer_grad
        sums_ref[0:1, :] = column_sum(grad * normal)
        sums_ref[1:2, :] = column_sum(grad)
        low = mixer_grad.astype(jnp.bfloat16)
        wide_grad_ref[...] = dot_tn(merged_ref[...], low).astype(jnp.bfloat16)
        merged_grad_ref[...] = dot_nt(low, merge_ref[...]).astype(jnp.bfloat16)


def mixer_layer(merged, start, cotangent, vectors, bias, w_merge, w_expand, w_reduce):
    rows = merged.shape[0]
    inner = w_expand.shape[1]
    width = inner // CHUNKS
    page = (rows, MODEL_WIDTH)

    def back_at(i):
        return jnp.clip(i - CHUNKS, 0, CHUNKS - 1)

    def whole(shape):
        return pl.BlockSpec(shape, lambda i: (0,) * len(shape))

    f32, bf16 = jnp.float32, jnp.bfloat16
    outs = [
        (page, bf16, whole(page)),
        (page, f32, whole(page)),
        (page, bf16, whole(page)),
        (
            (MODEL_WIDTH, inner + MODEL_WIDTH), bf16,
            pl.BlockSpec((MODEL_WIDTH, width), lambda i: (0, jnp.maximum(i - CHUNKS, 0))),
        ),
        ((inner, MODEL_WIDTH), bf16, pl.BlockSpec((width, MODEL_WIDTH), lambda i: (back_at(i), 0))),
        ((8, MODEL_WIDTH), f32, whole((8, MODEL_WIDTH))),
        ((CHUNKS, 1, width), f32, whole((CHUNKS, 1, width))),
    ]
    return pl.pallas_call(
        mixer_kernel,
        grid=(2 * CHUNKS + 1,),
        in_specs=[
            once(page),
            once(page),
            once(page),
            once(vectors.shape),
            once(bias.shape),
            once(w_merge.shape),
            pl.BlockSpec(memory_space=pl.ANY),
            pl.BlockSpec(memory_space=pl.ANY),
        ],
        out_specs=[spec for shape, kind, spec in outs],
        out_shape=[jax.ShapeDtypeStruct(shape, kind) for shape, kind, spec in outs],
        scratch_shapes=[
            pltpu.VMEM(page, f32),
            pltpu.VMEM(page, f32),
            pltpu.VMEM((rows, 128), f32),
            pltpu.VMEM(page, bf16),
            pltpu.VMEM((CHUNKS, rows, width), bf16),
            pltpu.VMEM((CHUNKS, rows, width), f32),
            pltpu.VMEM(page, f32),
            pltpu.VMEM(page, f32),
            pltpu.VMEM(page, bf16),
            pltpu.VMEM((MODEL_WIDTH, rows), bf16),
            pltpu.VMEM(w_expand.shape, bf16),
            pltpu.VMEM(w_reduce.shape, bf16),
            pltpu.SemaphoreType.DMA((2,)),
        ],
        compiler_params=pltpu.CompilerParams(vmem_limit_bytes=62 << 20),
        name="mixer_layer",
    )(merged, start, cotangent, vectors, bias, w_merge, w_expand, w_reduce)

AXES = ("dp", "pair")


def padded_rows(pieces):
    total = sum(piece.shape[0] for piece in pieces)
    rows = -(-total // 8) * 8
    whole = jnp.zeros((rows, 128), jnp.float32)
    start = 0
    for piece in pieces:
        stop = start + piece.shape[0]
        whole += jnp.pad(piece.astype(jnp.float32), ((start, rows - stop), (0, 128 - piece.shape[1])))
        start = stop
    return whole


def blocks_of(grad, devices):
    blocks = grad.astype(jnp.bfloat16).reshape(devices, grad.shape[0] // devices, grad.shape[1])
    return blocks if blocks.shape[1] % 8 == 0 else blocks.reshape(devices, -1, 128)


def per_device(
    text_inputs,
    region_features,
    text_masked,
    region_masked,
    text_anchors,
    region_anchors,
    backbone_weight,
    batch_gain,
    batch_shift,
    text_blank,
    region_blank,
    position_table,
    stream_weights,
    linear_bias,
    planar_bias,
    merge_weight,
    mixer_gain,
    mixer_shift,
    expand_weight,
    expand_bias,
    reduce_weight,
    reduce_bias,
    output_gain,
    output_shift,
    cotangent,
):
    devices = lax.axis_size(AXES)
    row_count = text_inputs.shape[0]
    token_total = row_count * devices
    share = MODEL_WIDTH // devices
    expand_share = expand_bias.shape[0]
    bias_rows = REL_B // devices
    vectors = (
        batch_gain, batch_shift, text_blank, region_blank, mixer_gain, mixer_shift, reduce_bias,
        output_gain, output_shift, expand_bias,
    )
    small = padded_rows([linear_bias, planar_bias, *(vector[None, :] for vector in vectors)])
    packed, w_backbone, w_stream, w_table = gather_all(
        (small, backbone_weight, stream_weights), (position_table,), 0
    )
    w_backbone, w_table, w_stream = (
        whole.reshape(-1, whole.shape[-1]) for whole in (w_backbone, w_table, w_stream)
    )

    anchor_rows = jnp.concatenate([text_anchors, region_anchors], axis=0)
    anchor_cols = anchor_rows.T
    hits = jnp.stack([text_masked, region_masked], axis=1)
    proj, merged_low, probs, lefts, start_sum, normal_feat, batch_scale, w_vectors, w_expand_bias, *wholes = forward_layer(
        region_features, w_backbone, w_table, text_inputs, hits, packed, w_stream, anchor_rows, anchor_cols,
        (expand_weight, reduce_weight, merge_weight), token_total, 4,
    )
    w_expand, w_reduce, w_merge = (whole.reshape(-1, whole.shape[-1]) for whole in wholes)
    (
        layer_output, mixer_in_grad, merged_grad, wide_grad, reduce_weight_grad, mixer_sums, expand_bias_grad,
    ) = mixer_layer(
        merged_low, start_sum, cotangent, w_vectors, w_expand_bias,
        w_merge, w_expand, w_reduce,
    )
    early = (reduce_weight_grad, wide_grad)
    (
        linear_sums, planar_sums, stream_weights_grad, position_table_grad, text_gradient, region_kept,
        start_sums, *early_shares,
    ) = backward_layer(
        proj, probs, merged_grad, anchor_rows, anchor_cols, lefts, w_stream, mixer_in_grad, normal_feat, hits,
        [blocks_of(grad, devices) for grad in early], 5,
    )
    vector_grads = jnp.concatenate([start_sums[:2], mixer_sums[:5]], axis=0)
    pieces = [
        linear_folded(linear_sums[:, 0]).T.reshape(devices, bias_rows, HEADS),
        planar_sums[:, 0].T.reshape(devices, bias_rows, HEADS),
        vector_grads.reshape(7, devices, share).transpose(1, 0, 2),
        expand_bias_grad.reshape(devices, 1, expand_share),
    ]
    rows = sum(piece.shape[1] for piece in pieces)
    pieces = [jnp.pad(piece, ((0, 0), (0, 0), (0, 128 - piece.shape[2]))) for piece in pieces]
    small_grads = jnp.pad(jnp.concatenate(pieces, axis=1), ((0, 0), (0, -rows % 8), (0, 0)))
    feature_gradient, totals, small, stream_share, backbone_weight_grad, table_share = last_layer(
        start_sums, region_kept, normal_feat, batch_scale, region_features, w_backbone,
        [small_grads, blocks_of(stream_weights_grad, devices)], blocks_of(position_table_grad, devices),
        token_total, 1,
    )
    reduce_share, wide_share = early_shares
    cut = expand_weight.shape[1]
    wides = [wide_share]
    if wide_share.shape[1] != wide_grad.shape[1]:
        wide_share = wide_share.reshape(-1, wide_grad.shape[1])
        wides, cut = [wide_share[:, :cut], wide_share[:, cut:]], 0
    (
        text_gradient, feature_gradient, backbone_weight_grad, table_share, stream_share, reduce_share_grad,
        expand_share_grad, merge_share_grad, linear_grad, planar_grad, *vector_grads,
    ) = finish(
        [
            text_gradient, feature_gradient, backbone_weight_grad, table_share, stream_share, reduce_share, *wides,
        ],
        cut, small, totals, share, expand_share, bias_rows,
    )
    vector_grads = [grad.reshape(-1) for grad in vector_grads]
    return (
        layer_output,
        text_gradient,
        feature_gradient,
        backbone_weight_grad,
        vector_grads[9],
        vector_grads[8],
        vector_grads[0],
        vector_grads[1],
        table_share.reshape(-1, position_table.shape[1]),
        stream_share.reshape(-1, stream_weights.shape[1]),
        linear_grad,
        planar_grad,
        merge_share_grad.reshape(-1, MODEL_WIDTH),
        vector_grads[2],
        vector_grads[3],
        expand_share_grad.reshape(-1, expand_weight.shape[1]),
        vector_grads[7],
        reduce_share_grad.reshape(-1, MODEL_WIDTH),
        vector_grads[4],
        vector_grads[5],
        vector_grads[6],
    )

def solution(mesh):
    in_specs = (
        P(("dp", "pair"), None),
        P(("dp", "pair"), None),
        P(("dp", "pair")),
        P(("dp", "pair")),
        P(None, ("dp", "pair")),
        P(None, ("dp", "pair")),
        P(("dp", "pair"), None),
        P(("dp", "pair")),
        P(("dp", "pair")),
        P(("dp", "pair")),
        P(("dp", "pair")),
        P(("dp", "pair"), None),
        P(("dp", "pair"), None),
        P(("dp", "pair"), None),
        P(("dp", "pair"), None),
        P(("dp", "pair"), None),
        P(("dp", "pair")),
        P(("dp", "pair")),
        P(("dp", "pair"), None),
        P(("dp", "pair")),
        P(("dp", "pair"), None),
        P(("dp", "pair")),
        P(("dp", "pair")),
        P(("dp", "pair")),
        P(("dp", "pair"), None),
    )
    out_specs = (
        P(("dp", "pair"), None),
        P(("dp", "pair"), None),
        P(("dp", "pair"), None),
        P(("dp", "pair"), None),
        P(("dp", "pair")),
        P(("dp", "pair")),
        P(("dp", "pair")),
        P(("dp", "pair")),
        P(("dp", "pair"), None),
        P(("dp", "pair"), None),
        P(("dp", "pair"), None),
        P(("dp", "pair"), None),
        P(("dp", "pair"), None),
        P(("dp", "pair")),
        P(("dp", "pair")),
        P(("dp", "pair"), None),
        P(("dp", "pair")),
        P(("dp", "pair"), None),
        P(("dp", "pair")),
        P(("dp", "pair")),
        P(("dp", "pair")),
    )
    return jax.shard_map(
        per_device, mesh=mesh, in_specs=in_specs, out_specs=out_specs, check_vma=False
    )
```

```python
from functools import partial
from types import SimpleNamespace

import jax
import jax.numpy as jnp
from jax import lax
from jax.experimental import pallas as pl
from jax.experimental.pallas import tpu as pltpu
from jax.sharding import PartitionSpec as P

HEADS = 12
HEAD_DIM = 64
COORDS = 1024
REL_B = 256
SP_SIDE = 16
PAGE_TOKENS = 256
MODEL_WIDTH = 768
SP_B = 256
COORD_STEP = 128
PAIRS = HEADS // 2
LANES = 2 * HEAD_DIM


def dot_nt(left, right):
    return lax.dot_general(left, right, (((1,), (1,)), ((), ())), preferred_element_type=jnp.float32)


def dot_tn(left, right):
    return lax.dot_general(left, right, (((0,), (0,)), ((), ())), preferred_element_type=jnp.float32)


def dot_nn(left, right):
    return lax.dot_general(left, right, (((1,), (0,)), ((), ())), preferred_element_type=jnp.float32)


def head_columns(stream, kind, pair):
    return pl.ds(pl.multiple_of(((5 * stream + kind) * PAIRS + pair) * LANES, LANES), LANES)


def make_boxes(rows_ref, cols_ref, box_ref):
    for stream in range(2):
        part = []
        for axis in range(2):
            along = rows_ref[2 * stream + axis : 2 * stream + axis + 1, :]
            down = cols_ref[:, 2 * stream + axis : 2 * stream + axis + 1]
            part.append(((along - down) >> 7) + SP_SIDE // 2)
        box_ref[stream] = part[0] * SP_SIDE + part[1]


def attend_pair(pair, proj_ref, linear_ref, planar_ref, box_ref, merged_ref, probs_ref):
    lane_head = lax.broadcasted_iota(jnp.int32, (PAGE_TOKENS, LANES), 1) // HEAD_DIM
    mixed = [None, None]
    for inner in range(2):
        head = 2 * pair + inner
        mine = lane_head == inner
        spread = jnp.broadcast_to(linear_ref[head], (PAGE_TOKENS, 2 * PAGE_TOKENS))
        linear_term = pltpu.roll(spread, PAGE_TOKENS + 1, 1, stride=1, stride_axis=0)[:, :PAGE_TOKENS]
        low_table = jnp.broadcast_to(planar_ref[head, :, :128], (PAGE_TOKENS, 128))
        high_table = jnp.broadcast_to(planar_ref[head, :, 128:], (PAGE_TOKENS, 128))
        total = None
        for stream in range(2):
            pieces = [proj_ref[:, head_columns(stream, kind, pair)] for kind in range(5)]
            zero = jnp.zeros_like(pieces[0])
            left = jnp.concatenate([jnp.where(mine, pieces[0], zero), jnp.where(mine, pieces[3], zero)], axis=1)
            right = jnp.concatenate([pieces[1], pieces[4]], axis=1)
            logits = dot_nt(left, right) * HEAD_DIM ** (-0.5)
            planar = []
            for half in range(2):
                box = box_ref[stream, :, 128 * half : 128 * half + 128]
                place = box & 127
                planar.append(
                    jnp.where(
                        box < 128,
                        jnp.take_along_axis(low_table, place, axis=1),
                        jnp.take_along_axis(high_table, place, axis=1),
                    )
                )
            logits = logits + linear_term + jnp.concatenate(planar, axis=1)
            top = jnp.max(logits, axis=-1, keepdims=True)
            shifted = jnp.exp(logits - top)
            probs = shifted / jnp.sum(shifted, axis=-1, keepdims=True)
            probs_ref[stream, inner] = probs
            part = dot_nn(probs.astype(jnp.bfloat16), pieces[2])
            total = part if total is None else total + part
        mixed[inner] = total
    merged_ref[...] = jnp.where(lane_head == 0, mixed[0], mixed[1]).astype(jnp.bfloat16)


def make_places(rows_ref, cols_ref, place_ref, turned_ref, mask_ref, flip_ref):
    lanes = lax.broadcasted_iota(jnp.int32, (PAGE_TOKENS, SP_B), 1)
    rows = lax.broadcasted_iota(jnp.int32, (PAGE_TOKENS, SP_B), 0)
    flip_ref[...] = (lanes + rows == PAGE_TOKENS - 1).astype(jnp.bfloat16)
    for stream in range(2):
        x_row = rows_ref[2 * stream : 2 * stream + 1, :]
        y_row = rows_ref[2 * stream + 1 : 2 * stream + 2, :]
        x_col = cols_ref[:, 2 * stream : 2 * stream + 1]
        y_col = cols_ref[:, 2 * stream + 1 : 2 * stream + 2]
        cell_row = (x_row >> 7) * SP_SIDE + (y_row >> 7)
        cell_col = (x_col >> 7) * SP_SIDE + (y_col >> 7)
        x_less = ((x_row & 127) < (x_col & 127)).astype(jnp.float32)
        y_less = ((y_row & 127) < (y_col & 127)).astype(jnp.float32)
        for x_side in range(2):
            for y_side in range(2):
                side = 2 * x_side + y_side
                place_ref[stream, side * PAGE_TOKENS : (side + 1) * PAGE_TOKENS, :] = (
                    lanes == cell_col + (SP_SIDE + 1 - SP_SIDE * x_side - y_side)
                ).astype(jnp.bfloat16)
                mask_ref[stream, side] = (
                    (x_less if x_side else 1.0 - x_less) * (y_less if y_side else 1.0 - y_less)
                ).astype(jnp.bfloat16)
        turned_ref[stream] = (rows[:128] == 127 - cell_row).astype(jnp.bfloat16)


def attend_back_pair(
    pair, pump, proj_ref, probs_ref, upstream_ref, grad_ref, linear_ref, planar_ref,
    place_ref, turned_ref, mask_ref, flip_ref,
):
    lane_head = lax.broadcasted_iota(jnp.int32, (PAGE_TOKENS, LANES), 1) // HEAD_DIM
    wide_head = jnp.concatenate([lane_head, lane_head], axis=1)
    upstream = upstream_ref[...]
    scale = HEAD_DIM ** (-0.5)
    diagonal = [None, None]
    for stream in range(2):
        pieces = [proj_ref[:, head_columns(stream, kind, pair)] for kind in range(5)]
        queries = jnp.concatenate([pieces[0], pieces[3]], axis=1)
        keys = jnp.concatenate([pieces[1], pieces[4]], axis=1)
        grads = []
        for inner in range(2):
            head = 2 * pair + inner
            mine = lane_head == inner
            grad_probs = dot_nt(jnp.where(mine, upstream, jnp.zeros_like(upstream)), pieces[2])
            probs = probs_ref[stream, inner]
            weighted = probs * grad_probs
            grad_logits = (weighted - probs * jnp.sum(weighted, axis=-1, keepdims=True)).astype(jnp.bfloat16)
            grads.append(
                (
                    dot_nn(grad_logits, keys) * scale,
                    dot_tn(grad_logits, queries) * scale,
                    dot_tn(probs.astype(jnp.bfloat16), upstream),
                )
            )
            parts = jnp.concatenate([grad_logits * mask_ref[stream, side] for side in range(4)], axis=1)
            placed = dot_nn(parts, place_ref[stream]).astype(jnp.bfloat16)
            cells = dot_nn(turned_ref[stream], placed)
            sums = jnp.sum(
                pltpu.roll(cells, SP_B - SP_SIDE // 2, 1, stride=1, stride_axis=0), axis=0, keepdims=True
            )
            if stream == 0:
                planar_ref[head] = sums
            else:
                planar_ref[head] += sums
            turned_over = dot_nn(flip_ref[...], grad_logits)
            diagonal[inner] = turned_over if stream == 0 else diagonal[inner] + turned_over
            pump(2 * stream + inner)
        query_grad, key_grad = (jnp.where(wide_head == 0, grads[0][k], grads[1][k]) for k in range(2))
        value_grad = jnp.where(lane_head == 0, grads[0][2], grads[1][2])
        for kind, value in enumerate(
            (query_grad[:, :LANES], key_grad[:, :LANES], value_grad, query_grad[:, LANES:], key_grad[:, LANES:])
        ):
            grad_ref[:, head_columns(stream, kind, pair)] = value.astype(jnp.bfloat16)
    for inner in range(2):
        padded = jnp.concatenate([diagonal[inner], jnp.zeros_like(diagonal[inner])], axis=1)
        linear_ref[2 * pair + inner] = jnp.sum(
            pltpu.roll(padded, 0, 1, stride=1, stride_axis=0), axis=0, keepdims=True
        )


def linear_folded(sums):
    first = REL_B // 2
    last = PAGE_TOKENS - 1 + REL_B // 2 - 1
    return jnp.concatenate(
        [
            jnp.sum(sums[:, :first], axis=1, keepdims=True),
            sums[:, first:last],
            jnp.sum(sums[:, last : 2 * PAGE_TOKENS - 1], axis=1, keepdims=True),
        ],
        axis=1,
    )


MESH = pl.DeviceIdType.MESH
RING = 4


def place():
    dp = lax.axis_index("dp")
    return dp // RING, lax.rem(dp, RING), lax.axis_index("pair")


def across(q, bit):
    other = lax.rem(q // bit, 2)
    return q + bit - 2 * bit * other


def greet(line):
    z, q, c = place()
    barrier = pltpu.get_barrier_semaphore()

    def signal(zz, qq, cc):
        pl.semaphore_signal(barrier, inc=1, device_id={"dp": zz * RING + qq, "pair": cc}, device_id_type=MESH)

    signal(z, across(q, 1), c)
    signal(z, across(q, 2), c)
    signal(z, q, 1 - c)

    @pl.when(z > 0)
    def _():
        signal(z - 1, q, c)

    @pl.when(z < line - 1)
    def _():
        signal(z + 1, q, c)

    ends = (z > 0).astype(jnp.int32) + (z < line - 1).astype(jnp.int32)
    pl.semaphore_wait(barrier, 3 + ends)


def spread(line, pumps, pump, first, work):
    total = line - first
    low, high = (first + total * (pump + k) // pumps for k in range(2))
    if high == low + 1:
        work(low)
    elif high > low:
        lax.fori_loop(low, high, lambda g, unused: (work(g), unused)[1], 0)


def gather_stages(line, ins, outs, sems):
    count = len(ins)
    (own_sem, z_send, z_recv, xy_send, xy_recv, d_send, d_recv, c_send, c_recv) = sems
    z, q, c = place()
    beside = (across(q, 1), across(q, 2))
    corner = across(across(q, 1), 2)

    def slot(zz, qq):
        return (zz * RING + qq) * 2 + c

    def remote(src, dst, send, recv, zz, qq, cc):
        return pltpu.make_async_remote_copy(
            src_ref=src, dst_ref=dst, send_sem=send, recv_sem=recv,
            device_id={"dp": zz * RING + qq, "pair": cc}, device_id_type=MESH,
        )

    def block(a, zz, qq):
        return outs[a].at[slot(zz, qq)]

    def halves(a):
        width = ins[a].shape[-1]
        cut = width // 2 if width % 256 == 0 else width
        return (0, cut), (cut, width - cut)

    def own(a):
        return pltpu.make_async_copy(ins[a], block(a, z, q), own_sem.at[a])

    def z_copy(a, way, step, first):
        zz = z - step if way == 0 else z + step
        target = z + 1 if way == 0 else z - 1
        src = ins[a] if first else block(a, zz, q)
        return remote(src, block(a, zz, q), z_send.at[way, a, step], z_recv.at[way, a, step], target, q, c)

    def xy_copy(a, axis, zz, first):
        src = ins[a] if first else block(a, zz, q)
        return remote(src, block(a, zz, q), xy_send.at[axis, a, zz], xy_recv.at[axis, a, zz], z, beside[axis], c)

    def d_copy(a, axis, zz):
        start, width = halves(a)[axis]
        part = outs[a].at[slot(zz, beside[axis]), :, pl.ds(start, width)]
        return remote(part, part, d_send.at[axis, a, zz], d_recv.at[axis, a, zz], z, beside[1 - axis], c)

    def c_copy(a, zz, qq, first):
        src = ins[a] if first else block(a, zz, qq)
        return remote(
            src, block(a, zz, qq), c_send.at[a, zz * RING + qq], c_recv.at[a, zz * RING + qq], z, q, 1 - c
        )

    def start_line():
        for a in range(count):
            own(a).start()
            for way in range(2):
                @pl.when(z < line - 1 if way == 0 else z > 0)
                def _():
                    z_copy(a, way, 0, True).start()
            c_copy(a, z, q, True).start()

    def start_ring():
        for a in range(count):
            for axis in range(2):
                xy_copy(a, axis, z, True).start()

    def arrived(a, zz):
        for axis in range(2):
            xy_copy(a, axis, zz, False).start()
        c_copy(a, zz, q, False).start()

    def passed_on(a, zz):
        for axis in range(2):
            start, width = halves(a)[axis]
            got = block(a, zz, beside[axis])
            remote(got, got, xy_send.at[axis, a, zz], xy_recv.at[axis, a, zz], z, beside[axis], c).wait_recv()
            if width:
                d_copy(a, axis, zz).start()
            c_copy(a, zz, beside[axis], False).start()

    def finished(a, zz):
        for axis in range(2):
            start, width = halves(a)[axis]
            if width:
                part = outs[a].at[slot(zz, corner), :, pl.ds(start, width)]
                remote(part, part, d_send.at[axis, a, zz], d_recv.at[axis, a, zz], z, beside[1 - axis], c).wait_recv()
        c_copy(a, zz, corner, False).start()

    def both_ways(g, work):
        @pl.when(z - g >= 0)
        def _():
            work(z - g)

        @pl.when(jnp.logical_and(z + g <= line - 1, g > 0))
        def _():
            work(z + g)

    def along(g):
        for a in range(count):
            @pl.when(z - g >= 0)
            def _():
                got = block(a, z - g, q)
                remote(got, got, z_send.at[0, a, g - 1], z_recv.at[0, a, g - 1], z, q, 1 - c).wait_recv()

                @pl.when(z < line - 1)
                def _():
                    z_copy(a, 0, g, False).start()

                arrived(a, z - g)

            @pl.when(z + g <= line - 1)
            def _():
                got = block(a, z + g, q)
                remote(got, got, z_send.at[1, a, g - 1], z_recv.at[1, a, g - 1], z, q, 1 - c).wait_recv()

                @pl.when(z > 0)
                def _():
                    z_copy(a, 1, g, False).start()

                arrived(a, z + g)

    def around(g):
        for a in range(count):
            both_ways(g, partial(passed_on, a))

    def home(g):
        for a in range(count):
            both_ways(g, partial(finished, a))

    def drain(zz, unused):
        for a in range(count):
            for axis in range(2):
                xy_copy(a, axis, zz, False).wait_send()
                if halves(a)[axis][1]:
                    d_copy(a, axis, zz).wait_send()
            for qq in range(RING):
                c_copy(a, zz, qq, False).wait_send()
                got = outs[a].at[(zz * RING + qq) * 2 + 1 - c]
                remote(
                    got, got, c_send.at[a, zz * RING + qq], c_recv.at[a, zz * RING + qq], z, q, 1 - c
                ).wait_recv()

            @pl.when(jnp.logical_and(z < line - 1, zz <= z))
            def _():
                z_copy(a, 0, z - zz, False).wait_send()

            @pl.when(jnp.logical_and(z > 0, zz >= z))
            def _():
                z_copy(a, 1, zz - z, False).wait_send()
        return unused

    def end():
        for a in range(count):
            own(a).wait()
        lax.fori_loop(0, line, drain, 0)

    return SimpleNamespace(
        start_line=start_line, start_ring=start_ring, along=along, around=around, home=home, end=end
    )


def gather_sems(line, count):
    dma = pltpu.SemaphoreType.DMA
    return [
        dma((count,)),
        *(dma((2, count, line)) for k in range(6)),
        dma((count, line * RING)),
        dma((count, line * RING)),
    ]


def group_of(zz):
    return pl.ds(zz * RING, RING)


def flat_gather_stages(line, ins, outs, sems):
    count = len(ins)
    own_sem, xy_send, xy_recv, d_send, d_recv, z_send, z_recv, c_send, c_recv = sems
    z, q, c = place()
    beside = (across(q, 1), across(q, 2))
    corner = across(across(q, 1), 2)

    def remote(src, dst, send, recv, zz, qq, cc):
        return pltpu.make_async_remote_copy(
            src_ref=src, dst_ref=dst, send_sem=send, recv_sem=recv,
            device_id={"dp": zz * RING + qq, "pair": cc}, device_id_type=MESH,
        )

    def block(a, qq):
        return outs[a].at[z * RING + qq, c]

    def halves(a):
        width = ins[a].shape[-1]
        return (0, width // 2), (width // 2, width // 2)

    def own(a):
        return pltpu.make_async_copy(ins[a], block(a, q), own_sem.at[a])

    def xy_copy(a, axis):
        return remote(ins[a], block(a, q), xy_send.at[axis, a], xy_recv.at[axis, a], z, beside[axis], c)

    def xy_got(a, axis):
        got = block(a, beside[axis])
        return remote(got, got, xy_send.at[axis, a], xy_recv.at[axis, a], z, beside[axis], c)

    def d_copy(a, axis, qq):
        start, width = halves(a)[axis]
        part = outs[a].at[z * RING + qq, c, :, pl.ds(start, width)]
        return remote(part, part, d_send.at[axis, a], d_recv.at[axis, a], z, beside[1 - axis], c)

    def z_copy(a, way, zz, target):
        part = outs[a].at[group_of(zz), c]
        return remote(part, part, z_send.at[way, a, zz], z_recv.at[way, a, zz], target, q, c)

    def c_copy(a, zz, cc):
        part = outs[a].at[group_of(zz), cc]
        return remote(part, part, c_send.at[a, zz], c_recv.at[a, zz], z, q, 1 - c)

    def ahead(way):
        return z < line - 1 if way == 0 else z > 0

    def start():
        for a in range(count):
            own(a).start()
            for axis in range(2):
                xy_copy(a, axis).start()

    def around():
        for a in range(count):
            for axis in range(2):
                xy_got(a, axis).wait_recv()
                d_copy(a, axis, beside[axis]).start()

    def home():
        for a in range(count):
            own(a).wait()
            for axis in range(2):
                d_copy(a, axis, corner).wait_recv()
            for way in range(2):
                @pl.when(ahead(way))
                def _():
                    z_copy(a, way, z, z + 1 - 2 * way).start()
            c_copy(a, z, c).start()

    def along(g):
        for a in range(count):
            for way in range(2):
                zz = z - g if way == 0 else z + g

                @pl.when(zz >= 0 if way == 0 else zz <= line - 1)
                def _():
                    z_copy(a, way, zz, z - 1 + 2 * way).wait_recv()

                    @pl.when(ahead(way))
                    def _():
                        z_copy(a, way, zz, z + 1 - 2 * way).start()

                    c_copy(a, zz, c).start()

    def end():
        for a in range(count):
            for axis in range(2):
                xy_copy(a, axis).wait_send()
                d_copy(a, axis, beside[axis]).wait_send()

            def drain(zz, unused):
                c_copy(a, zz, c).wait_send()
                c_copy(a, zz, 1 - c).wait_recv()
                for way in range(2):
                    @pl.when(jnp.logical_and(ahead(way), zz <= z if way == 0 else zz >= z))
                    def _():
                        z_copy(a, way, zz, z + 1 - 2 * way).wait_send()
                return unused

            lax.fori_loop(0, line, drain, 0)

    return SimpleNamespace(start=start, around=around, home=home, along=along, end=end)


def flat_gather_sems(line, count):
    dma = pltpu.SemaphoreType.DMA
    return [
        dma((count,)),
        *(dma((2, count)) for k in range(4)),
        *(dma((2, count, line)) for k in range(2)),
        *(dma((count, line)) for k in range(2)),
    ]


def gather_kernel(line, count, flat, *refs):
    both = count + flat
    ins, outs, sems = refs[:both], refs[both : 2 * both], refs[2 * both :]
    stages = gather_stages(line, ins[:count], outs[:count], sems[:9])
    plane = flat_gather_stages(line, ins[count:], outs[count:], sems[9:])
    greet(line)
    plane.start()
    stages.start_line()
    stages.start_ring()

    def generation(g, unused):
        stages.along(g)
        stages.around(g - 1)

        @pl.when(g == 1)
        def _():
            plane.around()

        @pl.when(g == 2)
        def _():
            plane.home()

        @pl.when(g >= 3)
        def _():
            stages.home(g - 3)

        return unused

    lax.fori_loop(1, line, generation, 0)
    if line == 2:
        plane.home()

    def rest(g, unused):
        @pl.when(g <= line - 1)
        def _():
            plane.along(g)

        @pl.when(g == 1)
        def _():
            stages.around(line - 1)

        @pl.when(g + line - 4 >= 0)
        def _():
            stages.home(g + line - 4)

        return unused

    lax.fori_loop(1, 4, rest, 0)
    lax.fori_loop(4, line, lambda g, unused: (plane.along(g), unused)[1], 0)
    stages.end()
    plane.end()


def gather_all(shards, flat_shards, collective_id):
    dp = lax.axis_size("dp")
    line = dp // RING
    count, flat = len(shards), len(flat_shards)
    wholes = pl.pallas_call(
        partial(gather_kernel, line, count, flat),
        in_specs=[pl.BlockSpec(memory_space=pl.ANY)] * (count + flat),
        out_specs=[pl.BlockSpec(memory_space=pl.ANY)] * (count + flat),
        out_shape=[
            *(jax.ShapeDtypeStruct((2 * dp, *shard.shape), shard.dtype) for shard in shards),
            *(jax.ShapeDtypeStruct((dp, 2, *shard.shape), shard.dtype) for shard in flat_shards),
        ],
        scratch_shapes=[*gather_sems(line, count), *flat_gather_sems(line, flat)],
        compiler_params=pltpu.CompilerParams(collective_id=collective_id, has_side_effects=True),
        name="gather_all",
    )(*shards, *flat_shards)
    return [whole.reshape(2 * dp, *whole.shape[-2:]) for whole in wholes]


def scatter_stages(line, ins, outs, scratch):
    count = len(ins)
    groups = [scratch[k * count : (k + 1) * count] for k in range(5)]
    mine, beside_sum, half_in, full_in, line_in = groups
    (own_sem, c_send, c_recv, d_send, d_recv, xy_send, xy_recv, z_send, z_recv) = scratch[5 * count :]
    z, q, c = place()
    beside = (across(q, 1), across(q, 2))
    corner = across(across(q, 1), 2)

    def remote(src, dst, send, recv, zz, qq, cc):
        return pltpu.make_async_remote_copy(
            src_ref=src, dst_ref=dst, send_sem=send, recv_sem=recv,
            device_id={"dp": zz * RING + qq, "pair": cc}, device_id_type=MESH,
        )

    def halves(a):
        width = outs[a].shape[-1]
        cut = width // 2 if width % 256 == 0 else width
        return (0, cut), (cut, width - cut)

    def wide(value):
        return value.astype(jnp.float32)

    def group(zz):
        return pl.ds(zz * RING, RING)

    def own(a, zz):
        return pltpu.make_async_copy(ins[a].at[group(zz), c], mine[a].at[group(zz)], own_sem.at[a, zz])

    def c_copy(a, zz):
        return remote(
            ins[a].at[group(zz), 1 - c], beside_sum[a].at[group(zz)], c_send.at[a, zz], c_recv.at[a, zz], z, q, 1 - c
        )

    def d_copy(a, axis, zz):
        start, width = halves(a)[axis]
        return remote(
            mine[a].at[zz * RING + corner, :, pl.ds(start, width)],
            half_in[a].at[zz, :, pl.ds(start, width)],
            d_send.at[axis, a, zz], d_recv.at[axis, a, zz], z, beside[axis], c,
        )

    def xy_copy(a, axis, zz):
        return remote(
            mine[a].at[zz * RING + beside[axis]], full_in[a].at[axis, zz],
            xy_send.at[axis, a, zz], xy_recv.at[axis, a, zz], z, beside[axis], c,
        )

    def z_copy(a, way, zz):
        return remote(
            mine[a].at[zz * RING + q], line_in[a].at[way, zz],
            z_send.at[way, a, zz], z_recv.at[way, a, zz], z + 1 if way == 0 else z - 1, q, c,
        )

    def both_ways(g, work):
        @pl.when(z - g >= 0)
        def _():
            work(z - g)

        @pl.when(jnp.logical_and(z + g <= line - 1, g > 0))
        def _():
            work(z + g)

    def begin(zz):
        for a in range(count):
            c_copy(a, zz).start()
            own(a, zz).start()

    def first(zz):
        for a in range(count):
            own(a, zz).wait()
            c_copy(a, zz).wait_recv()

            def one(qq, unused):
                k = zz * RING + qq
                mine[a][k] = mine[a][k] + beside_sum[a][k]
                return unused

            lax.fori_loop(0, RING, one, 0)
            for axis in range(2):
                if halves(a)[axis][1]:
                    d_copy(a, axis, zz).start()

    def second(zz):
        for a in range(count):
            for axis in range(2):
                start, width = halves(a)[axis]
                k = zz * RING + beside[1 - axis]
                if width:
                    d_copy(a, axis, zz).wait_recv()
                    mine[a][k, :, start : start + width] = (
                        mine[a][k, :, start : start + width] + half_in[a][zz, :, start : start + width]
                    )
                xy_copy(a, 1 - axis, zz).start()

    def third(zz):
        for a in range(count):
            k = zz * RING + q
            for axis in range(2):
                xy_copy(a, axis, zz).wait_recv()
            mine[a][k] = (
                wide(mine[a][k]) + wide(full_in[a][0, zz]) + wide(full_in[a][1, zz])
            ).astype(mine[a].dtype)
            for way in range(2):
                @pl.when(zz > z if way == 0 else zz < z)
                def _():
                    @pl.when(z > 0 if way == 0 else z < line - 1)
                    def _():
                        z_copy(a, way, zz).wait_recv()
                        mine[a][k] = mine[a][k] + line_in[a][way, zz]

                    z_copy(a, way, zz).start()

            @pl.when(zz == z)
            def _():
                outs[a][...] = wide(mine[a][k])
                for way in range(2):
                    @pl.when(z > 0 if way == 0 else z < line - 1)
                    def _():
                        z_copy(a, way, zz).wait_recv()
                        outs[a][...] += wide(line_in[a][way, zz])

    def start():
        def begin_all(step, unused):
            both_ways(line - 1 - step, begin)
            return unused

        lax.fori_loop(0, line, begin_all, 0)

    def drain(zz, unused):
        for a in range(count):
            for axis in range(2):
                xy_copy(a, axis, zz).wait_send()
                if halves(a)[axis][1]:
                    d_copy(a, axis, zz).wait_send()
            c_copy(a, zz).wait_send()
            for way in range(2):
                @pl.when(zz > z if way == 0 else zz < z)
                def _():
                    z_copy(a, way, zz).wait_send()
        return unused

    def end():
        lax.fori_loop(0, line, drain, 0)

    return SimpleNamespace(
        start=start,
        first=lambda step: both_ways(line - 1 - step, first),
        second=lambda step: both_ways(line - 1 - step, second),
        third=lambda step: both_ways(line - 1 - step, third),
        end=end,
    )


def scatter_scratch(line, blocks):
    dma = pltpu.SemaphoreType.DMA
    count = len(blocks)
    return [
        *(pltpu.VMEM((line * RING, *shape), kind) for shape, kind in blocks),
        *(pltpu.VMEM((line * RING, *shape), kind) for shape, kind in blocks),
        *(pltpu.VMEM((line, *shape), kind) for shape, kind in blocks),
        *(pltpu.VMEM((2, line, *shape), kind) for shape, kind in blocks),
        *(pltpu.VMEM((2, line, *shape), kind) for shape, kind in blocks),
        *(dma((count, line)) for k in range(3)),
        *(dma((2, count, line)) for k in range(6)),
    ]


def flat_scatter_stages(line, ins, outs, scratch):
    count = len(ins)
    mine, beside_sum, line_in, half_in, full_in = (scratch[k * count : (k + 1) * count] for k in range(5))
    own_sem, c_send, c_recv, z_send, z_recv, d_send, d_recv, xy_send, xy_recv = scratch[5 * count :]
    z, q, c = place()
    beside = (across(q, 1), across(q, 2))
    corner = across(across(q, 1), 2)

    def remote(src, dst, send, recv, zz, qq, cc):
        return pltpu.make_async_remote_copy(
            src_ref=src, dst_ref=dst, send_sem=send, recv_sem=recv,
            device_id={"dp": zz * RING + qq, "pair": cc}, device_id_type=MESH,
        )

    def halves(a):
        width = outs[a].shape[-1]
        cut = width // 2 if width % 256 == 0 else width
        return (0, cut), (cut, width - cut)

    def own(a, zz):
        return pltpu.make_async_copy(ins[a].at[group_of(zz), c], mine[a].at[group_of(zz)], own_sem.at[a, zz])

    def c_copy(a, zz):
        return remote(
            ins[a].at[group_of(zz), 1 - c], beside_sum[a].at[group_of(zz)], c_send.at[a, zz], c_recv.at[a, zz],
            z, q, 1 - c,
        )

    def z_copy(a, way, zz):
        return remote(
            mine[a].at[group_of(zz)], line_in[a].at[way, group_of(zz)], z_send.at[way, a, zz],
            z_recv.at[way, a, zz], z + 1 - 2 * way, q, c,
        )

    def d_copy(a, axis):
        start, width = halves(a)[axis]
        return remote(
            mine[a].at[z * RING + corner, :, pl.ds(start, width)], half_in[a].at[:, pl.ds(start, width)],
            d_send.at[axis, a], d_recv.at[axis, a], z, beside[axis], c,
        )

    def xy_copy(a, axis):
        return remote(
            mine[a].at[z * RING + beside[axis]], full_in[a].at[axis], xy_send.at[axis, a], xy_recv.at[axis, a],
            z, beside[axis], c,
        )

    def behind(way):
        return z > 0 if way == 0 else z < line - 1

    def both_ways(g, work):
        @pl.when(z - g >= 0)
        def _():
            work(z - g)

        @pl.when(jnp.logical_and(z + g <= line - 1, g > 0))
        def _():
            work(z + g)

    def add(a, zz, part):
        def one(qq, unused):
            k = zz * RING + qq
            mine[a][k] = mine[a][k] + part[k]
            return unused

        lax.fori_loop(0, RING, one, 0)

    def begin(zz):
        for a in range(count):
            c_copy(a, zz).start()
            own(a, zz).start()

    def first(zz):
        for a in range(count):
            own(a, zz).wait()
            c_copy(a, zz).wait_recv()
            add(a, zz, beside_sum[a])
            for way in range(2):
                @pl.when(jnp.logical_and(behind(way), zz >= z if way == 0 else zz <= z))
                def _():
                    z_copy(a, way, zz).wait_recv()
                    add(a, zz, line_in[a].at[way])

                @pl.when(zz > z if way == 0 else zz < z)
                def _():
                    z_copy(a, way, zz).start()

            @pl.when(zz == z)
            def _():
                for axis in range(2):
                    if halves(a)[axis][1]:
                        d_copy(a, axis).start()

    def second():
        for a in range(count):
            for axis in range(2):
                start, width = halves(a)[axis]
                k = z * RING + beside[1 - axis]
                if width:
                    d_copy(a, axis).wait_recv()
                    mine[a][k, :, start : start + width] = (
                        mine[a][k, :, start : start + width] + half_in[a][:, start : start + width]
                    )
                xy_copy(a, 1 - axis).start()

    def third():
        for a in range(count):
            for axis in range(2):
                xy_copy(a, axis).wait_recv()
            outs[a][...] = sum(
                part.astype(jnp.float32) for part in (mine[a][z * RING + q], full_in[a][0], full_in[a][1])
            )

    def start():
        lax.fori_loop(0, line, lambda step, unused: (both_ways(line - 1 - step, begin), unused)[1], 0)

    def end():
        for a in range(count):
            for axis in range(2):
                if halves(a)[axis][1]:
                    d_copy(a, axis).wait_send()
                xy_copy(a, axis).wait_send()

            def drain(zz, unused):
                c_copy(a, zz).wait_send()
                for way in range(2):
                    @pl.when(zz > z if way == 0 else zz < z)
                    def _():
                        z_copy(a, way, zz).wait_send()
                return unused

            lax.fori_loop(0, line, drain, 0)

    return SimpleNamespace(
        start=start, first=lambda step: both_ways(line - 1 - step, first), second=second, third=third, end=end
    )


def flat_scatter_scratch(line, blocks):
    dma = pltpu.SemaphoreType.DMA
    count = len(blocks)
    return [
        *(pltpu.VMEM((line * RING, *shape), kind) for shape, kind in blocks),
        *(pltpu.VMEM((line * RING, *shape), kind) for shape, kind in blocks),
        *(pltpu.VMEM((2, line * RING, *shape), kind) for shape, kind in blocks),
        *(pltpu.VMEM(shape, kind) for shape, kind in blocks),
        *(pltpu.VMEM((2, *shape), kind) for shape, kind in blocks),
        *(dma((count, line)) for k in range(3)),
        *(dma((2, count, line)) for k in range(2)),
        *(dma((2, count)) for k in range(4)),
    ]


def peers(line):
    z, q, c = place()
    cell = q * 2 + c
    near = RING * 2

    def near_place(k):
        other = lax.rem(cell + k, near)
        return other, {"dp": z * RING + other // 2, "pair": lax.rem(other, 2)}

    def far_place(k):
        other = lax.rem(z + k, line)
        return other, {"dp": other * RING + q, "pair": c}

    def each(places, stop, work):
        def one(k, unused):
            work(*places(k))
            return unused

        lax.fori_loop(1, stop, one, 0)

    return partial(each, near_place, near), partial(each, far_place, line)


def greet_peers(line):
    barrier = pltpu.get_barrier_semaphore()
    for each in peers(line):
        each(
            lambda other, device: pl.semaphore_signal(barrier, inc=1, device_id=device, device_id_type=MESH)
        )
    pl.semaphore_wait(barrier, 2 * RING + line - 2)


def exchange_stages(line, combine, value_ref, total_ref, scratch):
    near_ref, part_ref, far_ref, n_send, n_recv, f_send, f_recv = scratch
    z, q, c = place()
    cell = q * 2 + c
    each_near, each_far = peers(line)

    def near_copy(other, device, source):
        return pltpu.make_async_remote_copy(
            src_ref=value_ref, dst_ref=near_ref.at[source], send_sem=n_send.at[other], recv_sem=n_recv.at[source],
            device_id=device, device_id_type=MESH,
        )

    def far_copy(other, device, source):
        return pltpu.make_async_remote_copy(
            src_ref=part_ref, dst_ref=far_ref.at[source], send_sem=f_send.at[other], recv_sem=f_recv.at[source],
            device_id=device, device_id_type=MESH,
        )

    def near():
        each_near(lambda other, device: near_copy(other, device, cell).start())
        near_ref[cell] = value_ref[...]

    def far():
        each_near(lambda other, device: near_copy(other, device, other).wait_recv())
        part_ref[...] = combine(near_ref, 2 * RING, 1)
        each_far(lambda other, device: far_copy(other, device, z).start())
        far_ref[z] = part_ref[...]

    def total():
        each_far(lambda other, device: far_copy(other, device, other).wait_recv())
        total_ref[...] = combine(far_ref, line, 2 * RING)

    def end():
        each_near(lambda other, device: near_copy(other, device, cell).wait_send())
        each_far(lambda other, device: far_copy(other, device, z).wait_send())

    return SimpleNamespace(near=near, far=far, total=total, end=end)


def exchange_scratch(line, shape):
    dma = pltpu.SemaphoreType.DMA
    near = 2 * RING
    return [
        pltpu.VMEM((near, *shape), jnp.float32),
        pltpu.VMEM(shape, jnp.float32),
        pltpu.VMEM((line, *shape), jnp.float32),
        dma((near,)),
        dma((near,)),
        dma((line,)),
        dma((line,)),
    ]


def exchange_kernel(line, combine, value_ref, total_ref, *scratch):
    stages = exchange_stages(line, combine, value_ref, total_ref, scratch)
    greet_peers(line)
    stages.near()
    stages.far()
    stages.total()
    stages.end()


def add_up(parts, count, weight):
    return lax.fori_loop(1, count, lambda k, total: total + parts[k], parts[0])


def pool_statistics(rows, parts, count, weight):
    mean = lax.fori_loop(1, count, lambda k, total: total + parts[k, 0], parts[0, 0]) / count

    def squares(k, total):
        offset = parts[k, 0] - mean
        return total + parts[k, 1] + (rows * weight) * (offset * offset)

    return jnp.stack([mean, lax.fori_loop(0, count, squares, jnp.zeros_like(mean))])


def exchange(value, combine, collective_id, name):
    line = lax.axis_size("dp") // RING
    vmem = pl.BlockSpec(memory_space=pltpu.VMEM)
    return pl.pallas_call(
        partial(exchange_kernel, line, combine),
        in_specs=[vmem],
        out_specs=vmem,
        out_shape=jax.ShapeDtypeStruct(value.shape, value.dtype),
        scratch_shapes=exchange_scratch(line, value.shape),
        compiler_params=pltpu.CompilerParams(collective_id=collective_id, has_side_effects=True),
        name=name,
    )(value)


KINDS = 10


def source_of(column):
    stream = column // 5
    return 2 * stream + (column - 5 * stream) // 3


def once(shape):
    return pl.BlockSpec(shape, lambda i: (0,) * len(shape), pipeline_mode=pl.Buffered(1))


def at_steps(schedule):
    step = pl.program_id(0)
    for when, work in schedule:
        @pl.when(step == when)
        def _():
            for one in work:
                one()


batch_epsilon = 1e-05


def column_at_step(step):
    turn = jnp.clip(step - 1, 0, KINDS - 1)
    return jnp.where(turn >= 7, turn - 2, jnp.where(turn >= 5, turn + 3, turn))


VECTORS = 9
CHUNKS = 4


def unpack(packed_ref, vectors_ref, bias_ref, linear_ref, planar_ref):
    devices = packed_ref.shape[0]
    bias_rows = REL_B // devices

    def row(k):
        return packed_ref[:, k, :].astype(jnp.bfloat16)

    def lined_up(k, share, first):
        lane = lax.broadcasted_iota(jnp.int32, (128, MODEL_WIDTH), 1)
        spread = (lax.broadcasted_iota(jnp.int32, (128, MODEL_WIDTH), 0) == lax.rem(lane, share)).astype(jnp.bfloat16)
        owner = lax.broadcasted_iota(jnp.int32, (devices, MODEL_WIDTH), 1) // share + first
        mine = lax.broadcasted_iota(jnp.int32, (devices, MODEL_WIDTH), 0) == owner
        whole = dot_nn(row(k), spread)
        return jnp.sum(jnp.where(mine, whole, jnp.zeros_like(whole)), axis=0, keepdims=True)

    def table(first, width, shift):
        bucket = jnp.clip(lax.broadcasted_iota(jnp.int32, (devices, width), 1) - shift, 0, REL_B - 1)
        start = lax.broadcasted_iota(jnp.int32, (devices, width), 0) * bias_rows
        total = None
        for k in range(bias_rows):
            part = dot_tn(row(first + k), (bucket == start + k).astype(jnp.bfloat16))
            total = part if total is None else total + part
        return total

    vectors_ref[...] = jnp.zeros_like(vectors_ref)
    for k in range(VECTORS):
        vectors_ref[k : k + 1, :] = lined_up(2 * bias_rows + k, MODEL_WIDTH // devices, 0)
    share = CHUNKS * MODEL_WIDTH // devices
    for k in range(CHUNKS):
        bias_ref[k] = lined_up(2 * bias_rows + VECTORS, share, k * (MODEL_WIDTH // share))
    linear = table(0, 2 * PAGE_TOKENS, PAGE_TOKENS - 1 - REL_B // 2)
    planar = table(bias_rows, SP_B, 0)
    for head in range(HEADS):
        linear_ref[head] = linear[head : head + 1, :]
        planar_ref[head] = planar[head : head + 1, :]


def forward_kernel(line, count, token_total, *refs):
    (
        features_ref, backbone_hbm, table_hbm, text_ref, hits_ref, packed_ref, weight_ref, rows_ref, cols_ref,
    ) = refs[:9]
    ins = refs[9 : 9 + count]
    (
        proj_ref, merged_ref, probs_ref, lefts_ref, start_ref, normal_ref, scale_ref, vectors_ref, bias_ref,
    ) = refs[9 + count : 18 + count]
    outs = refs[18 + count : 18 + 2 * count]
    box_ref, conv_ref, local_ref, pooled_ref, linear_ref, planar_ref = refs[18 + 2 * count : 24 + 2 * count]
    backbone_ref, table_ref, fetch_sem, *rest = refs[24 + 2 * count :]
    rows = features_ref.shape[0]
    sums = exchange_stages(line, partial(pool_statistics, float(rows)), local_ref, pooled_ref, rest[:7])
    stages = gather_stages(line, ins[:-1], outs[:-1], rest[7:16])
    plane = flat_gather_stages(line, ins[-1:], outs[-1:], rest[16:])
    step = pl.program_id(0)

    def vector(k):
        return vectors_ref[k : k + 1, :]

    def hit_rows(stream):
        return jnp.broadcast_to(hits_ref[:, 4 + stream : 5 + stream] == 1, (rows, MODEL_WIDTH))

    @pl.when(step == 0)
    def _():
        fetches = [
            pltpu.make_async_copy(source, target, fetch_sem.at[k])
            for k, (source, target) in enumerate(((backbone_hbm, backbone_ref), (table_hbm, table_ref)))
        ]
        for fetch in fetches:
            fetch.start()
        greet_peers(line)
        stages.start_line()
        fetches[0].wait()
        conv = dot_nn(features_ref[...], backbone_ref[...])
        mean = jnp.mean(conv, axis=0, keepdims=True)
        center = conv - mean
        conv_ref[...] = conv
        local_ref[0] = mean
        local_ref[1] = jnp.sum(center * center, axis=0, keepdims=True)
        sums.near()
        plane.start()
        stages.start_ring()
        unpack(packed_ref, vectors_ref, bias_ref, linear_ref, planar_ref)
        make_boxes(rows_ref, cols_ref, box_ref)
        text_start = jnp.where(hit_rows(0), vector(2), text_ref[...].astype(jnp.float32))
        start_ref[...] = text_start
        lefts_ref[0] = text_start.astype(jnp.bfloat16)
        coords = lax.broadcasted_iota(jnp.int32, (rows, COORDS), 1)
        fetches[1].wait()
        for stream in range(2):
            space = None
            for axis in range(2):
                place = 2 * stream + axis
                hit = (coords == cols_ref[:, place : place + 1]).astype(jnp.bfloat16)
                part = dot_nn(hit, table_ref[:, axis * MODEL_WIDTH : (axis + 1) * MODEL_WIDTH])
                space = part if space is None else space + part
            lefts_ref[2 * stream + 1] = space.astype(jnp.bfloat16)
        sums.far()

    @pl.when(jnp.logical_and(step >= 1, step <= KINDS))
    def _():
        column = column_at_step(step)
        columns = pl.ds(pl.multiple_of(column * MODEL_WIDTH, MODEL_WIDTH), MODEL_WIDTH)
        proj_ref[:, columns] = dot_nn(lefts_ref[source_of(column)], weight_ref[...]).astype(jnp.bfloat16)

    @pl.when(step == 7)
    def _():
        sums.total()
        inverse = lax.rsqrt(pooled_ref[1] / token_total + batch_epsilon)
        normal = (conv_ref[...] - pooled_ref[0]) * inverse
        normal_ref[...] = normal
        scale_ref[...] = jnp.broadcast_to(vector(0) * inverse, scale_ref.shape)
        region_start = jnp.where(hit_rows(1), vector(3), normal * vector(0) + vector(1))
        start_ref[...] += region_start
        lefts_ref[2] = region_start.astype(jnp.bfloat16)

    @pl.when(step > KINDS)
    def _():
        attend_pair(step - 1 - KINDS, proj_ref, linear_ref, planar_ref, box_ref, merged_ref, probs_ref)

    def along(k):
        return lambda: spread(line, 3, k, 1, stages.along)

    def around(k):
        return lambda: spread(line, 4, k, 0, stages.around)

    def flat(k):
        return lambda: spread(line, 3, k, 1, plane.along)

    def home(k):
        return lambda: spread(line, 4, k, 0, stages.home)

    at_steps(
        [
            (1, [along(0), around(0)]),
            (5, [plane.around]),
            (8, [along(1)]),
            (11, [around(1), plane.home]),
            (13, [along(2), home(0)]),
            (14, [flat(0)]),
            (15, [around(2), home(1)]),
            (16, [flat(1), around(3), home(2), flat(2), home(3), sums.end, stages.end, plane.end]),
        ]
    )


def forward_layer(
    features, backbone, table, text, hits, packed, weights, anchor_rows, anchor_cols, shards, token_total,
    collective_id,
):
    dp = lax.axis_size("dp")
    line = dp // RING
    count = len(shards)
    anywhere = pl.BlockSpec(memory_space=pl.ANY)
    width = weights.shape[1]
    page = (PAGE_TOKENS, MODEL_WIDTH)
    f32, bf16 = jnp.float32, jnp.bfloat16

    def pair_at(i):
        return jnp.maximum(i - 1 - KINDS, 0)

    def whole(shape):
        return pl.BlockSpec(shape, lambda i: (0,) * len(shape))

    outs = [
        ((PAGE_TOKENS, width), bf16, whole((PAGE_TOKENS, width))),
        (page, bf16, pl.BlockSpec((PAGE_TOKENS, LANES), lambda i: (0, pair_at(i)))),
        (
            (2, HEADS, PAGE_TOKENS, PAGE_TOKENS), f32,
            pl.BlockSpec((2, 2, PAGE_TOKENS, PAGE_TOKENS), lambda i: (0, pair_at(i), 0, 0)),
        ),
        ((4, *page), bf16, whole((4, *page))),
        (page, f32, whole(page)),
        (page, f32, whole(page)),
        ((8, MODEL_WIDTH), f32, whole((8, MODEL_WIDTH))),
        ((16, MODEL_WIDTH), f32, whole((16, MODEL_WIDTH))),
        ((CHUNKS, 1, MODEL_WIDTH), f32, whole((CHUNKS, 1, MODEL_WIDTH))),
        *(((2 * dp, *shard.shape), shard.dtype, anywhere) for shard in shards[:-1]),
        ((dp, 2, *shards[-1].shape), shards[-1].dtype, anywhere),
    ]
    pool = (2, 1, MODEL_WIDTH)
    return pl.pallas_call(
        partial(forward_kernel, line, count, float(token_total)),
        grid=(1 + KINDS + PAIRS,),
        in_specs=[
            once(features.shape),
            anywhere,
            anywhere,
            once(text.shape),
            once(hits.shape),
            once(packed.shape),
            pl.BlockSpec((MODEL_WIDTH, MODEL_WIDTH), lambda i: (0, column_at_step(i))),
            once(anchor_rows.shape),
            once(anchor_cols.shape),
            *[anywhere] * count,
        ],
        out_specs=[spec for shape, kind, spec in outs],
        out_shape=[jax.ShapeDtypeStruct(shape, kind) for shape, kind, spec in outs],
        scratch_shapes=[
            pltpu.VMEM((2, PAGE_TOKENS, PAGE_TOKENS), jnp.int32),
            pltpu.VMEM(page, f32),
            pltpu.VMEM(pool, f32),
            pltpu.VMEM(pool, f32),
            pltpu.VMEM((HEADS, 1, 2 * PAGE_TOKENS), f32),
            pltpu.VMEM((HEADS, 1, SP_B), f32),
            pltpu.VMEM(backbone.shape, bf16),
            pltpu.VMEM(table.shape, bf16),
            pltpu.SemaphoreType.DMA((2,)),
            *exchange_scratch(line, pool),
            *gather_sems(line, count - 1),
            *flat_gather_sems(line, 1),
        ],
        compiler_params=pltpu.CompilerParams(
            collective_id=collective_id, has_side_effects=True, vmem_limit_bytes=62 << 20
        ),
        name="forward_layer",
    )(
        features, backbone, table, text, hits, packed, weights, anchor_rows, anchor_cols, *shards,
    )


TABLE_STEP = PAIRS + KINDS


def backward_kernel(line, count, *refs):
    (
        proj_ref, probs_ref, upstream_ref, rows_ref, cols_ref, lefts_hbm, weight_ref, mixer_grad_hbm, normal_hbm,
        hits_ref,
    ) = refs[:10]
    ins = refs[10 : 10 + count]
    (
        linear_ref, planar_ref, weight_grad_ref, table_grad_ref, text_grad_ref, region_grad_ref, sums_ref,
    ) = refs[10 + count : 17 + count]
    outs = refs[17 + count : 17 + 2 * count]
    grad_ref, turned_left_ref, input_grad_ref = refs[17 + 2 * count : 20 + 2 * count]
    helpers = refs[20 + 2 * count : 24 + 2 * count]
    lefts_ref, mixer_grad_ref, normal_ref, fetch_sem, *rest = refs[24 + 2 * count :]
    stages = scatter_stages(line, ins, outs, rest)
    step = pl.program_id(0)
    fetches = [
        pltpu.make_async_copy(source, target, fetch_sem.at[k])
        for k, (source, target) in enumerate(
            ((lefts_hbm, lefts_ref), (mixer_grad_hbm, mixer_grad_ref), (normal_hbm, normal_ref))
        )
    ]

    @pl.when(step == 0)
    def _():
        greet(line)
        stages.start()
        for fetch in fetches:
            fetch.start()
        make_places(rows_ref, cols_ref, *helpers)
        spread(line, 4, 0, 0, stages.first)

    def first(k):
        return lambda: spread(line, 4, k, 0, stages.first)

    def second(k):
        return lambda: spread(line, 4, k, 0, stages.second)

    def third(k):
        return lambda: spread(line, 4, k, 0, stages.third)

    slots = {
        1: [first(1)],
        5: [second(0), first(2)],
        9: [first(3), second(1)],
        17: [third(0), second(2)],
        21: [second(3)],
    }

    def pump(sub):
        at_steps([(slot // 4, work) for slot, work in slots.items() if slot % 4 == sub])

    @pl.when(step < PAIRS)
    def _():
        attend_back_pair(step, pump, proj_ref, probs_ref, upstream_ref, grad_ref, linear_ref, planar_ref, *helpers)

    @pl.when(jnp.logical_and(step >= PAIRS, step < TABLE_STEP))
    def _():
        column = step - PAIRS

        @pl.when(column == 0)
        def _():
            for fetch in fetches:
                fetch.wait()

        source = source_of(column)
        fresh = jnp.logical_or(column == 0, source != source_of(jnp.maximum(column - 1, 0)))
        grads = grad_ref[:, pl.ds(pl.multiple_of(column * MODEL_WIDTH, MODEL_WIDTH), MODEL_WIDTH)]

        @pl.when(fresh)
        def _():
            turned_left_ref[...] = lefts_ref[source].T

        weight_grad_ref[...] = dot_nn(turned_left_ref[...], grads).astype(jnp.bfloat16)
        back = dot_nt(grads, weight_ref[...])

        @pl.when(fresh)
        def _():
            input_grad_ref[source] = back

        @pl.when(jnp.logical_not(fresh))
        def _():
            input_grad_ref[source] += back

    @pl.when(step >= TABLE_STEP)
    def _():
        axis = step - TABLE_STEP
        coords = lax.broadcasted_iota(jnp.int32, (COORDS, PAGE_TOKENS), 0)
        total = None
        for stream in range(2):
            hit = (coords == rows_ref[pl.ds(2 * stream + axis, 1), :]).astype(jnp.bfloat16)
            part = dot_nn(hit, input_grad_ref[2 * stream + 1].astype(jnp.bfloat16))
            total = part if total is None else total + part
        table_grad_ref[...] = total.astype(jnp.bfloat16)

    @pl.when(step == TABLE_STEP + 1)
    def _():
        mixer_grad = mixer_grad_ref[...]
        sums_ref[...] = jnp.zeros_like(sums_ref)
        for stream, out_ref in enumerate((text_grad_ref, region_grad_ref)):
            grad = mixer_grad + input_grad_ref[2 * stream]
            hit = jnp.broadcast_to(hits_ref[:, 4 + stream : 5 + stream] == 1, grad.shape)
            zero = jnp.zeros_like(grad)
            kept = jnp.where(hit, zero, grad)
            out_ref[...] = kept
            sums_ref[stream : stream + 1, :] = jnp.sum(jnp.where(hit, grad, zero), axis=0, keepdims=True)
            if stream == 1:
                sums_ref[2:3, :] = jnp.sum(kept, axis=0, keepdims=True)
                sums_ref[3:4, :] = jnp.sum(kept * normal_ref[...], axis=0, keepdims=True)

    at_steps(
        [(PAIRS, [third(1)]), (PAIRS + 7, [third(2)]), (TABLE_STEP + 1, [third(3), stages.end])]
    )


def backward_layer(
    proj, probs, upstream, anchor_rows, anchor_cols, lefts, weights, mixer_grad, normal, hits, grads, collective_id
):
    dp = lax.axis_size("dp")
    line = dp // RING
    count = len(grads)
    blocks = [(grad.shape[1:], grad.dtype) for grad in grads]
    anywhere = pl.BlockSpec(memory_space=pl.ANY)
    page = (PAGE_TOKENS, MODEL_WIDTH)

    def pair_at(i):
        return jnp.minimum(i, PAIRS - 1)

    def column_at(i):
        return jnp.clip(i - PAIRS, 0, KINDS - 1)

    return pl.pallas_call(
        partial(backward_kernel, line, count),
        grid=(TABLE_STEP + 2,),
        in_specs=[
            once(proj.shape),
            pl.BlockSpec((2, 2, PAGE_TOKENS, PAGE_TOKENS), lambda i: (0, pair_at(i), 0, 0)),
            pl.BlockSpec((PAGE_TOKENS, LANES), lambda i: (0, pair_at(i))),
            once(anchor_rows.shape),
            once(anchor_cols.shape),
            anywhere,
            pl.BlockSpec((MODEL_WIDTH, MODEL_WIDTH), lambda i: (0, column_at(i))),
            anywhere,
            anywhere,
            once(hits.shape),
            *[anywhere] * count,
        ],
        out_specs=[
            pl.BlockSpec((HEADS, 1, 2 * PAGE_TOKENS), lambda i: (0, 0, 0)),
            pl.BlockSpec((HEADS, 1, SP_B), lambda i: (0, 0, 0)),
            pl.BlockSpec((MODEL_WIDTH, MODEL_WIDTH), lambda i: (0, column_at(i))),
            pl.BlockSpec((COORDS, MODEL_WIDTH), lambda i: (0, jnp.maximum(i - TABLE_STEP, 0))),
            pl.BlockSpec(page, lambda i: (0, 0)),
            pl.BlockSpec(page, lambda i: (0, 0)),
            pl.BlockSpec((8, MODEL_WIDTH), lambda i: (0, 0)),
            *(pl.BlockSpec(shape, lambda i: (0, 0)) for shape, kind in blocks),
        ],
        out_shape=[
            jax.ShapeDtypeStruct((HEADS, 1, 2 * PAGE_TOKENS), jnp.float32),
            jax.ShapeDtypeStruct((HEADS, 1, SP_B), jnp.float32),
            jax.ShapeDtypeStruct(weights.shape, jnp.bfloat16),
            jax.ShapeDtypeStruct((COORDS, 2 * MODEL_WIDTH), jnp.bfloat16),
            jax.ShapeDtypeStruct(page, jnp.float32),
            jax.ShapeDtypeStruct(page, jnp.float32),
            jax.ShapeDtypeStruct((8, MODEL_WIDTH), jnp.float32),
            *(jax.ShapeDtypeStruct(shape, jnp.float32) for shape, kind in blocks),
        ],
        scratch_shapes=[
            pltpu.VMEM(proj.shape, jnp.bfloat16),
            pltpu.VMEM((MODEL_WIDTH, PAGE_TOKENS), jnp.bfloat16),
            pltpu.VMEM((4, *page), jnp.float32),
            pltpu.VMEM((2, 4 * PAGE_TOKENS, SP_B), jnp.bfloat16),
            pltpu.VMEM((2, 128, PAGE_TOKENS), jnp.bfloat16),
            pltpu.VMEM((2, 4, PAGE_TOKENS, PAGE_TOKENS), jnp.bfloat16),
            pltpu.VMEM((PAGE_TOKENS, PAGE_TOKENS), jnp.bfloat16),
            pltpu.VMEM(lefts.shape, jnp.bfloat16),
            pltpu.VMEM(page, jnp.float32),
            pltpu.VMEM(page, jnp.float32),
            pltpu.SemaphoreType.DMA((3,)),
            *scatter_scratch(line, blocks),
        ],
        compiler_params=pltpu.CompilerParams(
            collective_id=collective_id, has_side_effects=True, vmem_limit_bytes=63 << 20
        ),
        name="backward_layer",
    )(
        proj, probs, upstream, anchor_rows, anchor_cols, lefts, weights, mixer_grad, normal, hits,
        *(grad.reshape(line * RING, 2, *grad.shape[1:]) for grad in grads),
    )


def last_kernel(line, count, token_total, *refs):
    sums_ref, kept_ref, normal_ref, scale_ref, features_hbm, backbone_hbm = refs[:6]
    ins = refs[6 : 7 + count]
    feature_grad_ref, total_ref = refs[7 + count : 9 + count]
    outs = refs[9 + count : 11 + 2 * count]
    turned_ref, conv_grad_ref, late_ref = refs[11 + 2 * count : 14 + 2 * count]
    rest = refs[14 + 2 * count :]
    features_ref, backbone_ref, fetch_sem, local_ref, *rest = rest
    sums = exchange_stages(line, add_up, local_ref, total_ref, rest[:7])
    stop = 7 + 5 * count + 9
    early = scatter_stages(line, ins[:count], outs[:count], rest[7:stop])
    late = scatter_stages(line, [late_ref], outs[count : count + 1], rest[stop : stop + 14])
    flat = flat_scatter_stages(line, ins[count:], outs[count + 1 :], rest[stop + 14 :])
    share = late_ref.shape[2]

    def first(stages, k):
        spread(line, 4, k, 0, stages.first)

    def second(stages, k):
        spread(line, 4, k, 0, stages.second)

    def third(stages, k):
        spread(line, 4, k, 0, stages.third)

    fetches = [
        pltpu.make_async_copy(source, target, fetch_sem.at[k])
        for k, (source, target) in enumerate(((features_hbm, features_ref), (backbone_hbm, backbone_ref)))
    ]
    greet_peers(line)
    local_ref[...] = sums_ref[2:4, :]
    sums.near()
    flat.start()
    early.start()
    for fetch in fetches:
        fetch.start()
    sums.far()
    first(flat, 0)
    first(early, 0)
    first(early, 1)
    sums.total()
    conv_grad_ref[...] = (
        scale_ref[0:1, :]
        * (kept_ref[...] - total_ref[0:1, :] / token_total - normal_ref[...] * (total_ref[1:2, :] / token_total))
    ).astype(jnp.bfloat16)
    second(early, 0)
    first(flat, 1)
    first(early, 2)
    first(early, 3)

    for fetch in fetches:
        fetch.wait()

    def turn(k, unused):
        columns = pl.ds(pl.multiple_of(k * 512, 512), 512)
        turned_ref[columns, :] = features_ref[:, columns].T
        return unused

    lax.fori_loop(0, features_ref.shape[1] // 512, turn, 0)
    width = min(512, 2 * share * line * RING)

    def backbone(k, unused):
        rows = pl.ds(pl.multiple_of(k * width, width), width)
        block = dot_nn(turned_ref[rows, :], conv_grad_ref[...])
        places = width // (2 * share)
        late_ref[pl.ds(k * places, places)] = block.reshape(places, 2, share, MODEL_WIDTH).astype(jnp.bfloat16)
        return unused

    lax.fori_loop(0, features_ref.shape[1] // width, backbone, 0)
    late.start()
    for k in range(4):
        first(late, k)
    first(flat, 2)
    second(early, 1)
    third(early, 0)

    def feature(k, unused):
        columns = pl.ds(pl.multiple_of(k * 512, 512), 512)
        feature_grad_ref[:, columns] = dot_nt(conv_grad_ref[...], backbone_ref[columns, :])
        return unused

    lax.fori_loop(0, features_ref.shape[1] // 512, feature, 0)
    first(flat, 3)
    for k in range(4):
        second(late, k)
    second(early, 2)
    flat.second()
    second(early, 3)
    third(early, 1)
    third(late, 0)
    third(late, 1)
    third(early, 2)
    third(late, 2)
    flat.third()
    third(early, 3)
    third(late, 3)
    sums.end()
    early.end()
    late.end()
    flat.end()


def last_layer(
    sums, kept, normal, scale, features, backbone, grads, flat_grad, token_total, collective_id
):
    dp = lax.axis_size("dp")
    line = dp // RING
    count = len(grads)
    blocks = [(grad.shape[1:], grad.dtype) for grad in grads]
    flat = [(flat_grad.shape[1:], flat_grad.dtype)]
    pair = (2, MODEL_WIDTH)
    channels = backbone.shape[0]
    late = [((channels // (2 * dp), MODEL_WIDTH), jnp.bfloat16)]
    anywhere = pl.BlockSpec(memory_space=pl.ANY)
    vmem = pl.BlockSpec(memory_space=pltpu.VMEM)
    return pl.pallas_call(
        partial(last_kernel, line, count, float(token_total)),
        in_specs=[*[vmem] * 4, *[anywhere] * (count + 3)],
        out_specs=[vmem] * (4 + count),
        out_shape=[
            jax.ShapeDtypeStruct(features.shape, jnp.float32),
            jax.ShapeDtypeStruct(pair, jnp.float32),
            *(jax.ShapeDtypeStruct(shape, jnp.float32) for shape, kind in blocks + late + flat),
        ],
        scratch_shapes=[
            pltpu.VMEM((channels, PAGE_TOKENS), jnp.bfloat16),
            pltpu.VMEM(kept.shape, jnp.bfloat16),
            pltpu.VMEM((dp, 2, *late[0][0]), jnp.bfloat16),
            pltpu.VMEM(features.shape, jnp.bfloat16),
            pltpu.VMEM(backbone.shape, jnp.bfloat16),
            pltpu.SemaphoreType.DMA((2,)),
            pltpu.VMEM(pair, jnp.float32),
            *exchange_scratch(line, pair),
            *scatter_scratch(line, blocks),
            *scatter_scratch(line, late),
            *flat_scatter_scratch(line, flat),
        ],
        compiler_params=pltpu.CompilerParams(
            collective_id=collective_id, has_side_effects=True, vmem_limit_bytes=63 << 20
        ),
        name="last_layer",
    )(
        sums, kept, normal, scale, features, backbone,
        *(grad.reshape(line * RING, 2, *grad.shape[1:]) for grad in [*grads, flat_grad]),
    )


def finish_kernel(pieces, share, expand_share, bias_rows, *refs):
    given = pieces[-1][0] + 1
    count = len(pieces)
    ins = refs[:given]
    small_ref, total_ref = refs[given : given + 2]
    refs = refs[given + 2 :]
    outs, small_outs, staged = refs[:count], refs[count : count + 12], refs[count + 12 : count + 24]
    sems, small_sems = refs[count + 24 :]
    copies = [
        pltpu.make_async_copy(ins[k].at[:, pl.ds(start, width)], outs[place], sems.at[place])
        for place, (k, start, width) in enumerate(pieces)
    ]
    for copy in copies:
        copy.start()
    staged[0][...] = small_ref[:bias_rows, :HEADS]
    staged[1][...] = small_ref[bias_rows : 2 * bias_rows, :HEADS]
    for k in range(7):
        staged[2 + k][...] = small_ref[2 * bias_rows + k : 2 * bias_rows + k + 1, :share]
    staged[9][...] = small_ref[2 * bias_rows + 7 : 2 * bias_rows + 8, :expand_share]
    owner = (lax.axis_index("dp") * 2 + lax.axis_index("pair")) * share
    chosen = lax.broadcasted_iota(jnp.int32, (MODEL_WIDTH, 128), 0) == (
        lax.broadcasted_iota(jnp.int32, (MODEL_WIDTH, 128), 1) + owner
    )
    owned = lax.dot_general(
        total_ref[...], chosen.astype(jnp.float32), (((1,), (0,)), ((), ())),
        precision=lax.Precision.HIGHEST, preferred_element_type=jnp.float32,
    )
    for k in range(2):
        staged[10 + k][...] = owned[k : k + 1, :share]
    small_copies = [pltpu.make_async_copy(staged[k], small_outs[k], small_sems.at[k]) for k in range(12)]
    for copy in small_copies:
        copy.start()
    for copy in copies + small_copies:
        copy.wait()


def finish(arrays, cut, small, totals, share, expand_share, bias_rows):
    pieces = [(k, 0, array.shape[1]) for k, array in enumerate(arrays)]
    if cut:
        k, start, width = pieces.pop()
        pieces += [(k, 0, cut), (k, cut, width - cut)]
    count = len(pieces)
    anywhere = pl.BlockSpec(memory_space=pl.ANY)
    vmem = pl.BlockSpec(memory_space=pltpu.VMEM)
    shapes = [(bias_rows, HEADS)] * 2 + [(1, share)] * 7 + [(1, expand_share)] + [(1, share)] * 2
    return pl.pallas_call(
        partial(finish_kernel, tuple(pieces), share, expand_share, bias_rows),
        in_specs=[vmem] * (len(arrays) + 2),
        out_specs=[anywhere] * (count + 12),
        out_shape=[
            *(jax.ShapeDtypeStruct((arrays[k].shape[0], width), jnp.float32) for k, start, width in pieces),
            *(jax.ShapeDtypeStruct(shape, jnp.float32) for shape in shapes),
        ],
        scratch_shapes=[
            *(pltpu.VMEM(shape, jnp.float32) for shape in shapes),
            pltpu.SemaphoreType.DMA((count,)),
            pltpu.SemaphoreType.DMA((12,)),
        ],
        name="finish",
    )(*arrays, small, totals)


norm_epsilon = 1e-05


def normal_parts(values):
    center = values - jnp.mean(values, axis=-1, keepdims=True)
    inverse = lax.rsqrt(jnp.mean(center * center, axis=-1, keepdims=True) + norm_epsilon)
    return center * inverse, inverse


def normal_back(normal, inverse, gain, grad):
    scaled = grad * gain
    return inverse * (
        scaled
        - jnp.mean(scaled, axis=-1, keepdims=True)
        - normal * jnp.mean(scaled * normal, axis=-1, keepdims=True)
    )


def mixer_kernel(
    merged_ref, start_ref, cotangent_ref, vectors_ref, bias_ref, merge_ref, expand_hbm, reduce_hbm,
    output_ref, mixer_grad_ref, merged_grad_ref, wide_grad_ref, reduce_grad_ref, sums_ref, bias_grad_ref,
    hidden_ref, normal_ref, inverse_ref, low_ref, active_ref, slope_ref, dense_ref, grad_ref, grad_low_ref,
    turned_ref, expand_ref, reduce_ref, fetch_sem,
):
    step = pl.program_id(0)
    chunk = lax.rem(step, CHUNKS)
    width = expand_ref.shape[1] // CHUNKS
    part = pl.ds(pl.multiple_of(chunk * width, width), width)

    def vector(k):
        return vectors_ref[k : k + 1, :]

    def column_sum(values):
        return jnp.sum(values, axis=0, keepdims=True)

    fetches = [
        pltpu.make_async_copy(source, target, fetch_sem.at[k])
        for k, (source, target) in enumerate(((expand_hbm, expand_ref), (reduce_hbm, reduce_ref)))
    ]

    @pl.when(step == 0)
    def _():
        for fetch in fetches:
            fetch.start()
        normal, inverse = normal_parts(start_ref[...] + dot_nn(merged_ref[...], merge_ref[...]))
        normal_ref[...] = normal
        inverse_ref[...] = jnp.broadcast_to(inverse, inverse_ref.shape)
        hidden = normal * vector(4) + vector(5)
        hidden_ref[...] = hidden
        low_ref[...] = hidden.astype(jnp.bfloat16)
        dense_ref[...] = jnp.zeros_like(dense_ref)
        for fetch in fetches:
            fetch.wait()

    @pl.when(step < CHUNKS)
    def _():
        inner = dot_nn(low_ref[...], expand_ref[:, part]) + bias_ref[chunk]
        share = 0.5 + 0.5 * lax.erf(inner * (0.5**0.5))
        active = (inner * share).astype(jnp.bfloat16)
        active_ref[chunk] = active
        slope_ref[chunk] = share + inner * jnp.exp(-0.5 * inner * inner) * (2.0 * jnp.pi) ** -0.5
        dense_ref[...] += dot_nn(active, reduce_ref[part, :])

    @pl.when(step == CHUNKS - 1)
    def _():
        normal, inverse = normal_parts(hidden_ref[...] + (dense_ref[...] + vector(6)))
        output_ref[...] = (normal * vector(7) + vector(8)).astype(jnp.bfloat16)
        upstream = cotangent_ref[...].astype(jnp.float32)
        grad = normal_back(normal, inverse, vector(7), upstream)
        grad_ref[...] = grad
        grad_low_ref[...] = grad.astype(jnp.bfloat16)
        sums_ref[2:3, :] = column_sum(grad)
        sums_ref[3:4, :] = column_sum(upstream * normal)
        sums_ref[4:5, :] = column_sum(upstream)
        turned_ref[...] = low_ref[...].T

    @pl.when(jnp.logical_and(step >= CHUNKS, step < 2 * CHUNKS))
    def _():
        grad_low = grad_low_ref[...]
        reduce_grad_ref[...] = dot_tn(active_ref[chunk], grad_low).astype(jnp.bfloat16)
        inner_low = (dot_nt(grad_low, reduce_ref[part, :]) * slope_ref[chunk]).astype(jnp.bfloat16)
        bias_grad_ref[chunk] = column_sum(inner_low.astype(jnp.float32))
        wide_grad_ref[...] = dot_nn(turned_ref[...], inner_low).astype(jnp.bfloat16)
        grad_ref[...] += dot_nt(inner_low, expand_ref[:, part])

    @pl.when(step == 2 * CHUNKS)
    def _():
        grad = grad_ref[...]
        normal = normal_ref[...]
        mixer_grad = normal_back(normal, inverse_ref[:, :1], vector(4), grad)
        mixer_grad_ref[...] = mixer_grad
        sums_ref[0:1, :] = column_sum(grad * normal)
        sums_ref[1:2, :] = column_sum(grad)
        low = mixer_grad.astype(jnp.bfloat16)
        wide_grad_ref[...] = dot_tn(merged_ref[...], low).astype(jnp.bfloat16)
        merged_grad_ref[...] = dot_nt(low, merge_ref[...]).astype(jnp.bfloat16)


def mixer_layer(merged, start, cotangent, vectors, bias, w_merge, w_expand, w_reduce):
    rows = merged.shape[0]
    inner = w_expand.shape[1]
    width = inner // CHUNKS
    page = (rows, MODEL_WIDTH)

    def back_at(i):
        return jnp.clip(i - CHUNKS, 0, CHUNKS - 1)

    def whole(shape):
        return pl.BlockSpec(shape, lambda i: (0,) * len(shape))

    f32, bf16 = jnp.float32, jnp.bfloat16
    outs = [
        (page, bf16, whole(page)),
        (page, f32, whole(page)),
        (page, bf16, whole(page)),
        (
            (MODEL_WIDTH, inner + MODEL_WIDTH), bf16,
            pl.BlockSpec((MODEL_WIDTH, width), lambda i: (0, jnp.maximum(i - CHUNKS, 0))),
        ),
        ((inner, MODEL_WIDTH), bf16, pl.BlockSpec((width, MODEL_WIDTH), lambda i: (back_at(i), 0))),
        ((8, MODEL_WIDTH), f32, whole((8, MODEL_WIDTH))),
        ((CHUNKS, 1, width), f32, whole((CHUNKS, 1, width))),
    ]
    return pl.pallas_call(
        mixer_kernel,
        grid=(2 * CHUNKS + 1,),
        in_specs=[
            once(page),
            once(page),
            once(page),
            once(vectors.shape),
            once(bias.shape),
            once(w_merge.shape),
            pl.BlockSpec(memory_space=pl.ANY),
            pl.BlockSpec(memory_space=pl.ANY),
        ],
        out_specs=[spec for shape, kind, spec in outs],
        out_shape=[jax.ShapeDtypeStruct(shape, kind) for shape, kind, spec in outs],
        scratch_shapes=[
            pltpu.VMEM(page, f32),
            pltpu.VMEM(page, f32),
            pltpu.VMEM((rows, 128), f32),
            pltpu.VMEM(page, bf16),
            pltpu.VMEM((CHUNKS, rows, width), bf16),
            pltpu.VMEM((CHUNKS, rows, width), f32),
            pltpu.VMEM(page, f32),
            pltpu.VMEM(page, f32),
            pltpu.VMEM(page, bf16),
            pltpu.VMEM((MODEL_WIDTH, rows), bf16),
            pltpu.VMEM(w_expand.shape, bf16),
            pltpu.VMEM(w_reduce.shape, bf16),
            pltpu.SemaphoreType.DMA((2,)),
        ],
        compiler_params=pltpu.CompilerParams(vmem_limit_bytes=62 << 20),
        name="mixer_layer",
    )(merged, start, cotangent, vectors, bias, w_merge, w_expand, w_reduce)

AXES = ("dp", "pair")


def padded_rows(pieces):
    total = sum(piece.shape[0] for piece in pieces)
    rows = -(-total // 8) * 8
    whole = jnp.zeros((rows, 128), jnp.float32)
    start = 0
    for piece in pieces:
        stop = start + piece.shape[0]
        whole += jnp.pad(piece.astype(jnp.float32), ((start, rows - stop), (0, 128 - piece.shape[1])))
        start = stop
    return whole


def blocks_of(grad, devices):
    blocks = grad.astype(jnp.bfloat16).reshape(devices, grad.shape[0] // devices, grad.shape[1])
    return blocks if blocks.shape[1] % 8 == 0 else blocks.reshape(devices, -1, 128)


def per_device(
    text_inputs,
    region_features,
    text_masked,
    region_masked,
    text_anchors,
    region_anchors,
    backbone_weight,
    batch_gain,
    batch_shift,
    text_blank,
    region_blank,
    position_table,
    stream_weights,
    linear_bias,
    planar_bias,
    merge_weight,
    mixer_gain,
    mixer_shift,
    expand_weight,
    expand_bias,
    reduce_weight,
    reduce_bias,
    output_gain,
    output_shift,
    cotangent,
):
    devices = lax.axis_size(AXES)
    row_count = text_inputs.shape[0]
    token_total = row_count * devices
    share = MODEL_WIDTH // devices
    expand_share = expand_bias.shape[0]
    bias_rows = REL_B // devices
    vectors = (
        batch_gain, batch_shift, text_blank, region_blank, mixer_gain, mixer_shift, reduce_bias,
        output_gain, output_shift, expand_bias,
    )
    small = padded_rows([linear_bias, planar_bias, *(vector[None, :] for vector in vectors)])
    packed, w_backbone, w_stream, w_table = gather_all(
        (small, backbone_weight, stream_weights), (position_table,), 0
    )
    w_backbone, w_table, w_stream = (
        whole.reshape(-1, whole.shape[-1]) for whole in (w_backbone, w_table, w_stream)
    )

    anchor_rows = jnp.concatenate(
        [text_anchors, region_anchors, text_masked[None, :], region_masked[None, :]], axis=0
    )
    anchor_cols = anchor_rows.T
    hits = anchor_cols
    proj, merged_low, probs, lefts, start_sum, normal_feat, batch_scale, w_vectors, w_expand_bias, *wholes = forward_layer(
        region_features, w_backbone, w_table, text_inputs, hits, packed, w_stream, anchor_rows, anchor_cols,
        (expand_weight, reduce_weight, merge_weight), token_total, 4,
    )
    w_expand, w_reduce, w_merge = (whole.reshape(-1, whole.shape[-1]) for whole in wholes)
    (
        layer_output, mixer_in_grad, merged_grad, wide_grad, reduce_weight_grad, mixer_sums, expand_bias_grad,
    ) = mixer_layer(
        merged_low, start_sum, cotangent, w_vectors, w_expand_bias,
        w_merge, w_expand, w_reduce,
    )
    early = (reduce_weight_grad, wide_grad)
    (
        linear_sums, planar_sums, stream_weights_grad, position_table_grad, text_gradient, region_kept,
        start_sums, *early_shares,
    ) = backward_layer(
        proj, probs, merged_grad, anchor_rows, anchor_cols, lefts, w_stream, mixer_in_grad, normal_feat, hits,
        [blocks_of(grad, devices) for grad in early], 5,
    )
    vector_grads = jnp.concatenate([start_sums[:2], mixer_sums[:5]], axis=0)
    pieces = [
        linear_folded(linear_sums[:, 0]).T.reshape(devices, bias_rows, HEADS),
        planar_sums[:, 0].T.reshape(devices, bias_rows, HEADS),
        vector_grads.reshape(7, devices, share).transpose(1, 0, 2),
        expand_bias_grad.reshape(devices, 1, expand_share),
    ]
    rows = sum(piece.shape[1] for piece in pieces)
    pieces = [jnp.pad(piece, ((0, 0), (0, 0), (0, 128 - piece.shape[2]))) for piece in pieces]
    small_grads = jnp.pad(jnp.concatenate(pieces, axis=1), ((0, 0), (0, -rows % 8), (0, 0)))
    feature_gradient, totals, small, stream_share, backbone_weight_grad, table_share = last_layer(
        start_sums, region_kept, normal_feat, batch_scale, region_features, w_backbone,
        [small_grads, blocks_of(stream_weights_grad, devices)], blocks_of(position_table_grad, devices),
        token_total, 1,
    )
    reduce_share, wide_share = early_shares
    cut = expand_weight.shape[1]
    wides = [wide_share]
    if wide_share.shape[1] != wide_grad.shape[1]:
        wide_share = wide_share.reshape(-1, wide_grad.shape[1])
        wides, cut = [wide_share[:, :cut], wide_share[:, cut:]], 0
    (
        text_gradient, feature_gradient, backbone_weight_grad, table_share, stream_share, reduce_share_grad,
        expand_share_grad, merge_share_grad, linear_grad, planar_grad, *vector_grads,
    ) = finish(
        [
            text_gradient, feature_gradient, backbone_weight_grad, table_share, stream_share, reduce_share, *wides,
        ],
        cut, small, totals, share, expand_share, bias_rows,
    )
    vector_grads = [grad.reshape(-1) for grad in vector_grads]
    return (
        layer_output,
        text_gradient,
        feature_gradient,
        backbone_weight_grad,
        vector_grads[9],
        vector_grads[8],
        vector_grads[0],
        vector_grads[1],
        table_share.reshape(-1, position_table.shape[1]),
        stream_share.reshape(-1, stream_weights.shape[1]),
        linear_grad,
        planar_grad,
        merge_share_grad.reshape(-1, MODEL_WIDTH),
        vector_grads[2],
        vector_grads[3],
        expand_share_grad.reshape(-1, expand_weight.shape[1]),
        vector_grads[7],
        reduce_share_grad.reshape(-1, MODEL_WIDTH),
        vector_grads[4],
        vector_grads[5],
        vector_grads[6],
    )

def solution(mesh):
    in_specs = (
        P(("dp", "pair"), None),
        P(("dp", "pair"), None),
        P(("dp", "pair")),
        P(("dp", "pair")),
        P(None, ("dp", "pair")),
        P(None, ("dp", "pair")),
        P(("dp", "pair"), None),
        P(("dp", "pair")),
        P(("dp", "pair")),
        P(("dp", "pair")),
        P(("dp", "pair")),
        P(("dp", "pair"), None),
        P(("dp", "pair"), None),
        P(("dp", "pair"), None),
        P(("dp", "pair"), None),
        P(("dp", "pair"), None),
        P(("dp", "pair")),
        P(("dp", "pair")),
        P(("dp", "pair"), None),
        P(("dp", "pair")),
        P(("dp", "pair"), None),
        P(("dp", "pair")),
        P(("dp", "pair")),
        P(("dp", "pair")),
        P(("dp", "pair"), None),
    )
    out_specs = (
        P(("dp", "pair"), None),
        P(("dp", "pair"), None),
        P(("dp", "pair"), None),
        P(("dp", "pair"), None),
        P(("dp", "pair")),
        P(("dp", "pair")),
        P(("dp", "pair")),
        P(("dp", "pair")),
        P(("dp", "pair"), None),
        P(("dp", "pair"), None),
        P(("dp", "pair"), None),
        P(("dp", "pair"), None),
        P(("dp", "pair"), None),
        P(("dp", "pair")),
        P(("dp", "pair")),
        P(("dp", "pair"), None),
        P(("dp", "pair")),
        P(("dp", "pair"), None),
        P(("dp", "pair")),
        P(("dp", "pair")),
        P(("dp", "pair")),
    )
    return jax.shard_map(
        per_device, mesh=mesh, in_specs=in_specs, out_specs=out_specs, check_vma=False
    )
```
